32 devices in a mesh: docs: 16 (over z, y, x), blk: 2 (over core).
Axes of the slice: x: 2, y: 2, z: 4, core: 2. Of those that a mesh axis runs over, the one named last changes fastest.
Arguments:
- text_tokens: bfloat16 [16, 736, 768], P('docs', 'blk'), may hold values from -6 to 6
- visual_tokens: bfloat16 [16, 96, 768], P('docs', 'blk'), may hold values from -6 to 6
- text_mask: int32 [16, 736], P('docs'), may hold values from 0 to 1, as said below
- visual_mask: int32 [16, 96], P('docs'), may hold values from 0 to 1, as said below
- w_qkv: bfloat16 [2, 768, 2304], P(None, 'docs'), may hold values from -0.3125 to 0.3125
- w_out: bfloat16 [2, 768, 768], P(None, 'docs'), may hold values from -1.5 to 1.5
- w_gate: bfloat16 [2, 768, 12], P(None, 'docs'), may hold values from -0.21875 to 0.21875
- w_up: bfloat16 [2, 768, 3072], P(None, 'docs'), may hold values from -0.21875 to 0.21875
- w_down: bfloat16 [2, 3072, 768], P(None, 'docs'), may hold values from -0.109375 to 0.109375
- gain_attn: bfloat16 [2, 768], P(None, 'docs'), may hold values from 0.5 to 1.5
- gain_ffn: bfloat16 [2, 768], P(None, 'docs'), may hold values from 0.5 to 1.5
- text_cotangent: bfloat16 [16, 736, 768], P('docs', 'blk'), may hold values from -6 to 6
- visual_cotangent: bfloat16 [16, 96, 768], P('docs', 'blk'), may hold values from -6 to 6
Outputs:
- text_out: bfloat16 [16, 736, 768], P('docs', 'blk')
- visual_out: bfloat16 [16, 96, 768], P('docs', 'blk')
- text_grad: float32 [16, 736, 768], P('docs', 'blk')
- visual_grad: float32 [16, 96, 768], P('docs', 'blk')
- grad_qkv: float32 [2, 768, 2304], P(None, 'docs')
- grad_out: float32 [2, 768, 768], P(None, 'docs')
- grad_gate: float32 [2, 768, 12], P(None, 'docs')
- grad_up: float32 [2, 768, 3072], P(None, 'docs')
- grad_down: float32 [2, 3072, 768], P(None, 'docs')
- grad_gain_attn: float32 [2, 768], P(None, 'docs')
- grad_gain_ffn: float32 [2, 768], P(None, 'docs')
The draws below stay inside these ranges and needn't reach their ends.
Inputs may be any that keep to these rules, and one draw needn't show every extreme that they name: `text_mask`: in each document the slots with mask 1 are a prefix holding at least one eighth of the 736 text slots (and at least one); some document has all 736 text slots valid. `visual_mask`: in each document the slots with mask 1 are a prefix of at least one visual slot; some document has all 96 visual slots valid.
All inputs are finite; a program needn't handle non-finite values.
Results may differ from the reference program's by a relative error of at most 0.017.
Values may be sent and summed in bfloat16 or wider, within the bound.
A program may use at most 256 MiB of HBM per device.

```python
import jax
import jax.numpy as jnp
from jax import lax

D = 768
HEADS = 12
FF = 3072
TS = 736
VS = 96
DOCS = 16


def prefix_mask(key, slot_count, shortest):
    lengths = jax.random.randint(key, (DOCS,), shortest, slot_count + 1)
    chosen = jax.random.randint(jax.random.fold_in(key, 7), (), 0, DOCS)
    lengths = jnp.where(jnp.arange(DOCS) == chosen, slot_count, lengths)
    return (jnp.arange(slot_count)[None, :] < lengths[:, None]).astype(jnp.int32)


def draw_text_mask(key, part):
    key = jax.random.fold_in(key, 11)
    return prefix_mask(key, TS, max(1, TS // 8))


def draw_visual_mask(key, part):
    key = jax.random.fold_in(key, 13)
    return prefix_mask(key, VS, 1)


def spiked(array, stream_key, source, target, parts, factor):
    def block_of(axis_at):
        return (jnp.arange(array.shape[axis_at]) // (array.shape[axis_at] // parts)).reshape((-1,) + (1,) * (array.ndim - 1 - axis_at))

    one_side = jax.random.permutation(stream_key, parts)[block_of(target)]
    second = (block_of(target) + parts // 2) % parts
    return jnp.where((block_of(source) == one_side) | (block_of(source) == second), factor * array, array)


def block_scale(own_key, extent, shards, smallest, top_value):
    level = 1.0
    for axis_at, blocks in shards:
        heights = jax.random.uniform(jax.random.fold_in(jax.random.fold_in(own_key, 6), axis_at), (blocks,), jnp.float32, smallest / len(shards), top_value / len(shards))
        level = level * jnp.repeat(jnp.exp(heights), extent[axis_at] // blocks).reshape((-1,) + (1,) * (len(extent) - 1 - axis_at))
    return level


def bell_draw(stream_key, dims, scale, limit, split=(), dtype=jnp.bfloat16):
    loudness = block_scale(stream_key, dims, split, -0.22, 0.18) if split else 1.0
    result = jax.random.normal(stream_key, dims, jnp.float32) * scale * loudness
    return jnp.minimum(jnp.maximum(result, -limit), limit).astype(dtype)


def noise_with(key, shape, spread, bound, pieces, heavy, held_as=jnp.bfloat16):
    array = spread * jax.random.normal(key, shape, jnp.float32)
    if pieces:
        array = array * block_scale(key, shape, pieces, -0.22, 0.18)
    return jnp.clip(spiked(array, jax.random.fold_in(key, 3), *heavy), -bound, bound).astype(held_as)


def setup_inputs(seed: int = 0) -> dict:
    key_list = jax.random.split(jax.random.key(seed), 14)
    text_tokens = noise_with(key_list[0], (DOCS, TS, D), 1.0, 6.0, ((0, 16), (1, 2)), (0, 2, 16, 2.0))
    visual_tokens = noise_with(key_list[1], (DOCS, VS, D), 1.0, 6.0, ((0, 16), (1, 2)), (0, 2, 16, 2.0))
    text_mask = draw_text_mask(jax.random.fold_in(key_list[13], 71), 0)
    visual_mask = draw_visual_mask(jax.random.fold_in(key_list[13], 71), 0)
    w_qkv = bell_draw(key_list[4], (2, D, 3 * D), (D // 2) ** -0.5, 0.3125, ((1, 16),))
    w_out = bell_draw(key_list[5], (2, D, D), 16 ** -0.5, 1.5, ((1, 16),))
    w_gate = bell_draw(key_list[6], (2, D, HEADS), D ** -0.5, 0.21875, ((1, 16),))
    w_up = bell_draw(key_list[7], (2, D, FF), D ** -0.5, 0.21875, ((1, 16),))
    w_down = bell_draw(key_list[8], (2, FF, D), FF ** -0.5, 0.109375, ((1, 16),))
    gain_attn = jnp.clip(1.0 + 0.1 * jax.random.normal(key_list[9], (2, D), jnp.float32), 0.5, 1.5).astype(jnp.bfloat16)
    gain_ffn = jnp.clip(1.0 + 0.1 * jax.random.normal(key_list[10], (2, D), jnp.float32), 0.5, 1.5).astype(jnp.bfloat16)
    text_cotangent = bell_draw(key_list[11], (DOCS, TS, D), 1.0, 6.0, ((0, 16), (1, 2)))
    visual_cotangent = bell_draw(key_list[12], (DOCS, VS, D), 1.0, 6.0, ((0, 16), (1, 2)))
    return dict(text_tokens=text_tokens, visual_tokens=visual_tokens, text_mask=text_mask, visual_mask=visual_mask, w_qkv=w_qkv, w_out=w_out, w_gate=w_gate, w_up=w_up, w_down=w_down, gain_attn=gain_attn, gain_ffn=gain_ffn, text_cotangent=text_cotangent, visual_cotangent=visual_cotangent)


@jax.custom_vjp
def low(v):
    return lax.optimization_barrier(v.astype(jnp.bfloat16)).astype(jnp.float32)

@jax.custom_vjp
def low_back(v):
    return v

def low_keep(v):
    return (low(v), None)

def low_pass(kept, grad):
    return (grad,)

def back_keep(v):
    return (v, None)

def back_low(kept, grad):
    return (low(grad),)
low.defvjp(low_keep, low_pass)
low_back.defvjp(back_keep, back_low)
epsilon = 1e-05
big_negative = -1e+30
highest = lax.Precision.HIGHEST

def layer_norm(values, gain):
    average = lax.optimization_barrier(jnp.mean(values, -1, keepdims=True))
    centred = values - average
    return centred * lax.rsqrt(lax.optimization_barrier(jnp.mean(centred * centred, -1, keepdims=True)) + epsilon) * gain

def product(left, weight):
    return jnp.dot(left, weight, precision=highest)

def attend(queries, key_part, value_part, key_valid, score_scale):
    scores = low_back(jnp.einsum('qhe,khe->hqk', queries, key_part, precision=highest) * score_scale)
    scores = jnp.where(key_valid[None, None, :], scores, big_negative)
    probs = jax.nn.softmax(scores, axis=-1)
    return low_back(jnp.einsum('hqk,khe->qhe', low(probs), value_part, precision=highest))

def modality_front(tokens, gain, qkv_weight, gate_weight):
    lowered = low(layer_norm(tokens, gain))
    qkv_low = low(low_back(product(lowered, qkv_weight)))
    gates = jax.nn.sigmoid(low_back(product(lowered, gate_weight)))
    return (qkv_low, gates)

def one_document(text_x, visual_x, text_valid, visual_valid, w_qkv, w_out, w_gate, w_up, w_down, gain_attn, gain_ffn):
    head_count = w_gate.shape[2]
    width = w_out.shape[1]
    score_scale = (width // head_count) ** (-0.5)
    fronts = [modality_front(text_x, gain_attn[0], w_qkv[0], w_gate[0]), modality_front(visual_x, gain_attn[1], w_qkv[1], w_gate[1])]
    valids = [text_valid > 0, visual_valid > 0]
    inputs = [text_x, visual_x]

    def split_part(qkv_low, which):
        return qkv_low[:, which * width:(which + 1) * width].reshape(qkv_low.shape[0], head_count, -1)
    results = []
    for index in range(2):
        other = 1 - index
        qkv_low, gates = fronts[index]
        queries = split_part(qkv_low, 0)
        own = attend(queries, split_part(qkv_low, 1), split_part(qkv_low, 2), valids[index], score_scale)
        cross = attend(queries, split_part(fronts[other][0], 1), split_part(fronts[other][0], 2), valids[other], score_scale)
        mixed = gates[..., None] * own + (1.0 - gates[..., None]) * cross
        mix_low = low(mixed.reshape(queries.shape[0], width))
        middle = inputs[index] + low_back(product(mix_low, w_out[index]))
        lowered_mid = low(layer_norm(middle, gain_ffn[index]))
        upward = low_back(product(lowered_mid, w_up[index]))
        branch = low_back(product(low(jax.nn.gelu(upward)), w_down[index]))
        results.append(middle + branch)
    return (results[0], results[1])

def reference(text_tokens, visual_tokens, text_mask, visual_mask, w_qkv, w_out, w_gate, w_up, w_down, gain_attn, gain_ffn, text_cotangent, visual_cotangent):
    params = tuple((weight.astype(jnp.float32) for weight in (w_qkv, w_out, w_gate, w_up, w_down, gain_attn, gain_ffn)))
    checked = jax.checkpoint(one_document)

    def forward(text_x, visual_x, p_qkv, p_out, p_gate, p_up, p_down, p_attn, p_ffn):

        def per_document(item):
            return checked(item[0], item[1], item[2], item[3], p_qkv, p_out, p_gate, p_up, p_down, p_attn, p_ffn)
        return lax.map(per_document, (text_x, visual_x, text_mask, visual_mask))
    outputs, pullback = jax.vjp(forward, text_tokens.astype(jnp.float32), visual_tokens.astype(jnp.float32), params[0], params[1], params[2], params[3], params[4], params[5], params[6])
    grads = pullback((text_cotangent.astype(jnp.float32), visual_cotangent.astype(jnp.float32)))
    return (outputs[0].astype(jnp.bfloat16), outputs[1].astype(jnp.bfloat16), grads[0], grads[1], grads[2], grads[3], grads[4], grads[5], grads[6], grads[7], grads[8])
```

```python
import functools

import jax
import jax.numpy as jnp
from jax import lax
from jax.experimental import pallas as pl
from jax.experimental.pallas import tpu as pltpu
from jax.sharding import PartitionSpec as P

epsilon = 1e-05
big_negative = -1e30
MESH = pl.DeviceIdType.MESH
lane = 128
row_tile = 16
vmem_limit = 56 * 1024 * 1024


def when(conditions, body):
    conditions = [condition for condition in conditions if condition is not None]
    if not conditions:
        body()
        return
    pl.when(functools.reduce(jnp.logical_and, conditions))(body)


class Place:
    def __init__(self, line_size):
        docs = lax.axis_index("docs")
        self.core = lax.axis_index("blk")
        self.line_size = line_size
        self.z, self.y, self.x = docs // 4, (docs // 2) % 2, docs % 2
        self.up_valid = self.z < line_size - 1
        self.down_valid = self.z > 0

    def index(self, z, flip_y=False, flip_x=False):
        y = 1 - self.y if flip_y else self.y
        x = 1 - self.x if flip_x else self.x
        return z * 4 + y * 2 + x

    def device(self, step):
        z, y, x = self.z, self.y, self.x
        docs = {
            "x": z * 4 + y * 2 + 1 - x,
            "y": z * 4 + (1 - y) * 2 + x,
            "up": (z + 1) * 4 + y * 2 + x,
            "down": (z - 1) * 4 + y * 2 + x,
        }[step]
        return (docs, self.core)

    def greet(self, other_core):
        barrier = pltpu.get_barrier_semaphore()

        def signal(device):
            pl.semaphore_signal(barrier, inc=1, device_id=device, device_id_type=MESH)

        signal(self.device("x"))
        signal(self.device("y"))
        pl.when(self.up_valid)(lambda: signal(self.device("up")))
        pl.when(self.down_valid)(lambda: signal(self.device("down")))
        if other_core:
            signal((self.index(self.z), 1 - self.core))
        peers = 3 if other_core else 2
        for valid in (self.up_valid, self.down_valid):
            peers = peers + jnp.where(valid, 1, 0)
        pl.semaphore_wait(barrier, peers)


targets = ("x", "y", "up", "down")


def dot(left, right):
    return jnp.dot(left, right, preferred_element_type=jnp.float32)


def dot_back(left, right):
    return lax.dot_general(left, right, (((1,), (1,)), ((), ())), preferred_element_type=jnp.float32)


def dot_rows(left, right):
    return lax.dot_general(left, right, (((0,), (0,)), ((), ())), preferred_element_type=jnp.float32)


def normalize(values):
    centred = values - jnp.mean(values, -1, keepdims=True)
    inverse = lax.rsqrt(jnp.mean(centred * centred, -1, keepdims=True) + epsilon)
    return centred * inverse, inverse


def over_rows(first, last, size, body):
    def step(at, carry):
        body(pl.ds(pl.multiple_of(first + at * size, row_tile), size))
        return carry

    lax.fori_loop(0, (last - first) // size, step, 0)


def over_columns(count, size, body):
    def step(at, carry):
        body(pl.ds(pl.multiple_of(at * size, size), size))
        return carry

    lax.fori_loop(0, count // size, step, 0)


def gelu_both(value):
    root = 0.7978845608028654
    square = value * value
    bent = jnp.tanh(root * (value + 0.044715 * value * square))
    cdf = 0.5 * (1.0 + bent)
    slope = cdf + 0.5 * value * (1.0 - bent * bent) * (root * (1.0 + 0.134145 * square))
    return value * cdf, slope


class Gather:
    def __init__(self, place, split_rows, owns, outs, send_sems, recv_sems, local_sems):
        self.place, self.split_rows, self.owns, self.outs = place, split_rows, owns, outs
        self.send_sems, self.recv_sems, self.local_sems = send_sems, recv_sems, local_sems
        self.sends = []

    def has(self, at, source_z):
        half = self.place.line_size // 2
        return source_z // half == self.place.core if self.split_rows[at] else None

    def block(self, at, source, s):
        rows = self.owns[at].shape[1]
        if self.split_rows[at]:
            source = source - self.place.core * (self.place.line_size // 2) * 4
        return self.outs[at].at[s, pl.ds(pl.multiple_of(source * rows, row_tile), rows), :]

    def mine(self, at, s):
        width = self.outs[at].shape[2]
        if self.owns[at].shape[2] == width:
            return self.owns[at].at[s]
        first = pl.multiple_of(self.place.core * width, lane)
        return self.owns[at].at[s, :, pl.ds(first, width)]

    def copy(self, at, source, s, step, own=False):
        return pltpu.make_async_remote_copy(
            src_ref=self.mine(at, s) if own else self.block(at, source, s),
            dst_ref=self.block(at, source, s),
            send_sem=self.send_sems.at[at, source, s, targets.index(step)],
            recv_sem=self.recv_sems.at[at, source, s],
            device_id=self.place.device(step),
            device_id_type=MESH,
        )

    def local(self, at, s):
        here = self.place.index(self.place.z)
        return pltpu.make_async_copy(
            self.mine(at, s), self.block(at, here, s), self.local_sems.at[at, s]
        )

    def send(self, conditions, *which):
        when(conditions, lambda: self.copy(*which).start())
        self.sends.append((conditions, which))

    def arrived(self, at, source, s):
        self.copy(at, source, s, "x").wait_recv()

    def own(self, at):
        place = self.place
        here = place.index(place.z)
        held = [self.has(at, place.z)]
        for s in range(2):
            when(held, lambda: self.local(at, s).start())
            self.send(held + [place.up_valid], at, here, s, "up", True)
            self.send(held + [place.down_valid], at, here, s, "down", True)
            self.send(held, at, here, s, "x", True)
            self.send(held, at, here, s, "y", True)

    def units(self, distance):
        place = self.place
        if distance == 0:
            return [(place.z, None, None)]
        return [
            (place.z - distance, place.z >= distance, ("up", place.up_valid)),
            (place.z + distance, place.z < place.line_size - distance, ("down", place.down_valid)),
        ]

    def relay(self, at, distance):
        for source_z, valid, _ in self.units(distance):
            conditions = [valid, self.has(at, source_z)]
            beside_x = self.place.index(source_z, flip_x=True)
            beside_y = self.place.index(source_z, flip_y=True)
            when(conditions, lambda: self.arrived(at, beside_x, 0))
            self.send(conditions, at, beside_x, 0, "y")
            when(conditions, lambda: self.arrived(at, beside_y, 1))
            self.send(conditions, at, beside_y, 1, "x")

    def line(self, at, distance):
        for source_z, valid, (step, onward) in self.units(distance):
            source = self.place.index(source_z)
            conditions = [valid, self.has(at, source_z)]
            for s in range(2):
                when(conditions, lambda: self.arrived(at, source, s))
                self.send(conditions + [onward], at, source, s, step)
                self.send(conditions, at, source, s, "x")
                self.send(conditions, at, source, s, "y")

    def round(self, at, distance):
        self.relay(at, distance - 1)
        if distance < self.place.line_size:
            self.line(at, distance)

    def rest(self, at):
        for distance in range(self.place.line_size):
            for source_z, valid, _ in self.units(distance):

                def wait():
                    self.arrived(at, self.place.index(source_z, flip_x=True), 1)
                    self.arrived(at, self.place.index(source_z, flip_y=True), 0)
                    for s in range(2):
                        self.arrived(at, self.place.index(source_z, True, True), s)

                when([valid, self.has(at, source_z)], wait)
        for s in range(2):
            when([self.has(at, self.place.z)], lambda: self.local(at, s).wait())

    def finish(self):
        for conditions, which in self.sends:
            when(conditions, lambda: self.copy(*which).wait_send())


class Moves:
    def __init__(self, place, local_sems, send_sems, recv_sems):
        self.other = (place.index(place.z), 1 - place.core)
        self.local_sems, self.send_sems, self.recv_sems = local_sems, send_sems, recv_sems
        self.locals, self.remotes = 0, 0

    def local(self, source, target):
        made = pltpu.make_async_copy(source, target, self.local_sems.at[self.locals])
        self.locals += 1
        made.start()
        return made

    def across(self, source, target):
        made = pltpu.make_async_remote_copy(
            src_ref=source,
            dst_ref=target,
            send_sem=self.send_sems.at[self.remotes],
            recv_sem=self.recv_sems.at[self.remotes],
            device_id=self.other,
            device_id_type=MESH,
        )
        self.remotes += 1
        made.start()
        return made


class Rows:
    def __init__(self, text, visual):
        self.text, self.visual = text, visual
        self.split = 2 * text
        self.count = 2 * (text + visual)
        self.spans = ((0, self.split), (self.split, self.count))
        self.own = ((0, text), (self.split, self.split + visual))
        self.other = ((text, self.split), (self.split + visual, self.count))
        self.packed = ((0, text), (text, text + visual))


def chunk_of(count):
    return max(size for size in range(row_tile, 385, row_tile) if count % size == 0)


def query_spans(count):
    edges = list(range(0, count - 256, 512)) + [count]
    return list(zip(edges[:-1], edges[1:]))


def head_wide(values, odd):
    empty = jnp.zeros_like(values)
    return jnp.concatenate([empty, values] if odd else [values, empty], 0)


def attend_pair(rows, head_width, at, qkv, bias, q_t, v_t, text_t, visual_t, logs):
    width = qkv.shape[1] // 3
    pair = 2 * head_width
    keys = qkv[:, pl.ds(pl.multiple_of(width + at * pair, lane), pair)]
    for odd in range(2):
        head = pl.ds(pl.multiple_of(at * pair + odd * head_width, head_width), head_width)
        for first, last in query_spans(rows.count):
            scores = dot(keys, head_wide(q_t[head, first:last], odd)) + bias[...]
            for t, target in enumerate((text_t, visual_t)):
                start, stop = rows.spans[t]
                part = scores[start:stop]
                top = jnp.max(part, 0, keepdims=True)
                raised = jnp.exp(part - top)
                total = jnp.sum(raised, 0, keepdims=True)
                probs = (raised * (1.0 / total)).astype(jnp.bfloat16)
                target[head, first:last] = dot(v_t[head, start:stop], probs)
                logs[pl.ds(8 * t + 2 * at + odd, 1), first:last] = top + jnp.log(total)


front_inputs = (
    "text", "visual", "text_dy", "visual_dy", "bias", "own_qkv", "own_up", "own_out", "own_down",
)
front_outputs = (
    "full_qkv", "full_up", "full_out", "full_down", "h", "qkv", "gates_t", "text_t", "visual_t",
    "logs", "mix_t", "middle", "hm", "act", "slope", "part_down", "dy",
)


def front_kernel(line_size, heads, scale, shapes, *refs):
    names = list(front_inputs) + ["out_" + name for name in front_outputs]
    names += [name for name, _, _ in shapes]
    sems = refs[len(names) :]
    held = dict(zip(names, refs))
    v = type("Refs", (), held)
    place = Place(line_size)
    rows = Rows(v.text.shape[1], v.visual.shape[1])
    gather = Gather(
        place,
        (False, False, True, True),
        (v.own_qkv, v.own_up, v.own_out, v.own_down),
        (v.out_full_qkv, v.out_full_up, v.out_full_out, v.out_full_down),
        *sems[:3],
    )
    moves = Moves(place, *sems[3:])
    qkv, up, out, down = range(4)
    width = v.qkv.shape[1] // 3
    head_width = width // heads
    size = chunk_of(rows.text)
    sizes = (size, chunk_of(rows.visual))
    saved = []

    def save(name):
        saved.append(moves.local(getattr(v, name), getattr(v, "out_" + name)))

    place.greet(True)
    gather.own(qkv)
    loads, swaps = [], []
    for inputs, target in (((v.text, v.visual), v.x), ((v.text_dy, v.visual_dy), v.dy)):
        for s in range(2):
            mine, others = rows.own[s], rows.other[s]
            loads.append(moves.local(inputs[s].at[0], target.at[mine[0] : mine[1]]))
            swaps.append(moves.across(inputs[s].at[0], target.at[others[0] : others[1]]))
    gather.own(out)
    for move in loads[:2]:
        move.wait()
    for move in swaps[:2]:
        move.wait_recv()

    def norm_rows(piece):
        v.wide[piece, :] = normalize(v.x[piece, :].astype(jnp.float32))[0]

    for s in range(2):
        over_rows(*rows.spans[s], sizes[s], norm_rows)
    gather.round(qkv, 1)
    gather.own(up)
    gather.round(qkv, 2)
    gather.round(out, 1)
    gather.round(qkv, 3)
    gather.round(out, 2)
    gather.round(qkv, 4)
    gather.round(up, 1)
    gather.round(out, 3)
    gather.rest(qkv)
    load_qkv = moves.local(v.out_full_qkv, v.w_qkv)
    gather.own(down)
    gather.round(out, 4)
    load_qkv.wait()

    gains = []
    for s in range(2):
        small = v.w_qkv[s, :, 3 * width :].astype(jnp.float32).T
        gains.append(small[heads : heads + 2])
        gain = small[heads : heads + 1]

        def gain_rows(piece):
            v.h[piece, :] = (v.wide[piece, :] * gain).astype(jnp.bfloat16)

        over_rows(*rows.spans[s], sizes[s], gain_rows)
    for s in range(2):
        first, last = rows.spans[s]

        def project(columns):
            v.qkv[first:last, columns] = dot(v.h[first:last, :], v.w_qkv[s, :, columns]).astype(
                jnp.bfloat16
            )

        even = 3 * width // 256 * 256
        over_columns(even, 256, project)
        tail = dot(v.h[first:last, :], v.w_qkv[s, :, even:])
        v.qkv[first:last, even:] = tail[:, : 3 * width - even].astype(jnp.bfloat16)
        v.gate_rows[first:last, :] = tail[:, 3 * width - even :]
    save("h")
    save("qkv")
    v.gates_t[...] = jax.nn.sigmoid(v.gate_rows[...].T[:8, :])
    save("gates_t")
    v.q_t[...] = (v.qkv[:, :width] * jnp.asarray(scale, jnp.bfloat16)).T
    v.v_t[...] = v.qkv[:, 2 * width :].T
    gather.round(up, 2)
    gather.rest(out)
    load_out = moves.local(v.out_full_out, v.w_out)
    for at in range(heads // 2):
        attend_pair(
            rows, head_width, at, v.qkv, v.bias, v.q_t, v.v_t, v.text_t, v.visual_t, v.logs
        )
        if at == 0:
            gather.round(up, 3)
            gather.round(down, 1)
        if at == 1:
            gather.round(up, 4)
            gather.round(down, 2)
    save("text_t")
    save("visual_t")
    save("logs")
    gather.round(down, 3)
    is_text = lax.broadcasted_iota(jnp.int32, (1, rows.count), 1) < rows.split
    for head in range(heads):
        span = slice(head * head_width, (head + 1) * head_width)
        gate = v.gates_t[head : head + 1, :]
        to_text = jnp.where(is_text, gate, 1.0 - gate)
        v.mix_t[span, :] = (
            to_text * v.text_t[span, :] + (1.0 - to_text) * v.visual_t[span, :]
        ).astype(jnp.bfloat16)
    save("mix_t")
    v.mix[...] = v.mix_t[...].T
    load_out.wait()
    for s in range(2):
        first, last = rows.spans[s]

        def branch(columns):
            v.wide[first:last, columns] = dot(v.mix[first:last, :], v.w_out[s, :, columns])

        over_columns(v.wide.shape[1], 256, branch)
    sums = []
    for s in range(2):
        others, packed = rows.other[s], rows.packed[s]
        sums.append(
            moves.across(
                v.wide.at[others[0] : others[1]], v.received.at[packed[0] : packed[1]]
            )
        )
    gather.round(down, 4)
    for s in range(2):
        sums[s].wait_recv()
        gain = gains[s][1:2]
        shift = rows.own[s][0] - rows.packed[s][0]

        def middle_rows(piece):
            full = pl.ds(pl.multiple_of(piece.start + shift, row_tile), piece.size)
            middle = (
                v.x[full, :].astype(jnp.float32) + v.wide[full, :] + v.received[piece, :]
            )
            v.middle[piece, :] = middle
            v.hm[full, :] = (normalize(middle)[0] * gain).astype(jnp.bfloat16)

        over_rows(*rows.packed[s], sizes[s], middle_rows)
        mine = rows.own[s]
        swaps.append(
            moves.across(
                v.hm.at[mine[0] : mine[1]],
                v.hm.at[rows.other[s][0] : rows.other[s][1]],
            )
        )
    save("middle")
    gather.rest(up)
    load_up = moves.local(v.out_full_up, v.w_up)
    for move in swaps[2:]:
        move.wait_recv()
    for move in loads[2:]:
        move.wait()
    save("hm")
    save("dy")
    load_up.wait()
    for s in range(2):
        first, last = rows.spans[s]

        def upward(columns):
            act, slope = gelu_both(dot(v.hm[first:last, :], v.w_up[s, :, columns]))
            v.act[first:last, columns] = act.astype(jnp.bfloat16)
            v.slope[first:last, columns] = slope.astype(jnp.bfloat16)

        over_columns(v.act.shape[1], 256, upward)
    save("act")
    save("slope")
    for s in range(2):
        first, last = rows.spans[s]

        def down_rows(piece):
            v.part_down[s, piece, :] = dot_rows(v.act[first:last, piece], v.dy[first:last, :]).astype(
                jnp.bfloat16
            )

        over_columns(v.act.shape[1], 256, down_rows)
    save("part_down")
    gather.rest(down)
    for move in swaps + sums:
        move.wait_send()
    for move in saved:
        move.wait()
    gather.finish()


def front(n_docs, heads, scale, *inputs):
    by_name = dict(zip(front_inputs, inputs))
    line_size = n_docs // 4
    count = 2 * (by_name["text"].shape[1] + by_name["visual"].shape[1])
    dim, wide = by_name["own_out"].shape[2], by_name["own_qkv"].shape[2]
    width = (wide - lane) // 3
    hidden = by_name["own_up"].shape[2] // 2
    low, full = jnp.bfloat16, jnp.float32
    shapes = {
        "h": ((count, dim), low),
        "qkv": ((count, 3 * width), low),
        "gates_t": ((8, count), full),
        "text_t": ((width, count), full),
        "visual_t": ((width, count), full),
        "logs": ((16, count), full),
        "mix_t": ((width, count), low),
        "middle": ((count // 2, dim), full),
        "hm": ((count, dim), low),
        "act": ((count, hidden), low),
        "slope": ((count, hidden), low),
        "part_down": ((2, hidden, dim), low),
        "dy": ((count, dim), low),
    }
    weights = {
        "full_qkv": ((2, dim, wide), low),
        "full_up": ((2, dim, hidden), low),
        "full_out": ((2, width, dim), low),
        "full_down": ((2, hidden, dim), low),
    }
    scratch = dict(shapes)
    scratch |= {
        "x": ((count, dim), low),
        "wide": ((count, dim), full),
        "received": ((count // 2, dim), full),
        "gate_rows": ((count, lane), full),
        "q_t": ((width, count), low),
        "v_t": ((width, count), low),
        "mix": ((count, width), low),
        "w_qkv": weights["full_qkv"],
        "w_up": weights["full_up"],
        "w_out": weights["full_out"],
    }
    scratch = tuple((name, *shape) for name, shape in scratch.items())
    any_space = pl.BlockSpec(memory_space=pl.ANY)
    specs = [any_space] * len(front_inputs)
    specs[front_inputs.index("bias")] = pl.BlockSpec(memory_space=pltpu.VMEM)
    results = pl.pallas_call(
        functools.partial(front_kernel, line_size, heads, scale, scratch),
        out_shape=[
            jax.ShapeDtypeStruct(*(weights | shapes)[name]) for name in front_outputs
        ],
        in_specs=specs,
        out_specs=[any_space] * len(front_outputs),
        scratch_shapes=[pltpu.VMEM(shape, dtype) for _, shape, dtype in scratch]
        + [
            pltpu.SemaphoreType.DMA((4, n_docs, 2, 4)),
            pltpu.SemaphoreType.DMA((4, n_docs, 2)),
            pltpu.SemaphoreType.DMA((4, 2)),
            pltpu.SemaphoreType.DMA((24,)),
            pltpu.SemaphoreType.DMA((12,)),
            pltpu.SemaphoreType.DMA((12,)),
        ],
        compiler_params=pltpu.CompilerParams(
            collective_id=0, has_side_effects=True, vmem_limit_bytes=vmem_limit
        ),
        name="gather_and_front",
    )(*inputs)
    return dict(zip(front_outputs, results))


def scatter_kernel(line_size, split_rows, *refs):
    count = len(split_rows)
    parts = refs[:count]
    grad_qkv, grad_small, grad_up, grad_out, grad_down = refs[count : count + 5]
    buffers = refs[count + 5 : count + 5 + 5 * count]
    diag, from_x, from_y, from_below, from_above = (
        buffers[kind * count : (kind + 1) * count] for kind in range(5)
    )
    send_sems, recv_sems, core_send, core_recv = refs[count + 5 + 5 * count :]
    place = Place(line_size)
    core, z = place.core, place.z
    half = line_size // 2
    kinds = (diag, from_x, from_y, from_below, from_above)

    def destination(step):
        chosen = 0
        for at in range(line_size):
            order = sorted(range(line_size), key=lambda other: (-abs(other - at), other))
            chosen = chosen + jnp.where(z == at, order[step], 0)
        return chosen

    def has(at, z_to):
        return z_to // half == core if split_rows[at] else None

    def slot(at, z_to):
        return z_to - core * half if split_rows[at] else z_to

    def part(at, z_to, s, flip_y, flip_x):
        rows = diag[at].shape[2]
        first = place.index(slot(at, z_to), flip_y, flip_x)
        return parts[at].at[s, pl.ds(pl.multiple_of(first * rows, row_tile), rows), :]

    def landed(kind, at, z_to, s):
        return kinds[kind][at].at[slot(at, z_to), s]

    def copy(source, kind, at, z_to, s, step, lane_of):
        return pltpu.make_async_remote_copy(
            src_ref=source,
            dst_ref=landed(kind, at, z_to, s),
            send_sem=send_sems.at[at, z_to, s, lane_of],
            recv_sem=recv_sems.at[at, z_to, s, kind],
            device_id=place.device(step),
            device_id_type=MESH,
        )

    def arrived(kind, at, z_to, s):
        copy(landed(kind, at, z_to, s), kind, at, z_to, s, "x", 0).wait_recv()

    def add(target, others, dtype=jnp.bfloat16):
        rows = target.shape[0]

        def body(step, carry):
            piece = pl.ds(pl.multiple_of(step * row_tile, row_tile), row_tile)
            total = others[0][piece, :].astype(jnp.float32)
            for other in others[1:]:
                total = total + other[piece, :].astype(jnp.float32)
            target[piece, :] = total.astype(dtype)
            return carry

        lax.fori_loop(0, rows // row_tile, body, 0)

    sends = []

    def send(conditions, *which):
        when(conditions, lambda: copy(*which).start())
        sends.append((conditions, which))

    def raw(step):
        z_to = destination(step)
        for at in range(count):
            conditions = [has(at, z_to)]
            send(conditions, part(at, z_to, 0, True, True), 0, at, z_to, 0, "y", 0)
            send(conditions, part(at, z_to, 1, True, True), 0, at, z_to, 1, "x", 0)
            send(conditions, part(at, z_to, 0, True, False), 2, at, z_to, 0, "y", 1)
            send(conditions, part(at, z_to, 1, False, True), 1, at, z_to, 1, "x", 1)

    def pair(step):
        z_to = destination(step)
        for at in range(count):
            for s in range(2):
                conditions = [has(at, z_to)]
                held = landed(0, at, z_to, s)

                def body():
                    arrived(0, at, z_to, s)
                    add(held, [held, part(at, z_to, s, s == 1, s == 0)])

                when(conditions, body)
                if s == 0:
                    send(conditions, held, 1, at, z_to, s, "x", 2)
                else:
                    send(conditions, held, 2, at, z_to, s, "y", 2)

    def store(at, s, total):
        for which in range(2):

            def body():
                if at == 0:
                    third = grad_qkv.shape[2] // 3
                    small = total[0].shape[1] - 3 * (third // 2)
                    for column in range(3):
                        mine = slice(column * (third // 2), (column + 1) * (third // 2))
                        first = column * third + which * (third // 2)
                        add_columns(grad_qkv, s, first, total, mine)
                    add_small(s, which, total, small)
                elif at == 1:
                    width = grad_up.shape[2] // 2
                    add_columns(grad_up, s, which * width, total, slice(0, width))

            pl.when(core == which)(body)

    def add_columns(target, s, first, total, columns):
        width = columns.stop - columns.start

        def body(step, carry):
            piece = pl.ds(pl.multiple_of(step * row_tile, row_tile), row_tile)
            value = total[0][piece, columns].astype(jnp.float32)
            for other in total[1:]:
                value = value + other[piece, columns].astype(jnp.float32)
            target[s, piece, first : first + width] = value
            return carry

        lax.fori_loop(0, target.shape[1] // row_tile, body, 0)

    def add_small(s, which, total, small):
        columns = slice(total[0].shape[1] - small, total[0].shape[1])

        def body(step, carry):
            piece = pl.ds(pl.multiple_of(step * row_tile, row_tile), row_tile)
            value = total[0][piece, columns].astype(jnp.float32)
            for other in total[1:]:
                value = value + other[piece, columns].astype(jnp.float32)
            grad_small[which, s, piece, :] = value
            return carry

        lax.fori_loop(0, grad_small.shape[2] // row_tile, body, 0)

    def finish(at, s, total):
        if at < 2:
            store(at, s, total)
        else:
            add((grad_out, grad_down)[at - 2].at[s], total, jnp.float32)

    def line(step):
        z_to = destination(step)
        for at in range(count):
            for s in range(2):
                conditions = [has(at, z_to)]
                held = landed(1, at, z_to, s)
                base = [held, landed(2, at, z_to, s), part(at, z_to, s, False, False)]
                below, above = landed(3, at, z_to, s), landed(4, at, z_to, s)

                def wait():
                    arrived(1, at, z_to, s)
                    arrived(2, at, z_to, s)

                when(conditions, wait)
                upward, downward = z_to > z, z_to < z
                here = z_to == z
                first, last = z == 0, z == line_size - 1
                inner = jnp.logical_and(z > 0, z < line_size - 1)

                def go_up():
                    arrived(3, at, z_to, s)
                    add(held, base + [below])

                def go_down():
                    arrived(4, at, z_to, s)
                    add(held, base + [above])

                when(conditions + [upward, first], lambda: add(held, base))
                when(conditions + [upward, z > 0], go_up)
                send(conditions + [upward], held, 3, at, z_to, s, "up", 3)
                when(conditions + [downward, last], lambda: add(held, base))
                when(conditions + [downward, z < line_size - 1], go_down)
                send(conditions + [downward], held, 4, at, z_to, s, "down", 4)

                def end_first():
                    arrived(4, at, z_to, s)
                    finish(at, s, base + [above])

                def end_last():
                    arrived(3, at, z_to, s)
                    finish(at, s, base + [below])

                def end_inner():
                    arrived(3, at, z_to, s)
                    arrived(4, at, z_to, s)
                    finish(at, s, base + [below, above])

                when(conditions + [here, first], end_first)
                when(conditions + [here, last], end_last)
                when(conditions + [here, inner], end_inner)

    place.greet(True)
    raw(0)
    for step in range(line_size + 1):
        if step + 1 < line_size:
            raw(step + 1)
        if step < line_size:
            pair(step)
        if step >= 1:
            line(step - 1)

    other_core = (place.index(z), 1 - core)

    def across(number, ref):
        return pltpu.make_async_remote_copy(
            src_ref=ref,
            dst_ref=ref,
            send_sem=core_send.at[number],
            recv_sem=core_recv.at[number],
            device_id=other_core,
            device_id_type=MESH,
        )

    third, width = grad_qkv.shape[2] // 3, grad_up.shape[2] // 2

    def columns_of(which):
        refs = []
        for s in range(2):
            for column in range(3):
                refs.append(
                    grad_qkv.at[s, :, pl.ds(column * third + which * (third // 2), third // 2)]
                )
            refs.append(grad_up.at[s, :, pl.ds(which * width, width)])
        refs.append(grad_small.at[which])
        return list(enumerate(refs))

    rows_of = [(9, grad_out), (10, grad_down)]
    owner = z // half == core
    for which in range(2):

        def start():
            for number, ref in columns_of(which):
                across(number, ref).start()

        pl.when(core == which)(start)

    def start_rows():
        for number, ref in rows_of:
            across(number, ref).start()

    pl.when(owner)(start_rows)
    for which in range(2):

        def wait():
            for number, ref in columns_of(which):
                across(number, ref).wait_send()
            for number, ref in columns_of(1 - which):
                across(number, ref).wait_recv()

        pl.when(core == which)(wait)

    def sent_rows():
        for number, ref in rows_of:
            across(number, ref).wait_send()

    def got_rows():
        for number, ref in rows_of:
            across(number, ref).wait_recv()

    pl.when(owner)(sent_rows)
    pl.when(jnp.logical_not(owner))(got_rows)
    for conditions, which in sends:
        when(conditions, lambda: copy(*which).wait_send())


def scatter_gradients(n_docs, part_qkv, part_up, part_out, part_down):
    line_size = n_docs // 4
    split_rows = (False, False, True, True)
    parts = (part_qkv, part_up, part_out, part_down)
    qkv_width = (part_qkv.shape[2] - lane) * 2
    rows = [
        part.shape[1] // (n_docs // 2 if split else n_docs)
        for part, split in zip(parts, split_rows)
    ]
    shapes = (
        jax.ShapeDtypeStruct((2, rows[0], qkv_width), jnp.float32),
        jax.ShapeDtypeStruct((2, 2, rows[0], lane), jnp.float32),
        jax.ShapeDtypeStruct((2, rows[1], part_up.shape[2] * 2), jnp.float32),
        jax.ShapeDtypeStruct((2, rows[2], part_out.shape[2]), jnp.float32),
        jax.ShapeDtypeStruct((2, rows[3], part_down.shape[2]), jnp.float32),
    )
    buffers = [
        pltpu.VMEM((line_size // 2 if split else line_size, 2, row, part.shape[2]), jnp.bfloat16)
        for part, split, row in zip(parts, split_rows, rows)
    ]
    vmem = pl.BlockSpec(memory_space=pltpu.VMEM)
    return pl.pallas_call(
        functools.partial(scatter_kernel, line_size, split_rows),
        out_shape=shapes,
        in_specs=[vmem] * 4,
        out_specs=[vmem] * 5,
        scratch_shapes=buffers * 5
        + [
            pltpu.SemaphoreType.DMA((4, line_size, 2, 5)),
            pltpu.SemaphoreType.DMA((4, line_size, 2, 5)),
            pltpu.SemaphoreType.DMA((11,)),
            pltpu.SemaphoreType.DMA((11,)),
        ],
        compiler_params=pltpu.CompilerParams(
            collective_id=1, has_side_effects=True, vmem_limit_bytes=vmem_limit
        ),
        name="scatter_gradients",
    )(*parts)


def swap(value):
    return lax.ppermute(value, "blk", [(0, 1), (1, 0)])


def both(own):
    return jnp.concatenate([own, swap(own)], 0)


def own_sum(partial):
    rows = partial.shape[0] // 2
    return partial[:rows] + swap(partial[rows:])


def normalize_back(gradient, normed, inverse, gain):
    scaled = gradient * gain
    grad_gain = jnp.sum(gradient * normed, 0)
    grad_input = inverse * (
        scaled
        - jnp.mean(scaled, -1, keepdims=True)
        - normed * jnp.mean(scaled * normed, -1, keepdims=True)
    )
    return grad_input, grad_gain


def heads_of(values, heads):
    return values.reshape(values.shape[0], heads, -1)


def attend(queries, keys, values, valid, scale):
    scores = jnp.einsum("qhe,khe->hqk", queries, keys, preferred_element_type=jnp.float32) * scale
    scores = jnp.where(valid, scores, big_negative)
    top = jnp.max(scores, -1)
    probs = jnp.where(valid, jnp.exp(scores - top[..., None]), 0.0)
    total = jnp.sum(probs, -1)
    weighted = jnp.einsum(
        "hqk,khe->qhe", probs.astype(jnp.bfloat16), values, preferred_element_type=jnp.float32
    )
    return weighted / total.T[..., None], top + jnp.log(total)


def attend_back(queries, keys, values, valid, scale, log_total, grad_output, output):
    delta = jnp.sum(grad_output.astype(jnp.float32) * output, -1).T
    scores = jnp.einsum("qhe,khe->hqk", queries, keys, preferred_element_type=jnp.float32) * scale
    probs = jnp.where(valid, jnp.exp(scores - log_total[..., None]), 0.0)
    grad_values = jnp.einsum(
        "hqk,qhe->khe", probs.astype(jnp.bfloat16), grad_output, preferred_element_type=jnp.float32
    )
    grad_probs = jnp.einsum("qhe,khe->hqk", grad_output, values, preferred_element_type=jnp.float32)
    grad_scores = (probs * (grad_probs - delta[..., None])).astype(jnp.bfloat16)
    grad_queries = (
        jnp.einsum("hqk,khe->qhe", grad_scores, keys, preferred_element_type=jnp.float32) * scale
    )
    grad_keys = (
        jnp.einsum("hqk,qhe->khe", grad_scores, queries, preferred_element_type=jnp.float32) * scale
    )
    return grad_queries, grad_keys, grad_values


def kernel_path(
    n_docs, heads, scale, valids, shard, w_up, w_out, w_down, text, visual, text_dy, visual_dy
):
    bias = jnp.where(jnp.concatenate(valids), 0.0, big_negative).astype(jnp.float32)[:, None]
    v = front(
        n_docs, heads, scale, text, visual, text_dy, visual_dy, bias, shard, w_up, w_out, w_down
    )
    width = v["full_out"].shape[1]
    rows = Rows(text.shape[1], visual.shape[1])
    tails, results, token_parts = [], [], []
    gains = [v["full_qkv"][s, :, 3 * width + heads : 3 * width + heads + 2].astype(jnp.float32) for s in range(2)]
    for s in range(2):
        a, b = rows.spans[s]
        pa, pb = rows.packed[s]
        dy = v["dy"][a:b]
        own_dy = (text_dy, visual_dy)[s][0]
        middle = v["middle"][pa:pb]
        results.append((middle + own_sum(dot(v["act"][a:b], v["full_down"][s]))).astype(jnp.bfloat16))
        du = (dot_back(dy, v["full_down"][s]) * v["slope"][a:b].astype(jnp.float32)).astype(jnp.bfloat16)
        part_up = dot_rows(v["hm"][a:b], du).astype(jnp.bfloat16)
        normed, inverse = normalize(middle)
        grad_in, part_gain = normalize_back(own_sum(dot_back(du, v["full_up"][s])), normed, inverse, gains[s][:, 1])
        grad_middle = own_dy.astype(jnp.float32) + grad_in
        grad_branch = both(grad_middle.astype(jnp.bfloat16))
        part_out = dot(v["mix_t"][:, a:b], grad_branch).astype(jnp.bfloat16)
        mix_grad = dot_back(v["full_out"][s], grad_branch)
        tails.append((grad_middle, part_up, part_out, mix_grad, part_gain))
    mix_grad = jnp.concatenate([tails[0][3], tails[1][3]], 1).reshape(heads, -1, rows.count)
    text_t = v["text_t"].reshape(heads, -1, rows.count)
    visual_t = v["visual_t"].reshape(heads, -1, rows.count)
    is_text = jnp.arange(rows.count) < rows.split
    gate = v["gates_t"][:heads]
    sign = jnp.where(is_text, 1.0, -1.0)
    gate_grad = (jnp.sum(mix_grad * (text_t - visual_t), 1) * sign * gate * (1.0 - gate)).astype(jnp.bfloat16)
    to_text = jnp.where(is_text, gate, 1.0 - gate)[:, None]
    outs_grad = ((to_text * mix_grad).astype(jnp.bfloat16), ((1.0 - to_text) * mix_grad).astype(jnp.bfloat16))
    hw = width // heads
    q, k, vv = (v["qkv"][:, i * width : (i + 1) * width].reshape(rows.count, heads, hw) for i in range(3))
    dq, dk, dv = 0.0, [], []
    for t in range(2):
        a, b = rows.spans[t]
        lse = v["logs"][8 * t : 8 * t + heads]
        valid = valids[t]
        sc = jnp.einsum("qhe,khe->hqk", q, k[a:b], preferred_element_type=jnp.float32) * scale
        p = jnp.where(valid, jnp.exp(sc - lse[..., None]), 0.0)
        do = outs_grad[t]
        delta = jnp.sum(do.astype(jnp.float32) * (text_t, visual_t)[t], 1)
        dp = jnp.einsum("heq,khe->hqk", do, vv[a:b], preferred_element_type=jnp.float32)
        ds = (p * (dp - delta[..., None])).astype(jnp.bfloat16)
        dv.append(jnp.einsum("hqk,heq->khe", p.astype(jnp.bfloat16), do, preferred_element_type=jnp.float32))
        dk.append(jnp.einsum("hqk,qhe->khe", ds, q, preferred_element_type=jnp.float32) * scale)
        dq = dq + jnp.einsum("hqk,khe->qhe", ds, k[a:b], preferred_element_type=jnp.float32) * scale
    dk, dv = jnp.concatenate(dk), jnp.concatenate(dv)
    wide = jnp.concatenate(
        [g.reshape(rows.count, width).astype(jnp.bfloat16) for g in (dq, dk, dv)]
        + [gate_grad.T, jnp.zeros((rows.count, lane - heads), jnp.bfloat16)], 1)
    parts = []
    token_grads = []
    for s in range(2):
        a, b = rows.spans[s]
        part = dot_rows(v["h"][a:b], wide[a:b])
        normed, inverse = normalize((text, visual)[s][0].astype(jnp.float32))
        grad_in, part_gain = normalize_back(own_sum(dot_back(wide[a:b], v["full_qkv"][s])), normed, inverse, gains[s][:, 0])
        token_grads.append((tails[s][0] + grad_in)[None])
        parts.append(jnp.concatenate([part[:, : 3 * width + heads], part_gain[:, None], tails[s][4][:, None], part[:, 3 * width + heads + 2 :]], 1).astype(jnp.bfloat16))
    grad_qkv, small, grad_up, grad_out, grad_down = scatter_gradients(
        n_docs, jnp.stack(parts), jnp.stack([tails[0][1], tails[1][1]]), jnp.stack([tails[0][2], tails[1][2]]), v["part_down"])
    grad_gate = jnp.concatenate([small[0, :, :, :heads], small[1, :, :, :heads]], 2)
    sums = small[0] + small[1]
    return (results[0][None], results[1][None], token_grads[0], token_grads[1], grad_qkv, grad_out, grad_gate, grad_up, grad_down, sums[:, :, heads], sums[:, :, heads + 1])


def on_device(
    n_docs,
    text_tokens,
    visual_tokens,
    text_mask,
    visual_mask,
    w_qkv,
    w_out,
    w_gate,
    w_up,
    w_down,
    gain_attn,
    gain_ffn,
    text_cotangent,
    visual_cotangent,
):
    core = lax.axis_index("blk")
    width = w_out.shape[2]
    all_heads = w_gate.shape[2]
    heads = all_heads // 2
    half = width // 2
    scale = (width // all_heads) ** (-0.5)
    use_kernels = n_docs == 16 and w_qkv.shape[1] % row_tile == 0

    def own_columns(array, size, start=0):
        return lax.dynamic_slice_in_dim(array, start + core * size, size, 2)

    own_tokens = (text_tokens[0], visual_tokens[0])
    own_grads = (text_cotangent[0], visual_cotangent[0])
    tokens = tuple(both(value) for value in own_tokens)
    grads_out = tuple(both(value) for value in own_grads)

    def reorder(mask):
        rows = mask.shape[1] // 2
        return (
            jnp.concatenate(
                [
                    lax.dynamic_slice_in_dim(mask[0], core * rows, rows),
                    lax.dynamic_slice_in_dim(mask[0], (1 - core) * rows, rows),
                ]
            )
            > 0
        )

    valids = (reorder(text_mask), reorder(visual_mask))

    pad = lane - heads - 2
    shard = jnp.concatenate(
        [own_columns(w_qkv, half, column * width) for column in range(3)]
        + [
            own_columns(w_gate, heads),
            gain_attn[..., None],
            gain_ffn[..., None],
            jnp.zeros(w_gate.shape[:2] + (pad,), jnp.bfloat16),
        ],
        2,
    )
    if use_kernels:
        return kernel_path(
            n_docs, heads, scale, valids, shard, w_up, w_out, w_down,
            text_tokens, visual_tokens, text_cotangent, visual_cotangent,
        )
    if True:
        gather = lambda array: lax.all_gather(array, "docs", axis=1, tiled=True)
        rows_half = lambda array: lax.dynamic_slice_in_dim(
            array, core * (array.shape[1] // 2), array.shape[1] // 2, 1
        )
        full_qkv = gather(shard)
        full_up = gather(own_columns(w_up, w_up.shape[2] // 2))
        full_out, full_down = rows_half(gather(w_out)), rows_half(gather(w_down))
    gains_attn = full_qkv[:, :, 3 * half + heads].astype(jnp.float32)
    gains_ffn = full_qkv[:, :, 3 * half + heads + 1].astype(jnp.float32)

    fronts = []
    for s in range(2):
        normed, inverse = normalize(tokens[s].astype(jnp.float32))
        lowered = (normed * gains_attn[s]).astype(jnp.bfloat16)
        wide = dot(lowered, full_qkv[s])
        low = wide[:, : 3 * half].astype(jnp.bfloat16)
        gates = jax.nn.sigmoid(wide[:, 3 * half : 3 * half + heads])
        queries, keys, values = (
            heads_of(low[:, column * half : (column + 1) * half], heads) for column in range(3)
        )
        fronts.append((normed, inverse, lowered, gates, queries, keys, values))

    outputs, totals = {}, {}
    for s in range(2):
        for t in range(2):
            outputs[s, t], totals[s, t] = attend(
                fronts[s][4], fronts[t][5], fronts[t][6], valids[t], scale
            )

    results, tails = [], []
    for s in range(2):
        gates = fronts[s][3][..., None]
        own, cross = outputs[s, s], outputs[s, 1 - s]
        mixed = gates * own + (1.0 - gates) * cross
        mix = mixed.reshape(mixed.shape[0], -1).astype(jnp.bfloat16)
        middle = own_tokens[s].astype(jnp.float32) + own_sum(dot(mix, full_out[s]))
        normed, inverse = normalize(middle)
        lowered = both((normed * gains_ffn[s]).astype(jnp.bfloat16))
        upward = dot(lowered, full_up[s])
        activated, gelu_back = jax.vjp(jax.nn.gelu, upward)
        act = activated.astype(jnp.bfloat16)
        results.append((middle + own_sum(dot(act, full_down[s]))).astype(jnp.bfloat16))
        part_down = dot_rows(act, grads_out[s]).astype(jnp.bfloat16)
        grad_up = gelu_back(dot_back(grads_out[s], full_down[s]))[0].astype(jnp.bfloat16)
        part_up = dot_rows(lowered, grad_up).astype(jnp.bfloat16)
        grad_in, part_gain = normalize_back(
            own_sum(dot_back(grad_up, full_up[s])), normed, inverse, gains_ffn[s]
        )
        grad_middle = own_grads[s].astype(jnp.float32) + grad_in
        grad_branch = both(grad_middle.astype(jnp.bfloat16))
        part_out = dot_rows(mix, grad_branch).astype(jnp.bfloat16)
        grad_mix = heads_of(dot_back(grad_branch, full_out[s]), heads)
        grad_gate = (
            jnp.sum(grad_mix * (own - cross), -1) * fronts[s][3] * (1.0 - fronts[s][3])
        ).astype(jnp.bfloat16)
        grad_own = (gates * grad_mix).astype(jnp.bfloat16)
        grad_cross = ((1.0 - gates) * grad_mix).astype(jnp.bfloat16)
        tails.append(
            (grad_middle, grad_gate, grad_own, grad_cross, part_out, part_up, part_down, part_gain)
        )

    backs = {}
    for s in range(2):
        for t in range(2):
            backs[s, t] = attend_back(
                fronts[s][4],
                fronts[t][5],
                fronts[t][6],
                valids[t],
                scale,
                totals[s, t],
                tails[s][2 if s == t else 3],
                outputs[s, t],
            )

    token_grads, parts_qkv = [], []
    for s in range(2):
        normed, inverse, lowered = fronts[s][:3]
        rows = lowered.shape[0]
        grad_q = backs[s, s][0] + backs[s, 1 - s][0]
        grad_k = backs[s, s][1] + backs[1 - s, s][1]
        grad_v = backs[s, s][2] + backs[1 - s, s][2]
        grad_wide = jnp.concatenate(
            [grad.reshape(rows, -1).astype(jnp.bfloat16) for grad in (grad_q, grad_k, grad_v)]
            + [tails[s][1], jnp.zeros((rows, lane - heads), jnp.bfloat16)],
            1,
        )
        part = dot_rows(lowered, grad_wide)
        own_rows = rows // 2
        grad_in, part_gain = normalize_back(
            own_sum(dot_back(grad_wide, full_qkv[s])),
            normed[:own_rows],
            inverse[:own_rows],
            gains_attn[s],
        )
        token_grads.append((tails[s][0] + grad_in)[None])
        parts_qkv.append(
            jnp.concatenate(
                [
                    part[:, : 3 * half + heads],
                    part_gain[:, None],
                    tails[s][7][:, None],
                    part[:, 3 * half + heads + 2 :],
                ],
                1,
            ).astype(jnp.bfloat16)
        )
    part_qkv = jnp.stack(parts_qkv)
    part_out, part_up, part_down = (
        jnp.stack([tails[0][at], tails[1][at]]) for at in (4, 5, 6)
    )
    if True:
        scatter = lambda array: lax.psum_scatter(
            array.astype(jnp.float32), "docs", scatter_dimension=1, tiled=True
        )

        def columns(own):
            other = swap(own)
            first = jnp.where(core == 0, own, other)
            second = jnp.where(core == 0, other, own)
            return first, second

        def rows_both(part):
            empty = jnp.zeros_like(part)
            first = jnp.where(core == 0, part, empty)
            second = jnp.where(core == 0, empty, part)
            return lax.psum(scatter(jnp.concatenate([first, second], 1)), "blk")

        qkv_first, qkv_second = columns(scatter(part_qkv))
        grad_qkv = jnp.concatenate(
            [
                piece[:, :, column * half : (column + 1) * half]
                for column in range(3)
                for piece in (qkv_first, qkv_second)
            ],
            2,
        )
        small = jnp.stack([qkv_first[:, :, 3 * half :], qkv_second[:, :, 3 * half :]])
        grad_up = jnp.concatenate(columns(scatter(part_up)), 2)
        grad_out, grad_down = rows_both(part_out), rows_both(part_down)
    grad_gate = jnp.concatenate([small[0, :, :, :heads], small[1, :, :, :heads]], 2)
    gains = small[0] + small[1]
    return (
        results[0][None],
        results[1][None],
        token_grads[0],
        token_grads[1],
        grad_qkv,
        grad_out,
        grad_gate,
        grad_up,
        grad_down,
        gains[:, :, heads],
        gains[:, :, heads + 1],
    )


def solution(mesh):
    rows = P("docs", "blk", None)
    weights = P(None, "docs", None)
    gains = P(None, "docs")
    in_specs = (
        (rows, rows, P("docs", None), P("docs", None)) + (weights,) * 5 + (gains,) * 2 + (rows,) * 2
    )
    out_specs = (rows,) * 4 + (weights,) * 5 + (gains,) * 2
    return jax.shard_map(
        functools.partial(on_device, mesh.shape["docs"]),
        mesh=mesh,
        in_specs=in_specs,
        out_specs=out_specs,
        check_vma=False,
    )
```

```python
import functools
import types
from typing import NamedTuple

import jax
import jax.numpy as jnp
from jax import lax
from jax.experimental import pallas as pl
from jax.experimental.pallas import tpu as pltpu
from jax.sharding import PartitionSpec as P

epsilon = 1e-05
big_negative = -1e30
MESH = pl.DeviceIdType.MESH
docs_axis, core_axis = "docs", "blk"
lane = 128
row_tile = 16
vmem_limit = 61 * 1024 * 1024
low, full = jnp.bfloat16, jnp.float32
by_x, by_y, upward, downward = range(4)
quads = ((False, False), (False, True), (True, False), (True, True))


def dot(left, right):
    return jnp.dot(left, right, preferred_element_type=full)


def dot_back(left, right):
    return lax.dot_general(left, right, (((1,), (1,)), ((), ())), preferred_element_type=full)


def dot_rows(left, right):
    return lax.dot_general(left, right, (((0,), (0,)), ((), ())), preferred_element_type=full)


def normalize(values):
    centred = values - jnp.mean(values, -1, keepdims=True)
    inverse = lax.rsqrt(jnp.mean(centred * centred, -1, keepdims=True) + epsilon)
    return centred * inverse, inverse


def over_rows(first, last, size, body):
    def step(at, carry):
        body(pl.ds(pl.multiple_of(first + at * size, row_tile), size))
        return carry

    lax.fori_loop(0, (last - first) // size, step, 0)


def over_columns(first, last, size, body):
    def step(at, carry):
        body(pl.ds(pl.multiple_of(first + at * size, lane), size))
        return carry

    lax.fori_loop(0, (last - first) // size, step, 0)


def gelu_both(value):
    root = 0.7978845608028654
    square = value * value
    bent = jnp.tanh(root * (value + 0.044715 * value * square))
    cdf = 0.5 * (1.0 + bent)
    slope = cdf + 0.5 * value * (1.0 - bent * bent) * (root * (1.0 + 0.134145 * square))
    return value * cdf, slope


def add_rows(target, others, first=0):
    size = max(size for size in (16, 32, 48) if others[0].shape[0] % size == 0)

    def body(step, carry):
        at = pl.multiple_of(step * size, row_tile)
        total = others[0][pl.ds(at, size), :].astype(full)
        for other in others[1:]:
            total = total + other[pl.ds(at, size), :].astype(full)
        target[pl.ds(first + at, size), :] = total.astype(target.dtype)
        return carry

    lax.fori_loop(0, others[0].shape[0] // size, body, 0)


def when(conditions, body):
    conditions = [condition for condition in conditions if condition is not None]
    if not conditions:
        body()
        return
    pl.when(functools.reduce(jnp.logical_and, conditions))(body)


def merged(*groups):
    space = types.SimpleNamespace()
    for group in groups:
        vars(space).update(group._asdict())
    return space


class Place:
    def __init__(self, line_size):
        docs = lax.axis_index(docs_axis)
        self.core = lax.axis_index(core_axis)
        self.line_size = line_size
        self.z, self.y, self.x = docs // 4, (docs // 2) % 2, docs % 2
        self.up_valid = self.z < line_size - 1
        self.down_valid = self.z > 0

    def index(self, z, flip_y=False, flip_x=False):
        y = 1 - self.y if flip_y else self.y
        x = 1 - self.x if flip_x else self.x
        return z * 4 + y * 2 + x

    def device(self, step):
        z, y, x = self.z, self.y, self.x
        docs = (
            z * 4 + y * 2 + 1 - x,
            z * 4 + (1 - y) * 2 + x,
            (z + 1) * 4 + y * 2 + x,
            (z - 1) * 4 + y * 2 + x,
        )[step]
        return (docs, self.core)

    def greet(self):
        barrier = pltpu.get_barrier_semaphore()

        def signal(device):
            pl.semaphore_signal(barrier, inc=1, device_id=device, device_id_type=MESH)

        signal(self.device(by_x))
        signal(self.device(by_y))
        pl.when(self.up_valid)(lambda: signal(self.device(upward)))
        pl.when(self.down_valid)(lambda: signal(self.device(downward)))
        signal((self.index(self.z), 1 - self.core))

    def meet(self):
        peers = 3
        for valid in (self.up_valid, self.down_valid):
            peers = peers + jnp.where(valid, 1, 0)
        pl.semaphore_wait(pltpu.get_barrier_semaphore(), peers)


class Piece(NamedTuple):
    array: int
    part: int
    first: int
    rows: int
    flip: int
    lines_late: bool


class Gather:
    def __init__(self, place, pieces, sizes, splits, owns, outs, send_sems, recv_sems, local_sems):
        self.place, self.pieces, self.sizes, self.splits = place, pieces, sizes, splits
        self.owns, self.outs = owns, outs
        self.send_sems, self.recv_sems, self.local_sems = send_sems, recv_sems, local_sems
        self.sends = []

    def has(self, at, source_z):
        half = self.place.line_size // 2
        return source_z // half == self.place.core if self.splits[self.pieces[at].array] else None

    def block(self, at, source):
        piece = self.pieces[at]
        if self.splits[piece.array]:
            source = source - self.place.core * (self.place.line_size // 2) * 4
        first = source * self.sizes[piece.array] + piece.first
        rows = pl.ds(pl.multiple_of(first, row_tile), piece.rows)
        return self.outs[piece.array].at[piece.part, rows, :]

    def mine(self, at):
        piece = self.pieces[at]
        ref, offset = self.owns[piece.array]
        first = pl.multiple_of(offset + piece.first, row_tile)
        return ref.at[piece.part, pl.ds(first, piece.rows), :]

    def copy(self, at, source, step, own=False):
        return pltpu.make_async_remote_copy(
            src_ref=self.mine(at) if own else self.block(at, source),
            dst_ref=self.block(at, source),
            send_sem=self.send_sems.at[at, source, step],
            recv_sem=self.recv_sems.at[at, source],
            device_id=self.place.device(step),
            device_id_type=MESH,
        )

    def local(self, at):
        here = self.place.index(self.place.z)
        return pltpu.make_async_copy(self.mine(at), self.block(at, here), self.local_sems.at[at])

    def send(self, conditions, *which):
        when(conditions, lambda: self.copy(*which).start())
        self.sends.append((conditions, which))

    def wait(self, conditions, at, source):
        when(conditions, lambda: self.copy(at, source, by_x).wait_recv())

    def units(self, distance):
        place = self.place
        if distance == 0:
            return [(place.z, None, None)]
        return [
            (place.z - distance, place.z >= distance, (upward, place.up_valid)),
            (place.z + distance, place.z < place.line_size - distance, (downward, place.down_valid)),
        ]

    def both_ways(self, conditions, at, source, own=False):
        self.send(conditions + [self.place.up_valid], at, source, upward, own)
        self.send(conditions + [self.place.down_valid], at, source, downward, own)

    def own(self, at):
        place = self.place
        here = place.index(place.z)
        held = [self.has(at, place.z)]
        when(held, lambda: self.local(at).start())
        self.both_ways(held, at, here, True)
        self.send(held, at, here, by_x, True)
        self.send(held, at, here, by_y, True)

    def beside(self, at, distance):
        piece = self.pieces[at]
        for source_z, valid, _ in self.units(distance):
            conditions = [valid, self.has(at, source_z)]
            for other in (0, 1):
                source = self.place.index(source_z, other == 1, other == 0)
                if other == piece.flip or piece.lines_late:
                    self.wait(conditions, at, source)
                if other == piece.flip:
                    self.send(conditions, at, source, by_x if other else by_y)
                if piece.lines_late:
                    self.both_ways(conditions, at, source)

    def along(self, at, distance, quad=quads[0]):
        for source_z, valid, (step, onward) in self.units(distance):
            source = self.place.index(source_z, *quad)
            conditions = [valid, self.has(at, source_z)]
            self.wait(conditions, at, source)
            self.send(conditions + [onward], at, source, step)
            if not self.pieces[at].lines_late:
                self.send(conditions, at, source, by_x)
                self.send(conditions, at, source, by_y)

    def late_round(self, at, number):
        place = self.place
        last = place.line_size - 1
        if number == 1:
            self.beside(at, 0)
        if number == 2:
            held = [self.has(at, place.z)]
            fourth = place.index(place.z, *quads[3])
            self.wait(held, at, fourth)
            self.both_ways(held, at, fourth)
        for quad, behind in zip(quads, (0, 1, 1, 2)):
            if 1 <= number - behind <= last:
                self.along(at, number - behind, quad)

    def rest(self, array):
        for at, piece in enumerate(self.pieces):
            if piece.array != array:
                continue
            if piece.lines_late:
                self.along(at, self.place.line_size - 1, quads[3])
            else:
                for distance in range(self.place.line_size):
                    for source_z, valid, _ in self.units(distance):
                        conditions = [valid, self.has(at, source_z)]
                        beside = (piece.flip == 0, piece.flip == 1)
                        self.wait(conditions, at, self.place.index(source_z, *beside))
                        self.wait(conditions, at, self.place.index(source_z, *quads[3]))
            when([self.has(at, self.place.z)], lambda: self.local(at).wait())

    def run(self, plan, stages):
        for kind, at, number in plan:
            if kind == 0:
                self.own(at)
            elif kind == 1:
                self.beside(at, number)
            elif kind == 2:
                self.along(at, number)
            elif kind == 3:
                self.late_round(at, number)
            elif kind == 4:
                self.rest(at)
            else:
                stages[at]()

    def finish(self):
        for conditions, which in self.sends:
            when(conditions, lambda: self.copy(*which).wait_send())


class Scatter:
    def __init__(self, place, pieces, splits, raws, parts, buffers, send_sems, recv_sems, finish):
        self.place, self.pieces, self.splits = place, pieces, splits
        self.raws, self.parts, self.buffers = raws, parts, buffers
        self.send_sems, self.recv_sems, self.finish_rows = send_sems, recv_sems, finish
        self.sends = []

    def has(self, at, z_to):
        half = self.place.line_size // 2
        return z_to // half == self.place.core if self.splits[self.pieces[at].array] else None

    def slot(self, at, z_to):
        half = self.place.line_size // 2
        return z_to - self.place.core * half if self.splits[self.pieces[at].array] else z_to

    def block(self, refs, at, z_to, quad):
        piece = self.pieces[at]
        ref = refs[piece.array]
        split = 2 if self.splits[piece.array] else 1
        rows = ref.shape[1] // (4 * self.place.line_size // split)
        first = self.place.index(self.slot(at, z_to), *quad) * rows + piece.first
        return ref.at[piece.part, pl.ds(pl.multiple_of(first, row_tile), piece.rows), :]

    def raw_of(self, at, z_to, quad):
        return self.block(self.raws, at, z_to, quad)

    def part_of(self, at, z_to, quad):
        return self.block(self.parts, at, z_to, quad)

    def landed(self, at, kind, z_to, quad=0):
        ref = self.buffers[at][kind]
        if not self.pieces[at].lines_late:
            return ref.at[self.slot(at, z_to)]
        return ref.at[self.slot(at, z_to), quad] if kind >= 3 else ref.at[0]

    def copy(self, source, at, kind, z_to, step, number, quad=0):
        arrival = kind if kind < 3 else 3 + (kind - 3) * 4 + quad
        return pltpu.make_async_remote_copy(
            src_ref=source,
            dst_ref=self.landed(at, kind, z_to, quad),
            send_sem=self.send_sems.at[at, z_to, number],
            recv_sem=self.recv_sems.at[at, z_to, arrival],
            device_id=self.place.device(step),
            device_id_type=MESH,
        )

    def arrived(self, at, kind, z_to, quad=0):
        held = self.landed(at, kind, z_to, quad)
        self.copy(held, at, kind, z_to, by_x, 0, quad).wait_recv()

    def send(self, conditions, *which):
        when(conditions, lambda: self.copy(*which).start())
        self.sends.append((conditions, which))

    def destination(self, step):
        size = self.place.line_size
        chosen = 0
        for at in range(size):
            order = sorted(range(size), key=lambda other: (-abs(other - at), other))
            chosen = chosen + jnp.where(self.place.z == at, order[step], 0)
        return chosen

    def raw(self, at, step):
        place = self.place
        z_to = self.destination(step)
        conditions = [self.has(at, z_to)]
        if not self.pieces[at].lines_late:
            self.plane_raw(conditions, self.raw_of, at, z_to)
            return
        first, last = place.z == 0, place.z == place.line_size - 1
        for number, quad in enumerate(quads):
            source = self.raw_of(at, z_to, quad)
            up = conditions + [first, z_to > place.z]
            self.send(up, source, at, 3, z_to, upward, number, number)
            down = conditions + [last, z_to < place.z]
            self.send(down, source, at, 4, z_to, downward, 4 + number, number)

    def plane_raw(self, conditions, source, at, z_to):
        if self.pieces[at].flip == 0:
            self.send(conditions, source(at, z_to, (True, True)), at, 0, z_to, by_y, 8)
            self.send(conditions, source(at, z_to, (True, False)), at, 2, z_to, by_y, 9)
        else:
            self.send(conditions, source(at, z_to, (True, True)), at, 0, z_to, by_x, 8)
            self.send(conditions, source(at, z_to, (False, True)), at, 1, z_to, by_x, 9)

    def plane_pair(self, conditions, at, z_to):
        flip = self.pieces[at].flip
        held = self.landed(at, 0, z_to)

        def body():
            self.arrived(at, 0, z_to)
            add_rows(held, [held, self.part_of(at, z_to, (flip == 1, flip == 0))])

        when(conditions, body)
        if flip == 0:
            self.send(conditions, held, at, 1, z_to, by_x, 10)
        else:
            self.send(conditions, held, at, 2, z_to, by_y, 10)

    def pair(self, at, step):
        z_to = self.destination(step)
        self.plane_pair([self.has(at, z_to)], at, z_to)

    def line(self, at, step):
        place, piece = self.place, self.pieces[at]
        z = place.z
        z_to = self.destination(step)
        conditions = [self.has(at, z_to)]
        first, last = z == 0, z == place.line_size - 1
        inner = jnp.logical_and(z > 0, z < place.line_size - 1)
        ways = (
            (3, [z_to > z], [first], [z > 0], upward, 0),
            (4, [z_to < z], [last], [z < place.line_size - 1], downward, 4),
        )
        ends = (([first], (4,)), ([last], (3,)), ([inner], (3, 4)))
        if not piece.lines_late:
            held = self.landed(at, 1, z_to)
            base = [held, self.landed(at, 2, z_to), self.part_of(at, z_to, quads[0])]

            def wait():
                self.arrived(at, 1, z_to)
                self.arrived(at, 2, z_to)

            when(conditions, wait)
            for kind, onward, starts, passes, step_to, number in ways:
                when(conditions + onward + starts, lambda: add_rows(held, base))

                def passing():
                    self.arrived(at, kind, z_to)
                    add_rows(held, base + [self.landed(at, kind, z_to)])

                when(conditions + onward + passes, passing)
                self.send(conditions + onward, held, at, kind, z_to, step_to, number)
            for which, kinds in ends:

                def end():
                    for kind in kinds:
                        self.arrived(at, kind, z_to)
                    self.finish_rows(piece, base + [self.landed(at, kind, z_to) for kind in kinds])

                when(conditions + [z_to == z] + which, end)
            return
        for kind, onward, _, passes, step_to, number in ways:
            for at_quad, quad in enumerate(quads):
                held = self.landed(at, kind, z_to, at_quad)

                def passing():
                    self.arrived(at, kind, z_to, at_quad)
                    add_rows(held, [held, self.part_of(at, z_to, quad)])

                which = conditions + onward + passes
                when(which, passing)
                self.send(which, held, at, kind, z_to, step_to, number + at_quad, at_quad)
        here = conditions + [z_to == z]
        for which, kinds in ends:

            def end():
                for at_quad, quad in reversed(list(enumerate(quads))):
                    own = self.part_of(at, z_to, quad)
                    for kind in kinds:
                        self.arrived(at, kind, z_to, at_quad)
                    add_rows(own, [own] + [self.landed(at, kind, z_to, at_quad) for kind in kinds])

            when(here + which, end)
        if step == place.line_size - 1:
            self.plane_raw(here, self.part_of, at, z_to)

    def tail(self, at):
        z, piece = self.place.z, self.pieces[at]
        conditions = [self.has(at, z)]
        self.plane_pair(conditions, at, z)

        def end():
            self.arrived(at, 1, z)
            self.arrived(at, 2, z)
            total = [self.landed(at, kind, z) for kind in (1, 2)] + [self.part_of(at, z, quads[0])]
            self.finish_rows(piece, total)

        when(conditions, end)

    def run(self, plan, stages):
        for kind, at, number in plan:
            if kind == 0:
                self.raw(at, number)
            elif kind == 1:
                self.pair(at, number)
            elif kind == 2:
                self.line(at, number)
            elif kind == 3:
                self.tail(at)
            else:
                stages[at]()

    def finish(self):
        for conditions, which in self.sends:
            when(conditions, lambda: self.copy(*which).wait_send())


class Moves:
    def __init__(self, place, local_sems, send_sems, recv_sems):
        self.other = (place.index(place.z), 1 - place.core)
        self.local_sems, self.send_sems, self.recv_sems = local_sems, send_sems, recv_sems
        self.locals, self.remotes = 0, 0
        self.to_end = []

    def local(self, source, target):
        made = pltpu.make_async_copy(source, target, self.local_sems.at[self.locals])
        self.locals += 1
        made.start()
        return made

    def save(self, source, target):
        self.to_end.append(self.local(source, target).wait)

    def across(self, source, target, arrives=None):
        sems = dict(
            send_sem=self.send_sems.at[self.remotes],
            recv_sem=self.recv_sems.at[self.remotes],
            device_id=self.other,
            device_id_type=MESH,
        )
        self.remotes += 1
        made = pltpu.make_async_remote_copy(src_ref=source, dst_ref=target, **sems)
        made.start()
        self.to_end.append(made.wait_send)
        arrives = target if arrives is None else arrives
        return pltpu.make_async_remote_copy(src_ref=arrives, dst_ref=arrives, **sems)

    def finish(self):
        for wait in self.to_end:
            wait()


class Rows:
    def __init__(self, text, visual):
        self.text, self.visual = text, visual
        self.split = 2 * text
        self.count = 2 * (text + visual)
        self.spans = ((0, self.split), (self.split, self.count))
        self.own = ((0, text), (self.split, self.split + visual))
        self.other = ((text, self.split), (self.split + visual, self.count))
        self.packed = ((0, text), (text, text + visual))
        self.sizes = (chunk_of(text), chunk_of(visual))

    def over(self, body):
        for s, (first, last) in enumerate(self.spans):
            over_rows(first, last, self.sizes[s], functools.partial(body, s))

    def over_own(self, s, body):
        shift = self.own[s][0] - self.packed[s][0]

        def shifted(piece):
            body(pl.ds(pl.multiple_of(piece.start + shift, row_tile), piece.size), piece)

        over_rows(*self.packed[s], self.sizes[s], shifted)

    def swap_parts(self, moves, wide, received):
        return [
            moves.across(wide.at[slice(*self.other[s])], received.at[slice(*self.packed[s])])
            for s in range(2)
        ]

    def swap_own(self, moves, ref, s):
        return moves.across(ref.at[slice(*self.own[s])], ref.at[slice(*self.other[s])])


def chunk_of(count):
    return max(size for size in range(row_tile, 385, row_tile) if count % size == 0)


def query_spans(count):
    edges = list(range(0, count - 256, 512)) + [count]
    return list(zip(edges[:-1], edges[1:]))


def head_wide(values, odd):
    empty = jnp.zeros_like(values)
    return jnp.concatenate([empty, values] if odd else [values, empty], 0)


def column_of(row, count):
    return jnp.broadcast_to(row, (lane, count)).T


def scratch_of(group):
    return [pltpu.VMEM(shape, dtype) for shape, dtype in group]


def shapes_of(group):
    return [jax.ShapeDtypeStruct(shape, dtype) for shape, dtype in group]


def same_as(arrays):
    return [(array.shape, array.dtype) for array in arrays]


def sems(*counts):
    return [pltpu.SemaphoreType.DMA(count if isinstance(count, tuple) else (count,)) for count in counts]


def specs_of(count, in_vmem):
    spaces = [pltpu.VMEM] * in_vmem + [pl.ANY] * (count - in_vmem)
    return [pl.BlockSpec(memory_space=space) for space in spaces]


front_pieces = (
    (0, 0, 0, 48, 0, False), (0, 1, 0, 48, 1, False), (1, 0, 0, 32, 0, False), (1, 0, 32, 16, 0, True),
    (1, 1, 0, 32, 1, False), (1, 1, 32, 16, 1, True), (2, 0, 0, 48, 0, False), (2, 1, 0, 48, 1, False),
    (3, 0, 0, 64, 0, False), (3, 0, 64, 32, 0, True), (3, 1, 0, 64, 1, False), (3, 1, 64, 32, 1, True),
)
front_plan = (
    (0, 1, 0), (0, 0, 0), (5, 0, 0), (0, 3, 0), (0, 6, 0), (2, 1, 1), (0, 5, 0), (1, 1, 0), (2, 0, 1),
    (0, 4, 0), (2, 1, 2), (3, 5, 1), (2, 0, 2), (2, 6, 1), (1, 0, 1), (1, 0, 0), (5, 1, 0), (0, 2, 0),
    (2, 1, 3), (1, 1, 2), (2, 0, 3), (0, 7, 0), (2, 7, 1), (1, 1, 3), (1, 0, 3), (3, 3, 1), (1, 0, 2),
    (2, 4, 1), (1, 1, 1), (1, 6, 0), (2, 2, 1), (0, 11, 0), (0, 10, 0), (0, 8, 0), (3, 5, 2), (2, 2, 2),
    (1, 2, 0), (2, 4, 2), (4, 0, 0), (2, 6, 2), (1, 7, 0), (3, 5, 3), (5, 2, 0), (5, 3, 0), (1, 7, 1),
    (3, 3, 2), (5, 4, 0), (2, 4, 3), (1, 6, 1), (2, 7, 2), (2, 8, 1), (5, 5, 0), (3, 5, 4), (3, 11, 1),
    (2, 6, 3), (1, 2, 2), (1, 6, 2), (2, 10, 1), (5, 6, 0), (1, 7, 2), (0, 9, 0), (5, 7, 0), (1, 2, 1),
    (1, 4, 2), (2, 7, 3), (1, 6, 3), (5, 8, 0), (2, 10, 2), (2, 8, 2), (1, 4, 1), (1, 7, 3), (3, 11, 2),
    (3, 3, 3), (2, 2, 3), (1, 8, 1), (5, 9, 0), (5, 10, 0), (1, 4, 3), (5, 11, 0), (4, 2, 0), (1, 4, 0),
    (5, 12, 0), (1, 10, 0), (1, 2, 3), (3, 9, 1), (3, 3, 4), (5, 13, 0), (1, 8, 2), (3, 11, 3), (2, 10, 3),
    (1, 10, 1), (4, 1, 0), (1, 10, 2), (5, 14, 0), (3, 9, 2), (5, 15, 0), (2, 8, 3), (5, 16, 0), (3, 9, 3),
    (1, 8, 0), (3, 11, 4), (1, 10, 3), (5, 17, 0), (1, 8, 3), (3, 9, 4), (5, 18, 0), (4, 3, 0),
)
ffn_pieces = (
    (0, 0, 0, 96, 0, False), (0, 1, 0, 96, 1, False),
)
ffn_plan = (
    (0, 1, 0), (0, 0, 0), (4, 0, 0), (0, 1, 1), (0, 0, 1), (1, 0, 0), (4, 1, 0), (1, 1, 0), (0, 1, 2),
    (4, 2, 0), (1, 0, 1), (0, 0, 2), (1, 1, 1), (2, 1, 0), (4, 3, 0), (2, 0, 0), (1, 0, 2), (0, 0, 3),
    (0, 1, 3), (1, 1, 2), (4, 4, 0), (2, 0, 1), (4, 5, 0), (2, 0, 2), (1, 0, 3), (1, 1, 3), (2, 1, 1),
    (2, 1, 2), (4, 6, 0), (2, 0, 3), (4, 7, 0), (2, 1, 3),
)
attention_pieces = (
    (0, 0, 0, 48, 0, False), (0, 1, 0, 32, 1, False), (0, 1, 32, 16, 1, True), (1, 0, 0, 48, 0, False),
    (1, 1, 0, 48, 1, False), (2, 0, 0, 48, 0, False), (2, 1, 0, 48, 1, False),
)
attention_plan = (
    (0, 0, 0), (0, 1, 0), (4, 0, 0), (0, 0, 1), (0, 0, 2), (0, 2, 0), (1, 0, 0), (0, 4, 0), (0, 2, 1),
    (0, 3, 0), (4, 1, 0), (0, 1, 1), (2, 2, 0), (4, 2, 0), (0, 4, 1), (0, 1, 2), (1, 4, 0), (0, 3, 1),
    (4, 3, 0), (0, 3, 2), (4, 4, 0), (0, 0, 3), (1, 1, 0), (4, 5, 0), (0, 4, 2), (0, 4, 3), (0, 3, 3),
    (1, 1, 1), (4, 6, 0), (1, 0, 1), (0, 1, 3), (1, 3, 0), (1, 3, 1), (1, 1, 2), (4, 7, 0), (1, 0, 2),
    (2, 0, 0), (1, 4, 1), (4, 8, 0), (0, 2, 2), (1, 1, 3), (1, 0, 3), (4, 9, 0), (2, 3, 0), (0, 6, 0),
    (1, 4, 2), (2, 4, 0), (2, 1, 0), (0, 5, 0), (2, 2, 1), (0, 6, 1), (2, 2, 2), (1, 6, 0), (1, 3, 2),
    (2, 1, 1), (0, 5, 1), (1, 5, 0), (0, 5, 2), (2, 0, 1), (2, 1, 2), (0, 2, 3), (2, 3, 1), (0, 6, 2),
    (2, 6, 0), (2, 2, 3), (2, 0, 2), (1, 5, 1), (1, 6, 1), (2, 3, 2), (2, 4, 1), (2, 5, 0), (1, 5, 2),
    (3, 2, 0), (1, 6, 2), (2, 0, 3), (1, 4, 3), (2, 1, 3), (2, 4, 2), (1, 3, 3), (0, 5, 3), (0, 6, 3),
    (2, 6, 1), (4, 10, 0), (4, 12, 0), (2, 5, 1), (2, 6, 2), (2, 5, 2), (2, 4, 3), (1, 5, 3), (1, 6, 3),
    (2, 3, 3), (4, 11, 0), (2, 6, 3), (2, 5, 3),
)


class FrontIn(NamedTuple):
    w_qkv: object
    w_gate: object
    w_up: object
    gain_attn: object
    gain_ffn: object
    text_mask: object
    visual_mask: object
    text: object
    visual: object
    text_dy: object
    visual_dy: object
    w_out: object
    w_down: object


class FrontOut(NamedTuple):
    full_qkv: object
    full_up: object
    full_out: object
    full_down: object
    h: object
    qkv: object
    gates_t: object
    text_t: object
    visual_t: object
    logs: object
    mix_t: object
    middle: object
    hm: object
    act: object
    slope: object
    part_down: object
    dy: object
    gains: object
    bias: object


class FrontKept(NamedTuple):
    s_h: object
    s_qkv: object
    s_gates_t: object
    s_text_t: object
    s_visual_t: object
    s_logs: object
    s_mix_t: object
    s_middle: object
    s_hm: object
    s_act: object
    s_slope: object
    s_part_down: object
    s_dy: object
    s_gains: object
    s_bias: object


class FrontScratch(NamedTuple):
    own_qkv: object
    own_up: object
    s_w_qkv: object
    s_w_up: object
    s_w_out: object
    x: object
    wide: object
    received: object
    gate_rows: object
    q_t: object
    v_t: object
    mix: object


def prepare_shards(v, core, heads):
    first = core == 0
    rows = v.w_qkv.shape[1]
    third = v.w_qkv.shape[2] // 3
    half = third // 2
    lanes = lax.broadcasted_iota(jnp.int32, (rows, lane), 1)
    for s in range(2):
        for at in range(3):
            columns = [v.w_qkv[s, :, at * third + way * half : at * third + (way + 1) * half] for way in (0, 1)]
            v.own_qkv[s, :, at * half : (at + 1) * half] = jnp.where(first, *columns)
        gate = v.w_gate[s, :, :].astype(full)
        gate = jnp.where(first, gate[:, :heads], gate[:, heads:])
        small = jnp.concatenate([gate, jnp.zeros((rows, lane - heads), full)], 1)
        for at, ref in enumerate((v.gain_attn, v.gain_ffn)):
            row = jnp.concatenate([ref[s : s + 1, :].astype(full), jnp.zeros((1, lane - rows), full)], 1)
            small = jnp.where(lanes == heads + at, jnp.broadcast_to(row, (lane, lane)).T[:rows], small)
        v.own_qkv[s, :, 3 * half :] = small.astype(low)


def prepare_hidden(v, core, block):
    first = core == 0
    for s in range(2):
        pieces = []
        for start in range(0, v.w_up.shape[2], 2 * block):
            ways = [v.w_up[s, :, start + way * block : start + (way + 1) * block].astype(full) for way in (0, 1)]
            pieces.append(jnp.where(first, *ways))
        v.own_up[s, :, :] = jnp.concatenate(pieces, 1).astype(low)


def prepare_bias(v, core):
    pieces = []
    for ref in (v.text_mask, v.visual_mask):
        mask = ref[...].astype(full)
        half = mask.shape[1] // 2
        swapped = jnp.concatenate([mask[:, half:], mask[:, :half]], 1)
        pieces.append(jnp.where(core == 0, mask, swapped))
    row = jnp.concatenate(pieces, 1)
    v.s_bias[...] = column_of(jnp.where(row > 0.0, 0.0, big_negative), row.shape[1])


def attend_head(rows, head_width, v, number):
    width = v.s_qkv.shape[1] // 3
    pair = 2 * head_width
    at, odd = number // 2, number % 2
    keys = v.s_qkv[:, width + at * pair : width + (at + 1) * pair]
    bias = v.s_bias[:, 0:1]
    head = slice(number * head_width, (number + 1) * head_width)
    for first, last in query_spans(rows.count):
        scores = dot(keys, head_wide(v.q_t[head, first:last], odd)) + bias
        for t, target in enumerate((v.s_text_t, v.s_visual_t)):
            start, stop = rows.spans[t]
            part = scores[start:stop]
            top = jnp.max(part, 0, keepdims=True)
            raised = jnp.exp(part - top)
            total = jnp.sum(raised, 0, keepdims=True)
            probs = (raised * (1.0 / total)).astype(low)
            target[head, first:last] = dot(v.v_t[head, start:stop], probs)
            row = 8 * t + number
            v.s_logs[row : row + 1, first:last] = top + jnp.log(total)


def front_kernel(line_size, heads, scale, pieces, plan, *refs):
    groups = []
    for group in (FrontIn, FrontOut, FrontKept, FrontScratch):
        count = len(group._fields)
        groups.append(group(*refs[:count]))
        refs = refs[count:]
    v = merged(*groups)
    place = Place(line_size)
    core = place.core
    rows = Rows(v.text.shape[1], v.visual.shape[1])
    shard, block = v.w_qkv.shape[1], v.w_down.shape[1] // 2
    gather = Gather(
        place,
        pieces,
        (shard, shard, shard, block),
        (False, False, True, False),
        ((v.own_qkv, 0), (v.own_up, 0), (v.w_out, 0), (v.w_down, core * block)),
        (v.full_qkv, v.full_up, v.full_out, v.full_down),
        *refs[:3],
    )
    moves = Moves(place, *refs[3:])
    width = v.s_qkv.shape[1] // 3
    head_width = width // heads
    hidden = v.s_act.shape[1]
    arrivals = {}

    place.greet()
    prepare_shards(v, core, heads)
    place.meet()
    loads, swaps = [], []
    for sources, target in (((v.text, v.visual), v.x), ((v.text_dy, v.visual_dy), v.s_dy)):
        for s in range(2):
            loads.append(moves.local(sources[s].at[0], target.at[slice(*rows.own[s])]))
            swaps.append(moves.across(sources[s].at[0], target.at[slice(*rows.other[s])]))

    def prepare():
        prepare_hidden(v, core, block)

    def norm():
        prepare_bias(v, core)
        moves.save(v.s_bias, v.bias)
        for s in range(2):
            loads[s].wait()
            swaps[s].wait_recv()

        def body(s, piece):
            v.wide[piece, :] = normalize(v.x[piece, :].astype(full))[0]

        rows.over(body)

    def lower():
        moves.local(v.full_qkv, v.s_w_qkv).wait()
        for s in range(2):
            small = v.s_w_qkv[s, :, 3 * width :].astype(full).T
            v.s_gains[s, :, :] = small[heads : heads + 2]

        def body(s, piece):
            v.s_h[piece, :] = (v.wide[piece, :] * v.s_gains[s, 0:1, :]).astype(low)

        rows.over(body)
        moves.save(v.s_gains, v.gains)
        moves.save(v.s_h, v.h)

    def project(s):
        first, last = rows.spans[s]
        even = 3 * width // 256 * 256

        def columns(piece):
            v.s_qkv[first:last, piece] = dot(v.s_h[first:last, :], v.s_w_qkv[s, :, piece]).astype(low)

        over_columns(0, even, 256, columns)
        rest = dot(v.s_h[first:last, :], v.s_w_qkv[s, :, even:])
        v.s_qkv[first:last, even:] = rest[:, : 3 * width - even].astype(low)
        v.gate_rows[first:last, :] = rest[:, 3 * width - even :]

    def project_visual():
        project(1)
        v.s_gates_t[...] = jax.nn.sigmoid(v.gate_rows[...].T[:8, :])
        v.q_t[...] = (v.s_qkv[:, :width] * jnp.asarray(scale, low)).T
        v.v_t[...] = v.s_qkv[:, 2 * width :].T
        moves.save(v.s_qkv, v.qkv)
        moves.save(v.s_gates_t, v.gates_t)

    def mix():
        moves.save(v.s_text_t, v.text_t)
        moves.save(v.s_visual_t, v.visual_t)
        moves.save(v.s_logs, v.logs)
        is_text = lax.broadcasted_iota(jnp.int32, (1, rows.count), 1) < rows.split
        for head in range(heads):
            span = slice(head * head_width, (head + 1) * head_width)
            gate = v.s_gates_t[head : head + 1, :]
            to_text = jnp.where(is_text, gate, 1.0 - gate)
            v.s_mix_t[span, :] = (
                to_text * v.s_text_t[span, :] + (1.0 - to_text) * v.s_visual_t[span, :]
            ).astype(low)
        v.mix[...] = v.s_mix_t[...].T
        moves.save(v.s_mix_t, v.mix_t)

    def branch():
        moves.local(v.full_out, v.s_w_out).wait()
        for s, (first, last) in enumerate(rows.spans):

            def columns(piece):
                v.wide[first:last, piece] = dot(v.mix[first:last, :], v.s_w_out[s, :, piece])

            over_columns(0, v.wide.shape[1], 256, columns)
        arrivals[0] = rows.swap_parts(moves, v.wide, v.received)

    def middle():
        arrivals[1] = []
        for s in range(2):
            arrivals[0][s].wait_recv()

            def body(piece, packed):
                value = v.x[piece, :].astype(full) + v.wide[piece, :] + v.received[packed, :]
                v.s_middle[packed, :] = value
                v.s_hm[piece, :] = (normalize(value)[0] * v.s_gains[s, 1:2, :]).astype(low)

            rows.over_own(s, body)
            arrivals[1].append(rows.swap_own(moves, v.s_hm, s))
        moves.save(v.s_middle, v.middle)

    def upward_part(s, start, stop):
        first, last = rows.spans[s]

        def columns(piece):
            act, slope = gelu_both(dot(v.s_hm[first:last, :], v.s_w_up[s, :, piece]))
            v.s_act[first:last, piece] = act.astype(low)
            v.s_slope[first:last, piece] = slope.astype(low)

        over_columns(start, stop, 256, columns)

    def up_first():
        load = moves.local(v.full_up, v.s_w_up)
        for s in range(2):
            arrivals[1][s].wait_recv()
            loads[2 + s].wait()
            swaps[2 + s].wait_recv()
        moves.save(v.s_hm, v.hm)
        moves.save(v.s_dy, v.dy)
        load.wait()
        upward_part(0, 0, hidden // 2)

    def up_second():
        upward_part(0, hidden // 2, hidden)

    def up_third():
        upward_part(1, 0, hidden)
        moves.save(v.s_act, v.act)
        moves.save(v.s_slope, v.slope)

    def down_part(s, start, stop):
        first, last = rows.spans[s]

        def columns(piece):
            v.s_part_down[s, piece, :] = dot_rows(v.s_act[first:last, piece], v.s_dy[first:last, :]).astype(low)

        over_columns(start, stop, 256, columns)

    def down_first():
        down_part(0, 0, hidden)

    def down_second():
        down_part(1, 0, hidden)
        moves.save(v.s_part_down, v.part_down)

    stages = [prepare, norm, lower, functools.partial(project, 0), project_visual]
    stages += [functools.partial(attend_head, rows, head_width, v, head) for head in range(heads)]
    stages += [mix, branch, middle, up_first, up_second, up_third, down_first, down_second]
    gather.run(plan, stages)
    moves.finish()
    gather.finish()


def front(n_docs, heads, scale, pieces, plan, inputs):
    line_size = n_docs // 4
    count = 2 * (inputs.text.shape[1] + inputs.visual.shape[1])
    dim = inputs.w_out.shape[2]
    width, hidden = inputs.w_qkv.shape[2] // 6, inputs.w_up.shape[2] // 2
    wide = 3 * width + lane
    shard = inputs.w_qkv.shape[1]
    kept = FrontKept(
        s_h=((count, dim), low),
        s_qkv=((count, 3 * width), low),
        s_gates_t=((8, count), full),
        s_text_t=((width, count), full),
        s_visual_t=((width, count), full),
        s_logs=((16, count), full),
        s_mix_t=((width, count), low),
        s_middle=((count // 2, dim), full),
        s_hm=((count, dim), low),
        s_act=((count, hidden), low),
        s_slope=((count, hidden), low),
        s_part_down=((2, hidden, dim), low),
        s_dy=((count, dim), low),
        s_gains=((2, 2, dim), full),
        s_bias=((count, lane), full),
    )
    weights = (
        ((2, dim, wide), low),
        ((2, dim, hidden), low),
        ((2, width, dim), low),
        ((2, hidden, dim), low),
    )
    scratch = FrontScratch(
        own_qkv=((2, shard, wide), low),
        own_up=((2, shard, hidden), low),
        s_w_qkv=weights[0],
        s_w_up=weights[1],
        s_w_out=weights[2],
        x=((count, dim), low),
        wide=((count, dim), full),
        received=((count // 2, dim), full),
        gate_rows=((count, lane), full),
        q_t=((width, count), low),
        v_t=((width, count), low),
        mix=((count, width), low),
    )
    results = FrontOut(*weights, *kept)
    values = pl.pallas_call(
        functools.partial(front_kernel, line_size, heads, scale, pieces, plan),
        out_shape=shapes_of(results),
        in_specs=specs_of(len(inputs), 7),
        out_specs=specs_of(len(results), 0),
        scratch_shapes=scratch_of(kept)
        + scratch_of(scratch)
        + sems((len(pieces), n_docs, 4), (len(pieces), n_docs), len(pieces), 32, 12, 12),
        compiler_params=pltpu.CompilerParams(
            collective_id=0, has_side_effects=True, vmem_limit_bytes=vmem_limit
        ),
        name="gather_and_front",
    )(*inputs)
    return FrontOut(*values)


def scatter_buffers(pieces, arrays, splits, n_docs):
    line_size = n_docs // 4
    group = []
    for piece in pieces:
        ends = line_size // 2 if splits[piece.array] else line_size
        block = (piece.rows, arrays[piece.array][0][2])
        if piece.lines_late:
            group += [((1, *block), low)] * 3 + [((ends, 4, *block), low)] * 2
        else:
            group += [((ends, *block), low)] * 5
    return scratch_of(group)


def grouped(refs, size):
    return [refs[first : first + size] for first in range(0, len(refs), size)]


def norm_back(grad, normed, inverse, gain):
    scaled = grad * gain
    return inverse * (
        scaled
        - jnp.mean(scaled, -1, keepdims=True)
        - normed * jnp.mean(scaled * normed, -1, keepdims=True)
    )


class FfnIn(NamedTuple):
    full_down: object
    dy: object
    slope: object
    full_up: object
    part_down: object
    hm: object
    middle: object
    gains: object
    act: object
    full_out: object
    mix_t: object
    text_t: object
    visual_t: object
    gates_t: object


class FfnLoaded(NamedTuple):
    s_full_down: object
    s_dy: object
    s_slope: object
    s_full_up: object
    s_part_down: object
    s_hm: object
    s_middle: object
    s_gains: object
    s_act: object
    s_full_out: object
    s_mix_t: object
    s_text_t: object
    s_visual_t: object
    s_gates_t: object


class FfnOut(NamedTuple):
    text_out: object
    visual_out: object
    grad_down: object
    part_up: object
    part_out: object
    grad_middle: object
    gain_part: object
    gate_grad_t: object
    text_grad_t: object
    visual_grad_t: object


class FfnScratch(NamedTuple):
    s_part_up: object
    s_part_out: object
    s_grad_middle: object
    s_gain_part: object
    s_gate_grad_t: object
    s_text_grad_t: object
    s_visual_grad_t: object
    stage: object
    wide: object
    wide_out: object
    received: object
    received_out: object
    branch: object
    result: object
    mix_grad: object
    mix_grad_t: object


def ffn_kernel(line_size, heads, pieces, plan, *refs):
    groups = []
    for group in (FfnIn, FfnOut, FfnLoaded, FfnScratch):
        count = len(group._fields)
        groups.append(group(*refs[:count]))
        refs = refs[count:]
    v = merged(*groups)
    buffers = grouped(refs[: 5 * len(pieces)], 5)
    send_sems, recv_sems, *move_sems = refs[5 * len(pieces) :]
    place = Place(line_size)
    moves = Moves(place, *move_sems)
    rows = Rows(v.text_out.shape[1], v.visual_out.shape[1])
    width = v.mix_t.shape[0]
    head_width = width // heads
    hidden, dim = v.act.shape[1], v.hm.shape[1]
    arrivals = {}

    def finish_rows(piece, total):
        add_rows(v.stage.at[piece.part], total, piece.first)

    scatter = Scatter(
        place, pieces, (False,), (v.part_down,), (v.s_part_down,), buffers, send_sems, recv_sems, finish_rows
    )
    place.greet()
    loads = FfnIn(*(moves.local(source, target) for source, target in zip(groups[0], groups[2])))
    place.meet()

    def back_hidden():
        loads.full_down.wait()
        loads.dy.wait()
        loads.slope.wait()
        for s, (first, last) in enumerate(rows.spans):

            def columns(piece):
                grad = dot_back(v.s_dy[first:last, :], v.s_full_down[s, piece, :])
                slope = v.s_slope[first:last, piece].astype(full)
                v.s_slope[first:last, piece] = (grad * slope).astype(low)

            over_columns(0, hidden, 256, columns)
        loads.part_down.wait()

    def back_up():
        loads.full_up.wait()
        for s, (first, last) in enumerate(rows.spans):

            def columns(piece):
                v.wide[first:last, piece] = dot_back(v.s_slope[first:last, :], v.s_full_up[s, piece, :])

            over_columns(0, dim, 256, columns)
        arrivals[0] = rows.swap_parts(moves, v.wide, v.received)

    def up_part():
        loads.hm.wait()
        for s, (first, last) in enumerate(rows.spans):

            def columns(piece):
                v.s_part_up[s, piece, :] = dot_rows(v.s_hm[first:last, piece], v.s_slope[first:last, :]).astype(low)

            over_columns(0, dim, 256, columns)
        moves.save(v.s_part_up, v.part_up)

    def middle():
        loads.middle.wait()
        loads.gains.wait()
        arrivals[1] = []
        for s in range(2):
            arrivals[0][s].wait_recv()
            v.s_gain_part[s, :, :] = jnp.zeros((8, dim), full)

            def body(piece, packed):
                normed, inverse = normalize(v.s_middle[packed, :])
                grad = v.wide[piece, :] + v.received[packed, :]
                v.s_gain_part[s, 0:1, :] += jnp.sum(grad * normed, 0, keepdims=True)
                grad = v.s_dy[piece, :].astype(full) + norm_back(grad, normed, inverse, v.s_gains[s, 1:2, :])
                v.s_grad_middle[packed, :] = grad
                v.branch[piece, :] = grad.astype(low)

            rows.over_own(s, body)
            arrivals[1].append(rows.swap_own(moves, v.branch, s))
        moves.save(v.s_gain_part, v.gain_part)
        moves.save(v.s_grad_middle, v.grad_middle)

    def result_part():
        loads.act.wait()
        for s, (first, last) in enumerate(rows.spans):

            def columns(piece):
                v.wide_out[first:last, piece] = dot(v.s_act[first:last, :], v.s_full_down[s, :, piece])

            over_columns(0, dim, 256, columns)
        arrivals[2] = rows.swap_parts(moves, v.wide_out, v.received_out)

    def out_part():
        loads.full_out.wait()
        loads.mix_t.wait()
        for s, (first, last) in enumerate(rows.spans):
            arrivals[1][s].wait_recv()
            v.s_part_out[s, :, :] = dot(v.s_mix_t[:, first:last], v.branch[first:last, :]).astype(low)
            v.mix_grad[first:last, :] = dot_back(v.branch[first:last, :], v.s_full_out[s, :, :])
        moves.save(v.s_part_out, v.part_out)

    def gates():
        loads.text_t.wait()
        loads.visual_t.wait()
        loads.gates_t.wait()
        v.mix_grad_t[...] = v.mix_grad[...].T
        is_text = lax.broadcasted_iota(jnp.int32, (1, rows.count), 1) < rows.split
        for head in range(heads):
            span = slice(head * head_width, (head + 1) * head_width)
            gate = v.s_gates_t[head : head + 1, :]
            to_text = jnp.where(is_text, gate, 1.0 - gate)
            grad = v.mix_grad_t[span, :]
            toward = jnp.sum(grad * (v.s_text_t[span, :] - v.s_visual_t[span, :]), 0, keepdims=True)
            v.s_gate_grad_t[head : head + 1, :] = (
                jnp.where(is_text, toward, -toward) * gate * (1.0 - gate)
            )
            v.s_text_grad_t[span, :] = (to_text * grad).astype(low)
            v.s_visual_grad_t[span, :] = ((1.0 - to_text) * grad).astype(low)
        v.s_gate_grad_t[heads:, :] = jnp.zeros((8 - heads, rows.count), full)
        moves.save(v.s_gate_grad_t, v.gate_grad_t)
        moves.save(v.s_text_grad_t, v.text_grad_t)
        moves.save(v.s_visual_grad_t, v.visual_grad_t)

    def result():
        for s in range(2):
            arrivals[2][s].wait_recv()

            def body(piece, packed):
                v.result[packed, :] = (
                    v.s_middle[packed, :] + v.wide_out[piece, :] + v.received_out[packed, :]
                ).astype(low)

            rows.over_own(s, body)
            out = (v.text_out, v.visual_out)[s]
            moves.save(v.result.at[slice(*rows.packed[s])], out.at[0])

    scatter.run(plan, [back_hidden, back_up, up_part, middle, result_part, out_part, gates, result])
    block = v.stage.shape[1]
    mine = lambda core: v.grad_down.at[:, pl.ds(pl.multiple_of(core * block, row_tile), block), :]
    moves.save(v.stage, mine(place.core))
    moves.across(v.stage, mine(place.core), mine(1 - place.core)).wait_recv()
    moves.finish()
    scatter.finish()


def ffn_back(n_docs, heads, pieces, plan, text, visual, inputs):
    line_size = n_docs // 4
    count, hidden = inputs.act.shape
    dim, width = inputs.hm.shape[1], inputs.mix_t.shape[0]
    rows = inputs.part_down.shape[1] // n_docs
    scratch = FfnScratch(
        s_part_up=((2, dim, hidden), low),
        s_part_out=((2, width, dim), low),
        s_grad_middle=((count // 2, dim), full),
        s_gain_part=((2, 8, dim), full),
        s_gate_grad_t=((8, count), full),
        s_text_grad_t=((width, count), low),
        s_visual_grad_t=((width, count), low),
        stage=((2, rows, dim), full),
        wide=((count, dim), full),
        wide_out=((count, dim), full),
        received=((count // 2, dim), full),
        received_out=((count // 2, dim), full),
        branch=((count, dim), low),
        result=((count // 2, dim), low),
        mix_grad=((count, width), full),
        mix_grad_t=((width, count), full),
    )
    results = FfnOut(
        (text.shape, low), (visual.shape, low), ((2, 2 * rows, dim), full), *scratch[:7]
    )
    loaded = same_as(inputs)
    values = pl.pallas_call(
        functools.partial(ffn_kernel, line_size, heads, pieces, plan),
        out_shape=shapes_of(results),
        in_specs=specs_of(len(inputs), 0),
        out_specs=specs_of(len(results), 0),
        scratch_shapes=scratch_of(loaded)
        + scratch_of(scratch)
        + scatter_buffers(pieces, same_as([inputs.part_down]), (False,), n_docs)
        + sems((len(pieces), line_size, 11), (len(pieces), line_size, 11), 32, 10, 10),
        compiler_params=pltpu.CompilerParams(
            collective_id=1, has_side_effects=True, vmem_limit_bytes=vmem_limit
        ),
        name="ffn_back_and_scatter",
    )(*inputs)
    return FfnOut(*values)


class AttentionIn(NamedTuple):
    qkv: object
    logs: object
    text_t: object
    visual_t: object
    text_grad_t: object
    visual_grad_t: object
    bias: object
    part_up: object
    part_out: object
    gate_grad_t: object
    full_qkv: object
    h: object
    grad_middle: object
    gains: object
    gain_part: object
    text: object
    visual: object


class AttentionLoaded(NamedTuple):
    s_qkv: object
    s_logs: object
    s_text_t: object
    s_visual_t: object
    s_text_grad_t: object
    s_visual_grad_t: object
    s_bias: object
    s_part_up: object
    s_part_out: object
    s_gate_grad_t: object
    s_full_qkv: object
    s_h: object
    s_grad_middle: object
    s_gains: object
    s_gain_part: object


class AttentionOut(NamedTuple):
    text_grad: object
    visual_grad: object
    grad_qkv: object
    grad_gate: object
    grad_up: object
    grad_out: object
    grad_gain_attn: object
    grad_gain_ffn: object


class AttentionScratch(NamedTuple):
    part_qkv: object
    x: object
    q_t: object
    k_t: object
    query_grad_t: object
    text_grad_n: object
    visual_grad_n: object
    key_sum: object
    value_sum: object
    grad_wide: object
    wide: object
    received: object
    gain_sum: object
    stage_up: object
    stage_out: object
    stage_qkv: object
    peer_up: object
    peer_small: object
    s_grad_up: object
    s_grad_gate: object
    s_grad_gain_attn: object
    s_grad_gain_ffn: object


def attend_head_back(rows, head_width, scale, v, number):
    width = v.s_qkv.shape[1] // 3
    pair = 2 * head_width
    at, odd = number // 2, number % 2
    columns = [slice(third * width + at * pair, third * width + (at + 1) * pair) for third in range(3)]
    keys, values = v.s_qkv[:, columns[1]], v.s_qkv[:, columns[2]]
    if not odd:
        v.key_sum[...] = jnp.zeros_like(v.key_sum)
        v.value_sum[...] = jnp.zeros_like(v.value_sum)
    mine = lax.broadcasted_iota(jnp.int32, (1, pair), 1) // head_width == odd
    bias = v.s_bias[:, 0:1]
    sets = (
        (v.s_text_t, v.s_text_grad_t, v.text_grad_n),
        (v.s_visual_t, v.s_visual_grad_t, v.visual_grad_n),
    )
    head = slice(number * head_width, (number + 1) * head_width)
    for first, last in query_spans(rows.count):
        scores = dot(keys, head_wide(v.q_t[head, first:last], odd)) + bias
        queries = jnp.where(mine, v.s_qkv[first:last, columns[0]] * jnp.asarray(scale, low), 0)
        pieces = []
        for t, (output_t, grad_t, grad) in enumerate(sets):
            start, stop = rows.spans[t]
            out_grad = grad_t[head, first:last]
            delta = jnp.sum(out_grad.astype(full) * output_t[head, first:last], 0, keepdims=True)
            row = 8 * t + number
            probs = jnp.exp(scores[start:stop] - v.s_logs[row : row + 1, first:last])
            grad_probs = dot(values[start:stop], head_wide(out_grad, odd))
            grad_scores = (probs * (grad_probs - delta)).astype(low)
            natural = jnp.where(mine, grad[first:last, columns[0]], 0)
            v.value_sum[start:stop, :] += dot(probs.astype(low), natural)
            v.key_sum[start:stop, :] += dot(grad_scores, queries)
            pieces.append(grad_scores)
        v.query_grad_t[head, first:last] = (
            dot(v.k_t[head, :], jnp.concatenate(pieces, 0)) * scale
        ).astype(low)
    if odd:
        v.grad_wide[:, columns[1]] = v.key_sum[...].astype(low)
        v.grad_wide[:, columns[2]] = v.value_sum[...].astype(low)


def attention_kernel(line_size, heads, scale, block, pieces, plan, *refs):
    groups = []
    for group in (AttentionIn, AttentionOut, AttentionLoaded, AttentionScratch):
        count = len(group._fields)
        groups.append(group(*refs[:count]))
        refs = refs[count:]
    v = merged(*groups)
    buffers = grouped(refs[: 5 * len(pieces)], 5)
    send_sems, recv_sems, *move_sems = refs[5 * len(pieces) :]
    place = Place(line_size)
    core = place.core
    moves = Moves(place, *move_sems)
    rows = Rows(v.text.shape[1], v.visual.shape[1])
    width = v.qkv.shape[1] // 3
    head_width = width // heads
    dim = v.h.shape[1]
    stages_of = (v.stage_up, v.stage_out, v.stage_qkv)
    arrivals = {}

    def finish_rows(piece, total):
        add_rows(stages_of[piece.array].at[piece.part], total, piece.first)

    scatter = Scatter(
        place,
        pieces,
        (False, True, False),
        (v.part_up, v.part_out, v.part_qkv),
        (v.s_part_up, v.s_part_out, v.part_qkv),
        buffers,
        send_sems,
        recv_sems,
        finish_rows,
    )
    place.greet()
    loads = AttentionIn(
        *(moves.local(source, target) for source, target in zip(groups[0], groups[2])),
        *(moves.local(ref.at[0], v.x.at[slice(*rows.packed[s])]) for s, ref in enumerate((v.text, v.visual))),
    )
    place.meet()

    def prepare():
        for load in loads[:7]:
            load.wait()
        v.q_t[...] = (v.s_qkv[:, :width] * jnp.asarray(scale, low)).T
        v.k_t[...] = v.s_qkv[:, width : 2 * width].T
        v.text_grad_n[...] = v.s_text_grad_t[...].T
        v.visual_grad_n[...] = v.s_visual_grad_t[...].T
        loads.part_up.wait()
        loads.part_out.wait()

    def back_qkv():
        loads.gate_grad_t.wait()
        loads.full_qkv.wait()
        v.grad_wide[:, :width] = v.query_grad_t[...].T
        empty = jnp.zeros((lane - 8, rows.count), full)
        v.grad_wide[:, 3 * width :] = jnp.concatenate([v.s_gate_grad_t[...], empty], 0).T.astype(low)
        for s, (first, last) in enumerate(rows.spans):

            def columns(piece):
                v.wide[first:last, piece] = dot_back(v.grad_wide[first:last, :], v.s_full_qkv[s, piece, :])

            over_columns(0, dim, 256, columns)
        arrivals[0] = rows.swap_parts(moves, v.wide, v.received)

    def qkv_part():
        loads.h.wait()
        for s, (first, last) in enumerate(rows.spans):

            def columns(piece):
                v.part_qkv[s, piece, :] = dot_rows(v.s_h[first:last, piece], v.grad_wide[first:last, :]).astype(low)

            over_columns(0, dim, 256, columns)

    def tokens():
        loads.grad_middle.wait()
        loads.gains.wait()
        loads.gain_part.wait()
        for s in range(2):
            loads[15 + s].wait()
            arrivals[0][s].wait_recv()
            v.gain_sum[s, :, :] = jnp.zeros((lane, dim), full)
            v.gain_sum[s, heads + 1 : heads + 2, :] = v.s_gain_part[s, 0:1, :]

            def body(piece, packed):
                normed, inverse = normalize(v.x[packed, :].astype(full))
                grad = v.wide[piece, :] + v.received[packed, :]
                v.gain_sum[s, heads : heads + 1, :] += jnp.sum(grad * normed, 0, keepdims=True)
                v.s_grad_middle[packed, :] += norm_back(grad, normed, inverse, v.s_gains[s, 0:1, :])

            rows.over_own(s, body)
            small = v.part_qkv[s, :, 3 * width :].astype(full) + v.gain_sum[s, :, :].T
            v.part_qkv[s, :, 3 * width :] = small.astype(low)
            ref = (v.text_grad, v.visual_grad)[s]
            moves.save(v.s_grad_middle.at[slice(*rows.packed[s])], ref.at[0])

    def share_up():
        arrivals[1] = moves.across(v.stage_up, v.peer_up)

    def share_out():
        owner = place.z // (line_size // 2) == core
        moves_out = (
            pltpu.make_async_copy(v.stage_out, v.grad_out, moves.local_sems.at[moves.locals]),
            pltpu.make_async_remote_copy(
                src_ref=v.stage_out,
                dst_ref=v.grad_out,
                send_sem=moves.send_sems.at[moves.remotes],
                recv_sem=moves.recv_sems.at[moves.remotes],
                device_id=moves.other,
                device_id_type=MESH,
            ),
        )
        moves.locals += 1
        moves.remotes += 1

        def start():
            for move in moves_out:
                move.start()

        def wait():
            moves_out[0].wait()
            moves_out[1].wait_send()

        pl.when(owner)(start)
        moves.to_end.append(lambda: pl.when(owner)(wait))
        moves.to_end.append(lambda: pl.when(jnp.logical_not(owner))(lambda: moves_out[1].wait_recv()))

    def finish_up():
        arrivals[1].wait_recv()
        first = core == 0
        for s in range(2):
            pieces = []
            for start in range(0, v.stage_up.shape[2], block):
                own, peer = (ref[s, :, start : start + block] for ref in (v.stage_up, v.peer_up))
                pieces += [jnp.where(first, own, peer), jnp.where(first, peer, own)]
            v.s_grad_up[s, :, :] = jnp.concatenate(pieces, 1)
        moves.save(v.s_grad_up, v.grad_up)

    stages = [prepare]
    stages += [functools.partial(attend_head_back, rows, head_width, scale, v, head) for head in range(heads)]
    stages += [back_qkv, qkv_part, tokens, share_up, share_out, finish_up]
    scatter.run(plan, stages)

    def mine(third, of):
        first = third * 2 * width + of * width
        return v.grad_qkv.at[:, :, pl.ds(pl.multiple_of(first, lane), width)]

    small = v.stage_qkv.at[:, :, 3 * width :]
    last = [moves.across(small, v.peer_small)]
    for third in range(3):
        source = v.stage_qkv.at[:, :, third * width : (third + 1) * width]
        moves.save(source, mine(third, core))
        last.append(moves.across(source, mine(third, core), mine(third, 1 - core)))
    last[0].wait_recv()
    for s in range(2):
        own, peer = v.stage_qkv[s, :, 3 * width :], v.peer_small[s, :, :]
        columns = own.shape[0]
        gates = [jnp.where(core == 0, own, peer)[:, :heads], jnp.where(core == 0, peer, own)[:, :heads]]
        v.s_grad_gate[s, :, :] = jnp.concatenate(gates, 1)
        both = jnp.concatenate([own + peer, jnp.zeros((lane - columns, lane), full)], 0).T
        v.s_grad_gain_attn[s : s + 1, :] = both[heads : heads + 1, :columns]
        v.s_grad_gain_ffn[s : s + 1, :] = both[heads + 1 : heads + 2, :columns]
    moves.save(v.s_grad_gate, v.grad_gate)
    moves.save(v.s_grad_gain_attn, v.grad_gain_attn)
    moves.save(v.s_grad_gain_ffn, v.grad_gain_ffn)
    for arrival in last[1:]:
        arrival.wait_recv()
    moves.finish()
    scatter.finish()


def attention_back(n_docs, heads, scale, pieces, plan, inputs):
    line_size = n_docs // 4
    count, dim = inputs.h.shape
    width, wide = inputs.qkv.shape[1] // 3, inputs.full_qkv.shape[2]
    hidden = inputs.part_up.shape[2]
    rows = dim // n_docs
    block = hidden // n_docs
    splits = (False, True, False)
    part_qkv = ((2, dim, wide), low)
    arrays = same_as([inputs.part_up, inputs.part_out]) + [part_qkv]
    results = AttentionOut(
        text_grad=(inputs.text.shape, full),
        visual_grad=(inputs.visual.shape, full),
        grad_qkv=((2, rows, 6 * width), full),
        grad_gate=((2, rows, 2 * heads), full),
        grad_up=((2, rows, 2 * hidden), full),
        grad_out=((2, rows, dim), full),
        grad_gain_attn=((2, rows), full),
        grad_gain_ffn=((2, rows), full),
    )
    scratch = AttentionScratch(
        part_qkv=part_qkv,
        x=((count // 2, dim), low),
        q_t=((width, count), low),
        k_t=((width, count), low),
        query_grad_t=((width, count), low),
        text_grad_n=((count, width), low),
        visual_grad_n=((count, width), low),
        key_sum=((count, lane), full),
        value_sum=((count, lane), full),
        grad_wide=((count, wide), low),
        wide=((count, dim), full),
        received=((count // 2, dim), full),
        gain_sum=((2, lane, dim), full),
        stage_up=((2, rows, hidden), full),
        stage_out=((2, rows, dim), full),
        stage_qkv=((2, rows, wide), full),
        peer_up=((2, rows, hidden), full),
        peer_small=((2, rows, lane), full),
        s_grad_up=results.grad_up,
        s_grad_gate=results.grad_gate,
        s_grad_gain_attn=results.grad_gain_attn,
        s_grad_gain_ffn=results.grad_gain_ffn,
    )
    loaded = same_as(inputs[:-2])
    values = pl.pallas_call(
        functools.partial(attention_kernel, line_size, heads, scale, block, pieces, plan),
        out_shape=shapes_of(results),
        in_specs=specs_of(len(inputs), 0),
        out_specs=specs_of(len(results), 0),
        scratch_shapes=scratch_of(loaded)
        + scratch_of(scratch)
        + scatter_buffers(pieces, arrays, splits, n_docs)
        + sems((len(pieces), line_size, 11), (len(pieces), line_size, 11), 32, 12, 12),
        compiler_params=pltpu.CompilerParams(
            collective_id=2, has_side_effects=True, vmem_limit_bytes=vmem_limit
        ),
        name="attention_back_and_scatter",
    )(*inputs)
    return AttentionOut(*values)


def kernel_path(n_docs, heads, scale, inputs):
    made = [tuple(Piece(*each) for each in pieces) for pieces in (front_pieces, ffn_pieces, attention_pieces)]
    first = front(n_docs, heads, scale, made[0], front_plan, inputs)
    ffn_inputs = FfnIn(*(getattr(first, name) for name in FfnIn._fields))
    second = ffn_back(n_docs, heads, made[1], ffn_plan, inputs.text, inputs.visual, ffn_inputs)
    known = merged(inputs, first, second)
    attention_inputs = AttentionIn(*(getattr(known, name) for name in AttentionIn._fields))
    third = attention_back(n_docs, heads, scale, made[2], attention_plan, attention_inputs)
    return (
        second.text_out,
        second.visual_out,
        third.text_grad,
        third.visual_grad,
        third.grad_qkv,
        third.grad_out,
        third.grad_gate,
        third.grad_up,
        second.grad_down,
        third.grad_gain_attn,
        third.grad_gain_ffn,
    )


def swap(value):
    return lax.ppermute(value, core_axis, [(0, 1), (1, 0)])


def both(own):
    return jnp.concatenate([own, swap(own)], 0)


def own_sum(partial):
    rows = partial.shape[0] // 2
    return partial[:rows] + swap(partial[rows:])


def normalize_back(gradient, normed, inverse, gain):
    scaled = gradient * gain
    grad_gain = jnp.sum(gradient * normed, 0)
    grad_input = inverse * (
        scaled
        - jnp.mean(scaled, -1, keepdims=True)
        - normed * jnp.mean(scaled * normed, -1, keepdims=True)
    )
    return grad_input, grad_gain


def heads_of(values, heads):
    return values.reshape(values.shape[0], heads, -1)


def attend(queries, keys, values, valid, scale):
    scores = jnp.einsum("qhe,khe->hqk", queries, keys, preferred_element_type=full) * scale
    scores = jnp.where(valid, scores, big_negative)
    top = jnp.max(scores, -1)
    probs = jnp.where(valid, jnp.exp(scores - top[..., None]), 0.0)
    total = jnp.sum(probs, -1)
    weighted = jnp.einsum(
        "hqk,khe->qhe", probs.astype(low), values, preferred_element_type=full
    )
    return weighted / total.T[..., None], top + jnp.log(total)


def attend_back(queries, keys, values, valid, scale, log_total, grad_output, output):
    delta = jnp.sum(grad_output.astype(full) * output, -1).T
    scores = jnp.einsum("qhe,khe->hqk", queries, keys, preferred_element_type=full) * scale
    probs = jnp.where(valid, jnp.exp(scores - log_total[..., None]), 0.0)
    grad_values = jnp.einsum(
        "hqk,qhe->khe", probs.astype(low), grad_output, preferred_element_type=full
    )
    grad_probs = jnp.einsum("qhe,khe->hqk", grad_output, values, preferred_element_type=full)
    grad_scores = (probs * (grad_probs - delta[..., None])).astype(low)
    grad_queries = (
        jnp.einsum("hqk,khe->qhe", grad_scores, keys, preferred_element_type=full) * scale
    )
    grad_keys = (
        jnp.einsum("hqk,qhe->khe", grad_scores, queries, preferred_element_type=full) * scale
    )
    return grad_queries, grad_keys, grad_values


def on_device(
    n_docs,
    text_tokens,
    visual_tokens,
    text_mask,
    visual_mask,
    w_qkv,
    w_out,
    w_gate,
    w_up,
    w_down,
    gain_attn,
    gain_ffn,
    text_cotangent,
    visual_cotangent,
):
    core = lax.axis_index(core_axis)
    width = w_out.shape[2]
    all_heads = w_gate.shape[2]
    heads = all_heads // 2
    half = width // 2
    scale = (width // all_heads) ** (-0.5)
    if n_docs == 16 and w_qkv.shape[1] % row_tile == 0:
        inputs = FrontIn(
            w_qkv=w_qkv,
            w_gate=w_gate,
            w_up=w_up,
            gain_attn=gain_attn,
            gain_ffn=gain_ffn,
            text_mask=text_mask,
            visual_mask=visual_mask,
            text=text_tokens,
            visual=visual_tokens,
            text_dy=text_cotangent,
            visual_dy=visual_cotangent,
            w_out=w_out,
            w_down=w_down,
        )
        return kernel_path(n_docs, heads, scale, inputs)

    def own_columns(array, size, start=0):
        return lax.dynamic_slice_in_dim(array, start + core * size, size, 2)

    own_tokens = (text_tokens[0], visual_tokens[0])
    own_grads = (text_cotangent[0], visual_cotangent[0])

    def reorder(mask):
        rows = mask.shape[1] // 2
        return (
            jnp.concatenate(
                [
                    lax.dynamic_slice_in_dim(mask[0], core * rows, rows),
                    lax.dynamic_slice_in_dim(mask[0], (1 - core) * rows, rows),
                ]
            )
            > 0
        )

    valids = (reorder(text_mask), reorder(visual_mask))

    pad = lane - heads - 2
    shard = jnp.concatenate(
        [own_columns(w_qkv, half, column * width) for column in range(3)]
        + [
            own_columns(w_gate, heads),
            gain_attn[..., None],
            gain_ffn[..., None],
            jnp.zeros(w_gate.shape[:2] + (pad,), low),
        ],
        2,
    )
    tokens = tuple(both(value) for value in own_tokens)
    grads_out = tuple(both(value) for value in own_grads)
    gather = lambda array: lax.all_gather(array, docs_axis, axis=1, tiled=True)
    rows_half = lambda array: lax.dynamic_slice_in_dim(
        array, core * (array.shape[1] // 2), array.shape[1] // 2, 1
    )
    full_qkv = gather(shard)
    full_up = gather(own_columns(w_up, w_up.shape[2] // 2))
    full_out, full_down = rows_half(gather(w_out)), rows_half(gather(w_down))
    gains_attn = full_qkv[:, :, 3 * half + heads].astype(full)
    gains_ffn = full_qkv[:, :, 3 * half + heads + 1].astype(full)

    fronts = []
    for s in range(2):
        normed, inverse = normalize(tokens[s].astype(full))
        lowered = (normed * gains_attn[s]).astype(low)
        wide = dot(lowered, full_qkv[s])
        narrow = wide[:, : 3 * half].astype(low)
        gates = jax.nn.sigmoid(wide[:, 3 * half : 3 * half + heads])
        queries, keys, values = (
            heads_of(narrow[:, column * half : (column + 1) * half], heads) for column in range(3)
        )
        fronts.append((normed, inverse, lowered, gates, queries, keys, values))

    outputs, totals = {}, {}
    for s in range(2):
        for t in range(2):
            outputs[s, t], totals[s, t] = attend(
                fronts[s][4], fronts[t][5], fronts[t][6], valids[t], scale
            )

    results, tails = [], []
    for s in range(2):
        gates = fronts[s][3][..., None]
        own, cross = outputs[s, s], outputs[s, 1 - s]
        mixed = gates * own + (1.0 - gates) * cross
        mix = mixed.reshape(mixed.shape[0], -1).astype(low)
        middle = own_tokens[s].astype(full) + own_sum(dot(mix, full_out[s]))
        normed, inverse = normalize(middle)
        lowered = both((normed * gains_ffn[s]).astype(low))
        upward = dot(lowered, full_up[s])
        activated, gelu_back = jax.vjp(jax.nn.gelu, upward)
        act = activated.astype(low)
        results.append((middle + own_sum(dot(act, full_down[s]))).astype(low))
        part_down = dot_rows(act, grads_out[s]).astype(low)
        grad_up = gelu_back(dot_back(grads_out[s], full_down[s]))[0].astype(low)
        part_up = dot_rows(lowered, grad_up).astype(low)
        grad_in, part_gain = normalize_back(
            own_sum(dot_back(grad_up, full_up[s])), normed, inverse, gains_ffn[s]
        )
        grad_middle = own_grads[s].astype(full) + grad_in
        grad_branch = both(grad_middle.astype(low))
        part_out = dot_rows(mix, grad_branch).astype(low)
        grad_mix = heads_of(dot_back(grad_branch, full_out[s]), heads)
        grad_gate = (
            jnp.sum(grad_mix * (own - cross), -1) * fronts[s][3] * (1.0 - fronts[s][3])
        ).astype(low)
        grad_own = (gates * grad_mix).astype(low)
        grad_cross = ((1.0 - gates) * grad_mix).astype(low)
        tails.append(
            (grad_middle, grad_gate, grad_own, grad_cross, part_out, part_up, part_down, part_gain)
        )

    backs = {}
    for s in range(2):
        for t in range(2):
            backs[s, t] = attend_back(
                fronts[s][4],
                fronts[t][5],
                fronts[t][6],
                valids[t],
                scale,
                totals[s, t],
                tails[s][2 if s == t else 3],
                outputs[s, t],
            )

    token_grads, parts_qkv = [], []
    for s in range(2):
        normed, inverse, lowered = fronts[s][:3]
        rows = lowered.shape[0]
        grad_q = backs[s, s][0] + backs[s, 1 - s][0]
        grad_k = backs[s, s][1] + backs[1 - s, s][1]
        grad_v = backs[s, s][2] + backs[1 - s, s][2]
        grad_wide = jnp.concatenate(
            [grad.reshape(rows, -1).astype(low) for grad in (grad_q, grad_k, grad_v)]
            + [tails[s][1], jnp.zeros((rows, lane - heads), low)],
            1,
        )
        part = dot_rows(lowered, grad_wide)
        own_rows = rows // 2
        grad_in, part_gain = normalize_back(
            own_sum(dot_back(grad_wide, full_qkv[s])),
            normed[:own_rows],
            inverse[:own_rows],
            gains_attn[s],
        )
        token_grads.append((tails[s][0] + grad_in)[None])
        parts_qkv.append(
            jnp.concatenate(
                [
                    part[:, : 3 * half + heads],
                    part_gain[:, None],
                    tails[s][7][:, None],
                    part[:, 3 * half + heads + 2 :],
                ],
                1,
            ).astype(low)
        )
    part_qkv = jnp.stack(parts_qkv)
    part_out, part_up, part_down = (
        jnp.stack([tails[0][at], tails[1][at]]) for at in (4, 5, 6)
    )
    scatter = lambda array: lax.psum_scatter(
        array.astype(full), docs_axis, scatter_dimension=1, tiled=True
    )

    def columns(own):
        other = swap(own)
        first = jnp.where(core == 0, own, other)
        second = jnp.where(core == 0, other, own)
        return first, second

    def rows_both(part):
        empty = jnp.zeros_like(part)
        first = jnp.where(core == 0, part, empty)
        second = jnp.where(core == 0, empty, part)
        return lax.psum(scatter(jnp.concatenate([first, second], 1)), core_axis)

    qkv_first, qkv_second = columns(scatter(part_qkv))
    grad_qkv = jnp.concatenate(
        [
            piece[:, :, column * half : (column + 1) * half]
            for column in range(3)
            for piece in (qkv_first, qkv_second)
        ],
        2,
    )
    small = jnp.stack([qkv_first[:, :, 3 * half :], qkv_second[:, :, 3 * half :]])
    grad_up = jnp.concatenate(columns(scatter(part_up)), 2)
    grad_out, grad_down = rows_both(part_out), rows_both(part_down)
    grad_gate = jnp.concatenate([small[0, :, :, :heads], small[1, :, :, :heads]], 2)
    gains = small[0] + small[1]
    return (
        results[0][None],
        results[1][None],
        token_grads[0],
        token_grads[1],
        grad_qkv,
        grad_out,
        grad_gate,
        grad_up,
        grad_down,
        gains[:, :, heads],
        gains[:, :, heads + 1],
    )


def solution(mesh):
    rows = P(docs_axis, core_axis, None)
    weights = P(None, docs_axis, None)
    gains = P(None, docs_axis)
    in_specs = (
        (rows, rows, P(docs_axis, None), P(docs_axis, None)) + (weights,) * 5 + (gains,) * 2 + (rows,) * 2
    )
    out_specs = (rows,) * 4 + (weights,) * 5 + (gains,) * 2
    return jax.shard_map(
        functools.partial(on_device, mesh.shape[docs_axis]),
        mesh=mesh,
        in_specs=in_specs,
        out_specs=out_specs,
        check_vma=False,
    )
```

```python
import functools
import types
from typing import NamedTuple

import jax
import jax.numpy as jnp
from jax import lax
from jax.experimental import pallas as pl
from jax.experimental.pallas import tpu as pltpu
from jax.sharding import PartitionSpec as P

epsilon = 1e-05
big_negative = -1e30
MESH = pl.DeviceIdType.MESH
docs_axis, core_axis = "docs", "blk"
lane = 128
row_tile = 16
vmem_limit = 61 * 1024 * 1024
low, full = jnp.bfloat16, jnp.float32
by_x, by_y, upward, downward, crosswise = range(5)
lines_first, planes_first, line_only, plane_shared = range(4)
quads = ((False, False), (False, True), (True, False), (True, True))


def dot(left, right):
    return jnp.dot(left, right, preferred_element_type=full)


def dot_back(left, right):
    return lax.dot_general(left, right, (((1,), (1,)), ((), ())), preferred_element_type=full)


def dot_rows(left, right):
    return lax.dot_general(left, right, (((0,), (0,)), ((), ())), preferred_element_type=full)


def normalize(values):
    centred = values - jnp.mean(values, -1, keepdims=True)
    inverse = lax.rsqrt(jnp.mean(centred * centred, -1, keepdims=True) + epsilon)
    return centred * inverse, inverse


def over_rows(first, last, size, body):
    def step(at, carry):
        body(pl.ds(pl.multiple_of(first + at * size, row_tile), size))
        return carry

    lax.fori_loop(0, (last - first) // size, step, 0)


def over_columns(first, last, size, body):
    def step(at, carry):
        body(pl.ds(pl.multiple_of(first + at * size, lane), size))
        return carry

    lax.fori_loop(0, (last - first) // size, step, 0)


def gelu_both(value):
    root = 0.7978845608028654
    square = value * value
    bent = jnp.tanh(root * (value + 0.044715 * value * square))
    cdf = 0.5 * (1.0 + bent)
    slope = cdf + 0.5 * value * (1.0 - bent * bent) * (root * (1.0 + 0.134145 * square))
    return value * cdf, slope


def add_rows(target, others, first=0):
    size = max(size for size in (16, 32, 48) if others[0].shape[0] % size == 0)

    def body(step, carry):
        at = pl.multiple_of(step * size, row_tile)
        total = others[0][pl.ds(at, size), :].astype(full)
        for other in others[1:]:
            total = total + other[pl.ds(at, size), :].astype(full)
        target[pl.ds(first + at, size), :] = total.astype(target.dtype)
        return carry

    lax.fori_loop(0, others[0].shape[0] // size, body, 0)


def when(conditions, body):
    conditions = [condition for condition in conditions if condition is not None]
    if not conditions:
        body()
        return
    pl.when(functools.reduce(jnp.logical_and, conditions))(body)


def merged(*groups):
    space = types.SimpleNamespace()
    for group in groups:
        vars(space).update(group._asdict())
    return space


class Place:
    def __init__(self, line_size):
        docs = lax.axis_index(docs_axis)
        self.core = lax.axis_index(core_axis)
        self.line_size = line_size
        self.z, self.y, self.x = docs // 4, (docs // 2) % 2, docs % 2
        self.up_valid = self.z < line_size - 1
        self.down_valid = self.z > 0

    def index(self, z, flip_y=False, flip_x=False):
        y = 1 - self.y if flip_y else self.y
        x = 1 - self.x if flip_x else self.x
        return z * 4 + y * 2 + x

    def device(self, step):
        z, y, x = self.z, self.y, self.x
        docs = (
            z * 4 + y * 2 + 1 - x,
            z * 4 + (1 - y) * 2 + x,
            (z + 1) * 4 + y * 2 + x,
            (z - 1) * 4 + y * 2 + x,
            z * 4 + (1 - y) * 2 + 1 - x,
        )[step]
        return (docs, self.core)

    def greet(self):
        barrier = pltpu.get_barrier_semaphore()

        def signal(device):
            pl.semaphore_signal(barrier, inc=1, device_id=device, device_id_type=MESH)

        for step in (by_x, by_y, crosswise):
            signal(self.device(step))
        pl.when(self.up_valid)(lambda: signal(self.device(upward)))
        pl.when(self.down_valid)(lambda: signal(self.device(downward)))
        signal((self.index(self.z), 1 - self.core))

    def meet(self):
        peers = 4
        for valid in (self.up_valid, self.down_valid):
            peers = peers + jnp.where(valid, 1, 0)
        pl.semaphore_wait(pltpu.get_barrier_semaphore(), peers)


class Piece(NamedTuple):
    array: int
    part: int
    first: int
    rows: int
    flip: int
    route: int


class Gather:
    def __init__(self, place, pieces, sizes, splits, owns, outs, send_sems, recv_sems, local_sems):
        self.place, self.pieces, self.sizes, self.splits = place, pieces, sizes, splits
        self.owns, self.outs = owns, outs
        self.send_sems, self.recv_sems, self.local_sems = send_sems, recv_sems, local_sems
        self.sends = []

    def has(self, at, source_z):
        half = self.place.line_size // 2
        return source_z // half == self.place.core if self.splits[self.pieces[at].array] else None

    def block(self, at, source):
        piece = self.pieces[at]
        if self.splits[piece.array]:
            source = source - self.place.core * (self.place.line_size // 2) * 4
        if piece.route == line_only:
            source = source // 4
        first = source * self.sizes[piece.array] + piece.first
        rows = pl.ds(pl.multiple_of(first, row_tile), piece.rows)
        return self.outs[piece.array].at[piece.part, rows, :]

    def mine(self, at, step=None):
        piece = self.pieces[at]
        ref, offset = self.owns[piece.array]
        if piece.route == plane_shared:
            to = self.place.index(0, step in (by_y, crosswise), step in (by_x, crosswise))
            return ref.at[to, pl.ds(piece.first, piece.rows), :]
        first = pl.multiple_of(offset + piece.first, row_tile)
        return ref.at[piece.part, pl.ds(first, piece.rows), :]

    def copy(self, at, source, step, own=False):
        return pltpu.make_async_remote_copy(
            src_ref=self.mine(at, step) if own else self.block(at, source),
            dst_ref=self.block(at, source),
            send_sem=self.send_sems.at[at, source, step],
            recv_sem=self.recv_sems.at[at, source],
            device_id=self.place.device(step),
            device_id_type=MESH,
        )

    def local(self, at):
        here = self.place.index(self.place.z)
        return pltpu.make_async_copy(self.mine(at), self.block(at, here), self.local_sems.at[at])

    def send(self, conditions, *which):
        when(conditions, lambda: self.copy(*which).start())
        self.sends.append((conditions, which))

    def wait(self, conditions, at, source):
        when(conditions, lambda: self.copy(at, source, by_x).wait_recv())

    def units(self, distance):
        place = self.place
        if distance == 0:
            return [(place.z, None, None)]
        return [
            (place.z - distance, place.z >= distance, (upward, place.up_valid)),
            (place.z + distance, place.z < place.line_size - distance, (downward, place.down_valid)),
        ]

    def both_ways(self, conditions, at, source, own=False):
        self.send(conditions + [self.place.up_valid], at, source, upward, own)
        self.send(conditions + [self.place.down_valid], at, source, downward, own)

    def own(self, at):
        place = self.place
        here = place.index(place.z)
        held = [self.has(at, place.z)]
        when(held, lambda: self.local(at).start())
        self.both_ways(held, at, here, True)
        route = self.pieces[at].route
        if route != line_only:
            self.send(held, at, here, by_x, True)
            self.send(held, at, here, by_y, True)
        if route == plane_shared:
            self.send(held, at, here, crosswise, True)

    def beside(self, at, distance):
        piece = self.pieces[at]
        for source_z, valid, _ in self.units(distance):
            conditions = [valid, self.has(at, source_z)]
            for other in (0, 1):
                source = self.place.index(source_z, other == 1, other == 0)
                if other == piece.flip or piece.route != lines_first:
                    self.wait(conditions, at, source)
                if other == piece.flip and piece.route != plane_shared:
                    self.send(conditions, at, source, by_x if other else by_y)
                if piece.route != lines_first:
                    self.both_ways(conditions, at, source)

    def along(self, at, distance, quad=quads[0]):
        for source_z, valid, (step, onward) in self.units(distance):
            source = self.place.index(source_z, *quad)
            conditions = [valid, self.has(at, source_z)]
            self.wait(conditions, at, source)
            self.send(conditions + [onward], at, source, step)
            if self.pieces[at].route == lines_first:
                self.send(conditions, at, source, by_x)
                self.send(conditions, at, source, by_y)

    def late_round(self, at, number):
        place = self.place
        last = place.line_size - 1
        if number == 1:
            self.beside(at, 0)
        if number == 2:
            held = [self.has(at, place.z)]
            fourth = place.index(place.z, *quads[3])
            self.wait(held, at, fourth)
            self.both_ways(held, at, fourth)
        for quad, behind in zip(quads, (0, 1, 1, 2)):
            if 1 <= number - behind <= last:
                self.along(at, number - behind, quad)

    def rest(self, array):
        for at, piece in enumerate(self.pieces):
            if piece.array != array:
                continue
            if piece.route in (planes_first, plane_shared):
                self.along(at, self.place.line_size - 1, quads[3])
            elif piece.route == lines_first:
                for distance in range(self.place.line_size):
                    for source_z, valid, _ in self.units(distance):
                        conditions = [valid, self.has(at, source_z)]
                        beside = (piece.flip == 0, piece.flip == 1)
                        self.wait(conditions, at, self.place.index(source_z, *beside))
                        self.wait(conditions, at, self.place.index(source_z, *quads[3]))
            when([self.has(at, self.place.z)], lambda: self.local(at).wait())

    def run(self, plan, stages):
        for kind, at, number in plan:
            if kind == 0:
                self.own(at)
            elif kind == 1:
                self.beside(at, number)
            elif kind == 2:
                self.along(at, number)
            elif kind == 3:
                self.late_round(at, number)
            elif kind == 4:
                self.rest(at)
            else:
                stages[at]()

    def finish(self):
        for conditions, which in self.sends:
            when(conditions, lambda: self.copy(*which).wait_send())


class Scatter:
    def __init__(self, place, pieces, splits, raws, parts, buffers, send_sems, recv_sems, finish):
        self.place, self.pieces, self.splits = place, pieces, splits
        self.raws, self.parts, self.buffers = raws, parts, buffers
        self.send_sems, self.recv_sems, self.finish_rows = send_sems, recv_sems, finish
        self.sends = []

    shares = ((quads[1], 1, by_x), (quads[2], 2, by_y), (quads[3], 0, crosswise))

    def has(self, at, z_to):
        half = self.place.line_size // 2
        return z_to // half == self.place.core if self.splits[self.pieces[at].array] else None

    def slot(self, at, z_to):
        half = self.place.line_size // 2
        return z_to - self.place.core * half if self.splits[self.pieces[at].array] else z_to

    def block(self, refs, at, z_to, quad):
        piece = self.pieces[at]
        ref = refs[piece.array]
        if piece.route == line_only:
            first = z_to * (ref.shape[1] // self.place.line_size) + piece.first
        else:
            split = 2 if self.splits[piece.array] else 1
            rows = ref.shape[1] // (4 * self.place.line_size // split)
            first = self.place.index(self.slot(at, z_to), *quad) * rows + piece.first
        return ref.at[piece.part, pl.ds(pl.multiple_of(first, row_tile), piece.rows), :]

    def quads(self, at):
        return quads[:1] if self.pieces[at].route == line_only else quads

    def raw_of(self, at, z_to, quad):
        return self.block(self.raws, at, z_to, quad)

    def part_of(self, at, z_to, quad):
        return self.block(self.parts, at, z_to, quad)

    def landed(self, at, kind, z_to, quad=0):
        ref = self.buffers[at][kind]
        if self.pieces[at].route == lines_first:
            return ref.at[self.slot(at, z_to)]
        return ref.at[self.slot(at, z_to), quad] if kind >= 3 else ref.at[0]

    def copy(self, source, at, kind, z_to, step, number, quad=0):
        arrival = kind if kind < 3 else 3 + (kind - 3) * 4 + quad
        return pltpu.make_async_remote_copy(
            src_ref=source,
            dst_ref=self.landed(at, kind, z_to, quad),
            send_sem=self.send_sems.at[at, z_to, number],
            recv_sem=self.recv_sems.at[at, z_to, arrival],
            device_id=self.place.device(step),
            device_id_type=MESH,
        )

    def arrived(self, at, kind, z_to, quad=0):
        held = self.landed(at, kind, z_to, quad)
        self.copy(held, at, kind, z_to, by_x, 0, quad).wait_recv()

    def send(self, conditions, *which):
        when(conditions, lambda: self.copy(*which).start())
        self.sends.append((conditions, which))

    def destination(self, step):
        size = self.place.line_size
        chosen = 0
        for at in range(size):
            order = sorted(range(size), key=lambda other: (-abs(other - at), other))
            chosen = chosen + jnp.where(self.place.z == at, order[step], 0)
        return chosen

    def raw(self, at, step):
        place = self.place
        z_to = self.destination(step)
        conditions = [self.has(at, z_to)]
        if self.pieces[at].route == lines_first:
            self.plane_raw(conditions, self.raw_of, at, z_to)
            return
        first, last = place.z == 0, place.z == place.line_size - 1
        for number, quad in enumerate(self.quads(at)):
            source = self.raw_of(at, z_to, quad)
            up = conditions + [first, z_to > place.z]
            self.send(up, source, at, 3, z_to, upward, number, number)
            down = conditions + [last, z_to < place.z]
            self.send(down, source, at, 4, z_to, downward, 4 + number, number)

    def plane_raw(self, conditions, source, at, z_to):
        if self.pieces[at].flip == 0:
            self.send(conditions, source(at, z_to, (True, True)), at, 0, z_to, by_y, 8)
            self.send(conditions, source(at, z_to, (True, False)), at, 2, z_to, by_y, 9)
        else:
            self.send(conditions, source(at, z_to, (True, True)), at, 0, z_to, by_x, 8)
            self.send(conditions, source(at, z_to, (False, True)), at, 1, z_to, by_x, 9)

    def plane_pair(self, conditions, at, z_to):
        flip = self.pieces[at].flip
        held = self.landed(at, 0, z_to)

        def body():
            self.arrived(at, 0, z_to)
            add_rows(held, [held, self.part_of(at, z_to, (flip == 1, flip == 0))])

        when(conditions, body)
        if flip == 0:
            self.send(conditions, held, at, 1, z_to, by_x, 10)
        else:
            self.send(conditions, held, at, 2, z_to, by_y, 10)

    def pair(self, at, step):
        z_to = self.destination(step)
        self.plane_pair([self.has(at, z_to)], at, z_to)

    def line(self, at, step):
        place, piece = self.place, self.pieces[at]
        z = place.z
        z_to = self.destination(step)
        conditions = [self.has(at, z_to)]
        first, last = z == 0, z == place.line_size - 1
        inner = jnp.logical_and(z > 0, z < place.line_size - 1)
        ways = (
            (3, [z_to > z], [first], [z > 0], upward, 0),
            (4, [z_to < z], [last], [z < place.line_size - 1], downward, 4),
        )
        ends = (([first], (4,)), ([last], (3,)), ([inner], (3, 4)))
        if piece.route == lines_first:
            held = self.landed(at, 1, z_to)
            base = [held, self.landed(at, 2, z_to), self.part_of(at, z_to, quads[0])]

            def wait():
                self.arrived(at, 1, z_to)
                self.arrived(at, 2, z_to)

            when(conditions, wait)
            for kind, onward, starts, passes, step_to, number in ways:
                when(conditions + onward + starts, lambda: add_rows(held, base))

                def passing():
                    self.arrived(at, kind, z_to)
                    add_rows(held, base + [self.landed(at, kind, z_to)])

                when(conditions + onward + passes, passing)
                self.send(conditions + onward, held, at, kind, z_to, step_to, number)
            for which, kinds in ends:

                def end():
                    for kind in kinds:
                        self.arrived(at, kind, z_to)
                    self.finish_rows(piece, base + [self.landed(at, kind, z_to) for kind in kinds])

                when(conditions + [z_to == z] + which, end)
            return
        for kind, onward, _, passes, step_to, number in ways:
            for at_quad, quad in enumerate(self.quads(at)):
                held = self.landed(at, kind, z_to, at_quad)

                def passing():
                    self.arrived(at, kind, z_to, at_quad)
                    add_rows(held, [held, self.part_of(at, z_to, quad)])

                which = conditions + onward + passes
                when(which, passing)
                self.send(which, held, at, kind, z_to, step_to, number + at_quad, at_quad)
        here = conditions + [z_to == z]
        for which, kinds in ends:

            def end():
                for at_quad, quad in reversed(list(enumerate(self.quads(at)))):
                    own = self.part_of(at, z_to, quad)
                    for kind in kinds:
                        self.arrived(at, kind, z_to, at_quad)
                    total = [own] + [self.landed(at, kind, z_to, at_quad) for kind in kinds]
                    if piece.route == planes_first or at_quad:
                        add_rows(own, total)
                    else:
                        self.finish_rows(piece, total)

            when(here + which, end)
        if step == place.line_size - 1 and piece.route == planes_first:
            self.plane_raw(here, self.part_of, at, z_to)
        if step == place.line_size - 1 and piece.route == plane_shared:
            for number, (quad, kind, step_to) in enumerate(self.shares):
                self.send(here, self.part_of(at, z_to, quad), at, kind, z_to, step_to, 8 + number)

    def tail(self, at):
        z, piece = self.place.z, self.pieces[at]
        if piece.route == plane_shared:
            for quad, kind, _ in self.shares:
                self.arrived(at, kind, z)
                self.finish_rows(piece, [self.landed(at, kind, z)], quad)
            return
        conditions = [self.has(at, z)]
        self.plane_pair(conditions, at, z)

        def end():
            self.arrived(at, 1, z)
            self.arrived(at, 2, z)
            total = [self.landed(at, kind, z) for kind in (1, 2)] + [self.part_of(at, z, quads[0])]
            self.finish_rows(piece, total)

        when(conditions, end)

    def run(self, plan, stages):
        for kind, at, number in plan:
            if kind == 0:
                self.raw(at, number)
            elif kind == 1:
                self.pair(at, number)
            elif kind == 2:
                self.line(at, number)
            elif kind == 3:
                self.tail(at)
            else:
                stages[at]()

    def finish(self):
        for conditions, which in self.sends:
            when(conditions, lambda: self.copy(*which).wait_send())


class Moves:
    def __init__(self, place, local_sems, send_sems, recv_sems):
        self.place = place
        self.other = (place.index(place.z), 1 - place.core)
        self.local_sems, self.send_sems, self.recv_sems = local_sems, send_sems, recv_sems
        self.locals, self.remotes = 0, 0
        self.to_end = []

    def local(self, source, target):
        made = pltpu.make_async_copy(source, target, self.local_sems.at[self.locals])
        self.locals += 1
        made.start()
        return made

    def save(self, source, target):
        self.to_end.append(self.local(source, target).wait)

    def across(self, source, target, arrives=None):
        sems = dict(
            send_sem=self.send_sems.at[self.remotes],
            recv_sem=self.recv_sems.at[self.remotes],
            device_id=self.other,
            device_id_type=MESH,
        )
        self.remotes += 1
        made = pltpu.make_async_remote_copy(src_ref=source, dst_ref=target, **sems)
        made.start()
        self.to_end.append(made.wait_send)
        arrives = target if arrives is None else arrives
        return pltpu.make_async_remote_copy(src_ref=arrives, dst_ref=arrives, **sems)

    def peer(self, source, target, step):
        made = pltpu.make_async_remote_copy(
            src_ref=source,
            dst_ref=target,
            send_sem=self.send_sems.at[self.remotes],
            recv_sem=self.recv_sems.at[self.remotes],
            device_id=self.place.device(step),
            device_id_type=MESH,
        )
        self.remotes += 1
        made.start()
        self.to_end.append(made.wait_send)
        return made

    def finish(self):
        for wait in self.to_end:
            wait()


class Rows:
    def __init__(self, text, visual):
        self.text, self.visual = text, visual
        self.split = 2 * text
        self.count = 2 * (text + visual)
        self.spans = ((0, self.split), (self.split, self.count))
        self.own = ((0, text), (self.split, self.split + visual))
        self.other = ((text, self.split), (self.split + visual, self.count))
        self.packed = ((0, text), (text, text + visual))
        self.sizes = (chunk_of(text), chunk_of(visual))

    def over(self, body):
        for s, (first, last) in enumerate(self.spans):
            over_rows(first, last, self.sizes[s], functools.partial(body, s))

    def over_own(self, s, body):
        shift = self.own[s][0] - self.packed[s][0]

        def shifted(piece):
            body(pl.ds(pl.multiple_of(piece.start + shift, row_tile), piece.size), piece)

        over_rows(*self.packed[s], self.sizes[s], shifted)

    def swap_parts(self, moves, wide, received, which=(0, 1)):
        return [
            moves.across(wide.at[slice(*self.other[s])], received.at[slice(*self.packed[s])])
            for s in which
        ]

    def swap_own(self, moves, ref, s):
        return moves.across(ref.at[slice(*self.own[s])], ref.at[slice(*self.other[s])])


class Plane:
    steps = (by_x, by_y, crosswise)

    def __init__(self, place, moves, size):
        self.place, self.moves, self.size = place, moves, size
        self.half = 4 * size

    def part(self, ref, at, count=1):
        return ref.at[at * self.size : (at + count) * self.size]

    def spread(self, own, target):
        other = self.moves.across(own, self.part(target, 4))
        return other, [
            self.moves.peer(own, self.part(target, 1 + at), step) for at, step in enumerate(self.steps)
        ]

    def pass_on(self, target, arrivals):
        for arrival in arrivals:
            arrival.wait_recv()
        return self.moves.across(self.part(target, 1, 3), self.part(target, 5, 3))

    def halve(self, wide, received):
        return self.moves.across(self.part(wide, 4, 4), received)

    def share(self, wide, received, outgoing, landing):
        outgoing[...] = (
            wide[self.size : self.half, :] + received[self.size : self.half, :]
        ).astype(outgoing.dtype)
        return [
            self.moves.peer(self.part(outgoing, at), self.part(landing, at), step)
            for at, step in enumerate(self.steps)
        ]

    def total(self, wide, received, landing):
        value = wide[: self.size, :] + received[: self.size, :]
        for at in range(3):
            value = value + landing[at * self.size : (at + 1) * self.size, :].astype(full)
        return value


def chunk_of(count):
    return max(size for size in range(row_tile, 385, row_tile) if count % size == 0)


def query_spans(count):
    edges = list(range(0, count - 256, 512)) + [count]
    return list(zip(edges[:-1], edges[1:]))


def head_wide(values, odd):
    empty = jnp.zeros_like(values)
    return jnp.concatenate([empty, values] if odd else [values, empty], 0)


def column_of(row, count):
    return jnp.broadcast_to(row, (lane, count)).T


def scratch_of(group):
    return [pltpu.VMEM(shape, dtype) for shape, dtype in group]


def shapes_of(group):
    return [jax.ShapeDtypeStruct(shape, dtype) for shape, dtype in group]


def same_as(arrays):
    return [(array.shape, array.dtype) for array in arrays]


def sems(*counts):
    return [pltpu.SemaphoreType.DMA(count if isinstance(count, tuple) else (count,)) for count in counts]


def specs_of(count, in_vmem):
    spaces = [pltpu.VMEM] * in_vmem + [pl.ANY] * (count - in_vmem)
    return [pl.BlockSpec(memory_space=space) for space in spaces]


front_pieces = (
    (0, 0, 0, 48, 0, 0), (0, 1, 0, 48, 1, 0), (1, 0, 0, 16, 0, 0), (1, 0, 16, 32, 1, 0),
    (2, 0, 0, 48, 0, 0), (2, 1, 0, 48, 1, 0), (3, 0, 0, 16, 0, 0), (3, 0, 16, 16, 1, 0),
    (3, 0, 32, 64, 0, 1), (4, 0, 0, 48, 0, 3), (5, 0, 0, 96, 0, 2),
)
front_plan = (
    (0, 1, 0), (5, 0, 0), (0, 9, 0), (0, 5, 0), (0, 0, 0), (2, 1, 1), (2, 0, 1), (2, 1, 2), (1, 1, 0),
    (2, 5, 1), (3, 9, 1), (0, 2, 0), (1, 0, 1), (2, 0, 2), (1, 1, 1), (0, 10, 0), (2, 1, 3), (0, 7, 0),
    (1, 5, 1), (3, 9, 2), (1, 1, 3), (2, 2, 1), (0, 6, 0), (2, 7, 1), (1, 0, 2), (5, 1, 0), (1, 0, 0),
    (2, 0, 3), (1, 1, 2), (2, 7, 2), (2, 5, 2), (2, 5, 3), (0, 4, 0), (1, 0, 3), (0, 3, 0), (2, 4, 1),
    (1, 5, 3), (2, 2, 2), (2, 6, 1), (2, 4, 2), (1, 7, 1), (0, 8, 0), (4, 0, 0), (1, 2, 0), (2, 7, 3),
    (2, 10, 1), (5, 2, 0), (5, 3, 0), (1, 5, 0), (3, 9, 3), (2, 2, 3), (2, 3, 1), (2, 10, 2), (2, 4, 3),
    (5, 4, 0), (5, 5, 0), (5, 6, 0), (3, 9, 4), (2, 3, 2), (1, 2, 3), (1, 4, 2), (5, 7, 0), (3, 8, 1),
    (2, 6, 2), (5, 8, 0), (1, 4, 3), (1, 5, 2), (1, 4, 1), (1, 3, 1), (1, 4, 0), (1, 3, 0), (2, 10, 3),
    (1, 7, 0), (4, 4, 0), (1, 2, 1), (1, 2, 2), (5, 9, 0), (5, 10, 0), (1, 3, 2), (1, 6, 0), (1, 6, 1),
    (5, 11, 0), (3, 8, 2), (1, 7, 2), (1, 7, 3), (4, 2, 0), (5, 12, 0), (2, 3, 3), (1, 3, 3), (5, 13, 0),
    (2, 6, 3), (5, 14, 0), (4, 5, 0), (5, 21, 0), (3, 8, 3), (4, 1, 0), (5, 16, 0), (1, 6, 3), (1, 6, 2),
    (5, 17, 0), (5, 22, 0), (5, 15, 0), (3, 8, 4), (5, 19, 0), (4, 3, 0), (5, 18, 0), (5, 20, 0),
)
ffn_pieces = (
    (0, 0, 0, 48, 0, 0), (0, 0, 48, 48, 1, 0), (1, 0, 0, 96, 0, 2),
)
ffn_plan = (
    (0, 1, 0), (0, 0, 0), (0, 2, 0), (0, 1, 1), (4, 2, 0), (0, 2, 1), (0, 0, 1), (0, 2, 2), (1, 0, 0),
    (0, 0, 2), (2, 2, 0), (1, 1, 0), (4, 0, 0), (4, 1, 0), (1, 0, 1), (0, 1, 2), (2, 2, 1), (4, 10, 0),
    (1, 1, 1), (2, 2, 2), (4, 4, 0), (4, 3, 0), (2, 0, 0), (0, 1, 3), (4, 9, 0), (2, 1, 0), (1, 0, 2),
    (1, 1, 2), (0, 2, 3), (0, 0, 3), (4, 5, 0), (4, 13, 0), (4, 7, 0), (2, 1, 1), (4, 8, 0), (1, 1, 3),
    (2, 0, 1), (2, 1, 2), (2, 0, 2), (4, 14, 0), (4, 6, 0), (1, 0, 3), (2, 2, 3), (4, 11, 0), (4, 12, 0),
    (2, 1, 3), (2, 0, 3), (4, 15, 0),
)
attention_pieces = (
    (0, 0, 0, 16, 0, 0), (0, 0, 16, 16, 1, 0), (0, 0, 32, 16, 1, 1), (1, 0, 0, 48, 0, 0),
    (1, 1, 0, 48, 1, 0), (2, 0, 0, 48, 0, 0), (2, 1, 0, 48, 1, 0), (3, 0, 0, 48, 0, 3),
)
attention_plan = (
    (0, 1, 0), (0, 7, 0), (0, 4, 0), (0, 3, 0), (0, 0, 0), (0, 1, 1), (0, 7, 1), (0, 2, 0), (4, 0, 0),
    (0, 0, 1), (0, 1, 2), (0, 0, 2), (4, 1, 0), (2, 7, 0), (1, 1, 0), (0, 2, 1), (1, 4, 0), (0, 3, 1),
    (0, 4, 1), (1, 0, 0), (1, 0, 1), (4, 2, 0), (4, 3, 0), (1, 4, 1), (0, 3, 2), (0, 3, 3), (2, 2, 0),
    (0, 2, 2), (0, 4, 2), (4, 4, 0), (0, 0, 3), (1, 1, 1), (1, 1, 2), (4, 5, 0), (1, 3, 0), (1, 4, 2),
    (1, 3, 1), (0, 7, 2), (2, 7, 1), (1, 3, 2), (0, 1, 3), (2, 7, 2), (0, 7, 3), (4, 6, 0), (4, 7, 0),
    (1, 3, 3), (1, 0, 2), (0, 4, 3), (2, 7, 3), (4, 8, 0), (2, 4, 0), (4, 9, 0), (0, 5, 0), (0, 6, 0),
    (2, 0, 0), (2, 4, 1), (0, 2, 3), (1, 0, 3), (2, 1, 0), (2, 3, 0), (2, 0, 1), (1, 5, 0), (0, 6, 1),
    (1, 6, 0), (2, 1, 1), (0, 5, 1), (2, 2, 1), (2, 3, 1), (1, 4, 3), (2, 0, 2), (2, 2, 2), (3, 7, 0),
    (2, 1, 2), (1, 1, 3), (2, 6, 0), (2, 4, 2), (1, 5, 1), (2, 0, 3), (0, 6, 2), (2, 3, 2), (2, 2, 3),
    (1, 6, 1), (0, 5, 2), (2, 5, 0), (2, 4, 3), (2, 5, 1), (1, 6, 2), (1, 5, 2), (0, 6, 3), (2, 3, 3),
    (2, 6, 1), (3, 2, 0), (0, 5, 3), (4, 13, 0), (2, 1, 3), (4, 10, 0), (2, 5, 2), (2, 6, 2), (1, 5, 3),
    (1, 6, 3), (4, 11, 0), (4, 12, 0), (2, 5, 3), (2, 6, 3),
)


class FrontIn(NamedTuple):
    w_qkv: object
    w_gate: object
    w_up: object
    gain_attn: object
    gain_ffn: object
    text_mask: object
    visual_mask: object
    text: object
    visual: object
    text_dy: object
    visual_dy: object
    w_out: object
    w_down: object


class FrontOut(NamedTuple):
    full_qkv: object
    full_up: object
    full_out: object
    full_down: object
    full_up_v: object
    full_down_v: object
    h: object
    qkv: object
    gates_t: object
    text_t: object
    visual_t: object
    logs: object
    mix_t: object
    middle: object
    hm: object
    hm_v: object
    act: object
    act_v: object
    slope: object
    slope_v: object
    part_down: object
    part_down_v: object
    dy: object
    dy_v: object
    gains: object
    bias: object


class FrontKept(NamedTuple):
    s_h: object
    s_qkv: object
    s_gates_t: object
    s_text_t: object
    s_visual_t: object
    s_logs: object
    s_mix_t: object
    s_middle: object
    s_hm: object
    s_hm_v: object
    s_act: object
    s_act_v: object
    s_slope: object
    s_slope_v: object
    s_part_down: object
    s_part_down_v: object
    s_dy: object
    s_dy_v: object
    s_gains: object
    s_bias: object


class FrontScratch(NamedTuple):
    own_qkv: object
    own_up: object
    own_up_v: object
    s_w_qkv: object
    s_w_up: object
    s_w_up_v: object
    s_w_out: object
    x: object
    wide: object
    received: object
    gate_rows: object
    q_t: object
    v_t: object
    mix: object


def prepare_shards(v, core, heads):
    first = core == 0
    rows = v.w_qkv.shape[1]
    third = v.w_qkv.shape[2] // 3
    half = third // 2
    for s in range(2):
        for at in range(3):
            columns = [v.w_qkv[s, :, at * third + way * half : at * third + (way + 1) * half] for way in (0, 1)]
            v.own_qkv[s, :, at * half : (at + 1) * half] = jnp.where(first, *columns)
        gate = v.w_gate[:, s, :].astype(full)
        gate = jnp.where(first, gate[:heads], gate[heads:])
        gains = [ref[s : s + 1, :].astype(full) for ref in (v.gain_attn, v.gain_ffn)]
        small = jnp.concatenate([gate, *gains, jnp.zeros((lane - heads - 2, rows), full)], 0)
        small = jnp.concatenate([small, jnp.zeros((lane, lane - rows), full)], 1).T[:rows]
        v.own_qkv[s, :, 3 * half :] = small.astype(low)


def prepare_hidden(v, core, block):
    first = core == 0
    pieces = []
    for s in range(2):
        for start in range(0, v.w_up.shape[2], 2 * block):
            ways = [v.w_up[s, :, start + way * block : start + (way + 1) * block].astype(full) for way in (0, 1)]
            pieces.append(jnp.where(first, *ways))
    count = len(pieces) // 2
    v.own_up[0, :, :] = jnp.concatenate(pieces[:count], 1).astype(low)
    for quad in range(4):
        v.own_up_v[quad, :, :] = jnp.concatenate(pieces[count + quad :: 4], 1).astype(low)


def prepare_bias(v, core):
    pieces = []
    for ref in (v.text_mask, v.visual_mask):
        mask = ref[...].astype(full)
        half = mask.shape[1] // 2
        swapped = jnp.concatenate([mask[:, half:], mask[:, :half]], 1)
        pieces.append(jnp.where(core == 0, mask, swapped))
    row = jnp.concatenate(pieces, 1)
    v.s_bias[...] = column_of(jnp.where(row > 0.0, 0.0, big_negative), row.shape[1])


def attend_head(rows, head_width, v, number):
    width = v.s_qkv.shape[1] // 3
    pair = 2 * head_width
    at, odd = number // 2, number % 2
    keys = v.s_qkv[:, width + at * pair : width + (at + 1) * pair]
    bias = v.s_bias[:, 0:1]
    head = slice(number * head_width, (number + 1) * head_width)
    for first, last in query_spans(rows.count):
        scores = dot(keys, head_wide(v.q_t[head, first:last], odd)) + bias
        for t, target in enumerate((v.s_text_t, v.s_visual_t)):
            start, stop = rows.spans[t]
            part = scores[start:stop]
            top = jnp.max(part, 0, keepdims=True)
            raised = jnp.exp(part - top)
            total = jnp.sum(raised, 0, keepdims=True)
            probs = (raised * (1.0 / total)).astype(low)
            target[head, first:last] = dot(v.v_t[head, start:stop], probs)
            row = 8 * t + number
            v.s_logs[row : row + 1, first:last] = top + jnp.log(total)


def front_kernel(line_size, heads, scale, pieces, plan, *refs):
    groups = []
    for group in (FrontIn, FrontOut, FrontKept, FrontScratch):
        count = len(group._fields)
        groups.append(group(*refs[:count]))
        refs = refs[count:]
    v = merged(*groups)
    place = Place(line_size)
    core = place.core
    rows = Rows(v.text.shape[1], v.visual.shape[1])
    shard, block = v.w_qkv.shape[1], v.w_down.shape[1] // 2
    owns = (
        (v.own_qkv, 0),
        (v.own_up, 0),
        (v.w_out, 0),
        (v.w_down, core * block),
        (v.own_up_v, 0),
        (v.w_down.at[pl.ds(1, 1)], core * block),
    )
    gather = Gather(
        place,
        pieces,
        (shard, shard, shard, block, shard, block),
        (False, False, True, False, False, False),
        owns,
        (v.s_w_qkv, v.s_w_up, v.s_w_out, v.full_down, v.s_w_up_v, v.full_down_v),
        *refs[:3],
    )
    moves = Moves(place, *refs[3:])
    width = v.s_qkv.shape[1] // 3
    head_width = width // heads
    hidden = v.s_act.shape[1]
    arrivals = {}

    place.greet()
    prepare_shards(v, core, heads)
    place.meet()
    plane = Plane(place, moves, rows.visual)
    loads, swaps = [], []
    for s, source in enumerate((v.text, v.visual)):
        loads.append(moves.local(source.at[0], v.x.at[slice(*rows.own[s])]))
        swaps.append(moves.across(source.at[0], v.x.at[slice(*rows.other[s])]))
    loads.append(moves.local(v.text_dy.at[0], v.s_dy.at[slice(*rows.own[0])]))
    loads.append(moves.local(v.visual_dy.at[0], plane.part(v.s_dy_v, 0)))
    swaps.append(moves.across(v.text_dy.at[0], v.s_dy.at[slice(*rows.other[0])]))

    def prepare():
        prepare_hidden(v, core, block)

    def norm():
        prepare_bias(v, core)
        moves.save(v.s_bias, v.bias)
        for s in range(2):
            loads[s].wait()
            swaps[s].wait_recv()

        def body(s, piece):
            v.wide[piece, :] = normalize(v.x[piece, :].astype(full))[0]

        rows.over(body)

    def lower():
        moves.save(v.s_w_qkv, v.full_qkv)
        for s in range(2):
            small = v.s_w_qkv[s, :, 3 * width :].astype(full).T
            v.s_gains[s, :, :] = small[heads : heads + 2]

        def body(s, piece):
            v.s_h[piece, :] = (v.wide[piece, :] * v.s_gains[s, 0:1, :]).astype(low)

        rows.over(body)
        moves.save(v.s_gains, v.gains)
        moves.save(v.s_h, v.h)

    def project(s):
        first, last = rows.spans[s]
        even = 3 * width // 256 * 256

        def columns(piece):
            v.s_qkv[first:last, piece] = dot(v.s_h[first:last, :], v.s_w_qkv[s, :, piece]).astype(low)

        over_columns(0, even, 256, columns)
        rest = dot(v.s_h[first:last, :], v.s_w_qkv[s, :, even:])
        v.s_qkv[first:last, even:] = rest[:, : 3 * width - even].astype(low)
        v.gate_rows[first:last, :] = rest[:, 3 * width - even :]

    def project_visual():
        project(1)
        v.s_gates_t[...] = jax.nn.sigmoid(v.gate_rows[...].T[:8, :])
        v.q_t[...] = (v.s_qkv[:, :width] * jnp.asarray(scale, low)).T
        v.v_t[...] = v.s_qkv[:, 2 * width :].T
        moves.save(v.s_qkv, v.qkv)
        moves.save(v.s_gates_t, v.gates_t)

    def mix():
        moves.save(v.s_text_t, v.text_t)
        moves.save(v.s_visual_t, v.visual_t)
        moves.save(v.s_logs, v.logs)
        is_text = lax.broadcasted_iota(jnp.int32, (1, rows.count), 1) < rows.split
        for head in range(heads):
            span = slice(head * head_width, (head + 1) * head_width)
            gate = v.s_gates_t[head : head + 1, :]
            to_text = jnp.where(is_text, gate, 1.0 - gate)
            v.s_mix_t[span, :] = (
                to_text * v.s_text_t[span, :] + (1.0 - to_text) * v.s_visual_t[span, :]
            ).astype(low)
        v.mix[...] = v.s_mix_t[...].T
        moves.save(v.s_mix_t, v.mix_t)

    def branch():
        moves.save(v.s_w_out, v.full_out)
        for s, (first, last) in enumerate(rows.spans):

            def columns(piece):
                v.wide[first:last, piece] = dot(v.mix[first:last, :], v.s_w_out[s, :, piece])

            over_columns(0, v.wide.shape[1], 256, columns)
        arrivals[0] = rows.swap_parts(moves, v.wide, v.received)

    def spread_dy():
        arrivals[2] = plane.spread(v.visual_dy.at[0], v.s_dy_v)

    def pass_dy():
        arrivals[3] = plane.pass_on(v.s_dy_v, arrivals[2][1])

    def middle_rows(s, ref, start):
        arrivals[0][s].wait_recv()

        def body(piece, packed):
            value = v.x[piece, :].astype(full) + v.wide[piece, :] + v.received[packed, :]
            v.s_middle[packed, :] = value
            to = pl.ds(pl.multiple_of(packed.start - start, row_tile), packed.size)
            ref[to, :] = (normalize(value)[0] * v.s_gains[s, 1:2, :]).astype(low)

        rows.over_own(s, body)

    def middle_visual():
        middle_rows(1, v.s_hm_v, rows.packed[1][0])
        arrivals[4] = plane.spread(plane.part(v.s_hm_v, 0), v.s_hm_v)

    def middle_text():
        middle_rows(0, v.s_hm, 0)
        arrivals[1] = rows.swap_own(moves, v.s_hm, 0)
        moves.save(v.s_middle, v.middle)

    def pass_hm():
        arrivals[5] = plane.pass_on(v.s_hm_v, arrivals[4][1])

    def up_part(hm, w_up, act_ref, slope_ref, start, stop):
        size = 256 if (stop - start) % 256 == 0 else lane

        def columns(piece):
            act, slope = gelu_both(dot(hm[...], w_up[0, :, piece]))
            act_ref[:, piece] = act.astype(low)
            slope_ref[:, piece] = slope.astype(low)

        over_columns(start, stop, size, columns)

    def up_first():
        moves.save(v.s_w_up, v.full_up)
        arrivals[1].wait_recv()
        loads[2].wait()
        swaps[2].wait_recv()
        moves.save(v.s_hm, v.hm)
        moves.save(v.s_dy, v.dy)
        up_part(v.s_hm, v.s_w_up, v.s_act, v.s_slope, 0, hidden // 2)

    def up_second():
        up_part(v.s_hm, v.s_w_up, v.s_act, v.s_slope, hidden // 2, hidden)
        moves.save(v.s_act, v.act)
        moves.save(v.s_slope, v.slope)

    def up_visual():
        moves.save(v.s_w_up_v, v.full_up_v)
        arrivals[4][0].wait_recv()
        arrivals[5].wait_recv()
        moves.save(v.s_hm_v, v.hm_v)
        up_part(v.s_hm_v, v.s_w_up_v, v.s_act_v, v.s_slope_v, 0, v.s_act_v.shape[1])
        moves.save(v.s_act_v, v.act_v)
        moves.save(v.s_slope_v, v.slope_v)

    def down_part(act, dy, part):
        count = act.shape[1]

        def columns(piece):
            part[0, piece, :] = dot_rows(act[:, piece], dy[...]).astype(low)

        over_columns(0, count, 256 if count % 256 == 0 else lane, columns)

    def down_text():
        down_part(v.s_act, v.s_dy, v.s_part_down)
        moves.save(v.s_part_down, v.part_down)

    def down_visual():
        loads[3].wait()
        arrivals[2][0].wait_recv()
        arrivals[3].wait_recv()
        moves.save(v.s_dy_v, v.dy_v)
        down_part(v.s_act_v, v.s_dy_v, v.s_part_down_v)
        moves.save(v.s_part_down_v, v.part_down_v)

    stages = [prepare, norm, lower, functools.partial(project, 0), project_visual]
    stages += [functools.partial(attend_head, rows, head_width, v, head) for head in range(heads)]
    stages += [mix, branch, middle_visual, middle_text, pass_hm, up_first, up_second, up_visual]
    stages += [down_text, down_visual, spread_dy, pass_dy]
    gather.run(plan, stages)
    moves.finish()
    gather.finish()


def front(n_docs, heads, scale, pieces, plan, inputs):
    line_size = n_docs // 4
    count = 2 * (inputs.text.shape[1] + inputs.visual.shape[1])
    dim = inputs.w_out.shape[2]
    width, hidden = inputs.w_qkv.shape[2] // 6, inputs.w_up.shape[2] // 2
    text, plane = 2 * inputs.text.shape[1], 8 * inputs.visual.shape[1]
    wide = 3 * width + lane
    shard = inputs.w_qkv.shape[1]
    kept = FrontKept(
        s_h=((count, dim), low),
        s_qkv=((count, 3 * width), low),
        s_gates_t=((8, count), full),
        s_text_t=((width, count), full),
        s_visual_t=((width, count), full),
        s_logs=((16, count), full),
        s_mix_t=((width, count), low),
        s_middle=((count // 2, dim), full),
        s_hm=((text, dim), low),
        s_hm_v=((plane, dim), low),
        s_act=((text, hidden), low),
        s_act_v=((plane, hidden // 4), low),
        s_slope=((text, hidden), low),
        s_slope_v=((plane, hidden // 4), low),
        s_part_down=((1, hidden, dim), low),
        s_part_down_v=((1, hidden // 4, dim), low),
        s_dy=((text, dim), low),
        s_dy_v=((plane, dim), low),
        s_gains=((2, 2, dim), full),
        s_bias=((count, lane), full),
    )
    weights = (
        ((2, dim, wide), low),
        ((1, dim, hidden), low),
        ((2, width, dim), low),
        ((1, hidden, dim), low),
        ((1, dim, hidden // 4), low),
        ((1, hidden // 4, dim), low),
    )
    scratch = FrontScratch(
        own_qkv=((2, shard, wide), low),
        own_up=((1, shard, hidden), low),
        own_up_v=((4, shard, hidden // 4), low),
        s_w_qkv=weights[0],
        s_w_up=weights[1],
        s_w_up_v=weights[4],
        s_w_out=weights[2],
        x=((count, dim), low),
        wide=((count, dim), full),
        received=((count // 2, dim), full),
        gate_rows=((count, lane), full),
        q_t=((width, count), low),
        v_t=((width, count), low),
        mix=((count, width), low),
    )
    results = FrontOut(*weights, *kept)
    values = pl.pallas_call(
        functools.partial(front_kernel, line_size, heads, scale, pieces, plan),
        out_shape=shapes_of(results),
        in_specs=specs_of(len(inputs), 7),
        out_specs=specs_of(len(results), 0),
        scratch_shapes=scratch_of(kept)
        + scratch_of(scratch)
        + sems((len(pieces), n_docs, 5), (len(pieces), n_docs), len(pieces), 40, 24, 24),
        compiler_params=pltpu.CompilerParams(
            collective_id=0, has_side_effects=True, vmem_limit_bytes=vmem_limit
        ),
        name="gather_and_front",
    )(*inputs)
    return FrontOut(*values)


def scatter_buffers(pieces, arrays, splits, n_docs):
    line_size = n_docs // 4
    group = []
    for piece in pieces:
        ends = line_size // 2 if splits[piece.array] else line_size
        block = (piece.rows, arrays[piece.array][0][2])
        if piece.route == lines_first:
            group += [((ends, *block), low)] * 5
        elif piece.route == line_only:
            group += [((1, row_tile, lane), low)] * 3 + [((ends, 1, *block), low)] * 2
        else:
            group += [((1, *block), low)] * 3 + [((ends, 4, *block), low)] * 2
    return scratch_of(group)


def grouped(refs, size):
    return [refs[first : first + size] for first in range(0, len(refs), size)]


def norm_back(grad, normed, inverse, gain):
    scaled = grad * gain
    return inverse * (
        scaled
        - jnp.mean(scaled, -1, keepdims=True)
        - normed * jnp.mean(scaled * normed, -1, keepdims=True)
    )


class FfnIn(NamedTuple):
    full_down: object
    dy: object
    slope: object
    full_up: object
    part_down: object
    hm: object
    middle: object
    gains: object
    act: object
    full_out: object
    mix_t: object
    text_t: object
    visual_t: object
    gates_t: object
    full_down_v: object
    dy_v: object
    slope_v: object
    full_up_v: object
    part_down_v: object
    hm_v: object
    act_v: object


class FfnLoaded(NamedTuple):
    s_full_down: object
    s_dy: object
    s_slope: object
    s_full_up: object
    s_part_down: object
    s_hm: object
    s_middle: object
    s_gains: object
    s_act: object
    s_full_out: object
    s_mix_t: object
    s_text_t: object
    s_visual_t: object
    s_gates_t: object
    s_full_down_v: object
    s_dy_v: object
    s_slope_v: object
    s_full_up_v: object
    s_part_down_v: object
    s_hm_v: object
    s_act_v: object


class FfnOut(NamedTuple):
    text_out: object
    visual_out: object
    stage_down: object
    part_up: object
    part_up_v: object
    part_out: object
    grad_middle: object
    gain_part: object
    gate_grad_t: object
    text_grad_t: object
    visual_grad_t: object


class FfnScratch(NamedTuple):
    s_part_up: object
    s_part_up_v: object
    s_part_out: object
    s_grad_middle: object
    s_gain_part: object
    s_gate_grad_t: object
    s_text_grad_t: object
    s_visual_grad_t: object
    stage: object
    wide: object
    wide_out: object
    received: object
    received_out: object
    branch: object
    result: object
    mix_grad: object
    mix_grad_t: object
    wide_v: object
    received_v: object
    outgoing_v: object
    landing_v: object
    wide_out_v: object
    received_out_v: object
    outgoing_out_v: object
    landing_out_v: object


def ffn_kernel(line_size, heads, pieces, plan, *refs):
    groups = []
    for group in (FfnIn, FfnOut, FfnLoaded, FfnScratch):
        count = len(group._fields)
        groups.append(group(*refs[:count]))
        refs = refs[count:]
    v = merged(*groups)
    buffers = grouped(refs[: 5 * len(pieces)], 5)
    send_sems, recv_sems, *move_sems = refs[5 * len(pieces) :]
    place = Place(line_size)
    moves = Moves(place, *move_sems)
    rows = Rows(v.text_out.shape[1], v.visual_out.shape[1])
    width = v.mix_t.shape[0]
    head_width = width // heads
    dim = v.hm.shape[1]
    arrivals = {}

    plane = Plane(place, moves, rows.visual)

    def finish_rows(piece, total):
        add_rows(v.stage.at[piece.array], total, piece.first)

    scatter = Scatter(
        place,
        pieces,
        (False, False),
        (v.part_down, v.part_down_v),
        (v.s_part_down, v.s_part_down_v),
        buffers,
        send_sems,
        recv_sems,
        finish_rows,
    )
    place.greet()
    loads = FfnIn(*(moves.local(source, target) for source, target in zip(groups[0], groups[2])))
    place.meet()

    def hidden(dy, w_down, slope):
        count = slope.shape[1]

        def columns(piece):
            grad = dot_back(dy[...], w_down[0, piece, :])
            slope[:, piece] = (grad * slope[:, piece].astype(full)).astype(low)

        over_columns(0, count, 256 if count % 256 == 0 else lane, columns)

    def hidden_visual():
        loads.full_down_v.wait()
        loads.dy_v.wait()
        loads.slope_v.wait()
        hidden(v.s_dy_v, v.s_full_down_v, v.s_slope_v)

    def hidden_text():
        loads.full_down.wait()
        loads.dy.wait()
        loads.slope.wait()
        hidden(v.s_dy, v.s_full_down, v.s_slope)
        loads.part_down.wait()
        loads.part_down_v.wait()

    def back_visual():
        loads.full_up_v.wait()
        v.wide_v[...] = dot_back(v.s_slope_v[...], v.s_full_up_v[0, :, :])
        arrivals[0] = plane.halve(v.wide_v, v.received_v)

    def share_visual():
        arrivals[0].wait_recv()
        arrivals[1] = plane.share(v.wide_v, v.received_v, v.outgoing_v, v.landing_v)

    def back_text():
        loads.full_up.wait()

        def columns(piece):
            v.wide[:, piece] = dot_back(v.s_slope[...], v.s_full_up[0, piece, :])

        over_columns(0, dim, 256, columns)
        arrivals[2] = rows.swap_parts(moves, v.wide, v.received, (0,))[0]

    def up_part(hm, slope, part):
        def columns(piece):
            part[0, piece, :] = dot_rows(hm[:, piece], slope[...]).astype(low)

        over_columns(0, dim, 256, columns)

    def up_text():
        loads.hm.wait()
        up_part(v.s_hm, v.s_slope, v.s_part_up)
        moves.save(v.s_part_up, v.part_up)

    def up_visual():
        loads.hm_v.wait()
        up_part(v.s_hm_v, v.s_slope_v, v.s_part_up_v)
        moves.save(v.s_part_up_v, v.part_up_v)

    def middle_rows(s, piece, packed, grad, dy):
        normed, inverse = normalize(v.s_middle[packed, :])
        v.s_gain_part[s, 0:1, :] += jnp.sum(grad * normed, 0, keepdims=True)
        grad = dy.astype(full) + norm_back(grad, normed, inverse, v.s_gains[s, 1:2, :])
        v.s_grad_middle[packed, :] = grad
        v.branch[piece, :] = grad.astype(low)

    def middle_visual():
        loads.middle.wait()
        loads.gains.wait()
        v.s_gain_part[...] = jnp.zeros_like(v.s_gain_part)
        for arrival in arrivals[1]:
            arrival.wait_recv()
        grad = plane.total(v.wide_v, v.received_v, v.landing_v)
        middle_rows(1, slice(*rows.own[1]), slice(*rows.packed[1]), grad, v.s_dy_v[: rows.visual, :])
        arrivals[3] = rows.swap_own(moves, v.branch, 1)

    def middle_text():
        arrivals[2].wait_recv()

        def body(piece, packed):
            grad = v.wide[piece, :] + v.received[packed, :]
            middle_rows(0, piece, packed, grad, v.s_dy[piece, :])

        rows.over_own(0, body)
        arrivals[4] = rows.swap_own(moves, v.branch, 0)
        moves.save(v.s_gain_part, v.gain_part)
        moves.save(v.s_grad_middle, v.grad_middle)

    def result_text():
        loads.act.wait()

        def columns(piece):
            v.wide_out[:, piece] = dot(v.s_act[...], v.s_full_down[0, :, piece])

        over_columns(0, dim, 256, columns)
        arrivals[5] = rows.swap_parts(moves, v.wide_out, v.received_out, (0,))[0]

    def result_visual():
        loads.act_v.wait()
        v.wide_out_v[...] = dot(v.s_act_v[...], v.s_full_down_v[0, :, :])
        arrivals[6] = plane.halve(v.wide_out_v, v.received_out_v)

    def share_result():
        arrivals[6].wait_recv()
        arrivals[7] = plane.share(v.wide_out_v, v.received_out_v, v.outgoing_out_v, v.landing_out_v)

    def out_part():
        loads.full_out.wait()
        loads.mix_t.wait()
        for s, (first, last) in enumerate(rows.spans):
            arrivals[4 - s].wait_recv()
            v.s_part_out[s, :, :] = dot(v.s_mix_t[:, first:last], v.branch[first:last, :]).astype(low)
            v.mix_grad[first:last, :] = dot_back(v.branch[first:last, :], v.s_full_out[s, :, :])
        moves.save(v.s_part_out, v.part_out)

    def gates():
        loads.text_t.wait()
        loads.visual_t.wait()
        loads.gates_t.wait()
        v.mix_grad_t[...] = v.mix_grad[...].T
        is_text = lax.broadcasted_iota(jnp.int32, (1, rows.count), 1) < rows.split
        for head in range(heads):
            span = slice(head * head_width, (head + 1) * head_width)
            gate = v.s_gates_t[head : head + 1, :]
            to_text = jnp.where(is_text, gate, 1.0 - gate)
            grad = v.mix_grad_t[span, :]
            toward = jnp.sum(grad * (v.s_text_t[span, :] - v.s_visual_t[span, :]), 0, keepdims=True)
            v.s_gate_grad_t[head : head + 1, :] = (
                jnp.where(is_text, toward, -toward) * gate * (1.0 - gate)
            )
            v.s_text_grad_t[span, :] = (to_text * grad).astype(low)
            v.s_visual_grad_t[span, :] = ((1.0 - to_text) * grad).astype(low)
        v.s_gate_grad_t[heads:, :] = jnp.zeros((8 - heads, rows.count), full)
        moves.save(v.s_gate_grad_t, v.gate_grad_t)
        moves.save(v.s_text_grad_t, v.text_grad_t)
        moves.save(v.s_visual_grad_t, v.visual_grad_t)

    def finish_text():
        arrivals[5].wait_recv()

        def body(piece, packed):
            v.result[packed, :] = (
                v.s_middle[packed, :] + v.wide_out[piece, :] + v.received_out[packed, :]
            ).astype(low)

        rows.over_own(0, body)
        moves.save(v.result.at[slice(*rows.packed[0])], v.text_out.at[0])

    def finish_visual():
        for arrival in arrivals[7]:
            arrival.wait_recv()
        packed = slice(*rows.packed[1])
        total = plane.total(v.wide_out_v, v.received_out_v, v.landing_out_v)
        v.result[packed, :] = (v.s_middle[packed, :] + total).astype(low)
        moves.save(v.result.at[packed], v.visual_out.at[0])

    stages = [hidden_visual, back_visual, hidden_text, share_visual, back_text, up_text, up_visual]
    stages += [middle_visual, middle_text, result_text, result_visual, out_part, gates, share_result]
    scatter.run(plan, stages + [finish_text, finish_visual])
    moves.save(v.stage, v.stage_down)
    moves.finish()
    scatter.finish()


def ffn_back(n_docs, heads, pieces, plan, text, visual, inputs):
    line_size = n_docs // 4
    hidden = inputs.act.shape[1]
    width, count = inputs.mix_t.shape
    dim = inputs.hm.shape[1]
    rows = inputs.part_down.shape[1] // n_docs
    plane = 8 * visual.shape[1]
    scratch = FfnScratch(
        s_part_up=((1, dim, hidden), low),
        s_part_up_v=((1, dim, hidden // 4), low),
        s_part_out=((2, width, dim), low),
        s_grad_middle=((count // 2, dim), full),
        s_gain_part=((2, 8, dim), full),
        s_gate_grad_t=((8, count), full),
        s_text_grad_t=((width, count), low),
        s_visual_grad_t=((width, count), low),
        stage=((2, rows, dim), full),
        wide=((2 * text.shape[1], dim), full),
        wide_out=((2 * text.shape[1], dim), full),
        received=((text.shape[1], dim), full),
        received_out=((text.shape[1], dim), full),
        branch=((count, dim), low),
        result=((count // 2, dim), low),
        mix_grad=((count, width), full),
        mix_grad_t=((width, count), full),
        wide_v=((plane, dim), full),
        received_v=((plane // 2, dim), full),
        outgoing_v=((3 * plane // 8, dim), low),
        landing_v=((3 * plane // 8, dim), low),
        wide_out_v=((plane, dim), full),
        received_out_v=((plane // 2, dim), full),
        outgoing_out_v=((3 * plane // 8, dim), low),
        landing_out_v=((3 * plane // 8, dim), low),
    )
    results = FfnOut(
        (text.shape, low), (visual.shape, low), scratch.stage, *scratch[:8]
    )
    loaded = same_as(inputs)
    values = pl.pallas_call(
        functools.partial(ffn_kernel, line_size, heads, pieces, plan),
        out_shape=shapes_of(results),
        in_specs=specs_of(len(inputs), 0),
        out_specs=specs_of(len(results), 0),
        scratch_shapes=scratch_of(loaded)
        + scratch_of(scratch)
        + scatter_buffers(pieces, same_as([inputs.part_down, inputs.part_down_v]), (False, False), n_docs)
        + sems((len(pieces), line_size, 11), (len(pieces), line_size, 11), 40, 24, 24),
        compiler_params=pltpu.CompilerParams(
            collective_id=1, has_side_effects=True, vmem_limit_bytes=vmem_limit
        ),
        name="ffn_back_and_scatter",
    )(*inputs)
    return FfnOut(*values)


class AttentionIn(NamedTuple):
    qkv: object
    logs: object
    text_t: object
    visual_t: object
    text_grad_t: object
    visual_grad_t: object
    bias: object
    part_up: object
    part_up_v: object
    part_out: object
    gate_grad_t: object
    full_qkv: object
    h: object
    grad_middle: object
    gains: object
    gain_part: object
    stage_down: object
    text: object
    visual: object


class AttentionLoaded(NamedTuple):
    s_qkv: object
    s_logs: object
    s_text_t: object
    s_visual_t: object
    s_text_grad_t: object
    s_visual_grad_t: object
    s_bias: object
    s_part_up: object
    s_part_up_v: object
    s_part_out: object
    s_gate_grad_t: object
    s_full_qkv: object
    s_h: object
    s_grad_middle: object
    s_gains: object
    s_gain_part: object
    s_stage_down: object


class AttentionOut(NamedTuple):
    text_grad: object
    visual_grad: object
    grad_down: object
    grad_qkv: object
    grad_gate: object
    grad_up: object
    grad_out: object
    grad_gain_attn: object
    grad_gain_ffn: object


class AttentionScratch(NamedTuple):
    part_qkv: object
    x: object
    q_t: object
    k_t: object
    query_grad_t: object
    text_grad_n: object
    visual_grad_n: object
    key_sum: object
    value_sum: object
    grad_wide: object
    wide: object
    received: object
    gain_sum: object
    stage_up: object
    stage_out: object
    stage_qkv: object
    stage_up_v: object
    peer_up: object
    peer_up_v: object
    peer_small: object
    s_grad_up: object
    s_grad_gate: object
    s_grad_gain_attn: object
    s_grad_gain_ffn: object


def attend_head_back(rows, head_width, scale, v, number):
    width = v.s_qkv.shape[1] // 3
    pair = 2 * head_width
    at, odd = number // 2, number % 2
    columns = [slice(third * width + at * pair, third * width + (at + 1) * pair) for third in range(3)]
    keys, values = v.s_qkv[:, columns[1]], v.s_qkv[:, columns[2]]
    if not odd:
        v.key_sum[...] = jnp.zeros_like(v.key_sum)
        v.value_sum[...] = jnp.zeros_like(v.value_sum)
    mine = lax.broadcasted_iota(jnp.int32, (1, pair), 1) // head_width == odd
    bias = v.s_bias[:, 0:1]
    sets = (
        (v.s_text_t, v.s_text_grad_t, v.text_grad_n),
        (v.s_visual_t, v.s_visual_grad_t, v.visual_grad_n),
    )
    head = slice(number * head_width, (number + 1) * head_width)
    for first, last in query_spans(rows.count):
        scores = dot(keys, head_wide(v.q_t[head, first:last], odd)) + bias
        queries = jnp.where(mine, v.s_qkv[first:last, columns[0]] * jnp.asarray(scale, low), 0)
        pieces = []
        for t, (output_t, grad_t, grad) in enumerate(sets):
            start, stop = rows.spans[t]
            out_grad = grad_t[head, first:last]
            delta = jnp.sum(out_grad.astype(full) * output_t[head, first:last], 0, keepdims=True)
            row = 8 * t + number
            probs = jnp.exp(scores[start:stop] - v.s_logs[row : row + 1, first:last])
            grad_probs = dot(values[start:stop], head_wide(out_grad, odd))
            grad_scores = (probs * (grad_probs - delta)).astype(low)
            natural = jnp.where(mine, grad[first:last, columns[0]], 0)
            v.value_sum[start:stop, :] += dot(probs.astype(low), natural)
            v.key_sum[start:stop, :] += dot(grad_scores, queries)
            pieces.append(grad_scores)
        v.query_grad_t[head, first:last] = (
            dot(v.k_t[head, :], jnp.concatenate(pieces, 0)) * scale
        ).astype(low)
    if odd:
        v.grad_wide[:, columns[1]] = v.key_sum[...].astype(low)
        v.grad_wide[:, columns[2]] = v.value_sum[...].astype(low)


def attention_kernel(line_size, heads, scale, block, pieces, plan, *refs):
    groups = []
    for group in (AttentionIn, AttentionOut, AttentionLoaded, AttentionScratch):
        count = len(group._fields)
        groups.append(group(*refs[:count]))
        refs = refs[count:]
    v = merged(*groups)
    buffers = grouped(refs[: 5 * len(pieces)], 5)
    send_sems, recv_sems, *move_sems = refs[5 * len(pieces) :]
    place = Place(line_size)
    core = place.core
    moves = Moves(place, *move_sems)
    rows = Rows(v.text.shape[1], v.visual.shape[1])
    width = v.qkv.shape[1] // 3
    head_width = width // heads
    dim = v.h.shape[1]
    stages_of = (v.stage_up, v.stage_out, v.stage_qkv)
    arrivals = {}

    def finish_rows(piece, total, quad=quads[0]):
        if piece.route == plane_shared:
            add_rows(v.stage_up_v.at[place.index(0, *quad)], total, piece.first)
        else:
            add_rows(stages_of[piece.array].at[piece.part], total, piece.first)

    scatter = Scatter(
        place,
        pieces,
        (False, True, False, False),
        (v.part_up, v.part_out, v.part_qkv, v.part_up_v),
        (v.s_part_up, v.s_part_out, v.part_qkv, v.s_part_up_v),
        buffers,
        send_sems,
        recv_sems,
        finish_rows,
    )
    place.greet()
    loads = AttentionIn(
        *(moves.local(source, target) for source, target in zip(groups[0], groups[2])),
        *(moves.local(ref.at[0], v.x.at[slice(*rows.packed[s])]) for s, ref in enumerate((v.text, v.visual))),
    )
    place.meet()

    def prepare():
        for load in loads[:7]:
            load.wait()
        v.q_t[...] = (v.s_qkv[:, :width] * jnp.asarray(scale, low)).T
        v.k_t[...] = v.s_qkv[:, width : 2 * width].T
        v.text_grad_n[...] = v.s_text_grad_t[...].T
        v.visual_grad_n[...] = v.s_visual_grad_t[...].T
        loads.part_up.wait()
        loads.part_up_v.wait()
        loads.part_out.wait()

    def back_qkv():
        loads.gate_grad_t.wait()
        loads.full_qkv.wait()
        v.grad_wide[:, :width] = v.query_grad_t[...].T
        empty = jnp.zeros((lane - 8, rows.count), full)
        v.grad_wide[:, 3 * width :] = jnp.concatenate([v.s_gate_grad_t[...], empty], 0).T.astype(low)
        for s, (first, last) in enumerate(rows.spans):

            def columns(piece):
                v.wide[first:last, piece] = dot_back(v.grad_wide[first:last, :], v.s_full_qkv[s, piece, :])

            over_columns(0, dim, 256, columns)
        arrivals[0] = rows.swap_parts(moves, v.wide, v.received)

    def qkv_part():
        loads.h.wait()
        for s, (first, last) in enumerate(rows.spans):

            def columns(piece):
                v.part_qkv[s, piece, :] = dot_rows(v.s_h[first:last, piece], v.grad_wide[first:last, :]).astype(low)

            over_columns(0, dim, 256, columns)

    def tokens():
        loads.grad_middle.wait()
        loads.gains.wait()
        loads.gain_part.wait()
        for s in range(2):
            loads[17 + s].wait()
            arrivals[0][s].wait_recv()
            v.gain_sum[s, :, :] = jnp.zeros((lane, dim), full)
            v.gain_sum[s, heads + 1 : heads + 2, :] = v.s_gain_part[s, 0:1, :]

            def body(piece, packed):
                normed, inverse = normalize(v.x[packed, :].astype(full))
                grad = v.wide[piece, :] + v.received[packed, :]
                v.gain_sum[s, heads : heads + 1, :] += jnp.sum(grad * normed, 0, keepdims=True)
                v.s_grad_middle[packed, :] += norm_back(grad, normed, inverse, v.s_gains[s, 0:1, :])

            rows.over_own(s, body)
            small = v.part_qkv[s, :, 3 * width :].astype(full) + v.gain_sum[s, :, :].T
            v.part_qkv[s, :, 3 * width :] = small.astype(low)
            ref = (v.text_grad, v.visual_grad)[s]
            moves.save(v.s_grad_middle.at[slice(*rows.packed[s])], ref.at[0])

    def share_down():
        loads.stage_down.wait()
        block = v.s_stage_down.shape[1]
        mine = lambda of: v.grad_down.at[:, pl.ds(pl.multiple_of(of * block, row_tile), block), :]
        moves.save(v.s_stage_down, mine(core))
        arrivals[3] = moves.across(v.s_stage_down, mine(core), mine(1 - core))

    def share_up():
        arrivals[1] = moves.across(v.stage_up, v.peer_up)
        arrivals[2] = moves.across(v.stage_up_v, v.peer_up_v)

    def share_out():
        owner = place.z // (line_size // 2) == core
        moves_out = (
            pltpu.make_async_copy(v.stage_out, v.grad_out, moves.local_sems.at[moves.locals]),
            pltpu.make_async_remote_copy(
                src_ref=v.stage_out,
                dst_ref=v.grad_out,
                send_sem=moves.send_sems.at[moves.remotes],
                recv_sem=moves.recv_sems.at[moves.remotes],
                device_id=moves.other,
                device_id_type=MESH,
            ),
        )
        moves.locals += 1
        moves.remotes += 1

        def start():
            for move in moves_out:
                move.start()

        def wait():
            moves_out[0].wait()
            moves_out[1].wait_send()

        pl.when(owner)(start)
        moves.to_end.append(lambda: pl.when(owner)(wait))
        moves.to_end.append(lambda: pl.when(jnp.logical_not(owner))(lambda: moves_out[1].wait_recv()))

    def finish_up():
        arrivals[1].wait_recv()
        arrivals[2].wait_recv()
        first = core == 0
        count = v.stage_up.shape[2] // block
        for s in range(2):
            pieces = []
            for at in range(count):
                if s == 0:
                    span = slice(at * block, (at + 1) * block)
                    own, peer = (ref[0, :, span] for ref in (v.stage_up, v.peer_up))
                else:
                    span = slice(at // 4 * block, (at // 4 + 1) * block)
                    own, peer = (ref[at % 4, :, span] for ref in (v.stage_up_v, v.peer_up_v))
                pieces += [jnp.where(first, own, peer), jnp.where(first, peer, own)]
            v.s_grad_up[s, :, :] = jnp.concatenate(pieces, 1)
        moves.save(v.s_grad_up, v.grad_up)

    stages = [prepare]
    stages += [functools.partial(attend_head_back, rows, head_width, scale, v, head) for head in range(heads)]
    stages += [back_qkv, qkv_part, tokens, share_up, share_out, finish_up, share_down]
    scatter.run(plan, stages)

    def mine(third, of):
        first = third * 2 * width + of * width
        return v.grad_qkv.at[:, :, pl.ds(pl.multiple_of(first, lane), width)]

    small = v.stage_qkv.at[:, :, 3 * width :]
    last = [moves.across(small, v.peer_small)]
    for third in range(3):
        source = v.stage_qkv.at[:, :, third * width : (third + 1) * width]
        moves.save(source, mine(third, core))
        last.append(moves.across(source, mine(third, core), mine(third, 1 - core)))
    last[0].wait_recv()
    for s in range(2):
        own, peer = v.stage_qkv[s, :, 3 * width :], v.peer_small[s, :, :]
        columns = own.shape[0]
        empty = jnp.zeros((lane - columns, lane), full)
        own, peer = (jnp.concatenate([value, empty], 0).T[:, :columns] for value in (own, peer))
        v.s_grad_gate[:heads, s, :] = jnp.where(core == 0, own, peer)[:heads]
        v.s_grad_gate[heads:, s, :] = jnp.where(core == 0, peer, own)[:heads]
        both = own + peer
        v.s_grad_gain_attn[s : s + 1, :] = both[heads : heads + 1]
        v.s_grad_gain_ffn[s : s + 1, :] = both[heads + 1 : heads + 2]
    moves.save(v.s_grad_gate, v.grad_gate)
    moves.save(v.s_grad_gain_attn, v.grad_gain_attn)
    moves.save(v.s_grad_gain_ffn, v.grad_gain_ffn)
    for arrival in last[1:] + [arrivals[3]]:
        arrival.wait_recv()
    moves.finish()
    scatter.finish()


def attention_back(n_docs, heads, scale, pieces, plan, inputs):
    line_size = n_docs // 4
    count, dim = inputs.h.shape
    width, wide = inputs.qkv.shape[1] // 3, inputs.full_qkv.shape[2]
    hidden = inputs.part_up.shape[2]
    rows = dim // n_docs
    block = hidden // n_docs
    splits = (False, True, False, False)
    part_qkv = ((2, dim, wide), low)
    arrays = same_as([inputs.part_up, inputs.part_out]) + [part_qkv] + same_as([inputs.part_up_v])
    results = AttentionOut(
        text_grad=(inputs.text.shape, full),
        visual_grad=(inputs.visual.shape, full),
        grad_down=((2, 2 * inputs.stage_down.shape[1], dim), full),
        grad_qkv=((2, rows, 6 * width), full),
        grad_gate=((2 * heads, 2, rows), full),
        grad_up=((2, rows, 2 * hidden), full),
        grad_out=((2, rows, dim), full),
        grad_gain_attn=((2, rows), full),
        grad_gain_ffn=((2, rows), full),
    )
    scratch = AttentionScratch(
        part_qkv=part_qkv,
        x=((count // 2, dim), low),
        q_t=((width, count), low),
        k_t=((width, count), low),
        query_grad_t=((width, count), low),
        text_grad_n=((count, width), low),
        visual_grad_n=((count, width), low),
        key_sum=((count, lane), full),
        value_sum=((count, lane), full),
        grad_wide=((count, wide), low),
        wide=((count, dim), full),
        received=((count // 2, dim), full),
        gain_sum=((2, lane, dim), full),
        stage_up=((1, rows, hidden), full),
        stage_out=((2, rows, dim), full),
        stage_qkv=((2, rows, wide), full),
        stage_up_v=((4, rows, hidden // 4), full),
        peer_up=((1, rows, hidden), full),
        peer_up_v=((4, rows, hidden // 4), full),
        peer_small=((2, rows, lane), full),
        s_grad_up=results.grad_up,
        s_grad_gate=results.grad_gate,
        s_grad_gain_attn=results.grad_gain_attn,
        s_grad_gain_ffn=results.grad_gain_ffn,
    )
    loaded = same_as(inputs[:-2])
    values = pl.pallas_call(
        functools.partial(attention_kernel, line_size, heads, scale, block, pieces, plan),
        out_shape=shapes_of(results),
        in_specs=specs_of(len(inputs), 0),
        out_specs=specs_of(len(results), 0),
        scratch_shapes=scratch_of(loaded)
        + scratch_of(scratch)
        + scatter_buffers(pieces, arrays, splits, n_docs)
        + sems((len(pieces), line_size, 11), (len(pieces), line_size, 11), 40, 16, 16),
        compiler_params=pltpu.CompilerParams(
            collective_id=2, has_side_effects=True, vmem_limit_bytes=vmem_limit
        ),
        name="attention_back_and_scatter",
    )(*inputs)
    return AttentionOut(*values)


def publish_kernel(count, *refs):
    sources, results, held = refs[:count], refs[count : 2 * count], refs[2 * count : 3 * count]
    arriving, leaving = refs[3 * count :]
    copies_in = [pltpu.make_async_copy(sources[at], held[at], arriving.at[at]) for at in range(count)]
    copies_out = [pltpu.make_async_copy(held[at], results[at], leaving.at[at]) for at in range(count)]
    for copy in copies_in:
        copy.start()
    for copy_in, copy_out in zip(copies_in, copies_out):
        copy_in.wait()
        copy_out.start()
    for copy in copies_out:
        copy.wait()


def publish(arrays):
    count = len(arrays)
    return pl.pallas_call(
        functools.partial(publish_kernel, count),
        out_shape=shapes_of(same_as(arrays)),
        in_specs=specs_of(count, 0),
        out_specs=specs_of(count, 0),
        scratch_shapes=scratch_of(same_as(arrays)) + sems(count, count),
        compiler_params=pltpu.CompilerParams(vmem_limit_bytes=vmem_limit),
        name="publish",
    )(*arrays)


def kernel_path(n_docs, heads, scale, inputs):
    made = [tuple(Piece(*each) for each in pieces) for pieces in (front_pieces, ffn_pieces, attention_pieces)]
    first = front(n_docs, heads, scale, made[0], front_plan, inputs)
    ffn_inputs = FfnIn(*(getattr(first, name) for name in FfnIn._fields))
    second = ffn_back(n_docs, heads, made[1], ffn_plan, inputs.text, inputs.visual, ffn_inputs)
    known = merged(inputs, first, second)
    attention_inputs = AttentionIn(*(getattr(known, name) for name in AttentionIn._fields))
    third = attention_back(n_docs, heads, scale, made[2], attention_plan, attention_inputs)
    results = (
        second.text_out,
        second.visual_out,
        third.text_grad,
        third.visual_grad,
        third.grad_qkv,
        third.grad_out,
        third.grad_gate,
        third.grad_up,
        third.grad_down,
        third.grad_gain_attn,
        third.grad_gain_ffn,
    )
    results = publish(results)
    return (*results[:6], jnp.transpose(results[6], (1, 2, 0)), *results[7:])


def swap(value):
    return lax.ppermute(value, core_axis, [(0, 1), (1, 0)])


def both(own):
    return jnp.concatenate([own, swap(own)], 0)


def own_sum(partial):
    rows = partial.shape[0] // 2
    return partial[:rows] + swap(partial[rows:])


def normalize_back(gradient, normed, inverse, gain):
    scaled = gradient * gain
    grad_gain = jnp.sum(gradient * normed, 0)
    grad_input = inverse * (
        scaled
        - jnp.mean(scaled, -1, keepdims=True)
        - normed * jnp.mean(scaled * normed, -1, keepdims=True)
    )
    return grad_input, grad_gain


def heads_of(values, heads):
    return values.reshape(values.shape[0], heads, -1)


def attend(queries, keys, values, valid, scale):
    scores = jnp.einsum("qhe,khe->hqk", queries, keys, preferred_element_type=full) * scale
    scores = jnp.where(valid, scores, big_negative)
    top = jnp.max(scores, -1)
    probs = jnp.where(valid, jnp.exp(scores - top[..., None]), 0.0)
    total = jnp.sum(probs, -1)
    weighted = jnp.einsum(
        "hqk,khe->qhe", probs.astype(low), values, preferred_element_type=full
    )
    return weighted / total.T[..., None], top + jnp.log(total)


def attend_back(queries, keys, values, valid, scale, log_total, grad_output, output):
    delta = jnp.sum(grad_output.astype(full) * output, -1).T
    scores = jnp.einsum("qhe,khe->hqk", queries, keys, preferred_element_type=full) * scale
    probs = jnp.where(valid, jnp.exp(scores - log_total[..., None]), 0.0)
    grad_values = jnp.einsum(
        "hqk,qhe->khe", probs.astype(low), grad_output, preferred_element_type=full
    )
    grad_probs = jnp.einsum("qhe,khe->hqk", grad_output, values, preferred_element_type=full)
    grad_scores = (probs * (grad_probs - delta[..., None])).astype(low)
    grad_queries = (
        jnp.einsum("hqk,khe->qhe", grad_scores, keys, preferred_element_type=full) * scale
    )
    grad_keys = (
        jnp.einsum("hqk,qhe->khe", grad_scores, queries, preferred_element_type=full) * scale
    )
    return grad_queries, grad_keys, grad_values


def on_device(
    n_docs,
    text_tokens,
    visual_tokens,
    text_mask,
    visual_mask,
    w_qkv,
    w_out,
    w_gate,
    w_up,
    w_down,
    gain_attn,
    gain_ffn,
    text_cotangent,
    visual_cotangent,
):
    core = lax.axis_index(core_axis)
    width = w_out.shape[2]
    all_heads = w_gate.shape[2]
    heads = all_heads // 2
    half = width // 2
    scale = (width // all_heads) ** (-0.5)
    if n_docs == 16 and w_qkv.shape[1] % row_tile == 0:
        inputs = FrontIn(
            w_qkv=w_qkv,
            w_gate=jnp.transpose(w_gate, (2, 0, 1)),
            w_up=w_up,
            gain_attn=gain_attn,
            gain_ffn=gain_ffn,
            text_mask=text_mask,
            visual_mask=visual_mask,
            text=text_tokens,
            visual=visual_tokens,
            text_dy=text_cotangent,
            visual_dy=visual_cotangent,
            w_out=w_out,
            w_down=w_down,
        )
        return kernel_path(n_docs, heads, scale, inputs)

    def own_columns(array, size, start=0):
        return lax.dynamic_slice_in_dim(array, start + core * size, size, 2)

    own_tokens = (text_tokens[0], visual_tokens[0])
    own_grads = (text_cotangent[0], visual_cotangent[0])

    def reorder(mask):
        rows = mask.shape[1] // 2
        return (
            jnp.concatenate(
                [
                    lax.dynamic_slice_in_dim(mask[0], core * rows, rows),
                    lax.dynamic_slice_in_dim(mask[0], (1 - core) * rows, rows),
                ]
            )
            > 0
        )

    valids = (reorder(text_mask), reorder(visual_mask))

    pad = lane - heads - 2
    shard = jnp.concatenate(
        [own_columns(w_qkv, half, column * width) for column in range(3)]
        + [
            own_columns(w_gate, heads),
            gain_attn[..., None],
            gain_ffn[..., None],
            jnp.zeros(w_gate.shape[:2] + (pad,), low),
        ],
        2,
    )
    tokens = tuple(both(value) for value in own_tokens)
    grads_out = tuple(both(value) for value in own_grads)
    gather = lambda array: lax.all_gather(array, docs_axis, axis=1, tiled=True)
    rows_half = lambda array: lax.dynamic_slice_in_dim(
        array, core * (array.shape[1] // 2), array.shape[1] // 2, 1
    )
    full_qkv = gather(shard)
    full_up = gather(own_columns(w_up, w_up.shape[2] // 2))
    full_out, full_down = rows_half(gather(w_out)), rows_half(gather(w_down))
    gains_attn = full_qkv[:, :, 3 * half + heads].astype(full)
    gains_ffn = full_qkv[:, :, 3 * half + heads + 1].astype(full)

    fronts = []
    for s in range(2):
        normed, inverse = normalize(tokens[s].astype(full))
        lowered = (normed * gains_attn[s]).astype(low)
        wide = dot(lowered, full_qkv[s])
        narrow = wide[:, : 3 * half].astype(low)
        gates = jax.nn.sigmoid(wide[:, 3 * half : 3 * half + heads])
        queries, keys, values = (
            heads_of(narrow[:, column * half : (column + 1) * half], heads) for column in range(3)
        )
        fronts.append((normed, inverse, lowered, gates, queries, keys, values))

    outputs, totals = {}, {}
    for s in range(2):
        for t in range(2):
            outputs[s, t], totals[s, t] = attend(
                fronts[s][4], fronts[t][5], fronts[t][6], valids[t], scale
            )

    results, tails = [], []
    for s in range(2):
        gates = fronts[s][3][..., None]
        own, cross = outputs[s, s], outputs[s, 1 - s]
        mixed = gates * own + (1.0 - gates) * cross
        mix = mixed.reshape(mixed.shape[0], -1).astype(low)
        middle = own_tokens[s].astype(full) + own_sum(dot(mix, full_out[s]))
        normed, inverse = normalize(middle)
        lowered = both((normed * gains_ffn[s]).astype(low))
        upward = dot(lowered, full_up[s])
        activated, gelu_back = jax.vjp(jax.nn.gelu, upward)
        act = activated.astype(low)
        results.append((middle + own_sum(dot(act, full_down[s]))).astype(low))
        part_down = dot_rows(act, grads_out[s]).astype(low)
        grad_up = gelu_back(dot_back(grads_out[s], full_down[s]))[0].astype(low)
        part_up = dot_rows(lowered, grad_up).astype(low)
        grad_in, part_gain = normalize_back(
            own_sum(dot_back(grad_up, full_up[s])), normed, inverse, gains_ffn[s]
        )
        grad_middle = own_grads[s].astype(full) + grad_in
        grad_branch = both(grad_middle.astype(low))
        part_out = dot_rows(mix, grad_branch).astype(low)
        grad_mix = heads_of(dot_back(grad_branch, full_out[s]), heads)
        grad_gate = (
            jnp.sum(grad_mix * (own - cross), -1) * fronts[s][3] * (1.0 - fronts[s][3])
        ).astype(low)
        grad_own = (gates * grad_mix).astype(low)
        grad_cross = ((1.0 - gates) * grad_mix).astype(low)
        tails.append(
            (grad_middle, grad_gate, grad_own, grad_cross, part_out, part_up, part_down, part_gain)
        )

    backs = {}
    for s in range(2):
        for t in range(2):
            backs[s, t] = attend_back(
                fronts[s][4],
                fronts[t][5],
                fronts[t][6],
                valids[t],
                scale,
                totals[s, t],
                tails[s][2 if s == t else 3],
                outputs[s, t],
            )

    token_grads, parts_qkv = [], []
    for s in range(2):
        normed, inverse, lowered = fronts[s][:3]
        rows = lowered.shape[0]
        grad_q = backs[s, s][0] + backs[s, 1 - s][0]
        grad_k = backs[s, s][1] + backs[1 - s, s][1]
        grad_v = backs[s, s][2] + backs[1 - s, s][2]
        grad_wide = jnp.concatenate(
            [grad.reshape(rows, -1).astype(low) for grad in (grad_q, grad_k, grad_v)]
            + [tails[s][1], jnp.zeros((rows, lane - heads), low)],
            1,
        )
        part = dot_rows(lowered, grad_wide)
        own_rows = rows // 2
        grad_in, part_gain = normalize_back(
            own_sum(dot_back(grad_wide, full_qkv[s])),
            normed[:own_rows],
            inverse[:own_rows],
            gains_attn[s],
        )
        token_grads.append((tails[s][0] + grad_in)[None])
        parts_qkv.append(
            jnp.concatenate(
                [
                    part[:, : 3 * half + heads],
                    part_gain[:, None],
                    tails[s][7][:, None],
                    part[:, 3 * half + heads + 2 :],
                ],
                1,
            ).astype(low)
        )
    part_qkv = jnp.stack(parts_qkv)
    part_out, part_up, part_down = (
        jnp.stack([tails[0][at], tails[1][at]]) for at in (4, 5, 6)
    )
    scatter = lambda array: lax.psum_scatter(
        array.astype(full), docs_axis, scatter_dimension=1, tiled=True
    )

    def columns(own):
        other = swap(own)
        first = jnp.where(core == 0, own, other)
        second = jnp.where(core == 0, other, own)
        return first, second

    def rows_both(part):
        empty = jnp.zeros_like(part)
        first = jnp.where(core == 0, part, empty)
        second = jnp.where(core == 0, empty, part)
        return lax.psum(scatter(jnp.concatenate([first, second], 1)), core_axis)

    qkv_first, qkv_second = columns(scatter(part_qkv))
    grad_qkv = jnp.concatenate(
        [
            piece[:, :, column * half : (column + 1) * half]
            for column in range(3)
            for piece in (qkv_first, qkv_second)
        ],
        2,
    )
    small = jnp.stack([qkv_first[:, :, 3 * half :], qkv_second[:, :, 3 * half :]])
    grad_up = jnp.concatenate(columns(scatter(part_up)), 2)
    grad_out, grad_down = rows_both(part_out), rows_both(part_down)
    grad_gate = jnp.concatenate([small[0, :, :, :heads], small[1, :, :, :heads]], 2)
    gains = small[0] + small[1]
    return (
        results[0][None],
        results[1][None],
        token_grads[0],
        token_grads[1],
        grad_qkv,
        grad_out,
        grad_gate,
        grad_up,
        grad_down,
        gains[:, :, heads],
        gains[:, :, heads + 1],
    )


def solution(mesh):
    rows = P(docs_axis, core_axis, None)
    weights = P(None, docs_axis, None)
    gains = P(None, docs_axis)
    in_specs = (
        (rows, rows, P(docs_axis, None), P(docs_axis, None)) + (weights,) * 5 + (gains,) * 2 + (rows,) * 2
    )
    out_specs = (rows,) * 4 + (weights,) * 5 + (gains,) * 2
    return jax.shard_map(
        functools.partial(on_device, mesh.shape[docs_axis]),
        mesh=mesh,
        in_specs=in_specs,
        out_specs=out_specs,
        check_vma=False,
    )
```

```python
import functools
import types
from typing import NamedTuple

import jax
import jax.numpy as jnp
from jax import lax
from jax.experimental import pallas as pl
from jax.experimental.pallas import tpu as pltpu
from jax.sharding import PartitionSpec as P

epsilon = 1e-05
big_negative = -1e30
MESH = pl.DeviceIdType.MESH
docs_axis, core_axis = "docs", "blk"
lane = 128
row_tile = 16
vmem_limit = 61 * 1024 * 1024
low, full = jnp.bfloat16, jnp.float32
by_x, by_y, upward, downward, crosswise = range(5)
lines_first, planes_first, line_only, plane_shared = range(4)
quads = ((False, False), (False, True), (True, False), (True, True))


def dot(left, right):
    return jnp.dot(left, right, preferred_element_type=full)


def dot_back(left, right):
    return lax.dot_general(left, right, (((1,), (1,)), ((), ())), preferred_element_type=full)


def dot_rows(left, right):
    return lax.dot_general(left, right, (((0,), (0,)), ((), ())), preferred_element_type=full)


def normalize(values):
    centred = values - jnp.mean(values, -1, keepdims=True)
    inverse = lax.rsqrt(jnp.mean(centred * centred, -1, keepdims=True) + epsilon)
    return centred * inverse, inverse


def over_rows(first, last, size, body):
    def step(at, carry):
        body(pl.ds(pl.multiple_of(first + at * size, row_tile), size))
        return carry

    lax.fori_loop(0, (last - first) // size, step, 0)


def over_columns(first, last, size, body):
    def step(at, carry):
        body(pl.ds(pl.multiple_of(first + at * size, lane), size))
        return carry

    lax.fori_loop(0, (last - first) // size, step, 0)


def gelu_both(value):
    root = 0.7978845608028654
    square = value * value
    bent = jnp.tanh(root * (value + 0.044715 * value * square))
    cdf = 0.5 * (1.0 + bent)
    slope = cdf + 0.5 * value * (1.0 - bent * bent) * (root * (1.0 + 0.134145 * square))
    return value * cdf, slope


def add_rows(target, others, first=0):
    size = max(size for size in (16, 32, 48) if others[0].shape[0] % size == 0)

    def body(step, carry):
        at = pl.multiple_of(step * size, row_tile)
        total = others[0][pl.ds(at, size), :].astype(full)
        for other in others[1:]:
            total = total + other[pl.ds(at, size), :].astype(full)
        target[pl.ds(first + at, size), :] = total.astype(target.dtype)
        return carry

    lax.fori_loop(0, others[0].shape[0] // size, body, 0)


def when(conditions, body):
    conditions = [condition for condition in conditions if condition is not None]
    if not conditions:
        body()
        return
    pl.when(functools.reduce(jnp.logical_and, conditions))(body)


def merged(*groups):
    space = types.SimpleNamespace()
    for group in groups:
        vars(space).update(group._asdict())
    return space


class Place:
    def __init__(self, line_size):
        docs = lax.axis_index(docs_axis)
        self.core = lax.axis_index(core_axis)
        self.line_size = line_size
        self.z, self.y, self.x = docs // 4, (docs // 2) % 2, docs % 2
        self.up_valid = self.z < line_size - 1
        self.down_valid = self.z > 0

    def index(self, z, flip_y=False, flip_x=False):
        y = 1 - self.y if flip_y else self.y
        x = 1 - self.x if flip_x else self.x
        return z * 4 + y * 2 + x

    def device(self, step):
        z, y, x = self.z, self.y, self.x
        docs = (
            z * 4 + y * 2 + 1 - x,
            z * 4 + (1 - y) * 2 + x,
            (z + 1) * 4 + y * 2 + x,
            (z - 1) * 4 + y * 2 + x,
            z * 4 + (1 - y) * 2 + 1 - x,
        )[step]
        return (docs, self.core)

    def greet(self):
        barrier = pltpu.get_barrier_semaphore()

        def signal(device):
            pl.semaphore_signal(barrier, inc=1, device_id=device, device_id_type=MESH)

        for step in (by_x, by_y, crosswise):
            signal(self.device(step))
        pl.when(self.up_valid)(lambda: signal(self.device(upward)))
        pl.when(self.down_valid)(lambda: signal(self.device(downward)))
        signal((self.index(self.z), 1 - self.core))

    def meet(self):
        peers = 4
        for valid in (self.up_valid, self.down_valid):
            peers = peers + jnp.where(valid, 1, 0)
        pl.semaphore_wait(pltpu.get_barrier_semaphore(), peers)


class Piece(NamedTuple):
    array: int
    part: int
    first: int
    rows: int
    flip: int
    route: int


class Gather:
    def __init__(self, place, pieces, sizes, splits, owns, outs, send_sems, recv_sems, local_sems):
        self.place, self.pieces, self.sizes, self.splits = place, pieces, sizes, splits
        self.owns, self.outs = owns, outs
        self.send_sems, self.recv_sems, self.local_sems = send_sems, recv_sems, local_sems

    def has(self, at, source_z):
        half = self.place.line_size // 2
        return source_z // half == self.place.core if self.splits[self.pieces[at].array] else None

    def block(self, at, source):
        piece = self.pieces[at]
        if self.splits[piece.array]:
            source = source - self.place.core * (self.place.line_size // 2) * 4
        if piece.route == line_only:
            source = source // 4
        first = source * self.sizes[piece.array] + piece.first
        rows = pl.ds(pl.multiple_of(first, row_tile), piece.rows)
        return self.outs[piece.array].at[piece.part, rows, :]

    def mine(self, at, step=None):
        piece = self.pieces[at]
        ref, offset = self.owns[piece.array]
        if piece.route == plane_shared:
            to = self.place.index(0, step in (by_y, crosswise), step in (by_x, crosswise))
            return ref.at[to, pl.ds(piece.first, piece.rows), :]
        first = pl.multiple_of(offset + piece.first, row_tile)
        return ref.at[piece.part, pl.ds(first, piece.rows), :]

    def copy(self, at, source, step, own=False):
        return pltpu.make_async_remote_copy(
            src_ref=self.mine(at, step) if own else self.block(at, source),
            dst_ref=self.block(at, source),
            send_sem=self.send_sems.at[at, step],
            recv_sem=self.recv_sems.at[at, source],
            device_id=self.place.device(step),
            device_id_type=MESH,
        )

    def local(self, at):
        here = self.place.index(self.place.z)
        return pltpu.make_async_copy(self.mine(at), self.block(at, here), self.local_sems.at[at])

    def send(self, conditions, *which):
        when(conditions, lambda: self.copy(*which).start())

    def wait(self, conditions, at, source):
        when(conditions, lambda: self.copy(at, source, by_x).wait_recv())

    def units(self, distance):
        place = self.place
        if distance == 0:
            return [(place.z, None, None)]
        return [
            (place.z - distance, place.z >= distance, (upward, place.up_valid)),
            (place.z + distance, place.z < place.line_size - distance, (downward, place.down_valid)),
        ]

    def both_ways(self, conditions, at, source, own=False):
        self.send(conditions + [self.place.up_valid], at, source, upward, own)
        self.send(conditions + [self.place.down_valid], at, source, downward, own)

    def own(self, at):
        place = self.place
        here = place.index(place.z)
        held = [self.has(at, place.z)]
        when(held, lambda: self.local(at).start())
        self.both_ways(held, at, here, True)
        route = self.pieces[at].route
        if route != line_only:
            self.send(held, at, here, by_x, True)
            self.send(held, at, here, by_y, True)
        if route == plane_shared:
            self.send(held, at, here, crosswise, True)

    def beside(self, at, distance):
        piece = self.pieces[at]
        for source_z, valid, _ in self.units(distance):
            conditions = [valid, self.has(at, source_z)]
            for other in (0, 1):
                source = self.place.index(source_z, other == 1, other == 0)
                if other == piece.flip or piece.route != lines_first:
                    self.wait(conditions, at, source)
                if other == piece.flip and piece.route != plane_shared:
                    self.send(conditions, at, source, by_x if other else by_y)
                if piece.route != lines_first:
                    self.both_ways(conditions, at, source)

    def along(self, at, distance, quad=quads[0]):
        for source_z, valid, (step, onward) in self.units(distance):
            source = self.place.index(source_z, *quad)
            conditions = [valid, self.has(at, source_z)]
            self.wait(conditions, at, source)
            self.send(conditions + [onward], at, source, step)
            if self.pieces[at].route == lines_first:
                self.send(conditions, at, source, by_x)
                self.send(conditions, at, source, by_y)

    def late_round(self, at, number):
        place = self.place
        last = place.line_size - 1
        if number == 1:
            self.beside(at, 0)
        if number == 2:
            held = [self.has(at, place.z)]
            fourth = place.index(place.z, *quads[3])
            self.wait(held, at, fourth)
            self.both_ways(held, at, fourth)
        for quad, behind in zip(quads, (0, 1, 1, 2)):
            if 1 <= number - behind <= last:
                self.along(at, number - behind, quad)

    def rest(self, array):
        for at, piece in enumerate(self.pieces):
            if piece.array != array:
                continue
            if piece.route in (planes_first, plane_shared):
                self.along(at, self.place.line_size - 1, quads[3])
            elif piece.route == lines_first:
                for distance in range(self.place.line_size):
                    for source_z, valid, _ in self.units(distance):
                        conditions = [valid, self.has(at, source_z)]
                        beside = (piece.flip == 0, piece.flip == 1)
                        self.wait(conditions, at, self.place.index(source_z, *beside))
                        self.wait(conditions, at, self.place.index(source_z, *quads[3]))
            when([self.has(at, self.place.z)], lambda: self.local(at).wait())

    def run(self, plan, stages):
        for kind, at, number in plan:
            if kind == 0:
                self.own(at)
            elif kind == 1:
                self.beside(at, number)
            elif kind == 2:
                self.along(at, number)
            elif kind == 3:
                self.late_round(at, number)
            elif kind == 4:
                self.rest(at)
            else:
                stages[at]()

    def sent(self, at, step, blocks):
        piece = self.pieces[at]
        total = self.outs[piece.array].at[piece.part, pl.ds(0, blocks * piece.rows), :]
        pltpu.make_async_remote_copy(
            src_ref=total,
            dst_ref=total,
            send_sem=self.send_sems.at[at, step],
            recv_sem=self.recv_sems.at[at, 0],
            device_id=self.place.device(step),
            device_id_type=MESH,
        ).wait_send()

    def finish(self):
        size, place = self.place.line_size, self.place
        for at, piece in enumerate(self.pieces):
            split = self.splits[piece.array]
            planes = size // 2 if split else size
            if piece.route == lines_first:
                self.sent(at, by_x, planes * (1 + piece.flip))
                self.sent(at, by_y, planes * (2 - piece.flip))
            elif piece.route == planes_first:
                self.sent(at, by_x, 1 + piece.flip)
                self.sent(at, by_y, 2 - piece.flip)
            elif piece.route == plane_shared:
                for step in (by_x, by_y, crosswise):
                    self.sent(at, step, 1)
            chips = 4 if piece.route in (planes_first, plane_shared) else 1
            for z in range(size):
                for core in range(2 if split else 1):
                    held = [source for source in range(size) if not split or source // (size // 2) == core]
                    here = [place.z == z] + ([place.core == core] if split else [])
                    up = chips * sum(source <= z for source in held) if z < size - 1 else 0
                    down = chips * sum(source >= z for source in held) if z > 0 else 0
                    if up:
                        when(here, lambda: self.sent(at, upward, up))
                    if down:
                        when(here, lambda: self.sent(at, downward, down))


class Scatter:
    def __init__(self, place, pieces, splits, raws, parts, buffers, send_sems, recv_sems, finish):
        self.place, self.pieces, self.splits = place, pieces, splits
        self.raws, self.parts, self.buffers = raws, parts, buffers
        self.send_sems, self.recv_sems, self.finish_rows = send_sems, recv_sems, finish
        self.first = arrival_offsets(pieces, place.line_size)

    shares = ((quads[1], 1, by_x), (quads[2], 2, by_y), (quads[3], 0, crosswise))

    def has(self, at, z_to):
        half = self.place.line_size // 2
        return z_to // half == self.place.core if self.splits[self.pieces[at].array] else None

    def slot(self, at, z_to):
        half = self.place.line_size // 2
        return z_to - self.place.core * half if self.splits[self.pieces[at].array] else z_to

    def block(self, refs, at, z_to, quad):
        piece = self.pieces[at]
        ref = refs[piece.array]
        if piece.route == line_only:
            first = z_to * (ref.shape[1] // self.place.line_size) + piece.first
        else:
            split = 2 if self.splits[piece.array] else 1
            rows = ref.shape[1] // (4 * self.place.line_size // split)
            first = self.place.index(self.slot(at, z_to), *quad) * rows + piece.first
        return ref.at[piece.part, pl.ds(pl.multiple_of(first, row_tile), piece.rows), :]

    def quads(self, at):
        return quads[:1] if self.pieces[at].route == line_only else quads

    def raw_of(self, at, z_to, quad):
        return self.block(self.raws, at, z_to, quad)

    def part_of(self, at, z_to, quad):
        return self.block(self.parts, at, z_to, quad)

    def landed(self, at, kind, z_to, quad=0):
        ref = self.buffers[at][kind]
        if self.pieces[at].route == lines_first:
            return ref.at[self.slot(at, z_to)]
        return ref.at[self.slot(at, z_to), quad] if kind >= 3 else ref.at[0]

    def arrival(self, at, kind, z_to, quad):
        route = self.pieces[at].route
        if route == lines_first:
            return self.first[at] + z_to * 5 + kind
        if kind < 3:
            return self.first[at] + kind
        chips = len(self.quads(at))
        return self.first[at] + 3 + (z_to * 2 + kind - 3) * chips + quad

    def copy(self, source, at, kind, z_to, step, quad=0):
        return pltpu.make_async_remote_copy(
            src_ref=source,
            dst_ref=self.landed(at, kind, z_to, quad),
            send_sem=self.send_sems.at[at],
            recv_sem=self.recv_sems.at[self.arrival(at, kind, z_to, quad)],
            device_id=self.place.device(step),
            device_id_type=MESH,
        )

    def arrived(self, at, kind, z_to, quad=0):
        held = self.landed(at, kind, z_to, quad)
        self.copy(held, at, kind, z_to, by_x, quad).wait_recv()

    def send(self, conditions, *which):
        when(conditions, lambda: self.copy(*which).start())

    def destination(self, step):
        size = self.place.line_size
        chosen = 0
        for at in range(size):
            order = sorted(range(size), key=lambda other: (-abs(other - at), other))
            chosen = chosen + jnp.where(self.place.z == at, order[step], 0)
        return chosen

    def raw(self, at, step):
        place = self.place
        z_to = self.destination(step)
        conditions = [self.has(at, z_to)]
        if self.pieces[at].route == lines_first:
            self.plane_raw(conditions, self.raw_of, at, z_to)
            return
        first, last = place.z == 0, place.z == place.line_size - 1
        for number, quad in enumerate(self.quads(at)):
            source = self.raw_of(at, z_to, quad)
            up = conditions + [first, z_to > place.z]
            self.send(up, source, at, 3, z_to, upward, number)
            down = conditions + [last, z_to < place.z]
            self.send(down, source, at, 4, z_to, downward, number)

    def plane_raw(self, conditions, source, at, z_to):
        if self.pieces[at].flip == 0:
            self.send(conditions, source(at, z_to, (True, True)), at, 0, z_to, by_y)
            self.send(conditions, source(at, z_to, (True, False)), at, 2, z_to, by_y)
        else:
            self.send(conditions, source(at, z_to, (True, True)), at, 0, z_to, by_x)
            self.send(conditions, source(at, z_to, (False, True)), at, 1, z_to, by_x)

    def plane_pair(self, conditions, at, z_to):
        flip = self.pieces[at].flip
        held = self.landed(at, 0, z_to)

        def body():
            self.arrived(at, 0, z_to)
            add_rows(held, [held, self.part_of(at, z_to, (flip == 1, flip == 0))])

        when(conditions, body)
        if flip == 0:
            self.send(conditions, held, at, 1, z_to, by_x)
        else:
            self.send(conditions, held, at, 2, z_to, by_y)

    def pair(self, at, step):
        z_to = self.destination(step)
        self.plane_pair([self.has(at, z_to)], at, z_to)

    def line(self, at, step):
        place, piece = self.place, self.pieces[at]
        z = place.z
        z_to = self.destination(step)
        conditions = [self.has(at, z_to)]
        first, last = z == 0, z == place.line_size - 1
        inner = jnp.logical_and(z > 0, z < place.line_size - 1)
        ways = (
            (3, [z_to > z], [first], [z > 0], upward),
            (4, [z_to < z], [last], [z < place.line_size - 1], downward),
        )
        ends = (([first], (4,)), ([last], (3,)), ([inner], (3, 4)))
        if piece.route == lines_first:
            held = self.landed(at, 1, z_to)
            base = [held, self.landed(at, 2, z_to), self.part_of(at, z_to, quads[0])]

            def wait():
                self.arrived(at, 1, z_to)
                self.arrived(at, 2, z_to)

            when(conditions, wait)
            for kind, onward, starts, passes, step_to in ways:
                when(conditions + onward + starts, lambda: add_rows(held, base))

                def passing():
                    self.arrived(at, kind, z_to)
                    add_rows(held, base + [self.landed(at, kind, z_to)])

                when(conditions + onward + passes, passing)
                self.send(conditions + onward, held, at, kind, z_to, step_to)
            for which, kinds in ends:

                def end():
                    for kind in kinds:
                        self.arrived(at, kind, z_to)
                    self.finish_rows(piece, base + [self.landed(at, kind, z_to) for kind in kinds])

                when(conditions + [z_to == z] + which, end)
            return
        for kind, onward, _, passes, step_to in ways:
            for at_quad, quad in enumerate(self.quads(at)):
                held = self.landed(at, kind, z_to, at_quad)

                def passing():
                    self.arrived(at, kind, z_to, at_quad)
                    add_rows(held, [held, self.part_of(at, z_to, quad)])

                which = conditions + onward + passes
                when(which, passing)
                self.send(which, held, at, kind, z_to, step_to, at_quad)
        here = conditions + [z_to == z]
        for which, kinds in ends:

            def end():
                for at_quad, quad in reversed(list(enumerate(self.quads(at)))):
                    own = self.part_of(at, z_to, quad)
                    for kind in kinds:
                        self.arrived(at, kind, z_to, at_quad)
                    total = [own] + [self.landed(at, kind, z_to, at_quad) for kind in kinds]
                    if piece.route == planes_first or at_quad:
                        add_rows(own, total)
                    else:
                        self.finish_rows(piece, total)

            when(here + which, end)
        if step == place.line_size - 1 and piece.route == planes_first:
            self.plane_raw(here, self.part_of, at, z_to)
        if step == place.line_size - 1 and piece.route == plane_shared:
            for quad, kind, step_to in self.shares:
                self.send(here, self.part_of(at, z_to, quad), at, kind, z_to, step_to)

    def tail(self, at):
        z, piece = self.place.z, self.pieces[at]
        if piece.route == plane_shared:
            for quad, kind, _ in self.shares:
                self.arrived(at, kind, z)
                self.finish_rows(piece, [self.landed(at, kind, z)], quad)
            return
        conditions = [self.has(at, z)]
        self.plane_pair(conditions, at, z)

        def end():
            self.arrived(at, 1, z)
            self.arrived(at, 2, z)
            total = [self.landed(at, kind, z) for kind in (1, 2)] + [self.part_of(at, z, quads[0])]
            self.finish_rows(piece, total)

        when(conditions, end)

    def run(self, plan, stages):
        for kind, at, number in plan:
            if kind == 0:
                self.raw(at, number)
            elif kind == 1:
                self.pair(at, number)
            elif kind == 2:
                self.line(at, number)
            elif kind == 3:
                self.tail(at)
            else:
                stages[at]()

    def sent(self, at, blocks):
        piece = self.pieces[at]
        total = self.raws[piece.array].at[piece.part, pl.ds(0, blocks * piece.rows), :]
        pltpu.make_async_remote_copy(
            src_ref=total,
            dst_ref=total,
            send_sem=self.send_sems.at[at],
            recv_sem=self.recv_sems.at[0],
            device_id=self.place.device(by_x),
            device_id_type=MESH,
        ).wait_send()

    def finish(self):
        size, place = self.place.line_size, self.place
        for at, piece in enumerate(self.pieces):
            if self.splits[piece.array]:
                half = place.z // (size // 2) == place.core
                when([half], lambda: self.sent(at, 3 * (size // 2) + size // 2 - 1))
                when([jnp.logical_not(half)], lambda: self.sent(at, 4 * (size // 2)))
            elif piece.route == lines_first:
                self.sent(at, 4 * size - 1)
            elif piece.route == line_only:
                self.sent(at, size - 1)
            else:
                self.sent(at, 4 * (size - 1) + 3)


def arrival_offsets(pieces, line_size):
    offsets = [0]
    for piece in pieces:
        chips = 1 if piece.route == line_only else 4
        count = 5 * line_size if piece.route == lines_first else 3 + 2 * line_size * chips
        offsets.append(offsets[-1] + count)
    return offsets


class Moves:
    def __init__(self, place, local_sems, send_sems, recv_sems):
        self.place = place
        self.other = (place.index(place.z), 1 - place.core)
        self.local_sems, self.send_sems, self.recv_sems = local_sems, send_sems, recv_sems
        self.locals, self.remotes = 0, 0
        self.to_end = []

    def local(self, source, target):
        made = pltpu.make_async_copy(source, target, self.local_sems.at[self.locals])
        self.locals += 1
        made.start()
        return made

    def save(self, source, target):
        self.to_end.append(self.local(source, target).wait)

    def across(self, source, target, arrives=None):
        sems = dict(
            send_sem=self.send_sems.at[self.remotes],
            recv_sem=self.recv_sems.at[self.remotes],
            device_id=self.other,
            device_id_type=MESH,
        )
        self.remotes += 1
        made = pltpu.make_async_remote_copy(src_ref=source, dst_ref=target, **sems)
        made.start()
        self.to_end.append(made.wait_send)
        arrives = target if arrives is None else arrives
        return pltpu.make_async_remote_copy(src_ref=arrives, dst_ref=arrives, **sems)

    def peer(self, source, target, step, arrives=None):
        sems = dict(
            send_sem=self.send_sems.at[self.remotes],
            recv_sem=self.recv_sems.at[self.remotes],
            device_id=self.place.device(step),
            device_id_type=MESH,
        )
        self.remotes += 1
        made = pltpu.make_async_remote_copy(src_ref=source, dst_ref=target, **sems)
        made.start()
        self.to_end.append(made.wait_send)
        arrives = target if arrives is None else arrives
        return pltpu.make_async_remote_copy(src_ref=arrives, dst_ref=arrives, **sems)

    def finish(self):
        assert self.locals == self.local_sems.shape[0] and self.remotes == self.send_sems.shape[0]
        for wait in self.to_end:
            wait()


class Rows:
    def __init__(self, text, visual):
        self.text, self.visual = text, visual
        self.split = 2 * text
        self.count = 2 * (text + visual)
        self.spans = ((0, self.split), (self.split, self.count))
        self.own = ((0, text), (self.split, self.split + visual))
        self.other = ((text, self.split), (self.split + visual, self.count))
        self.packed = ((0, text), (text, text + visual))
        self.sizes = (chunk_of(text), chunk_of(visual))

    def over_own(self, s, body):
        shift = self.own[s][0] - self.packed[s][0]

        def shifted(piece):
            body(pl.ds(pl.multiple_of(piece.start + shift, row_tile), piece.size), piece)

        over_rows(*self.packed[s], self.sizes[s], shifted)

    def swap_parts(self, moves, wide, received, which=(0, 1)):
        return [
            moves.across(wide.at[slice(*self.other[s])], received.at[slice(*self.packed[s])])
            for s in which
        ]

    def swap_own(self, moves, ref, s):
        return moves.across(ref.at[slice(*self.own[s])], ref.at[slice(*self.other[s])])


class Plane:
    steps = (by_x, by_y, crosswise)

    def __init__(self, place, moves, size):
        self.place, self.moves, self.size = place, moves, size
        self.half = 4 * size

    def chip(self, step=None):
        return self.place.index(0, step in (by_y, crosswise), step in (by_x, crosswise))

    def document(self, at):
        return [slice(first, first + self.size) for first in (at * self.size, self.half + at * self.size)]

    def part(self, ref, at, count=1):
        return ref.at[at * self.size : (at + count) * self.size]

    def spread(self, own, target):
        other = self.moves.across(own, self.part(target, 4))
        return other, [
            self.moves.peer(own, self.part(target, 1 + at), step) for at, step in enumerate(self.steps)
        ]

    def pass_on(self, target, arrivals):
        for arrival in arrivals:
            arrival.wait_recv()
        return self.moves.across(self.part(target, 1, 3), self.part(target, 5, 3))

    def halve(self, wide, received):
        return self.moves.across(self.part(wide, 4, 4), received)

    def share(self, wide, received, outgoing, landing):
        outgoing[...] = (
            wide[self.size : self.half, :] + received[self.size : self.half, :]
        ).astype(outgoing.dtype)
        return [
            self.moves.peer(self.part(outgoing, at), self.part(landing, at), step)
            for at, step in enumerate(self.steps)
        ]

    def total(self, wide, received, landing):
        value = wide[: self.size, :] + received[: self.size, :]
        for at in range(3):
            value = value + landing[at * self.size : (at + 1) * self.size, :].astype(full)
        return value


def chunk_of(count):
    return max(size for size in range(row_tile, 385, row_tile) if count % size == 0)


def query_spans(count):
    edges = list(range(0, count - 256, 512)) + [count]
    return list(zip(edges[:-1], edges[1:]))


def head_wide(values, odd):
    empty = jnp.zeros_like(values)
    return jnp.concatenate([empty, values] if odd else [values, empty], 0)


def column_of(row, count):
    return jnp.broadcast_to(row, (lane, count)).T


def scratch_of(group):
    return [pltpu.VMEM(shape, dtype) for shape, dtype in group]


def shapes_of(group):
    return [jax.ShapeDtypeStruct(shape, dtype) for shape, dtype in group]


def same_as(arrays):
    return [(array.shape, array.dtype) for array in arrays]


def sems(*counts):
    return [pltpu.SemaphoreType.DMA(count if isinstance(count, tuple) else (count,)) for count in counts]


def specs_of(count, in_vmem):
    spaces = [pltpu.VMEM] * in_vmem + [pl.ANY] * (count - in_vmem)
    return [pl.BlockSpec(memory_space=space) for space in spaces]


front_pieces = (
    (0, 0, 0, 32, 0, 0), (0, 0, 32, 16, 1, 0), (1, 0, 0, 32, 0, 0), (1, 0, 32, 16, 1, 0),
    (2, 0, 0, 48, 0, 0), (2, 1, 0, 48, 1, 0), (3, 0, 0, 32, 0, 0), (3, 0, 32, 16, 1, 0),
    (3, 0, 48, 48, 1, 1), (4, 0, 0, 48, 0, 3), (5, 0, 0, 96, 0, 2), (6, 0, 0, 48, 0, 3),
    (7, 0, 0, 48, 1, 0),
)
front_plan = (
    (0, 4, 0), (0, 11, 0), (5, 23, 0), (0, 1, 0), (0, 8, 0), (3, 11, 1), (2, 4, 1), (5, 25, 0), (0, 12, 0),
    (3, 11, 2), (2, 12, 1), (0, 7, 0), (5, 0, 0), (0, 0, 0), (0, 6, 0), (2, 12, 2), (3, 11, 3), (2, 1, 1),
    (2, 0, 1), (3, 11, 4), (5, 26, 0), (0, 5, 0), (2, 4, 2), (2, 12, 3), (0, 9, 0), (2, 0, 2), (0, 3, 0),
    (1, 1, 0), (0, 10, 0), (2, 1, 2), (1, 12, 3), (1, 4, 2), (1, 0, 2), (1, 12, 0), (0, 2, 0), (2, 0, 3),
    (2, 5, 1), (2, 10, 1), (1, 0, 0), (1, 12, 1), (1, 0, 1), (2, 1, 3), (1, 12, 2), (3, 9, 1), (2, 4, 3),
    (1, 1, 2), (3, 8, 1), (4, 6, 0), (2, 5, 2), (5, 1, 0), (1, 0, 3), (1, 1, 3), (1, 1, 1), (2, 2, 1),
    (2, 10, 2), (4, 7, 0), (5, 4, 0), (5, 5, 0), (2, 7, 1), (5, 24, 0), (1, 5, 1), (4, 0, 0), (3, 9, 2),
    (2, 3, 1), (5, 2, 0), (5, 3, 0), (1, 5, 2), (2, 6, 1), (1, 4, 3), (2, 5, 3), (1, 2, 1), (1, 5, 0),
    (2, 2, 2), (5, 6, 0), (5, 7, 0), (5, 8, 0), (1, 4, 0), (5, 9, 0), (1, 4, 1), (2, 7, 2), (2, 3, 2),
    (3, 8, 2), (1, 5, 3), (1, 2, 0), (5, 10, 0), (5, 11, 0), (2, 2, 3), (1, 3, 1), (2, 3, 3), (5, 12, 0),
    (5, 13, 0), (2, 6, 2), (2, 10, 3), (1, 2, 2), (4, 2, 0), (5, 14, 0), (1, 3, 0), (2, 7, 3), (1, 3, 2),
    (3, 9, 3), (2, 6, 3), (1, 7, 1), (1, 2, 3), (1, 3, 3), (1, 7, 0), (1, 7, 3), (3, 8, 3), (5, 16, 0),
    (5, 15, 0), (3, 9, 4), (1, 7, 2), (1, 6, 1), (1, 6, 2), (4, 5, 0), (1, 6, 0), (4, 1, 0), (5, 18, 0),
    (5, 19, 0), (3, 8, 4), (5, 17, 0), (1, 6, 3), (5, 21, 0), (4, 4, 0), (5, 20, 0), (4, 3, 0), (5, 22, 0),
)
ffn_pieces = (
    (0, 0, 0, 48, 0, 0), (0, 0, 48, 48, 1, 0), (1, 0, 0, 96, 0, 2),
)
ffn_plan = (
    (0, 0, 0), (0, 2, 0), (0, 1, 0), (0, 1, 1), (0, 1, 2), (0, 0, 1), (4, 2, 0), (2, 2, 0), (0, 0, 2),
    (0, 2, 1), (4, 0, 0), (4, 1, 0), (1, 1, 0), (4, 9, 0), (2, 2, 1), (1, 0, 0), (1, 0, 1), (0, 2, 2),
    (4, 3, 0), (0, 2, 3), (2, 2, 2), (4, 4, 0), (0, 0, 3), (1, 0, 2), (1, 1, 1), (4, 10, 0), (2, 0, 0),
    (1, 1, 2), (0, 1, 3), (4, 5, 0), (2, 1, 0), (4, 13, 0), (4, 7, 0), (2, 0, 1), (4, 8, 0), (4, 6, 0),
    (2, 2, 3), (2, 1, 1), (2, 1, 2), (1, 0, 3), (1, 1, 3), (4, 14, 0), (2, 0, 2), (4, 11, 0), (4, 12, 0),
    (4, 15, 0), (2, 0, 3), (2, 1, 3),
)
attention_pieces = (
    (0, 0, 0, 16, 0, 0), (0, 0, 16, 32, 1, 0), (1, 0, 0, 48, 0, 0), (1, 1, 0, 48, 1, 0),
    (2, 0, 0, 32, 1, 0), (2, 0, 32, 16, 0, 0), (3, 0, 0, 48, 0, 3), (4, 0, 0, 48, 0, 3),
    (5, 0, 0, 48, 0, 0), (5, 1, 0, 48, 1, 0),
)
attention_plan = (
    (0, 1, 0), (0, 0, 0), (0, 3, 0), (0, 3, 1), (0, 1, 1), (4, 0, 0), (0, 0, 1), (4, 1, 0), (0, 2, 0),
    (4, 2, 0), (1, 3, 0), (0, 6, 0), (0, 2, 1), (0, 2, 2), (4, 3, 0), (0, 1, 2), (2, 6, 0), (0, 3, 2),
    (1, 1, 0), (1, 0, 0), (4, 4, 0), (4, 5, 0), (0, 2, 3), (1, 3, 1), (4, 6, 0), (4, 7, 0), (1, 2, 0),
    (2, 1, 0), (0, 3, 3), (4, 9, 0), (2, 0, 0), (1, 2, 1), (0, 6, 1), (0, 5, 0), (0, 4, 0), (0, 0, 2),
    (0, 0, 3), (4, 10, 0), (0, 6, 2), (4, 8, 0), (4, 12, 0), (1, 1, 1), (2, 2, 0), (1, 4, 0), (1, 0, 1),
    (2, 3, 0), (0, 4, 1), (2, 6, 1), (4, 11, 0), (0, 7, 0), (0, 7, 1), (4, 13, 0), (4, 14, 0), (0, 9, 0),
    (1, 5, 0), (0, 9, 1), (1, 0, 2), (1, 2, 2), (0, 6, 3), (0, 8, 0), (2, 6, 2), (1, 1, 2), (2, 3, 1),
    (2, 7, 0), (1, 9, 0), (0, 8, 1), (2, 0, 1), (0, 4, 2), (1, 8, 0), (0, 5, 1), (2, 4, 0), (0, 9, 2),
    (2, 0, 2), (0, 7, 2), (0, 8, 2), (1, 4, 1), (1, 0, 3), (0, 5, 2), (2, 7, 1), (1, 9, 1), (0, 1, 3),
    (1, 8, 1), (1, 4, 2), (1, 5, 1), (2, 7, 2), (0, 8, 3), (2, 9, 0), (2, 6, 3), (2, 1, 1), (2, 2, 1),
    (1, 3, 2), (1, 3, 3), (1, 8, 2), (2, 1, 2), (1, 1, 3), (2, 9, 1), (2, 8, 0), (0, 4, 3), (0, 7, 3),
    (2, 5, 0), (1, 9, 2), (1, 2, 3), (0, 5, 3), (1, 5, 2), (2, 8, 1), (1, 8, 3), (2, 5, 1), (2, 4, 1),
    (2, 8, 2), (2, 3, 2), (3, 6, 0), (2, 0, 3), (4, 18, 0), (2, 2, 2), (0, 9, 3), (1, 4, 3), (2, 1, 3),
    (4, 15, 0), (2, 9, 2), (2, 4, 2), (2, 7, 3), (1, 5, 3), (2, 2, 3), (2, 5, 2), (1, 9, 3), (2, 3, 3),
    (4, 17, 0), (2, 4, 3), (2, 8, 3), (3, 7, 0), (4, 16, 0), (2, 9, 3), (2, 5, 3),
)


class FrontIn(NamedTuple):
    w_qkv: object
    w_gate: object
    w_up: object
    gain_attn: object
    gain_ffn: object
    text_mask: object
    visual_mask: object
    text: object
    visual: object
    text_dy: object
    visual_dy: object
    w_out: object
    w_down: object


class FrontOut(NamedTuple):
    full_qkv: object
    full_up: object
    full_out: object
    full_down: object
    full_up_v: object
    full_down_v: object
    full_qkv_v: object
    full_small_v: object
    h: object
    h_v: object
    qkv: object
    gates_t: object
    text_t: object
    visual_t: object
    logs: object
    mix_t: object
    middle: object
    hm: object
    hm_v: object
    act: object
    act_v: object
    slope: object
    slope_v: object
    part_down: object
    part_down_v: object
    dy: object
    dy_v: object
    gains: object
    bias: object


class FrontKept(NamedTuple):
    s_h: object
    s_h_v: object
    s_qkv: object
    s_gates_t: object
    s_text_t: object
    s_visual_t: object
    s_logs: object
    s_mix_t: object
    s_middle: object
    s_hm: object
    s_hm_v: object
    s_act: object
    s_act_v: object
    s_slope: object
    s_slope_v: object
    s_part_down: object
    s_part_down_v: object
    s_dy: object
    s_dy_v: object
    s_gains: object
    s_bias: object


class FrontScratch(NamedTuple):
    shard_qkv: object
    shard_gate: object
    shard_up: object
    shard_attn: object
    shard_ffn: object
    shard_text_mask: object
    shard_visual_mask: object
    own_qkv: object
    own_qkv_v: object
    own_small_v: object
    own_up: object
    own_up_v: object
    s_w_qkv: object
    s_w_qkv_v: object
    s_w_small_v: object
    s_w_up: object
    s_w_up_v: object
    s_w_out: object
    x: object
    x_v: object
    wide: object
    qkv_v: object
    landing_qkv: object
    received: object
    gate_rows: object
    q_t: object
    v_t: object
    mix: object


def prepare_shards(v, core, heads):
    first = core == 0
    rows = v.shard_qkv.shape[1]
    third = v.shard_qkv.shape[2] // 3
    half = third // 2
    for s in range(2):
        for pair in range(half // lane):
            for at in range(3):
                start = at * third + pair * lane
                columns = [v.shard_qkv[s, :, start + way * half : start + way * half + lane] for way in (0, 1)]
                chosen = jnp.where(first, *columns)
                if s == 0:
                    to = (3 * pair + at) * lane
                    v.own_qkv[0, :, to : to + lane] = chosen
                else:
                    v.own_qkv_v[pair, :, at * lane : (at + 1) * lane] = chosen
        gate = v.shard_gate[:, s, :].astype(full)
        gate = jnp.where(first, gate[:heads], gate[heads:])
        gains = [ref[s : s + 1, :].astype(full) for ref in (v.shard_attn, v.shard_ffn)]
        small = jnp.concatenate([gate, *gains, jnp.zeros((lane - heads - 2, rows), full)], 0)
        small = jnp.concatenate([small, jnp.zeros((lane, lane - rows), full)], 1).T[:rows]
        if s == 0:
            v.own_qkv[0, :, 3 * half :] = small.astype(low)
        else:
            v.own_small_v[0, :, :] = small.astype(low)
    for pair in range(half // lane, 4):
        v.own_qkv_v[pair, :, :] = jnp.zeros(v.own_qkv_v.shape[1:], low)


def prepare_hidden(v, core, block):
    first = core == 0
    pieces = []
    for s in range(2):
        for start in range(0, v.shard_up.shape[2], 2 * block):
            ways = [v.shard_up[s, :, start + way * block : start + (way + 1) * block].astype(full) for way in (0, 1)]
            pieces.append(jnp.where(first, *ways))
    count = len(pieces) // 2
    v.own_up[0, :, :] = jnp.concatenate(pieces[:count], 1).astype(low)
    for quad in range(4):
        v.own_up_v[quad, :, :] = jnp.concatenate(pieces[count + quad :: 4], 1).astype(low)


def prepare_bias(v, core):
    pieces = []
    for ref in (v.shard_text_mask, v.shard_visual_mask):
        mask = ref[...].astype(full)
        half = mask.shape[1] // 2
        swapped = jnp.concatenate([mask[:, half:], mask[:, :half]], 1)
        pieces.append(jnp.where(core == 0, mask, swapped))
    row = jnp.concatenate(pieces, 1)
    v.s_bias[...] = column_of(jnp.where(row > 0.0, 0.0, big_negative), row.shape[1])


def attend_head(rows, head_width, v, number):
    pair = 2 * head_width
    at, odd = number // 2, number % 2
    keys = v.s_qkv[:, (3 * at + 1) * pair : (3 * at + 2) * pair]
    bias = v.s_bias[:, 0:1]
    head = slice(number * head_width, (number + 1) * head_width)
    for first, last in query_spans(rows.count):
        scores = dot(keys, head_wide(v.q_t[head, first:last], odd)) + bias
        for t, target in enumerate((v.s_text_t, v.s_visual_t)):
            start, stop = rows.spans[t]
            part = scores[start:stop]
            top = jnp.max(part, 0, keepdims=True)
            raised = jnp.exp(part - top)
            total = jnp.sum(raised, 0, keepdims=True)
            probs = (raised * (1.0 / total)).astype(low)
            target[head, first:last] = dot(v.v_t[head, start:stop], probs)
            row = 8 * t + number
            v.s_logs[row : row + 1, first:last] = top + jnp.log(total)


def front_kernel(line_size, heads, scale, pieces, plan, *refs):
    groups = []
    for group in (FrontIn, FrontOut, FrontKept, FrontScratch):
        count = len(group._fields)
        groups.append(group(*refs[:count]))
        refs = refs[count:]
    v = merged(*groups)
    place = Place(line_size)
    core = place.core
    rows = Rows(v.text.shape[1], v.visual.shape[1])
    shard, block = v.shard_qkv.shape[1], v.w_down.shape[1] // 2
    owns = (
        (v.own_qkv, 0),
        (v.own_up, 0),
        (v.w_out, 0),
        (v.w_down, core * block),
        (v.own_up_v, 0),
        (v.w_down.at[pl.ds(1, 1)], core * block),
        (v.own_qkv_v, 0),
        (v.own_small_v, 0),
    )
    gather = Gather(
        place,
        pieces,
        (shard, shard, shard, block, shard, block, shard, shard),
        (False, False, True, False, False, False, False, False),
        owns,
        (
            v.s_w_qkv, v.s_w_up, v.s_w_out, v.full_down, v.s_w_up_v, v.full_down_v, v.s_w_qkv_v,
            v.s_w_small_v,
        ),
        *refs[:3],
    )
    moves = Moves(place, *refs[3:])
    width = v.s_qkv.shape[1] // 3
    head_width = width // heads
    hidden = v.s_act.shape[1]
    arrivals = {}

    place.greet()
    shards = [moves.local(source, target) for source, target in zip(groups[0][:7], groups[3][:7])]
    shards[0].wait()
    shards[1].wait()
    shards[3].wait()
    shards[4].wait()
    prepare_shards(v, core, heads)
    place.meet()
    plane = Plane(place, moves, rows.visual)
    loads = [
        moves.local(v.text.at[0], v.x.at[slice(*rows.own[0])]),
        moves.local(v.visual.at[0], plane.part(v.x_v, 0)),
        moves.local(v.text_dy.at[0], v.s_dy.at[slice(*rows.own[0])]),
        moves.local(v.visual_dy.at[0], plane.part(v.s_dy_v, 0)),
    ]
    swaps = [
        moves.across(v.text.at[0], v.x.at[slice(*rows.other[0])]),
        moves.across(v.text_dy.at[0], v.s_dy.at[slice(*rows.other[0])]),
    ]

    def prepare():
        shards[2].wait()
        prepare_hidden(v, core, block)

    def norm():
        shards[5].wait()
        shards[6].wait()
        prepare_bias(v, core)
        moves.save(v.s_bias, v.bias)
        loads[0].wait()
        swaps[0].wait_recv()

        def body(piece):
            v.wide[piece, :] = normalize(v.x[piece, :].astype(full))[0]

        over_rows(0, rows.split, rows.sizes[0], body)

    def gains_of(s, small):
        v.s_gains[s, :, :] = small.astype(full).T[heads : heads + 2]

    def lower_text():
        moves.save(v.s_w_qkv, v.full_qkv)
        gains_of(0, v.s_w_qkv[0, :, 3 * width :])

        def body(piece):
            v.s_h[piece, :] = (v.wide[piece, :] * v.s_gains[0, 0:1, :]).astype(low)

        over_rows(0, rows.split, rows.sizes[0], body)
        moves.save(v.s_h, v.h)

    def project_text():
        even = 3 * width // 256 * 256

        def columns(piece):
            v.s_qkv[: rows.split, piece] = dot(v.s_h[...], v.s_w_qkv[0, :, piece]).astype(low)

        over_columns(0, even, 256, columns)
        rest = dot(v.s_h[...], v.s_w_qkv[0, :, even:])
        v.s_qkv[: rows.split, even:] = rest[:, : 3 * width - even].astype(low)
        v.gate_rows[: rows.split, :] = rest[:, 3 * width - even :]

    def spread_x():
        arrivals[6] = plane.spread(v.visual.at[0], v.x_v)

    def pass_x():
        arrivals[7] = plane.pass_on(v.x_v, arrivals[6][1])

    def lower_visual():
        moves.save(v.s_w_small_v, v.full_small_v)
        loads[1].wait()
        arrivals[6][0].wait_recv()
        arrivals[7].wait_recv()
        gains_of(1, v.s_w_small_v[0, :, :])
        v.s_h_v[...] = (normalize(v.x_v[...].astype(full))[0] * v.s_gains[1, 0:1, :]).astype(low)
        moves.save(v.s_h_v, v.h_v)
        for at, piece in enumerate(plane.document(0)):
            first = rows.split + at * rows.visual
            v.gate_rows[first : first + rows.visual, :] = dot(v.s_h_v[piece, :], v.s_w_small_v[0, :, :])

    def project_visual():
        moves.save(v.s_w_qkv_v, v.full_qkv_v)
        v.qkv_v[...] = dot(v.s_h_v[...], v.s_w_qkv_v[0, :, :]).astype(low)
        landing = lambda chip, half: v.landing_qkv.at[chip, half * rows.visual : (half + 1) * rows.visual]
        arrivals[8] = []
        for half, piece in enumerate(plane.document(0)):
            v.landing_qkv[plane.chip(), half * rows.visual : (half + 1) * rows.visual, :] = v.qkv_v[piece, :]
        for at, step in enumerate(plane.steps):
            for half, piece in enumerate(plane.document(1 + at)):
                source = v.qkv_v.at[piece]
                arrivals[8].append(
                    moves.peer(source, landing(plane.chip(), half), step, landing(plane.chip(step), half))
                )

    def receive_visual():
        for arrival in arrivals[8]:
            arrival.wait_recv()
        pair = 3 * lane
        for at in range(heads // 2):
            v.s_qkv[rows.split :, at * pair : (at + 1) * pair] = v.landing_qkv[at, :, :]
            span = slice(at * lane, (at + 1) * lane)
            queries = v.s_qkv[:, at * pair : at * pair + lane] * jnp.asarray(scale, low)
            v.q_t[span, :] = queries.T
            v.v_t[span, :] = v.s_qkv[:, at * pair + 2 * lane : (at + 1) * pair].T
        v.s_gates_t[...] = jax.nn.sigmoid(v.gate_rows[...].T[:8, :])
        moves.save(v.s_gains, v.gains)
        moves.save(v.s_qkv, v.qkv)
        moves.save(v.s_gates_t, v.gates_t)

    def mix():
        moves.save(v.s_text_t, v.text_t)
        moves.save(v.s_visual_t, v.visual_t)
        moves.save(v.s_logs, v.logs)
        is_text = lax.broadcasted_iota(jnp.int32, (1, rows.count), 1) < rows.split
        for head in range(heads):
            span = slice(head * head_width, (head + 1) * head_width)
            gate = v.s_gates_t[head : head + 1, :]
            to_text = jnp.where(is_text, gate, 1.0 - gate)
            v.s_mix_t[span, :] = (
                to_text * v.s_text_t[span, :] + (1.0 - to_text) * v.s_visual_t[span, :]
            ).astype(low)
        v.mix[...] = v.s_mix_t[...].T
        moves.save(v.s_mix_t, v.mix_t)

    def branch():
        moves.save(v.s_w_out, v.full_out)
        for s, (first, last) in enumerate(rows.spans):

            def columns(piece):
                v.wide[first:last, piece] = dot(v.mix[first:last, :], v.s_w_out[s, :, piece])

            over_columns(0, v.wide.shape[1], 256, columns)
        arrivals[0] = rows.swap_parts(moves, v.wide, v.received)

    def spread_dy():
        arrivals[2] = plane.spread(v.visual_dy.at[0], v.s_dy_v)

    def pass_dy():
        arrivals[3] = plane.pass_on(v.s_dy_v, arrivals[2][1])

    def middle_rows(s, x, ref, start):
        arrivals[0][s].wait_recv()

        def body(piece, packed):
            to = pl.ds(pl.multiple_of(packed.start - start, row_tile), packed.size)
            value = x[to, :].astype(full) + v.wide[piece, :] + v.received[packed, :]
            v.s_middle[packed, :] = value
            ref[to, :] = (normalize(value)[0] * v.s_gains[s, 1:2, :]).astype(low)

        rows.over_own(s, body)
        packed = slice(*rows.packed[s])
        moves.save(v.s_middle.at[packed], v.middle.at[packed])

    def middle_visual():
        middle_rows(1, v.x_v, v.s_hm_v, rows.packed[1][0])
        arrivals[4] = plane.spread(plane.part(v.s_hm_v, 0), v.s_hm_v)

    def middle_text():
        middle_rows(0, v.x, v.s_hm, 0)
        arrivals[1] = rows.swap_own(moves, v.s_hm, 0)

    def pass_hm():
        arrivals[5] = plane.pass_on(v.s_hm_v, arrivals[4][1])

    def up_part(hm, w_up, act_ref, slope_ref, start, stop):
        size = 256 if (stop - start) % 256 == 0 else lane

        def columns(piece):
            act, slope = gelu_both(dot(hm[...], w_up[0, :, piece]))
            act_ref[:, piece] = act.astype(low)
            slope_ref[:, piece] = slope.astype(low)

        over_columns(start, stop, size, columns)

    def up_first():
        moves.save(v.s_w_up, v.full_up)
        arrivals[1].wait_recv()
        loads[2].wait()
        swaps[1].wait_recv()
        moves.save(v.s_hm, v.hm)
        moves.save(v.s_dy, v.dy)
        up_part(v.s_hm, v.s_w_up, v.s_act, v.s_slope, 0, hidden // 2)

    def up_second():
        up_part(v.s_hm, v.s_w_up, v.s_act, v.s_slope, hidden // 2, hidden)
        moves.save(v.s_act, v.act)
        moves.save(v.s_slope, v.slope)

    def up_visual():
        moves.save(v.s_w_up_v, v.full_up_v)
        arrivals[4][0].wait_recv()
        arrivals[5].wait_recv()
        moves.save(v.s_hm_v, v.hm_v)
        up_part(v.s_hm_v, v.s_w_up_v, v.s_act_v, v.s_slope_v, 0, v.s_act_v.shape[1])
        moves.save(v.s_act_v, v.act_v)
        moves.save(v.s_slope_v, v.slope_v)

    def down_part(act, dy, part):
        count = act.shape[1]

        def columns(piece):
            part[0, piece, :] = dot_rows(act[:, piece], dy[...]).astype(low)

        over_columns(0, count, 256 if count % 256 == 0 else lane, columns)

    def down_text():
        down_part(v.s_act, v.s_dy, v.s_part_down)
        moves.save(v.s_part_down, v.part_down)

    def down_visual():
        loads[3].wait()
        arrivals[2][0].wait_recv()
        arrivals[3].wait_recv()
        moves.save(v.s_dy_v, v.dy_v)
        down_part(v.s_act_v, v.s_dy_v, v.s_part_down_v)
        moves.save(v.s_part_down_v, v.part_down_v)

    stages = [prepare, norm, lower_text, project_text, lower_visual, project_visual, receive_visual]
    stages += [functools.partial(attend_head, rows, head_width, v, head) for head in range(heads)]
    stages += [mix, branch, middle_visual, middle_text, pass_hm, up_first, up_second, up_visual]
    stages += [down_text, down_visual, spread_dy, pass_dy, spread_x, pass_x]
    gather.run(plan, stages)
    moves.finish()
    gather.finish()


def front(n_docs, heads, scale, pieces, plan, inputs):
    line_size = n_docs // 4
    count = 2 * (inputs.text.shape[1] + inputs.visual.shape[1])
    dim = inputs.w_out.shape[2]
    width, hidden = inputs.w_qkv.shape[2] // 6, inputs.w_up.shape[2] // 2
    text, plane = 2 * inputs.text.shape[1], 8 * inputs.visual.shape[1]
    wide = 3 * width + lane
    shard = inputs.w_qkv.shape[1]
    kept = FrontKept(
        s_h=((text, dim), low),
        s_h_v=((plane, dim), low),
        s_qkv=((count, 3 * width), low),
        s_gates_t=((8, count), full),
        s_text_t=((width, count), full),
        s_visual_t=((width, count), full),
        s_logs=((16, count), full),
        s_mix_t=((width, count), low),
        s_middle=((count // 2, dim), full),
        s_hm=((text, dim), low),
        s_hm_v=((plane, dim), low),
        s_act=((text, hidden), low),
        s_act_v=((plane, hidden // 4), low),
        s_slope=((text, hidden), low),
        s_slope_v=((plane, hidden // 4), low),
        s_part_down=((1, hidden, dim), low),
        s_part_down_v=((1, hidden // 4, dim), low),
        s_dy=((text, dim), low),
        s_dy_v=((plane, dim), low),
        s_gains=((2, 2, dim), full),
        s_bias=((count, lane), full),
    )
    weights = (
        ((1, dim, wide), low),
        ((1, dim, hidden), low),
        ((2, width, dim), low),
        ((1, hidden, dim), low),
        ((1, dim, hidden // 4), low),
        ((1, hidden // 4, dim), low),
        ((1, dim, 3 * lane), low),
        ((1, dim, lane), low),
    )
    shards = same_as(inputs[:7])
    scratch = FrontScratch(
        shard_qkv=shards[0],
        shard_gate=shards[1],
        shard_up=shards[2],
        shard_attn=shards[3],
        shard_ffn=shards[4],
        shard_text_mask=shards[5],
        shard_visual_mask=shards[6],
        own_qkv=((1, shard, wide), low),
        own_qkv_v=((4, shard, 3 * lane), low),
        own_small_v=((1, shard, lane), low),
        own_up=((1, shard, hidden), low),
        own_up_v=((4, shard, hidden // 4), low),
        s_w_qkv=weights[0],
        s_w_qkv_v=weights[6],
        s_w_small_v=weights[7],
        s_w_up=weights[1],
        s_w_up_v=weights[4],
        s_w_out=weights[2],
        x=((text, dim), low),
        x_v=((plane, dim), low),
        wide=((count, dim), full),
        qkv_v=((plane, 3 * lane), low),
        landing_qkv=((4, 2 * inputs.visual.shape[1], 3 * lane), low),
        received=((count // 2, dim), full),
        gate_rows=((count, lane), full),
        q_t=((width, count), low),
        v_t=((width, count), low),
        mix=((count, width), low),
    )
    results = FrontOut(*weights, *kept)
    values = pl.pallas_call(
        functools.partial(front_kernel, line_size, heads, scale, pieces, plan),
        out_shape=shapes_of(results),
        in_specs=specs_of(len(inputs), 0),
        out_specs=specs_of(len(results), 0),
        scratch_shapes=scratch_of(kept)
        + scratch_of(scratch)
        + sems((len(pieces), 5), (len(pieces), n_docs), len(pieces), 39, 26, 26),
        compiler_params=pltpu.CompilerParams(
            collective_id=0, has_side_effects=True, vmem_limit_bytes=vmem_limit
        ),
        name="gather_and_front",
    )(*inputs)
    return FrontOut(*values)


def scatter_buffers(pieces, arrays, splits, n_docs):
    line_size = n_docs // 4
    group = []
    for piece in pieces:
        ends = line_size // 2 if splits[piece.array] else line_size
        block = (piece.rows, arrays[piece.array][0][2])
        if piece.route == lines_first:
            group += [((ends, *block), low)] * 5
        elif piece.route == line_only:
            group += [((1, row_tile, lane), low)] * 3 + [((ends, 1, *block), low)] * 2
        else:
            group += [((1, *block), low)] * 3 + [((ends, 4, *block), low)] * 2
    return scratch_of(group)


def grouped(refs, size):
    return [refs[first : first + size] for first in range(0, len(refs), size)]


def norm_back(grad, normed, inverse, gain):
    scaled = grad * gain
    return inverse * (
        scaled
        - jnp.mean(scaled, -1, keepdims=True)
        - normed * jnp.mean(scaled * normed, -1, keepdims=True)
    )


class FfnIn(NamedTuple):
    full_down: object
    dy: object
    slope: object
    full_up: object
    part_down: object
    hm: object
    middle: object
    gains: object
    act: object
    full_out: object
    mix_t: object
    text_t: object
    visual_t: object
    gates_t: object
    full_down_v: object
    dy_v: object
    slope_v: object
    full_up_v: object
    part_down_v: object
    hm_v: object
    act_v: object


class FfnLoaded(NamedTuple):
    s_full_down: object
    s_dy: object
    s_slope: object
    s_full_up: object
    s_part_down: object
    s_hm: object
    s_middle: object
    s_gains: object
    s_act: object
    s_full_out: object
    s_mix_t: object
    s_text_t: object
    s_visual_t: object
    s_gates_t: object
    s_full_down_v: object
    s_dy_v: object
    s_slope_v: object
    s_full_up_v: object
    s_part_down_v: object
    s_hm_v: object
    s_act_v: object


class FfnOut(NamedTuple):
    text_out: object
    visual_out: object
    stage_down: object
    part_up: object
    part_up_v: object
    part_out: object
    grad_middle: object
    gain_part: object
    gate_grad_t: object
    text_grad_t: object
    visual_grad_t: object


class FfnScratch(NamedTuple):
    s_part_up: object
    s_part_up_v: object
    s_part_out: object
    s_grad_middle: object
    s_gain_part: object
    s_gate_grad_t: object
    s_text_grad_t: object
    s_visual_grad_t: object
    stage: object
    wide: object
    wide_out: object
    received: object
    received_out: object
    branch: object
    result: object
    mix_grad: object
    mix_grad_t: object
    wide_v: object
    received_v: object
    outgoing_v: object
    landing_v: object
    wide_out_v: object
    received_out_v: object
    outgoing_out_v: object
    landing_out_v: object


def ffn_kernel(line_size, heads, pieces, plan, *refs):
    groups = []
    for group in (FfnIn, FfnOut, FfnLoaded, FfnScratch):
        count = len(group._fields)
        groups.append(group(*refs[:count]))
        refs = refs[count:]
    v = merged(*groups)
    buffers = grouped(refs[: 5 * len(pieces)], 5)
    send_sems, recv_sems, *move_sems = refs[5 * len(pieces) :]
    place = Place(line_size)
    moves = Moves(place, *move_sems)
    rows = Rows(v.text_out.shape[1], v.visual_out.shape[1])
    width = v.mix_t.shape[0]
    head_width = width // heads
    dim = v.hm.shape[1]
    arrivals = {}

    plane = Plane(place, moves, rows.visual)

    def finish_rows(piece, total):
        add_rows(v.stage.at[piece.array], total, piece.first)

    scatter = Scatter(
        place,
        pieces,
        (False, False),
        (v.part_down, v.part_down_v),
        (v.s_part_down, v.s_part_down_v),
        buffers,
        send_sems,
        recv_sems,
        finish_rows,
    )
    place.greet()
    loads = FfnIn(*(moves.local(source, target) for source, target in zip(groups[0], groups[2])))
    place.meet()

    def hidden(dy, w_down, slope):
        count = slope.shape[1]

        def columns(piece):
            grad = dot_back(dy[...], w_down[0, piece, :])
            slope[:, piece] = (grad * slope[:, piece].astype(full)).astype(low)

        over_columns(0, count, 256 if count % 256 == 0 else lane, columns)

    def hidden_visual():
        loads.full_down_v.wait()
        loads.dy_v.wait()
        loads.slope_v.wait()
        hidden(v.s_dy_v, v.s_full_down_v, v.s_slope_v)

    def hidden_text():
        loads.full_down.wait()
        loads.dy.wait()
        loads.slope.wait()
        hidden(v.s_dy, v.s_full_down, v.s_slope)
        loads.part_down.wait()
        loads.part_down_v.wait()

    def back_visual():
        loads.full_up_v.wait()
        v.wide_v[...] = dot_back(v.s_slope_v[...], v.s_full_up_v[0, :, :])
        arrivals[0] = plane.halve(v.wide_v, v.received_v)

    def share_visual():
        arrivals[0].wait_recv()
        arrivals[1] = plane.share(v.wide_v, v.received_v, v.outgoing_v, v.landing_v)

    def back_text():
        loads.full_up.wait()

        def columns(piece):
            v.wide[:, piece] = dot_back(v.s_slope[...], v.s_full_up[0, piece, :])

        over_columns(0, dim, 256, columns)
        arrivals[2] = rows.swap_parts(moves, v.wide, v.received, (0,))[0]

    def up_part(hm, slope, part):
        def columns(piece):
            part[0, piece, :] = dot_rows(hm[:, piece], slope[...]).astype(low)

        over_columns(0, dim, 256, columns)

    def up_text():
        loads.hm.wait()
        up_part(v.s_hm, v.s_slope, v.s_part_up)
        moves.save(v.s_part_up, v.part_up)

    def up_visual():
        loads.hm_v.wait()
        up_part(v.s_hm_v, v.s_slope_v, v.s_part_up_v)
        moves.save(v.s_part_up_v, v.part_up_v)

    def middle_rows(s, piece, packed, grad, dy):
        normed, inverse = normalize(v.s_middle[packed, :])
        v.s_gain_part[s, 0:1, :] += jnp.sum(grad * normed, 0, keepdims=True)
        grad = dy.astype(full) + norm_back(grad, normed, inverse, v.s_gains[s, 1:2, :])
        v.s_grad_middle[packed, :] = grad
        v.branch[piece, :] = grad.astype(low)

    def middle_visual():
        loads.middle.wait()
        loads.gains.wait()
        v.s_gain_part[...] = jnp.zeros_like(v.s_gain_part)
        for arrival in arrivals[1]:
            arrival.wait_recv()
        grad = plane.total(v.wide_v, v.received_v, v.landing_v)
        middle_rows(1, slice(*rows.own[1]), slice(*rows.packed[1]), grad, v.s_dy_v[: rows.visual, :])
        arrivals[3] = rows.swap_own(moves, v.branch, 1)

    def middle_text():
        arrivals[2].wait_recv()

        def body(piece, packed):
            grad = v.wide[piece, :] + v.received[packed, :]
            middle_rows(0, piece, packed, grad, v.s_dy[piece, :])

        rows.over_own(0, body)
        arrivals[4] = rows.swap_own(moves, v.branch, 0)
        moves.save(v.s_gain_part, v.gain_part)
        moves.save(v.s_grad_middle, v.grad_middle)

    def result_text():
        loads.act.wait()

        def columns(piece):
            v.wide_out[:, piece] = dot(v.s_act[...], v.s_full_down[0, :, piece])

        over_columns(0, dim, 256, columns)
        arrivals[5] = rows.swap_parts(moves, v.wide_out, v.received_out, (0,))[0]

    def result_visual():
        loads.act_v.wait()
        v.wide_out_v[...] = dot(v.s_act_v[...], v.s_full_down_v[0, :, :])
        arrivals[6] = plane.halve(v.wide_out_v, v.received_out_v)

    def share_result():
        arrivals[6].wait_recv()
        arrivals[7] = plane.share(v.wide_out_v, v.received_out_v, v.outgoing_out_v, v.landing_out_v)

    def out_part():
        loads.full_out.wait()
        loads.mix_t.wait()
        for s, (first, last) in enumerate(rows.spans):
            arrivals[4 - s].wait_recv()
            v.s_part_out[s, :, :] = dot(v.s_mix_t[:, first:last], v.branch[first:last, :]).astype(low)
            v.mix_grad[first:last, :] = dot_back(v.branch[first:last, :], v.s_full_out[s, :, :])
        moves.save(v.s_part_out, v.part_out)

    def gates():
        loads.text_t.wait()
        loads.visual_t.wait()
        loads.gates_t.wait()
        v.mix_grad_t[...] = v.mix_grad[...].T
        is_text = lax.broadcasted_iota(jnp.int32, (1, rows.count), 1) < rows.split
        for head in range(heads):
            span = slice(head * head_width, (head + 1) * head_width)
            gate = v.s_gates_t[head : head + 1, :]
            to_text = jnp.where(is_text, gate, 1.0 - gate)
            grad = v.mix_grad_t[span, :]
            toward = jnp.sum(grad * (v.s_text_t[span, :] - v.s_visual_t[span, :]), 0, keepdims=True)
            v.s_gate_grad_t[head : head + 1, :] = (
                jnp.where(is_text, toward, -toward) * gate * (1.0 - gate)
            )
            v.s_text_grad_t[span, :] = (to_text * grad).astype(low)
            v.s_visual_grad_t[span, :] = ((1.0 - to_text) * grad).astype(low)
        v.s_gate_grad_t[heads:, :] = jnp.zeros((8 - heads, rows.count), full)
        moves.save(v.s_gate_grad_t, v.gate_grad_t)
        moves.save(v.s_text_grad_t, v.text_grad_t)
        moves.save(v.s_visual_grad_t, v.visual_grad_t)

    def finish_text():
        arrivals[5].wait_recv()

        def body(piece, packed):
            v.result[packed, :] = (
                v.s_middle[packed, :] + v.wide_out[piece, :] + v.received_out[packed, :]
            ).astype(low)

        rows.over_own(0, body)
        moves.save(v.result.at[slice(*rows.packed[0])], v.text_out.at[0])

    def finish_visual():
        for arrival in arrivals[7]:
            arrival.wait_recv()
        packed = slice(*rows.packed[1])
        total = plane.total(v.wide_out_v, v.received_out_v, v.landing_out_v)
        v.result[packed, :] = (v.s_middle[packed, :] + total).astype(low)
        moves.save(v.result.at[packed], v.visual_out.at[0])

    stages = [hidden_visual, back_visual, hidden_text, share_visual, back_text, up_text, up_visual]
    stages += [middle_visual, middle_text, result_text, result_visual, out_part, gates, share_result]
    scatter.run(plan, stages + [finish_text, finish_visual])
    moves.save(v.stage, v.stage_down)
    moves.finish()
    scatter.finish()


def ffn_back(n_docs, heads, pieces, plan, text, visual, inputs):
    line_size = n_docs // 4
    hidden = inputs.act.shape[1]
    width, count = inputs.mix_t.shape
    dim = inputs.hm.shape[1]
    rows = inputs.part_down.shape[1] // n_docs
    plane = 8 * visual.shape[1]
    scratch = FfnScratch(
        s_part_up=((1, dim, hidden), low),
        s_part_up_v=((1, dim, hidden // 4), low),
        s_part_out=((2, width, dim), low),
        s_grad_middle=((count // 2, dim), full),
        s_gain_part=((2, 8, dim), full),
        s_gate_grad_t=((8, count), full),
        s_text_grad_t=((width, count), low),
        s_visual_grad_t=((width, count), low),
        stage=((2, rows, dim), full),
        wide=((2 * text.shape[1], dim), full),
        wide_out=((2 * text.shape[1], dim), full),
        received=((text.shape[1], dim), full),
        received_out=((text.shape[1], dim), full),
        branch=((count, dim), low),
        result=((count // 2, dim), low),
        mix_grad=((count, width), full),
        mix_grad_t=((width, count), full),
        wide_v=((plane, dim), full),
        received_v=((plane // 2, dim), full),
        outgoing_v=((3 * plane // 8, dim), low),
        landing_v=((3 * plane // 8, dim), low),
        wide_out_v=((plane, dim), full),
        received_out_v=((plane // 2, dim), full),
        outgoing_out_v=((3 * plane // 8, dim), low),
        landing_out_v=((3 * plane // 8, dim), low),
    )
    results = FfnOut(
        (text.shape, low), (visual.shape, low), scratch.stage, *scratch[:8]
    )
    loaded = same_as(inputs)
    values = pl.pallas_call(
        functools.partial(ffn_kernel, line_size, heads, pieces, plan),
        out_shape=shapes_of(results),
        in_specs=specs_of(len(inputs), 0),
        out_specs=specs_of(len(results), 0),
        scratch_shapes=scratch_of(loaded)
        + scratch_of(scratch)
        + scatter_buffers(pieces, same_as([inputs.part_down, inputs.part_down_v]), (False, False), n_docs)
        + sems(len(pieces), arrival_offsets(pieces, line_size)[-1], 32, 12, 12),
        compiler_params=pltpu.CompilerParams(
            collective_id=1, has_side_effects=True, vmem_limit_bytes=vmem_limit
        ),
        name="ffn_back_and_scatter",
    )(*inputs)
    return FfnOut(*values)


class AttentionIn(NamedTuple):
    qkv: object
    logs: object
    text_t: object
    visual_t: object
    text_grad_t: object
    visual_grad_t: object
    bias: object
    part_up: object
    part_up_v: object
    part_out: object
    gate_grad_t: object
    full_qkv: object
    full_qkv_v: object
    full_small_v: object
    h: object
    h_v: object
    grad_middle: object
    gains: object
    gain_part: object
    stage_down: object
    text: object
    visual: object


class AttentionLoaded(NamedTuple):
    s_qkv: object
    s_logs: object
    s_text_t: object
    s_visual_t: object
    s_text_grad_t: object
    s_visual_grad_t: object
    s_bias: object
    s_part_up: object
    s_part_up_v: object
    s_part_out: object
    s_gate_grad_t: object
    s_full_qkv: object
    s_full_qkv_v: object
    s_full_small_v: object
    s_h: object
    s_h_v: object
    s_grad_middle: object
    s_gains: object
    s_gain_part: object
    s_stage_down: object


class AttentionOut(NamedTuple):
    text_grad: object
    visual_grad: object
    grad_down: object
    grad_qkv: object
    grad_gate: object
    grad_up: object
    grad_out: object
    grad_gain_attn: object
    grad_gain_ffn: object


class AttentionScratch(NamedTuple):
    part_qkv: object
    part_qkv_v: object
    part_small: object
    x: object
    q_t: object
    k_t: object
    query_grad_t: object
    text_grad_n: object
    visual_grad_n: object
    key_sum: object
    value_sum: object
    grad_wide: object
    wide: object
    received: object
    grad_v: object
    wide_v: object
    received_v: object
    outgoing_v: object
    landing_v: object
    gain_sum: object
    gains_row: object
    stage_up: object
    stage_out: object
    stage_qkv: object
    stage_up_v: object
    stage_qkv_v: object
    stage_small: object
    own_qkv: object
    peer_up: object
    peer_up_v: object
    peer_small: object
    s_grad_up: object
    s_grad_gate: object
    s_grad_gain_attn: object
    s_grad_gain_ffn: object


def attend_head_back(rows, head_width, scale, v, number):
    pair = 2 * head_width
    at, odd = number // 2, number % 2
    columns = [slice((3 * at + third) * pair, (3 * at + third + 1) * pair) for third in range(3)]
    wide = slice(at * pair, (at + 1) * pair)
    keys, values = v.s_qkv[:, columns[1]], v.s_qkv[:, columns[2]]
    if not odd:
        v.key_sum[...] = jnp.zeros_like(v.key_sum)
        v.value_sum[...] = jnp.zeros_like(v.value_sum)
    mine = lax.broadcasted_iota(jnp.int32, (1, pair), 1) // head_width == odd
    bias = v.s_bias[:, 0:1]
    sets = (
        (v.s_text_t, v.s_text_grad_t, v.text_grad_n),
        (v.s_visual_t, v.s_visual_grad_t, v.visual_grad_n),
    )
    head = slice(number * head_width, (number + 1) * head_width)
    for first, last in query_spans(rows.count):
        scores = dot(keys, head_wide(v.q_t[head, first:last], odd)) + bias
        queries = jnp.where(mine, v.s_qkv[first:last, columns[0]] * jnp.asarray(scale, low), 0)
        pieces = []
        for t, (output_t, grad_t, grad) in enumerate(sets):
            start, stop = rows.spans[t]
            out_grad = grad_t[head, first:last]
            delta = jnp.sum(out_grad.astype(full) * output_t[head, first:last], 0, keepdims=True)
            row = 8 * t + number
            probs = jnp.exp(scores[start:stop] - v.s_logs[row : row + 1, first:last])
            grad_probs = dot(values[start:stop], head_wide(out_grad, odd))
            grad_scores = (probs * (grad_probs - delta)).astype(low)
            natural = jnp.where(mine, grad[first:last, wide], 0)
            v.value_sum[start:stop, :] += dot(probs.astype(low), natural)
            v.key_sum[start:stop, :] += dot(grad_scores, queries)
            pieces.append(grad_scores)
        v.query_grad_t[head, first:last] = (
            dot(v.k_t[head, :], jnp.concatenate(pieces, 0)) * scale
        ).astype(low)
    if odd:
        v.grad_wide[:, columns[0]] = v.query_grad_t[wide, :].T
        v.grad_wide[:, columns[1]] = v.key_sum[...].astype(low)
        v.grad_wide[:, columns[2]] = v.value_sum[...].astype(low)


def attention_kernel(line_size, heads, scale, block, pieces, plan, *refs):
    groups = []
    for group in (AttentionIn, AttentionOut, AttentionLoaded, AttentionScratch):
        count = len(group._fields)
        groups.append(group(*refs[:count]))
        refs = refs[count:]
    v = merged(*groups)
    buffers = grouped(refs[: 5 * len(pieces)], 5)
    send_sems, recv_sems, *move_sems = refs[5 * len(pieces) :]
    place = Place(line_size)
    core = place.core
    moves = Moves(place, *move_sems)
    rows = Rows(v.text.shape[1], v.visual.shape[1])
    width = v.qkv.shape[1] // 3
    head_width = width // heads
    dim = v.h.shape[1]
    stages_of = (v.stage_up, v.stage_out, v.stage_qkv, v.stage_up_v, v.stage_qkv_v, v.stage_small)
    arrivals = {}
    plane = Plane(place, moves, rows.visual)

    def finish_rows(piece, total, quad=quads[0]):
        part = place.index(0, *quad) if piece.route == plane_shared else piece.part
        add_rows(stages_of[piece.array].at[part], total, piece.first)

    scatter = Scatter(
        place,
        pieces,
        (False, True, False, False, False, False),
        (v.part_up, v.part_out, v.part_qkv, v.part_up_v, v.part_qkv_v, v.part_small),
        (v.s_part_up, v.s_part_out, v.part_qkv, v.s_part_up_v, v.part_qkv_v, v.part_small),
        buffers,
        send_sems,
        recv_sems,
        finish_rows,
    )
    place.greet()
    loads = AttentionIn(
        *(moves.local(source, target) for source, target in zip(groups[0], groups[2])),
        *(moves.local(ref.at[0], v.x.at[slice(*rows.packed[s])]) for s, ref in enumerate((v.text, v.visual))),
    )
    place.meet()

    def prepare():
        for load in loads[:7]:
            load.wait()
        for at in range(heads // 2):
            span, first = slice(at * lane, (at + 1) * lane), 3 * at * lane
            v.q_t[span, :] = (v.s_qkv[:, first : first + lane] * jnp.asarray(scale, low)).T
            v.k_t[span, :] = v.s_qkv[:, first + lane : first + 2 * lane].T
        v.text_grad_n[...] = v.s_text_grad_t[...].T
        v.visual_grad_n[...] = v.s_visual_grad_t[...].T
        loads.part_up.wait()
        loads.part_up_v.wait()
        loads.part_out.wait()

    def send_visual():
        loads.gate_grad_t.wait()
        empty = jnp.zeros((lane - 8, rows.count), full)
        v.grad_wide[:, 3 * width : 3 * width + lane] = (
            jnp.concatenate([v.s_gate_grad_t[...], empty], 0).T.astype(low)
        )
        v.grad_wide[:, 3 * width + lane :] = jnp.zeros((rows.count, 2 * lane), low)
        arrivals[4] = []
        pair = 3 * lane
        for half, piece in enumerate(plane.document(0)):
            first = rows.split + half * rows.visual
            span = slice(first, first + rows.visual)
            of = lambda step: v.grad_wide.at[span, pl.ds(pl.multiple_of(plane.chip(step) * pair, lane), pair)]
            arrivals[4].append(moves.local(of(None), v.grad_v.at[piece]).wait)
            for at, step in enumerate(plane.steps):
                target = v.grad_v.at[plane.document(1 + at)[half]]
                arrivals[4].append(moves.peer(of(step), target, step).wait_recv)

    def back_text():
        loads.full_qkv.wait()

        def columns(piece):
            grad = v.grad_wide[: rows.split, : 3 * width + lane]
            v.wide[:, piece] = dot_back(grad, v.s_full_qkv[0, piece, :])

        over_columns(0, dim, 256, columns)
        arrivals[0] = rows.swap_parts(moves, v.wide, v.received, (0,))[0]

    def text_part():
        loads.h.wait()

        def columns(piece):
            grad = dot_rows(v.s_h[:, piece], v.grad_wide[: rows.split, : 3 * width + lane])
            v.part_qkv[0, piece, :] = grad[:, : 3 * width].astype(low)
            v.gain_sum[0, piece, :] = grad[:, 3 * width :]

        over_columns(0, dim, 256, columns)

    def back_visual():
        loads.full_qkv_v.wait()
        loads.full_small_v.wait()
        for wait in arrivals[4]:
            wait()
        v.wide_v[...] = dot_back(v.grad_v[...], v.s_full_qkv_v[0, :, :])
        for half, piece in enumerate(plane.document(0)):
            first = rows.split + half * rows.visual
            small = v.grad_wide[first : first + rows.visual, 3 * width : 3 * width + lane]
            v.wide_v[piece, :] += dot_back(small, v.s_full_small_v[0, :, :])
        arrivals[5] = plane.halve(v.wide_v, v.received_v)

    def visual_part():
        loads.h_v.wait()

        def columns(piece):
            v.part_qkv_v[0, piece, :] = dot_rows(v.s_h_v[:, piece], v.grad_v[...]).astype(low)

        over_columns(0, dim, 256, columns)
        total = 0.0
        for half, piece in enumerate(plane.document(0)):
            first = rows.split + half * rows.visual
            small = v.grad_wide[first : first + rows.visual, 3 * width : 3 * width + lane]
            total = total + dot_rows(v.s_h_v[piece, :], small)
        v.gain_sum[1, :, :] = total

    def share_visual():
        arrivals[5].wait_recv()
        arrivals[6] = plane.share(v.wide_v, v.received_v, v.outgoing_v, v.landing_v)

    def token_rows(s, packed, grad):
        normed, inverse = normalize(v.x[packed, :].astype(full))
        v.gains_row[s, heads : heads + 1, :] += jnp.sum(grad * normed, 0, keepdims=True)
        v.s_grad_middle[packed, :] += norm_back(grad, normed, inverse, v.s_gains[s, 0:1, :])

    def small_part(s):
        small = v.gain_sum[s, :, :] + v.gains_row[s, :, :].T
        v.part_small[s, :, :] = small.astype(low)
        ref = (v.text_grad, v.visual_grad)[s]
        moves.save(v.s_grad_middle.at[slice(*rows.packed[s])], ref.at[0])

    def tokens_text():
        loads.grad_middle.wait()
        loads.gains.wait()
        loads.gain_part.wait()
        v.gains_row[...] = jnp.zeros_like(v.gains_row)
        for s in range(2):
            loads[-2 + s].wait()
            v.gains_row[s, heads + 1 : heads + 2, :] = v.s_gain_part[s, 0:1, :]
        arrivals[0].wait_recv()

        def body(piece, packed):
            token_rows(0, packed, v.wide[piece, :] + v.received[packed, :])

        rows.over_own(0, body)
        small_part(0)

    def tokens_visual():
        for arrival in arrivals[6]:
            arrival.wait_recv()
        grad = plane.total(v.wide_v, v.received_v, v.landing_v)
        token_rows(1, slice(*rows.packed[1]), grad)
        small_part(1)

    def share_down():
        loads.stage_down.wait()
        block = v.s_stage_down.shape[1]
        mine = lambda of: v.grad_down.at[:, pl.ds(pl.multiple_of(of * block, row_tile), block), :]
        moves.save(v.s_stage_down, mine(core))
        arrivals[3] = moves.across(v.s_stage_down, mine(core), mine(1 - core))

    def share_up():
        arrivals[1] = moves.across(v.stage_up, v.peer_up)
        arrivals[2] = moves.across(v.stage_up_v, v.peer_up_v)

    def share_out():
        owner = place.z // (line_size // 2) == core
        moves_out = (
            pltpu.make_async_copy(v.stage_out, v.grad_out, moves.local_sems.at[moves.locals]),
            pltpu.make_async_remote_copy(
                src_ref=v.stage_out,
                dst_ref=v.grad_out,
                send_sem=moves.send_sems.at[moves.remotes],
                recv_sem=moves.recv_sems.at[moves.remotes],
                device_id=moves.other,
                device_id_type=MESH,
            ),
        )
        moves.locals += 1
        moves.remotes += 1

        def start():
            for move in moves_out:
                move.start()

        def wait():
            moves_out[0].wait()
            moves_out[1].wait_send()

        pl.when(owner)(start)
        moves.to_end.append(lambda: pl.when(owner)(wait))
        moves.to_end.append(lambda: pl.when(jnp.logical_not(owner))(lambda: moves_out[1].wait_recv()))

    def finish_up():
        arrivals[1].wait_recv()
        arrivals[2].wait_recv()
        first = core == 0
        count = v.stage_up.shape[2] // block
        for s in range(2):
            pieces = []
            for at in range(count):
                if s == 0:
                    span = slice(at * block, (at + 1) * block)
                    own, peer = (ref[0, :, span] for ref in (v.stage_up, v.peer_up))
                else:
                    span = slice(at // 4 * block, (at // 4 + 1) * block)
                    own, peer = (ref[at % 4, :, span] for ref in (v.stage_up_v, v.peer_up_v))
                pieces += [jnp.where(first, own, peer), jnp.where(first, peer, own)]
            v.s_grad_up[s, :, :] = jnp.concatenate(pieces, 1)
        moves.save(v.s_grad_up, v.grad_up)

    stages = [prepare]
    stages += [functools.partial(attend_head_back, rows, head_width, scale, v, head) for head in range(heads)]
    stages += [send_visual, back_text, text_part, back_visual, visual_part, share_visual]
    stages += [tokens_text, tokens_visual, share_up, share_out, finish_up, share_down]
    scatter.run(plan, stages)

    def mine(third, of):
        first = third * 2 * width + of * width
        return v.grad_qkv.at[:, :, pl.ds(pl.multiple_of(first, lane), width)]

    last = [moves.across(v.stage_small, v.peer_small)]
    for third in range(3):
        for at in range(heads // 2):
            to = slice(at * lane, (at + 1) * lane)
            v.own_qkv[third, 0, :, to] = v.stage_qkv[0, :, (3 * at + third) * lane : (3 * at + third + 1) * lane]
            v.own_qkv[third, 1, :, to] = v.stage_qkv_v[at, :, third * lane : (third + 1) * lane]
        source = v.own_qkv.at[third]
        moves.save(source, mine(third, core))
        last.append(moves.across(source, mine(third, core), mine(third, 1 - core)))
    last[0].wait_recv()
    for s in range(2):
        own, peer = v.stage_small[s, :, :], v.peer_small[s, :, :]
        columns = own.shape[0]
        empty = jnp.zeros((lane - columns, lane), full)
        own, peer = (jnp.concatenate([value, empty], 0).T[:, :columns] for value in (own, peer))
        v.s_grad_gate[:heads, s, :] = jnp.where(core == 0, own, peer)[:heads]
        v.s_grad_gate[heads:, s, :] = jnp.where(core == 0, peer, own)[:heads]
        both = own + peer
        v.s_grad_gain_attn[s : s + 1, :] = both[heads : heads + 1]
        v.s_grad_gain_ffn[s : s + 1, :] = both[heads + 1 : heads + 2]
    moves.save(v.s_grad_gate, v.grad_gate)
    moves.save(v.s_grad_gain_attn, v.grad_gain_attn)
    moves.save(v.s_grad_gain_ffn, v.grad_gain_ffn)
    for arrival in last[1:] + [arrivals[3]]:
        arrival.wait_recv()
    moves.finish()
    scatter.finish()


def attention_back(n_docs, heads, scale, pieces, plan, inputs):
    line_size = n_docs // 4
    count, dim = inputs.qkv.shape[0], inputs.h.shape[1]
    width = inputs.qkv.shape[1] // 3
    text, visual = inputs.text.shape[1], inputs.visual.shape[1]
    hidden = inputs.part_up.shape[2]
    rows = dim // n_docs
    block = hidden // n_docs
    splits = (False, True, False, False, False, False)
    parts = (((1, dim, 3 * width), low), ((1, dim, 3 * lane), low), ((2, dim, lane), low))
    arrays = same_as([inputs.part_up, inputs.part_out]) + [parts[0]] + same_as([inputs.part_up_v])
    arrays += parts[1:]
    results = AttentionOut(
        text_grad=(inputs.text.shape, full),
        visual_grad=(inputs.visual.shape, full),
        grad_down=((2, 2 * inputs.stage_down.shape[1], dim), full),
        grad_qkv=((2, rows, 6 * width), full),
        grad_gate=((2 * heads, 2, rows), full),
        grad_up=((2, rows, 2 * hidden), full),
        grad_out=((2, rows, dim), full),
        grad_gain_attn=((2, rows), full),
        grad_gain_ffn=((2, rows), full),
    )
    scratch = AttentionScratch(
        part_qkv=parts[0],
        part_qkv_v=parts[1],
        part_small=parts[2],
        x=((count // 2, dim), low),
        q_t=((width, count), low),
        k_t=((width, count), low),
        query_grad_t=((width, count), low),
        text_grad_n=((count, width), low),
        visual_grad_n=((count, width), low),
        key_sum=((count, lane), full),
        value_sum=((count, lane), full),
        grad_wide=((count, 3 * width + 3 * lane), low),
        wide=((2 * text, dim), full),
        received=((text, dim), full),
        grad_v=((8 * visual, 3 * lane), low),
        wide_v=((8 * visual, dim), full),
        received_v=((4 * visual, dim), full),
        outgoing_v=((3 * visual, dim), low),
        landing_v=((3 * visual, dim), low),
        gain_sum=((2, dim, lane), full),
        gains_row=((2, lane, dim), full),
        stage_up=((1, rows, hidden), full),
        stage_out=((2, rows, dim), full),
        stage_qkv=((1, rows, 3 * width), full),
        stage_up_v=((4, rows, hidden // 4), full),
        stage_qkv_v=((4, rows, 3 * lane), full),
        stage_small=((2, rows, lane), full),
        own_qkv=((3, 2, rows, width), full),
        peer_up=((1, rows, hidden), full),
        peer_up_v=((4, rows, hidden // 4), full),
        peer_small=((2, rows, lane), full),
        s_grad_up=results.grad_up,
        s_grad_gate=results.grad_gate,
        s_grad_gain_attn=results.grad_gain_attn,
        s_grad_gain_ffn=results.grad_gain_ffn,
    )
    loaded = same_as(inputs[:-2])
    values = pl.pallas_call(
        functools.partial(attention_kernel, line_size, heads, scale, block, pieces, plan),
        out_shape=shapes_of(results),
        in_specs=specs_of(len(inputs), 0),
        out_specs=specs_of(len(results), 0),
        scratch_shapes=scratch_of(loaded)
        + scratch_of(scratch)
        + scatter_buffers(pieces, arrays, splits, n_docs)
        + sems(len(pieces), arrival_offsets(pieces, line_size)[-1], 35, 19, 19),
        compiler_params=pltpu.CompilerParams(
            collective_id=2, has_side_effects=True, vmem_limit_bytes=vmem_limit
        ),
        name="attention_back_and_scatter",
    )(*inputs)
    return AttentionOut(*values)


def publish_kernel(count, *refs):
    sources, results, held = refs[:count], refs[count : 2 * count], refs[2 * count : 3 * count]
    arriving, leaving = refs[3 * count :]
    copies_in = [pltpu.make_async_copy(sources[at], held[at], arriving.at[at]) for at in range(count)]
    copies_out = [pltpu.make_async_copy(held[at], results[at], leaving.at[at]) for at in range(count)]
    for copy in copies_in:
        copy.start()
    for copy_in, copy_out in zip(copies_in, copies_out):
        copy_in.wait()
        copy_out.start()
    for copy in copies_out:
        copy.wait()


def publish(arrays):
    count = len(arrays)
    return pl.pallas_call(
        functools.partial(publish_kernel, count),
        out_shape=shapes_of(same_as(arrays)),
        in_specs=specs_of(count, 0),
        out_specs=specs_of(count, 0),
        scratch_shapes=scratch_of(same_as(arrays)) + sems(count, count),
        compiler_params=pltpu.CompilerParams(vmem_limit_bytes=vmem_limit),
        name="publish",
    )(*arrays)


def kernel_path(n_docs, heads, scale, inputs):
    made = [tuple(Piece(*each) for each in pieces) for pieces in (front_pieces, ffn_pieces, attention_pieces)]
    first = front(n_docs, heads, scale, made[0], front_plan, inputs)
    ffn_inputs = FfnIn(*(getattr(first, name) for name in FfnIn._fields))
    second = ffn_back(n_docs, heads, made[1], ffn_plan, inputs.text, inputs.visual, ffn_inputs)
    known = merged(inputs, first, second)
    attention_inputs = AttentionIn(*(getattr(known, name) for name in AttentionIn._fields))
    third = attention_back(n_docs, heads, scale, made[2], attention_plan, attention_inputs)
    results = (
        second.text_out,
        second.visual_out,
        third.text_grad,
        third.visual_grad,
        third.grad_qkv,
        third.grad_out,
        third.grad_gate,
        third.grad_up,
        third.grad_down,
        third.grad_gain_attn,
        third.grad_gain_ffn,
    )
    results = publish(results)
    return (*results[:6], jnp.transpose(results[6], (1, 2, 0)), *results[7:])


def swap(value):
    return lax.ppermute(value, core_axis, [(0, 1), (1, 0)])


def both(own):
    return jnp.concatenate([own, swap(own)], 0)


def own_sum(partial):
    rows = partial.shape[0] // 2
    return partial[:rows] + swap(partial[rows:])


def normalize_back(gradient, normed, inverse, gain):
    scaled = gradient * gain
    grad_gain = jnp.sum(gradient * normed, 0)
    grad_input = inverse * (
        scaled
        - jnp.mean(scaled, -1, keepdims=True)
        - normed * jnp.mean(scaled * normed, -1, keepdims=True)
    )
    return grad_input, grad_gain


def heads_of(values, heads):
    return values.reshape(values.shape[0], heads, -1)


def attend(queries, keys, values, valid, scale):
    scores = jnp.einsum("qhe,khe->hqk", queries, keys, preferred_element_type=full) * scale
    scores = jnp.where(valid, scores, big_negative)
    top = jnp.max(scores, -1)
    probs = jnp.where(valid, jnp.exp(scores - top[..., None]), 0.0)
    total = jnp.sum(probs, -1)
    weighted = jnp.einsum(
        "hqk,khe->qhe", probs.astype(low), values, preferred_element_type=full
    )
    return weighted / total.T[..., None], top + jnp.log(total)


def attend_back(queries, keys, values, valid, scale, log_total, grad_output, output):
    delta = jnp.sum(grad_output.astype(full) * output, -1).T
    scores = jnp.einsum("qhe,khe->hqk", queries, keys, preferred_element_type=full) * scale
    probs = jnp.where(valid, jnp.exp(scores - log_total[..., None]), 0.0)
    grad_values = jnp.einsum(
        "hqk,qhe->khe", probs.astype(low), grad_output, preferred_element_type=full
    )
    grad_probs = jnp.einsum("qhe,khe->hqk", grad_output, values, preferred_element_type=full)
    grad_scores = (probs * (grad_probs - delta[..., None])).astype(low)
    grad_queries = (
        jnp.einsum("hqk,khe->qhe", grad_scores, keys, preferred_element_type=full) * scale
    )
    grad_keys = (
        jnp.einsum("hqk,qhe->khe", grad_scores, queries, preferred_element_type=full) * scale
    )
    return grad_queries, grad_keys, grad_values


def on_device(
    n_docs,
    text_tokens,
    visual_tokens,
    text_mask,
    visual_mask,
    w_qkv,
    w_out,
    w_gate,
    w_up,
    w_down,
    gain_attn,
    gain_ffn,
    text_cotangent,
    visual_cotangent,
):
    core = lax.axis_index(core_axis)
    width = w_out.shape[2]
    all_heads = w_gate.shape[2]
    heads = all_heads // 2
    half = width // 2
    scale = (width // all_heads) ** (-0.5)
    if n_docs == 16 and w_qkv.shape[1] % row_tile == 0:
        inputs = FrontIn(
            w_qkv=w_qkv,
            w_gate=jnp.transpose(w_gate, (2, 0, 1)),
            w_up=w_up,
            gain_attn=gain_attn,
            gain_ffn=gain_ffn,
            text_mask=text_mask,
            visual_mask=visual_mask,
            text=text_tokens,
            visual=visual_tokens,
            text_dy=text_cotangent,
            visual_dy=visual_cotangent,
            w_out=w_out,
            w_down=w_down,
        )
        return kernel_path(n_docs, heads, scale, inputs)

    def own_columns(array, size, start=0):
        return lax.dynamic_slice_in_dim(array, start + core * size, size, 2)

    own_tokens = (text_tokens[0], visual_tokens[0])
    own_grads = (text_cotangent[0], visual_cotangent[0])

    def reorder(mask):
        rows = mask.shape[1] // 2
        return (
            jnp.concatenate(
                [
                    lax.dynamic_slice_in_dim(mask[0], core * rows, rows),
                    lax.dynamic_slice_in_dim(mask[0], (1 - core) * rows, rows),
                ]
            )
            > 0
        )

    valids = (reorder(text_mask), reorder(visual_mask))

    pad = lane - heads - 2
    shard = jnp.concatenate(
        [own_columns(w_qkv, half, column * width) for column in range(3)]
        + [
            own_columns(w_gate, heads),
            gain_attn[..., None],
            gain_ffn[..., None],
            jnp.zeros(w_gate.shape[:2] + (pad,), low),
        ],
        2,
    )
    tokens = tuple(both(value) for value in own_tokens)
    grads_out = tuple(both(value) for value in own_grads)
    gather = lambda array: lax.all_gather(array, docs_axis, axis=1, tiled=True)
    rows_half = lambda array: lax.dynamic_slice_in_dim(
        array, core * (array.shape[1] // 2), array.shape[1] // 2, 1
    )
    full_qkv = gather(shard)
    full_up = gather(own_columns(w_up, w_up.shape[2] // 2))
    full_out, full_down = rows_half(gather(w_out)), rows_half(gather(w_down))
    gains_attn = full_qkv[:, :, 3 * half + heads].astype(full)
    gains_ffn = full_qkv[:, :, 3 * half + heads + 1].astype(full)

    fronts = []
    for s in range(2):
        normed, inverse = normalize(tokens[s].astype(full))
        lowered = (normed * gains_attn[s]).astype(low)
        wide = dot(lowered, full_qkv[s])
        narrow = wide[:, : 3 * half].astype(low)
        gates = jax.nn.sigmoid(wide[:, 3 * half : 3 * half + heads])
        queries, keys, values = (
            heads_of(narrow[:, column * half : (column + 1) * half], heads) for column in range(3)
        )
        fronts.append((normed, inverse, lowered, gates, queries, keys, values))

    outputs, totals = {}, {}
    for s in range(2):
        for t in range(2):
            outputs[s, t], totals[s, t] = attend(
                fronts[s][4], fronts[t][5], fronts[t][6], valids[t], scale
            )

    results, tails = [], []
    for s in range(2):
        gates = fronts[s][3][..., None]
        own, cross = outputs[s, s], outputs[s, 1 - s]
        mixed = gates * own + (1.0 - gates) * cross
        mix = mixed.reshape(mixed.shape[0], -1).astype(low)
        middle = own_tokens[s].astype(full) + own_sum(dot(mix, full_out[s]))
        normed, inverse = normalize(middle)
        lowered = both((normed * gains_ffn[s]).astype(low))
        upward = dot(lowered, full_up[s])
        activated, gelu_back = jax.vjp(jax.nn.gelu, upward)
        act = activated.astype(low)
        results.append((middle + own_sum(dot(act, full_down[s]))).astype(low))
        part_down = dot_rows(act, grads_out[s]).astype(low)
        grad_up = gelu_back(dot_back(grads_out[s], full_down[s]))[0].astype(low)
        part_up = dot_rows(lowered, grad_up).astype(low)
        grad_in, part_gain = normalize_back(
            own_sum(dot_back(grad_up, full_up[s])), normed, inverse, gains_ffn[s]
        )
        grad_middle = own_grads[s].astype(full) + grad_in
        grad_branch = both(grad_middle.astype(low))
        part_out = dot_rows(mix, grad_branch).astype(low)
        grad_mix = heads_of(dot_back(grad_branch, full_out[s]), heads)
        grad_gate = (
            jnp.sum(grad_mix * (own - cross), -1) * fronts[s][3] * (1.0 - fronts[s][3])
        ).astype(low)
        grad_own = (gates * grad_mix).astype(low)
        grad_cross = ((1.0 - gates) * grad_mix).astype(low)
        tails.append(
            (grad_middle, grad_gate, grad_own, grad_cross, part_out, part_up, part_down, part_gain)
        )

    backs = {}
    for s in range(2):
        for t in range(2):
            backs[s, t] = attend_back(
                fronts[s][4],
                fronts[t][5],
                fronts[t][6],
                valids[t],
                scale,
                totals[s, t],
                tails[s][2 if s == t else 3],
                outputs[s, t],
            )

    token_grads, parts_qkv = [], []
    for s in range(2):
        normed, inverse, lowered = fronts[s][:3]
        rows = lowered.shape[0]
        grad_q = backs[s, s][0] + backs[s, 1 - s][0]
        grad_k = backs[s, s][1] + backs[1 - s, s][1]
        grad_v = backs[s, s][2] + backs[1 - s, s][2]
        grad_wide = jnp.concatenate(
            [grad.reshape(rows, -1).astype(low) for grad in (grad_q, grad_k, grad_v)]
            + [tails[s][1], jnp.zeros((rows, lane - heads), low)],
            1,
        )
        part = dot_rows(lowered, grad_wide)
        own_rows = rows // 2
        grad_in, part_gain = normalize_back(
            own_sum(dot_back(grad_wide, full_qkv[s])),
            normed[:own_rows],
            inverse[:own_rows],
            gains_attn[s],
        )
        token_grads.append((tails[s][0] + grad_in)[None])
        parts_qkv.append(
            jnp.concatenate(
                [
                    part[:, : 3 * half + heads],
                    part_gain[:, None],
                    tails[s][7][:, None],
                    part[:, 3 * half + heads + 2 :],
                ],
                1,
            ).astype(low)
        )
    part_qkv = jnp.stack(parts_qkv)
    part_out, part_up, part_down = (
        jnp.stack([tails[0][at], tails[1][at]]) for at in (4, 5, 6)
    )
    scatter = lambda array: lax.psum_scatter(
        array.astype(full), docs_axis, scatter_dimension=1, tiled=True
    )

    def columns(own):
        other = swap(own)
        first = jnp.where(core == 0, own, other)
        second = jnp.where(core == 0, other, own)
        return first, second

    def rows_both(part):
        empty = jnp.zeros_like(part)
        first = jnp.where(core == 0, part, empty)
        second = jnp.where(core == 0, empty, part)
        return lax.psum(scatter(jnp.concatenate([first, second], 1)), core_axis)

    qkv_first, qkv_second = columns(scatter(part_qkv))
    grad_qkv = jnp.concatenate(
        [
            piece[:, :, column * half : (column + 1) * half]
            for column in range(3)
            for piece in (qkv_first, qkv_second)
        ],
        2,
    )
    small = jnp.stack([qkv_first[:, :, 3 * half :], qkv_second[:, :, 3 * half :]])
    grad_up = jnp.concatenate(columns(scatter(part_up)), 2)
    grad_out, grad_down = rows_both(part_out), rows_both(part_down)
    grad_gate = jnp.concatenate([small[0, :, :, :heads], small[1, :, :, :heads]], 2)
    gains = small[0] + small[1]
    return (
        results[0][None],
        results[1][None],
        token_grads[0],
        token_grads[1],
        grad_qkv,
        grad_out,
        grad_gate,
        grad_up,
        grad_down,
        gains[:, :, heads],
        gains[:, :, heads + 1],
    )


def solution(mesh):
    rows = P(docs_axis, core_axis, None)
    weights = P(None, docs_axis, None)
    gains = P(None, docs_axis)
    in_specs = (
        (rows, rows, P(docs_axis, None), P(docs_axis, None)) + (weights,) * 5 + (gains,) * 2 + (rows,) * 2
    )
    out_specs = (rows,) * 4 + (weights,) * 5 + (gains,) * 2
    return jax.shard_map(
        functools.partial(on_device, mesh.shape[docs_axis]),
        mesh=mesh,
        in_specs=in_specs,
        out_specs=out_specs,
        check_vma=False,
    )
```

```python
import functools
import types
from typing import NamedTuple

import jax
import jax.numpy as jnp
from jax import lax
from jax.experimental import pallas as pl
from jax.experimental.pallas import tpu as pltpu
from jax.sharding import PartitionSpec as P

epsilon = 1e-05
big_negative = -1e30
MESH = pl.DeviceIdType.MESH
docs_axis, core_axis = "docs", "blk"
lane = 128
row_tile = 16
vmem_limit = 61 * 1024 * 1024
low, full = jnp.bfloat16, jnp.float32
by_x, by_y, upward, downward, crosswise = range(5)
lines_first, planes_first, line_only, plane_shared = range(4)
quads = ((False, False), (False, True), (True, False), (True, True))


def dot(left, right):
    return jnp.dot(left, right, preferred_element_type=full)


def dot_back(left, right):
    return lax.dot_general(left, right, (((1,), (1,)), ((), ())), preferred_element_type=full)


def dot_rows(left, right):
    return lax.dot_general(left, right, (((0,), (0,)), ((), ())), preferred_element_type=full)


def normalize(values):
    centred = values - jnp.mean(values, -1, keepdims=True)
    inverse = lax.rsqrt(jnp.mean(centred * centred, -1, keepdims=True) + epsilon)
    return centred * inverse, inverse


def over_rows(first, last, size, body):
    def step(at, carry):
        body(pl.ds(pl.multiple_of(first + at * size, row_tile), size))
        return carry

    lax.fori_loop(0, (last - first) // size, step, 0)


def over_columns(first, last, size, body):
    def step(at, carry):
        body(pl.ds(pl.multiple_of(first + at * size, lane), size))
        return carry

    lax.fori_loop(0, (last - first) // size, step, 0)


def gelu_both(value):
    root = 0.7978845608028654
    square = value * value
    bent = jnp.tanh(root * (value + 0.044715 * value * square))
    cdf = 0.5 * (1.0 + bent)
    slope = cdf + 0.5 * value * (1.0 - bent * bent) * (root * (1.0 + 0.134145 * square))
    return value * cdf, slope


def add_rows(target, others, first=0):
    size = max(size for size in (16, 32, 48) if others[0].shape[0] % size == 0)

    def body(step, carry):
        at = pl.multiple_of(step * size, row_tile)
        total = others[0][pl.ds(at, size), :].astype(full)
        for other in others[1:]:
            total = total + other[pl.ds(at, size), :].astype(full)
        target[pl.ds(first + at, size), :] = total.astype(target.dtype)
        return carry

    lax.fori_loop(0, others[0].shape[0] // size, body, 0)


def when(conditions, body):
    conditions = [condition for condition in conditions if condition is not None]
    if not conditions:
        body()
        return
    pl.when(functools.reduce(jnp.logical_and, conditions))(body)


def merged(*groups):
    space = types.SimpleNamespace()
    for group in groups:
        vars(space).update(group._asdict())
    return space


class Place:
    def __init__(self, line_size):
        docs = lax.axis_index(docs_axis)
        self.core = lax.axis_index(core_axis)
        self.line_size = line_size
        self.z, self.y, self.x = docs // 4, (docs // 2) % 2, docs % 2
        self.up_valid = self.z < line_size - 1
        self.down_valid = self.z > 0

    def index(self, z, flip_y=False, flip_x=False):
        y = 1 - self.y if flip_y else self.y
        x = 1 - self.x if flip_x else self.x
        return z * 4 + y * 2 + x

    def device(self, step):
        z, y, x = self.z, self.y, self.x
        docs = (
            z * 4 + y * 2 + 1 - x,
            z * 4 + (1 - y) * 2 + x,
            (z + 1) * 4 + y * 2 + x,
            (z - 1) * 4 + y * 2 + x,
            z * 4 + (1 - y) * 2 + 1 - x,
        )[step]
        return (docs, self.core)

    def greet(self):
        barrier = pltpu.get_barrier_semaphore()

        def signal(device):
            pl.semaphore_signal(barrier, inc=1, device_id=device, device_id_type=MESH)

        for step in (by_x, by_y, crosswise):
            signal(self.device(step))
        pl.when(self.up_valid)(lambda: signal(self.device(upward)))
        pl.when(self.down_valid)(lambda: signal(self.device(downward)))
        signal((self.index(self.z), 1 - self.core))

    def meet(self):
        peers = 4
        for valid in (self.up_valid, self.down_valid):
            peers = peers + jnp.where(valid, 1, 0)
        pl.semaphore_wait(pltpu.get_barrier_semaphore(), peers)


class Piece(NamedTuple):
    array: int
    part: int
    first: int
    rows: int
    flip: int
    route: int


class Gather:
    def __init__(self, place, pieces, sizes, splits, owns, outs, send_sems, recv_sems, local_sems):
        self.place, self.pieces, self.sizes, self.splits = place, pieces, sizes, splits
        self.owns, self.outs = owns, outs
        self.send_sems, self.recv_sems, self.local_sems = send_sems, recv_sems, local_sems

    def has(self, at, source_z):
        half = self.place.line_size // 2
        return source_z // half == self.place.core if self.splits[self.pieces[at].array] else None

    def block(self, at, source):
        piece = self.pieces[at]
        if self.splits[piece.array]:
            source = source - self.place.core * (self.place.line_size // 2) * 4
        if piece.route == line_only:
            source = source // 4
        first = source * self.sizes[piece.array] + piece.first
        rows = pl.ds(pl.multiple_of(first, row_tile), piece.rows)
        return self.outs[piece.array].at[piece.part, rows, :]

    def mine(self, at, step=None):
        piece = self.pieces[at]
        ref, offset = self.owns[piece.array]
        if piece.route == plane_shared:
            to = self.place.index(0, step in (by_y, crosswise), step in (by_x, crosswise))
            return ref.at[to, pl.ds(piece.first, piece.rows), :]
        first = pl.multiple_of(offset + piece.first, row_tile)
        return ref.at[piece.part, pl.ds(first, piece.rows), :]

    def copy(self, at, source, step, own=False):
        return pltpu.make_async_remote_copy(
            src_ref=self.mine(at, step) if own else self.block(at, source),
            dst_ref=self.block(at, source),
            send_sem=self.send_sems.at[at, step],
            recv_sem=self.recv_sems.at[at, source],
            device_id=self.place.device(step),
            device_id_type=MESH,
        )

    def local(self, at):
        here = self.place.index(self.place.z)
        return pltpu.make_async_copy(self.mine(at), self.block(at, here), self.local_sems.at[at])

    def send(self, conditions, *which):
        when(conditions, lambda: self.copy(*which).start())

    def wait(self, conditions, at, source):
        when(conditions, lambda: self.copy(at, source, by_x).wait_recv())

    def units(self, distance):
        place = self.place
        if distance == 0:
            return [(place.z, None, None)]
        return [
            (place.z - distance, place.z >= distance, (upward, place.up_valid)),
            (place.z + distance, place.z < place.line_size - distance, (downward, place.down_valid)),
        ]

    def both_ways(self, conditions, at, source, own=False):
        self.send(conditions + [self.place.up_valid], at, source, upward, own)
        self.send(conditions + [self.place.down_valid], at, source, downward, own)

    def own(self, at):
        place = self.place
        here = place.index(place.z)
        held = [self.has(at, place.z)]
        when(held, lambda: self.local(at).start())
        self.both_ways(held, at, here, True)
        route = self.pieces[at].route
        if route != line_only:
            self.send(held, at, here, by_x, True)
            self.send(held, at, here, by_y, True)
        if route == plane_shared:
            self.send(held, at, here, crosswise, True)

    def beside(self, at, distance):
        piece = self.pieces[at]
        for source_z, valid, _ in self.units(distance):
            conditions = [valid, self.has(at, source_z)]
            for other in (0, 1):
                source = self.place.index(source_z, other == 1, other == 0)
                if other == piece.flip or piece.route != lines_first:
                    self.wait(conditions, at, source)
                if other == piece.flip and piece.route != plane_shared:
                    self.send(conditions, at, source, by_x if other else by_y)
                if piece.route != lines_first:
                    self.both_ways(conditions, at, source)

    def along(self, at, distance, quad=quads[0]):
        for source_z, valid, (step, onward) in self.units(distance):
            source = self.place.index(source_z, *quad)
            conditions = [valid, self.has(at, source_z)]
            self.wait(conditions, at, source)
            self.send(conditions + [onward], at, source, step)
            if self.pieces[at].route == lines_first:
                self.send(conditions, at, source, by_x)
                self.send(conditions, at, source, by_y)

    def late_round(self, at, number):
        place = self.place
        last = place.line_size - 1
        if number == 1:
            self.beside(at, 0)
        if number == 2:
            held = [self.has(at, place.z)]
            fourth = place.index(place.z, *quads[3])
            self.wait(held, at, fourth)
            self.both_ways(held, at, fourth)
        for quad, behind in zip(quads, (0, 1, 1, 2)):
            if 1 <= number - behind <= last:
                self.along(at, number - behind, quad)

    def rest(self, array):
        for at, piece in enumerate(self.pieces):
            if piece.array != array:
                continue
            if piece.route in (planes_first, plane_shared):
                self.along(at, self.place.line_size - 1, quads[3])
            elif piece.route == lines_first:
                for distance in range(self.place.line_size):
                    for source_z, valid, _ in self.units(distance):
                        conditions = [valid, self.has(at, source_z)]
                        beside = (piece.flip == 0, piece.flip == 1)
                        self.wait(conditions, at, self.place.index(source_z, *beside))
                        self.wait(conditions, at, self.place.index(source_z, *quads[3]))
            when([self.has(at, self.place.z)], lambda: self.local(at).wait())

    def run(self, plan, stages):
        for kind, at, number in plan:
            if kind == 0:
                self.own(at)
            elif kind == 1:
                self.beside(at, number)
            elif kind == 2:
                self.along(at, number)
            elif kind == 3:
                self.late_round(at, number)
            elif kind == 4:
                self.rest(at)
            else:
                stages[at]()

    def sent(self, at, step, blocks):
        piece = self.pieces[at]
        total = self.outs[piece.array].at[piece.part, pl.ds(0, blocks * piece.rows), :]
        pltpu.make_async_remote_copy(
            src_ref=total,
            dst_ref=total,
            send_sem=self.send_sems.at[at, step],
            recv_sem=self.recv_sems.at[at, 0],
            device_id=self.place.device(step),
            device_id_type=MESH,
        ).wait_send()

    def finish(self):
        size, place = self.place.line_size, self.place
        for at, piece in enumerate(self.pieces):
            split = self.splits[piece.array]
            planes = size // 2 if split else size
            if piece.route == lines_first:
                self.sent(at, by_x, planes * (1 + piece.flip))
                self.sent(at, by_y, planes * (2 - piece.flip))
            elif piece.route == planes_first:
                self.sent(at, by_x, 1 + piece.flip)
                self.sent(at, by_y, 2 - piece.flip)
            elif piece.route == plane_shared:
                for step in (by_x, by_y, crosswise):
                    self.sent(at, step, 1)
            chips = 4 if piece.route in (planes_first, plane_shared) else 1
            for z in range(size):
                for core in range(2 if split else 1):
                    held = [source for source in range(size) if not split or source // (size // 2) == core]
                    here = [place.z == z] + ([place.core == core] if split else [])
                    up = chips * sum(source <= z for source in held) if z < size - 1 else 0
                    down = chips * sum(source >= z for source in held) if z > 0 else 0
                    if up:
                        when(here, lambda: self.sent(at, upward, up))
                    if down:
                        when(here, lambda: self.sent(at, downward, down))


class Scatter:
    def __init__(self, place, pieces, splits, raws, parts, buffers, send_sems, recv_sems, finish):
        self.place, self.pieces, self.splits = place, pieces, splits
        self.raws, self.parts, self.buffers = raws, parts, buffers
        self.send_sems, self.recv_sems, self.finish_rows = send_sems, recv_sems, finish
        self.first = arrival_offsets(pieces, place.line_size)

    shares = ((quads[1], 1, by_x), (quads[2], 2, by_y), (quads[3], 0, crosswise))

    def has(self, at, z_to):
        half = self.place.line_size // 2
        return z_to // half == self.place.core if self.splits[self.pieces[at].array] else None

    def slot(self, at, z_to):
        half = self.place.line_size // 2
        return z_to - self.place.core * half if self.splits[self.pieces[at].array] else z_to

    def block(self, refs, at, z_to, quad):
        piece = self.pieces[at]
        ref = refs[piece.array]
        if piece.route == line_only:
            first = z_to * (ref.shape[1] // self.place.line_size) + piece.first
        else:
            split = 2 if self.splits[piece.array] else 1
            rows = ref.shape[1] // (4 * self.place.line_size // split)
            first = self.place.index(self.slot(at, z_to), *quad) * rows + piece.first
        return ref.at[piece.part, pl.ds(pl.multiple_of(first, row_tile), piece.rows), :]

    def quads(self, at):
        return quads[:1] if self.pieces[at].route == line_only else quads

    def raw_of(self, at, z_to, quad):
        return self.block(self.raws, at, z_to, quad)

    def part_of(self, at, z_to, quad):
        return self.block(self.parts, at, z_to, quad)

    def landed(self, at, kind, z_to, quad=0):
        ref = self.buffers[at][kind]
        if self.pieces[at].route == lines_first:
            return ref.at[self.slot(at, z_to)]
        return ref.at[self.slot(at, z_to), quad] if kind >= 3 else ref.at[0]

    def arrival(self, at, kind, z_to, quad):
        route = self.pieces[at].route
        if route == lines_first:
            return self.first[at] + z_to * 5 + kind
        if kind < 3:
            return self.first[at] + kind
        chips = len(self.quads(at))
        return self.first[at] + 3 + (z_to * 2 + kind - 3) * chips + quad

    def copy(self, source, at, kind, z_to, step, quad=0):
        return pltpu.make_async_remote_copy(
            src_ref=source,
            dst_ref=self.landed(at, kind, z_to, quad),
            send_sem=self.send_sems.at[at],
            recv_sem=self.recv_sems.at[self.arrival(at, kind, z_to, quad)],
            device_id=self.place.device(step),
            device_id_type=MESH,
        )

    def arrived(self, at, kind, z_to, quad=0):
        held = self.landed(at, kind, z_to, quad)
        self.copy(held, at, kind, z_to, by_x, quad).wait_recv()

    def send(self, conditions, *which):
        when(conditions, lambda: self.copy(*which).start())

    def destination(self, step):
        size = self.place.line_size
        chosen = 0
        for at in range(size):
            order = sorted(range(size), key=lambda other: (-abs(other - at), other))
            chosen = chosen + jnp.where(self.place.z == at, order[step], 0)
        return chosen

    def raw(self, at, step):
        place = self.place
        z_to = self.destination(step)
        conditions = [self.has(at, z_to)]
        if self.pieces[at].route == lines_first:
            self.plane_raw(conditions, self.raw_of, at, z_to)
            return
        first, last = place.z == 0, place.z == place.line_size - 1
        for number, quad in enumerate(self.quads(at)):
            source = self.raw_of(at, z_to, quad)
            up = conditions + [first, z_to > place.z]
            self.send(up, source, at, 3, z_to, upward, number)
            down = conditions + [last, z_to < place.z]
            self.send(down, source, at, 4, z_to, downward, number)

    def plane_raw(self, conditions, source, at, z_to):
        if self.pieces[at].flip == 0:
            self.send(conditions, source(at, z_to, (True, True)), at, 0, z_to, by_y)
            self.send(conditions, source(at, z_to, (True, False)), at, 2, z_to, by_y)
        else:
            self.send(conditions, source(at, z_to, (True, True)), at, 0, z_to, by_x)
            self.send(conditions, source(at, z_to, (False, True)), at, 1, z_to, by_x)

    def plane_pair(self, conditions, at, z_to):
        flip = self.pieces[at].flip
        held = self.landed(at, 0, z_to)

        def body():
            self.arrived(at, 0, z_to)
            add_rows(held, [held, self.part_of(at, z_to, (flip == 1, flip == 0))])

        when(conditions, body)
        if flip == 0:
            self.send(conditions, held, at, 1, z_to, by_x)
        else:
            self.send(conditions, held, at, 2, z_to, by_y)

    def pair(self, at, step):
        z_to = self.destination(step)
        self.plane_pair([self.has(at, z_to)], at, z_to)

    def line(self, at, step):
        place, piece = self.place, self.pieces[at]
        z = place.z
        z_to = self.destination(step)
        conditions = [self.has(at, z_to)]
        first, last = z == 0, z == place.line_size - 1
        inner = jnp.logical_and(z > 0, z < place.line_size - 1)
        ways = (
            (3, [z_to > z], [first], [z > 0], upward),
            (4, [z_to < z], [last], [z < place.line_size - 1], downward),
        )
        ends = (([first], (4,)), ([last], (3,)), ([inner], (3, 4)))
        if piece.route == lines_first:
            held = self.landed(at, 1, z_to)
            base = [held, self.landed(at, 2, z_to), self.part_of(at, z_to, quads[0])]

            def wait():
                self.arrived(at, 1, z_to)
                self.arrived(at, 2, z_to)

            when(conditions, wait)
            for kind, onward, starts, passes, step_to in ways:
                when(conditions + onward + starts, lambda: add_rows(held, base))

                def passing():
                    self.arrived(at, kind, z_to)
                    add_rows(held, base + [self.landed(at, kind, z_to)])

                when(conditions + onward + passes, passing)
                self.send(conditions + onward, held, at, kind, z_to, step_to)
            for which, kinds in ends:

                def end():
                    for kind in kinds:
                        self.arrived(at, kind, z_to)
                    self.finish_rows(piece, base + [self.landed(at, kind, z_to) for kind in kinds])

                when(conditions + [z_to == z] + which, end)
            return
        for kind, onward, _, passes, step_to in ways:
            for at_quad, quad in enumerate(self.quads(at)):
                held = self.landed(at, kind, z_to, at_quad)

                def passing():
                    self.arrived(at, kind, z_to, at_quad)
                    add_rows(held, [held, self.part_of(at, z_to, quad)])

                which = conditions + onward + passes
                when(which, passing)
                self.send(which, held, at, kind, z_to, step_to, at_quad)
        here = conditions + [z_to == z]
        for which, kinds in ends:

            def end():
                for at_quad, quad in reversed(list(enumerate(self.quads(at)))):
                    own = self.part_of(at, z_to, quad)
                    for kind in kinds:
                        self.arrived(at, kind, z_to, at_quad)
                    total = [own] + [self.landed(at, kind, z_to, at_quad) for kind in kinds]
                    if piece.route == planes_first or at_quad:
                        add_rows(own, total)
                    else:
                        self.finish_rows(piece, total)

            when(here + which, end)
        if step == place.line_size - 1 and piece.route == planes_first:
            self.plane_raw(here, self.part_of, at, z_to)
        if step == place.line_size - 1 and piece.route == plane_shared:
            for quad, kind, step_to in self.shares:
                self.send(here, self.part_of(at, z_to, quad), at, kind, z_to, step_to)

    def tail(self, at):
        z, piece = self.place.z, self.pieces[at]
        if piece.route == plane_shared:
            for quad, kind, _ in self.shares:
                self.arrived(at, kind, z)
                self.finish_rows(piece, [self.landed(at, kind, z)], quad)
            return
        conditions = [self.has(at, z)]
        self.plane_pair(conditions, at, z)

        def end():
            self.arrived(at, 1, z)
            self.arrived(at, 2, z)
            total = [self.landed(at, kind, z) for kind in (1, 2)] + [self.part_of(at, z, quads[0])]
            self.finish_rows(piece, total)

        when(conditions, end)

    def run(self, plan, stages):
        for kind, at, number in plan:
            if kind == 0:
                self.raw(at, number)
            elif kind == 1:
                self.pair(at, number)
            elif kind == 2:
                self.line(at, number)
            elif kind == 3:
                self.tail(at)
            else:
                stages[at]()

    def sent(self, at, blocks):
        piece = self.pieces[at]
        total = self.raws[piece.array].at[piece.part, pl.ds(0, blocks * piece.rows), :]
        pltpu.make_async_remote_copy(
            src_ref=total,
            dst_ref=total,
            send_sem=self.send_sems.at[at],
            recv_sem=self.recv_sems.at[0],
            device_id=self.place.device(by_x),
            device_id_type=MESH,
        ).wait_send()

    def finish(self):
        size, place = self.place.line_size, self.place
        for at, piece in enumerate(self.pieces):
            if self.splits[piece.array]:
                half = place.z // (size // 2) == place.core
                when([half], lambda: self.sent(at, 3 * (size // 2) + size // 2 - 1))
                when([jnp.logical_not(half)], lambda: self.sent(at, 4 * (size // 2)))
            elif piece.route == lines_first:
                self.sent(at, 4 * size - 1)
            elif piece.route == line_only:
                self.sent(at, size - 1)
            else:
                self.sent(at, 4 * (size - 1) + 3)


def arrival_offsets(pieces, line_size):
    offsets = [0]
    for piece in pieces:
        chips = 1 if piece.route == line_only else 4
        count = 5 * line_size if piece.route == lines_first else 3 + 2 * line_size * chips
        offsets.append(offsets[-1] + count)
    return offsets


class Moves:
    def __init__(self, place, local_sems, send_sems, recv_sems):
        self.place = place
        self.other = (place.index(place.z), 1 - place.core)
        self.local_sems, self.send_sems, self.recv_sems = local_sems, send_sems, recv_sems
        self.locals, self.remotes = 0, 0
        self.to_end = []

    def local(self, source, target):
        made = pltpu.make_async_copy(source, target, self.local_sems.at[self.locals])
        self.locals += 1
        made.start()
        return made

    def save(self, source, target):
        self.to_end.append(self.local(source, target).wait)

    def across(self, source, target, arrives=None):
        sems = dict(
            send_sem=self.send_sems.at[self.remotes],
            recv_sem=self.recv_sems.at[self.remotes],
            device_id=self.other,
            device_id_type=MESH,
        )
        self.remotes += 1
        made = pltpu.make_async_remote_copy(src_ref=source, dst_ref=target, **sems)
        made.start()
        self.to_end.append(made.wait_send)
        arrives = target if arrives is None else arrives
        return pltpu.make_async_remote_copy(src_ref=arrives, dst_ref=arrives, **sems)

    def peer(self, source, target, step, arrives=None):
        sems = dict(
            send_sem=self.send_sems.at[self.remotes],
            recv_sem=self.recv_sems.at[self.remotes],
            device_id=self.place.device(step),
            device_id_type=MESH,
        )
        self.remotes += 1
        made = pltpu.make_async_remote_copy(src_ref=source, dst_ref=target, **sems)
        made.start()
        self.to_end.append(made.wait_send)
        arrives = target if arrives is None else arrives
        return pltpu.make_async_remote_copy(src_ref=arrives, dst_ref=arrives, **sems)

    def finish(self):
        assert self.locals == self.local_sems.shape[0] and self.remotes == self.send_sems.shape[0]
        for wait in self.to_end:
            wait()


class Rows:
    def __init__(self, text, visual):
        self.text, self.visual = text, visual
        self.split = 2 * text
        self.count = 2 * (text + visual)
        self.spans = ((0, self.split), (self.split, self.count))
        self.own = ((0, text), (self.split, self.split + visual))
        self.other = ((text, self.split), (self.split + visual, self.count))
        self.packed = ((0, text), (text, text + visual))
        self.sizes = (chunk_of(text), chunk_of(visual))

    def over_own(self, s, body):
        shift = self.own[s][0] - self.packed[s][0]

        def shifted(piece):
            body(pl.ds(pl.multiple_of(piece.start + shift, row_tile), piece.size), piece)

        over_rows(*self.packed[s], self.sizes[s], shifted)

    def swap_parts(self, moves, wide, received, which=(0, 1)):
        return [
            moves.across(wide.at[slice(*self.other[s])], received.at[slice(*self.packed[s])])
            for s in which
        ]

    def swap_own(self, moves, ref, s):
        return moves.across(ref.at[slice(*self.own[s])], ref.at[slice(*self.other[s])])


class Plane:
    steps = (by_x, by_y, crosswise)

    def __init__(self, place, moves, size):
        self.place, self.moves, self.size = place, moves, size
        self.half = 4 * size

    def chip(self, step=None):
        return self.place.index(0, step in (by_y, crosswise), step in (by_x, crosswise))

    def document(self, at):
        return [slice(first, first + self.size) for first in (at * self.size, self.half + at * self.size)]

    def part(self, ref, at, count=1):
        return ref.at[at * self.size : (at + count) * self.size]

    def spread(self, own, target):
        other = self.moves.across(own, self.part(target, 4))
        return other, [
            self.moves.peer(own, self.part(target, 1 + at), step) for at, step in enumerate(self.steps[:2])
        ]

    def relay(self, target, arrivals):
        moves, core = self.moves, self.place.core
        made = [
            pltpu.make_async_remote_copy(
                src_ref=self.part(target, 1 + at),
                dst_ref=self.part(target, 3),
                send_sem=moves.send_sems.at[moves.remotes],
                recv_sem=moves.recv_sems.at[moves.remotes],
                device_id=self.place.device(step),
                device_id_type=MESH,
            )
            for at, step in enumerate((by_y, by_x))
        ]
        moves.remotes += 1
        for at in range(2):

            def pass_along():
                arrivals[at].wait_recv()
                made[at].start()

            pl.when(core == at)(pass_along)
            moves.to_end.append(functools.partial(pl.when(core == at), made[at].wait_send))
        return made[0]

    def pass_on(self, target, arrivals, fourth):
        for at in range(2):
            pl.when(self.place.core != at)(arrivals[at].wait_recv)
        fourth.wait_recv()
        return self.moves.across(self.part(target, 1, 3), self.part(target, 5, 3))

    def halve(self, wide, received):
        return self.moves.across(self.part(wide, 4, 4), received)

    def share(self, wide, received, outgoing, landing):
        outgoing[...] = (
            wide[self.size : self.half, :] + received[self.size : self.half, :]
        ).astype(outgoing.dtype)
        return [
            self.moves.peer(self.part(outgoing, at), self.part(landing, at), step)
            for at, step in enumerate(self.steps)
        ]

    def total(self, wide, received, landing):
        value = wide[: self.size, :] + received[: self.size, :]
        for at in range(3):
            value = value + landing[at * self.size : (at + 1) * self.size, :].astype(full)
        return value


def chunk_of(count):
    return max(size for size in range(row_tile, 385, row_tile) if count % size == 0)


def query_spans(count):
    edges = list(range(0, count - 256, 512)) + [count]
    return list(zip(edges[:-1], edges[1:]))


def head_wide(values, odd):
    empty = jnp.zeros_like(values)
    return jnp.concatenate([empty, values] if odd else [values, empty], 0)


def column_of(row, count):
    return jnp.broadcast_to(row, (lane, count)).T


def scratch_of(group):
    return [pltpu.VMEM(shape, dtype) for shape, dtype in group]


def shapes_of(group):
    return [jax.ShapeDtypeStruct(shape, dtype) for shape, dtype in group]


def same_as(arrays):
    return [(array.shape, array.dtype) for array in arrays]


def sems(*counts):
    return [pltpu.SemaphoreType.DMA(count if isinstance(count, tuple) else (count,)) for count in counts]


def specs_of(count, in_vmem):
    spaces = [pltpu.VMEM] * in_vmem + [pl.ANY] * (count - in_vmem)
    return [pl.BlockSpec(memory_space=space) for space in spaces]


front_pieces = (
    (0, 0, 0, 32, 0, 0), (0, 0, 32, 16, 1, 0), (1, 0, 0, 16, 0, 0), (1, 0, 16, 32, 1, 0),
    (3, 0, 0, 32, 0, 0), (3, 0, 32, 16, 1, 0), (3, 0, 48, 48, 0, 1), (2, 0, 0, 48, 0, 0),
    (2, 1, 0, 48, 1, 0), (4, 0, 0, 48, 0, 3), (5, 0, 0, 96, 0, 2), (6, 0, 0, 48, 0, 3),
    (7, 0, 0, 48, 1, 0),
)
front_plan = (
    (5, 25, 0), (0, 6, 0), (5, 27, 0), (0, 12, 0), (0, 0, 0), (0, 7, 0), (0, 5, 0), (2, 12, 1), (0, 1, 0),
    (0, 11, 0), (2, 0, 1), (2, 12, 2), (0, 4, 0), (2, 7, 1), (2, 5, 1), (5, 0, 0), (5, 23, 0), (0, 2, 0),
    (2, 7, 2), (2, 12, 3), (1, 12, 1), (2, 0, 2), (2, 1, 1), (3, 11, 1), (1, 12, 3), (0, 9, 0), (2, 1, 2),
    (2, 0, 3), (2, 7, 3), (2, 5, 2), (2, 2, 1), (3, 11, 2), (5, 28, 0), (0, 8, 0), (1, 12, 2), (1, 12, 0),
    (2, 1, 3), (1, 0, 3), (2, 5, 3), (1, 7, 3), (1, 1, 0), (3, 11, 3), (5, 1, 0), (1, 0, 2), (3, 9, 1),
    (2, 8, 1), (1, 0, 0), (3, 9, 2), (5, 26, 0), (4, 7, 0), (3, 11, 4), (2, 8, 2), (1, 1, 2), (1, 1, 1),
    (5, 4, 0), (1, 0, 1), (0, 3, 0), (1, 1, 3), (4, 6, 0), (5, 5, 0), (2, 8, 3), (2, 2, 2), (3, 6, 1),
    (2, 4, 1), (2, 3, 1), (1, 5, 0), (1, 7, 0), (4, 0, 0), (0, 10, 0), (5, 2, 0), (5, 3, 0), (3, 9, 3),
    (5, 6, 0), (1, 8, 1), (2, 2, 3), (5, 7, 0), (1, 8, 3), (1, 7, 1), (1, 3, 0), (1, 7, 2), (1, 8, 0),
    (1, 8, 2), (2, 3, 2), (5, 8, 0), (5, 9, 0), (3, 6, 2), (1, 4, 0), (1, 2, 3), (2, 4, 2), (5, 10, 0),
    (5, 11, 0), (1, 5, 2), (5, 12, 0), (2, 3, 3), (1, 2, 2), (5, 13, 0), (4, 2, 0), (1, 2, 0), (1, 3, 2),
    (3, 9, 4), (5, 14, 0), (1, 3, 1), (2, 10, 1), (1, 2, 1), (1, 3, 3), (5, 15, 0), (5, 16, 0), (1, 4, 1),
    (3, 6, 3), (1, 5, 1), (5, 29, 0), (2, 10, 2), (1, 4, 2), (4, 4, 0), (4, 1, 0), (1, 5, 3), (2, 4, 3),
    (5, 18, 0), (5, 30, 0), (5, 19, 0), (5, 24, 0), (3, 6, 4), (1, 4, 3), (5, 17, 0), (5, 21, 0),
    (5, 20, 0), (5, 22, 0), (2, 10, 3), (4, 3, 0), (4, 5, 0),
)
ffn_pieces = (
    (0, 0, 0, 48, 0, 0), (0, 0, 48, 48, 1, 0), (1, 0, 0, 96, 0, 2),
)
ffn_plan = (
    (0, 1, 0), (0, 2, 0), (0, 0, 0), (0, 2, 1), (0, 1, 1), (0, 1, 2), (0, 0, 1), (4, 2, 0), (2, 2, 0),
    (0, 2, 2), (1, 1, 0), (4, 0, 0), (1, 0, 0), (4, 1, 0), (2, 2, 1), (1, 1, 1), (0, 0, 2), (4, 4, 0),
    (4, 3, 0), (4, 6, 0), (1, 0, 1), (4, 10, 0), (2, 2, 2), (1, 1, 2), (0, 1, 3), (2, 1, 0), (4, 9, 0),
    (0, 0, 3), (2, 0, 0), (1, 0, 2), (4, 13, 0), (2, 1, 1), (0, 2, 3), (4, 7, 0), (4, 8, 0), (1, 1, 3),
    (2, 0, 1), (2, 1, 2), (4, 5, 0), (2, 0, 2), (2, 2, 3), (1, 0, 3), (4, 11, 0), (4, 12, 0), (4, 15, 0),
    (2, 1, 3), (4, 14, 0), (2, 0, 3),
)
attention_pieces = (
    (0, 0, 0, 32, 0, 0), (0, 0, 32, 16, 1, 0), (1, 0, 0, 48, 0, 0), (1, 1, 0, 48, 1, 0),
    (2, 0, 0, 32, 1, 0), (2, 0, 32, 16, 0, 0), (3, 0, 0, 48, 0, 3), (4, 0, 0, 48, 0, 3),
    (5, 0, 0, 48, 0, 0), (5, 1, 0, 48, 1, 0),
)
attention_plan = (
    (0, 1, 0), (0, 0, 0), (0, 2, 0), (0, 1, 1), (0, 1, 2), (4, 0, 0), (4, 1, 0), (1, 1, 0), (0, 6, 0),
    (0, 1, 3), (0, 3, 0), (1, 0, 0), (0, 0, 1), (4, 2, 0), (4, 3, 0), (4, 4, 0), (1, 2, 0), (1, 0, 1),
    (1, 1, 1), (0, 0, 2), (4, 5, 0), (0, 3, 1), (4, 6, 0), (4, 7, 0), (0, 6, 1), (4, 9, 0), (0, 5, 0),
    (2, 6, 0), (1, 3, 0), (0, 4, 0), (0, 5, 1), (2, 1, 0), (0, 6, 2), (0, 2, 1), (4, 10, 0), (1, 0, 2),
    (4, 11, 0), (0, 4, 1), (0, 7, 0), (2, 6, 1), (1, 1, 2), (0, 7, 1), (1, 4, 0), (4, 8, 0), (4, 12, 0),
    (0, 5, 2), (0, 4, 2), (2, 7, 0), (1, 4, 1), (2, 6, 2), (2, 0, 0), (1, 2, 1), (0, 2, 2), (1, 5, 0),
    (2, 3, 0), (0, 6, 3), (4, 13, 0), (2, 1, 1), (2, 2, 0), (1, 5, 1), (2, 1, 2), (4, 14, 0), (0, 8, 0),
    (0, 0, 3), (0, 9, 0), (0, 9, 1), (0, 3, 2), (0, 4, 3), (2, 0, 1), (0, 8, 1), (0, 8, 2), (0, 7, 2),
    (2, 7, 1), (2, 7, 2), (0, 9, 2), (1, 1, 3), (1, 9, 0), (1, 5, 2), (1, 8, 0), (1, 3, 1), (0, 8, 3),
    (1, 9, 1), (0, 2, 3), (2, 5, 0), (2, 6, 3), (0, 3, 3), (1, 3, 2), (2, 4, 0), (2, 0, 2), (0, 5, 3),
    (0, 7, 3), (1, 8, 1), (1, 0, 3), (2, 2, 1), (1, 9, 2), (2, 9, 0), (1, 4, 2), (2, 8, 0), (1, 2, 2),
    (2, 4, 1), (2, 1, 3), (2, 3, 1), (1, 2, 3), (4, 18, 0), (1, 4, 3), (1, 8, 2), (2, 5, 1), (3, 6, 0),
    (2, 5, 2), (1, 8, 3), (1, 3, 3), (0, 9, 3), (2, 9, 1), (2, 8, 1), (2, 3, 2), (1, 5, 3), (2, 0, 3),
    (4, 15, 0), (2, 2, 2), (2, 7, 3), (2, 8, 2), (2, 4, 2), (2, 9, 2), (1, 9, 3), (4, 17, 0), (3, 7, 0),
    (2, 5, 3), (2, 2, 3), (2, 8, 3), (2, 3, 3), (4, 16, 0), (2, 4, 3), (2, 9, 3),
)


class FrontIn(NamedTuple):
    w_qkv: object
    w_gate: object
    w_up: object
    gain_attn: object
    gain_ffn: object
    text_mask: object
    visual_mask: object
    text: object
    visual: object
    text_dy: object
    visual_dy: object
    w_out: object
    w_down: object


class FrontOut(NamedTuple):
    full_qkv: object
    full_up: object
    full_out: object
    full_down: object
    full_up_v: object
    full_down_v: object
    full_qkv_v: object
    full_small_v: object
    h: object
    h_v: object
    qkv: object
    gates_t: object
    text_t: object
    visual_t: object
    logs: object
    mix_t: object
    middle: object
    hm: object
    hm_v: object
    act: object
    act_v: object
    slope: object
    slope_v: object
    part_down: object
    part_down_v: object
    dy: object
    dy_v: object
    gains: object
    bias: object


class FrontKept(NamedTuple):
    s_h: object
    s_h_v: object
    s_qkv: object
    s_gates_t: object
    s_text_t: object
    s_visual_t: object
    s_logs: object
    s_mix_t: object
    s_middle: object
    s_hm: object
    s_hm_v: object
    s_act: object
    s_act_v: object
    s_slope: object
    s_slope_v: object
    s_part_down: object
    s_part_down_v: object
    s_dy: object
    s_dy_v: object
    s_gains: object
    s_bias: object


class FrontScratch(NamedTuple):
    shard_qkv: object
    shard_gate: object
    shard_up: object
    shard_attn: object
    shard_ffn: object
    shard_text_mask: object
    shard_visual_mask: object
    own_qkv: object
    own_qkv_v: object
    own_small_v: object
    own_up: object
    own_up_v: object
    s_w_qkv: object
    s_w_qkv_v: object
    s_w_small_v: object
    s_w_up: object
    s_w_up_v: object
    s_w_out: object
    x: object
    x_v: object
    wide: object
    qkv_v: object
    landing_qkv: object
    received: object
    gate_rows: object
    q_t: object
    v_t: object
    mix: object


def prepare_shards(v, core, heads):
    first = core == 0
    rows = v.shard_qkv.shape[1]
    third = v.shard_qkv.shape[2] // 3
    half = third // 2
    for s in range(2):
        for pair in range(half // lane):
            for at in range(3):
                start = at * third + pair * lane
                columns = [v.shard_qkv[s, :, start + way * half : start + way * half + lane] for way in (0, 1)]
                chosen = jnp.where(first, *columns)
                if s == 0:
                    to = (3 * pair + at) * lane
                    v.own_qkv[0, :, to : to + lane] = chosen
                else:
                    v.own_qkv_v[pair, :, at * lane : (at + 1) * lane] = chosen
        gate = v.shard_gate[:, s, :].astype(full)
        gate = jnp.where(first, gate[:heads], gate[heads:])
        gains = [ref[s : s + 1, :].astype(full) for ref in (v.shard_attn, v.shard_ffn)]
        small = jnp.concatenate([gate, *gains, jnp.zeros((lane - heads - 2, rows), full)], 0)
        small = jnp.concatenate([small, jnp.zeros((lane, lane - rows), full)], 1).T[:rows]
        if s == 0:
            v.own_qkv[0, :, 3 * half :] = small.astype(low)
        else:
            v.own_small_v[0, :, :] = small.astype(low)
    for pair in range(half // lane, 4):
        v.own_qkv_v[pair, :, :] = jnp.zeros(v.own_qkv_v.shape[1:], low)


def prepare_hidden(v, core, block):
    first = core == 0
    pieces = []
    for s in range(2):
        for start in range(0, v.shard_up.shape[2], 2 * block):
            ways = [v.shard_up[s, :, start + way * block : start + (way + 1) * block].astype(full) for way in (0, 1)]
            pieces.append(jnp.where(first, *ways))
    count = len(pieces) // 2
    v.own_up[0, :, :] = jnp.concatenate(pieces[:count], 1).astype(low)
    for quad in range(4):
        v.own_up_v[quad, :, :] = jnp.concatenate(pieces[count + quad :: 4], 1).astype(low)


def prepare_bias(v, core):
    pieces = []
    for ref in (v.shard_text_mask, v.shard_visual_mask):
        mask = ref[...].astype(full)
        half = mask.shape[1] // 2
        swapped = jnp.concatenate([mask[:, half:], mask[:, :half]], 1)
        pieces.append(jnp.where(core == 0, mask, swapped))
    row = jnp.concatenate(pieces, 1)
    v.s_bias[...] = column_of(jnp.where(row > 0.0, 0.0, big_negative), row.shape[1])


def attend_head(rows, head_width, v, number):
    pair = 2 * head_width
    at, odd = number // 2, number % 2
    keys = v.s_qkv[:, (3 * at + 1) * pair : (3 * at + 2) * pair]
    bias = v.s_bias[:, 0:1]
    head = slice(number * head_width, (number + 1) * head_width)
    for first, last in query_spans(rows.count):
        scores = dot(keys, head_wide(v.q_t[head, first:last], odd)) + bias
        for t, target in enumerate((v.s_text_t, v.s_visual_t)):
            start, stop = rows.spans[t]
            part = scores[start:stop]
            top = jnp.max(part, 0, keepdims=True)
            raised = jnp.exp(part - top)
            total = jnp.sum(raised, 0, keepdims=True)
            probs = (raised * (1.0 / total)).astype(low)
            target[head, first:last] = dot(v.v_t[head, start:stop], probs)
            row = 8 * t + number
            v.s_logs[row : row + 1, first:last] = top + jnp.log(total)


def front_kernel(line_size, heads, scale, pieces, plan, *refs):
    groups = []
    for group in (FrontIn, FrontOut, FrontKept, FrontScratch):
        count = len(group._fields)
        groups.append(group(*refs[:count]))
        refs = refs[count:]
    v = merged(*groups)
    place = Place(line_size)
    core = place.core
    rows = Rows(v.text.shape[1], v.visual.shape[1])
    shard, block = v.shard_qkv.shape[1], v.w_down.shape[1] // 2
    owns = (
        (v.own_qkv, 0),
        (v.own_up, 0),
        (v.w_out, 0),
        (v.w_down, core * block),
        (v.own_up_v, 0),
        (v.w_down.at[pl.ds(1, 1)], core * block),
        (v.own_qkv_v, 0),
        (v.own_small_v, 0),
    )
    gather = Gather(
        place,
        pieces,
        (shard, shard, shard, block, shard, block, shard, shard),
        (False, False, True, False, False, False, False, False),
        owns,
        (
            v.s_w_qkv, v.s_w_up, v.s_w_out, v.full_down, v.s_w_up_v, v.full_down_v, v.s_w_qkv_v,
            v.s_w_small_v,
        ),
        *refs[:3],
    )
    moves = Moves(place, *refs[3:])
    width = v.s_qkv.shape[1] // 3
    head_width = width // heads
    hidden = v.s_act.shape[1]
    arrivals = {}

    place.greet()
    shards = [moves.local(source, target) for source, target in zip(groups[0][:7], groups[3][:7])]
    place.meet()
    plane = Plane(place, moves, rows.visual)
    loads = [
        moves.local(v.text.at[0], v.x.at[slice(*rows.own[0])]),
        moves.local(v.visual.at[0], plane.part(v.x_v, 0)),
        moves.local(v.text_dy.at[0], v.s_dy.at[slice(*rows.own[0])]),
        moves.local(v.visual_dy.at[0], plane.part(v.s_dy_v, 0)),
    ]
    swaps = [
        moves.across(v.text.at[0], v.x.at[slice(*rows.other[0])]),
        moves.across(v.text_dy.at[0], v.s_dy.at[slice(*rows.other[0])]),
    ]

    def prepare_qkv():
        for at in (0, 1, 3, 4):
            shards[at].wait()
        prepare_shards(v, core, heads)

    def prepare():
        shards[2].wait()
        prepare_hidden(v, core, block)

    def norm():
        shards[5].wait()
        shards[6].wait()
        prepare_bias(v, core)
        moves.save(v.s_bias, v.bias)
        loads[0].wait()
        swaps[0].wait_recv()

        def body(piece):
            v.wide[piece, :] = normalize(v.x[piece, :].astype(full))[0]

        over_rows(0, rows.split, rows.sizes[0], body)

    def gains_of(s, small):
        v.s_gains[s, :, :] = small.astype(full).T[heads : heads + 2]

    def lower_text():
        moves.save(v.s_w_qkv, v.full_qkv)
        gains_of(0, v.s_w_qkv[0, :, 3 * width :])

        def body(piece):
            v.s_h[piece, :] = (v.wide[piece, :] * v.s_gains[0, 0:1, :]).astype(low)

        over_rows(0, rows.split, rows.sizes[0], body)
        moves.save(v.s_h, v.h)

    def project_text():
        even = 3 * width // 256 * 256

        def columns(piece):
            v.s_qkv[: rows.split, piece] = dot(v.s_h[...], v.s_w_qkv[0, :, piece]).astype(low)

        over_columns(0, even, 256, columns)
        rest = dot(v.s_h[...], v.s_w_qkv[0, :, even:])
        v.s_qkv[: rows.split, even:] = rest[:, : 3 * width - even].astype(low)
        v.gate_rows[: rows.split, :] = rest[:, 3 * width - even :]

    def spread_x():
        arrivals[6] = plane.spread(v.visual.at[0], v.x_v)

    def relay_x():
        arrivals[9] = plane.relay(v.x_v, arrivals[6][1])

    def pass_x():
        arrivals[7] = plane.pass_on(v.x_v, arrivals[6][1], arrivals[9])

    def lower_visual():
        moves.save(v.s_w_small_v, v.full_small_v)
        loads[1].wait()
        arrivals[6][0].wait_recv()
        arrivals[7].wait_recv()
        gains_of(1, v.s_w_small_v[0, :, :])
        v.s_h_v[...] = (normalize(v.x_v[...].astype(full))[0] * v.s_gains[1, 0:1, :]).astype(low)
        moves.save(v.s_h_v, v.h_v)
        for at, piece in enumerate(plane.document(0)):
            first = rows.split + at * rows.visual
            v.gate_rows[first : first + rows.visual, :] = dot(v.s_h_v[piece, :], v.s_w_small_v[0, :, :])

    def project_visual():
        moves.save(v.s_w_qkv_v, v.full_qkv_v)
        v.qkv_v[...] = dot(v.s_h_v[...], v.s_w_qkv_v[0, :, :]).astype(low)
        landing = lambda chip, half: v.landing_qkv.at[chip, half * rows.visual : (half + 1) * rows.visual]
        arrivals[8] = []
        for half, piece in enumerate(plane.document(0)):
            v.landing_qkv[plane.chip(), half * rows.visual : (half + 1) * rows.visual, :] = v.qkv_v[piece, :]
        for at, step in enumerate(plane.steps):
            for half, piece in enumerate(plane.document(1 + at)):
                source = v.qkv_v.at[piece]
                arrivals[8].append(
                    moves.peer(source, landing(plane.chip(), half), step, landing(plane.chip(step), half))
                )

    def receive_visual():
        for arrival in arrivals[8]:
            arrival.wait_recv()
        pair = 3 * lane
        for at in range(heads // 2):
            v.s_qkv[rows.split :, at * pair : (at + 1) * pair] = v.landing_qkv[at, :, :]
            span = slice(at * lane, (at + 1) * lane)
            queries = v.s_qkv[:, at * pair : at * pair + lane] * jnp.asarray(scale, low)
            v.q_t[span, :] = queries.T
            v.v_t[span, :] = v.s_qkv[:, at * pair + 2 * lane : (at + 1) * pair].T
        v.s_gates_t[...] = jax.nn.sigmoid(v.gate_rows[...].T[:8, :])
        moves.save(v.s_gains, v.gains)
        moves.save(v.s_qkv, v.qkv)
        moves.save(v.s_gates_t, v.gates_t)

    def mix():
        moves.save(v.s_text_t, v.text_t)
        moves.save(v.s_visual_t, v.visual_t)
        moves.save(v.s_logs, v.logs)
        is_text = lax.broadcasted_iota(jnp.int32, (1, rows.count), 1) < rows.split
        for head in range(heads):
            span = slice(head * head_width, (head + 1) * head_width)
            gate = v.s_gates_t[head : head + 1, :]
            to_text = jnp.where(is_text, gate, 1.0 - gate)
            v.s_mix_t[span, :] = (
                to_text * v.s_text_t[span, :] + (1.0 - to_text) * v.s_visual_t[span, :]
            ).astype(low)
        v.mix[...] = v.s_mix_t[...].T
        moves.save(v.s_mix_t, v.mix_t)

    def branch():
        moves.save(v.s_w_out, v.full_out)
        for s, (first, last) in enumerate(rows.spans):

            def columns(piece):
                v.wide[first:last, piece] = dot(v.mix[first:last, :], v.s_w_out[s, :, piece])

            over_columns(0, v.wide.shape[1], 256, columns)
        arrivals[0] = rows.swap_parts(moves, v.wide, v.received)

    def spread_dy():
        arrivals[2] = plane.spread(v.visual_dy.at[0], v.s_dy_v)

    def relay_dy():
        arrivals[10] = plane.relay(v.s_dy_v, arrivals[2][1])

    def pass_dy():
        arrivals[3] = plane.pass_on(v.s_dy_v, arrivals[2][1], arrivals[10])

    def middle_rows(s, x, ref, start):
        arrivals[0][s].wait_recv()

        def body(piece, packed):
            to = pl.ds(pl.multiple_of(packed.start - start, row_tile), packed.size)
            value = x[to, :].astype(full) + v.wide[piece, :] + v.received[packed, :]
            v.s_middle[packed, :] = value
            ref[to, :] = (normalize(value)[0] * v.s_gains[s, 1:2, :]).astype(low)

        rows.over_own(s, body)
        packed = slice(*rows.packed[s])
        moves.save(v.s_middle.at[packed], v.middle.at[packed])

    def middle_visual():
        middle_rows(1, v.x_v, v.s_hm_v, rows.packed[1][0])
        arrivals[4] = plane.spread(plane.part(v.s_hm_v, 0), v.s_hm_v)

    def middle_text():
        middle_rows(0, v.x, v.s_hm, 0)
        arrivals[1] = rows.swap_own(moves, v.s_hm, 0)

    def relay_hm():
        arrivals[11] = plane.relay(v.s_hm_v, arrivals[4][1])

    def pass_hm():
        arrivals[5] = plane.pass_on(v.s_hm_v, arrivals[4][1], arrivals[11])

    def up_part(hm, w_up, act_ref, slope_ref, start, stop):
        size = 256 if (stop - start) % 256 == 0 else lane

        def columns(piece):
            act, slope = gelu_both(dot(hm[...], w_up[0, :, piece]))
            act_ref[:, piece] = act.astype(low)
            slope_ref[:, piece] = slope.astype(low)

        over_columns(start, stop, size, columns)

    def up_first():
        moves.save(v.s_w_up, v.full_up)
        arrivals[1].wait_recv()
        loads[2].wait()
        swaps[1].wait_recv()
        moves.save(v.s_hm, v.hm)
        moves.save(v.s_dy, v.dy)
        up_part(v.s_hm, v.s_w_up, v.s_act, v.s_slope, 0, hidden // 2)

    def up_second():
        up_part(v.s_hm, v.s_w_up, v.s_act, v.s_slope, hidden // 2, hidden)
        moves.save(v.s_act, v.act)
        moves.save(v.s_slope, v.slope)

    def up_visual():
        moves.save(v.s_w_up_v, v.full_up_v)
        arrivals[4][0].wait_recv()
        arrivals[5].wait_recv()
        moves.save(v.s_hm_v, v.hm_v)
        up_part(v.s_hm_v, v.s_w_up_v, v.s_act_v, v.s_slope_v, 0, v.s_act_v.shape[1])
        moves.save(v.s_act_v, v.act_v)
        moves.save(v.s_slope_v, v.slope_v)

    def down_part(act, dy, part):
        count = act.shape[1]

        def columns(piece):
            part[0, piece, :] = dot_rows(act[:, piece], dy[...]).astype(low)

        over_columns(0, count, 256 if count % 256 == 0 else lane, columns)

    def down_text():
        down_part(v.s_act, v.s_dy, v.s_part_down)
        moves.save(v.s_part_down, v.part_down)

    def down_visual():
        loads[3].wait()
        arrivals[2][0].wait_recv()
        arrivals[3].wait_recv()
        moves.save(v.s_dy_v, v.dy_v)
        down_part(v.s_act_v, v.s_dy_v, v.s_part_down_v)
        moves.save(v.s_part_down_v, v.part_down_v)

    stages = [prepare, norm, lower_text, project_text, lower_visual, project_visual, receive_visual]
    stages += [functools.partial(attend_head, rows, head_width, v, head) for head in range(heads)]
    stages += [mix, branch, middle_visual, middle_text, pass_hm, up_first, up_second, up_visual]
    stages += [down_text, down_visual, spread_dy, pass_dy, spread_x, pass_x]
    stages += [prepare_qkv, relay_x, relay_dy, relay_hm]
    gather.run(plan, stages)
    moves.finish()
    gather.finish()


def front(n_docs, heads, scale, pieces, plan, inputs):
    line_size = n_docs // 4
    count = 2 * (inputs.text.shape[1] + inputs.visual.shape[1])
    dim = inputs.w_out.shape[2]
    width, hidden = inputs.w_qkv.shape[2] // 6, inputs.w_up.shape[2] // 2
    text, plane = 2 * inputs.text.shape[1], 8 * inputs.visual.shape[1]
    wide = 3 * width + lane
    shard = inputs.w_qkv.shape[1]
    kept = FrontKept(
        s_h=((text, dim), low),
        s_h_v=((plane, dim), low),
        s_qkv=((count, 3 * width), low),
        s_gates_t=((8, count), full),
        s_text_t=((width, count), full),
        s_visual_t=((width, count), full),
        s_logs=((16, count), full),
        s_mix_t=((width, count), low),
        s_middle=((count // 2, dim), full),
        s_hm=((text, dim), low),
        s_hm_v=((plane, dim), low),
        s_act=((text, hidden), low),
        s_act_v=((plane, hidden // 4), low),
        s_slope=((text, hidden), low),
        s_slope_v=((plane, hidden // 4), low),
        s_part_down=((1, hidden, dim), low),
        s_part_down_v=((1, hidden // 4, dim), low),
        s_dy=((text, dim), low),
        s_dy_v=((plane, dim), low),
        s_gains=((2, 2, dim), full),
        s_bias=((count, lane), full),
    )
    weights = (
        ((1, dim, wide), low),
        ((1, dim, hidden), low),
        ((2, width, dim), low),
        ((1, hidden, dim), low),
        ((1, dim, hidden // 4), low),
        ((1, hidden // 4, dim), low),
        ((1, dim, 3 * lane), low),
        ((1, dim, lane), low),
    )
    shards = same_as(inputs[:7])
    scratch = FrontScratch(
        shard_qkv=shards[0],
        shard_gate=shards[1],
        shard_up=shards[2],
        shard_attn=shards[3],
        shard_ffn=shards[4],
        shard_text_mask=shards[5],
        shard_visual_mask=shards[6],
        own_qkv=((1, shard, wide), low),
        own_qkv_v=((4, shard, 3 * lane), low),
        own_small_v=((1, shard, lane), low),
        own_up=((1, shard, hidden), low),
        own_up_v=((4, shard, hidden // 4), low),
        s_w_qkv=weights[0],
        s_w_qkv_v=weights[6],
        s_w_small_v=weights[7],
        s_w_up=weights[1],
        s_w_up_v=weights[4],
        s_w_out=weights[2],
        x=((text, dim), low),
        x_v=((plane, dim), low),
        wide=((count, dim), full),
        qkv_v=((plane, 3 * lane), low),
        landing_qkv=((4, 2 * inputs.visual.shape[1], 3 * lane), low),
        received=((count // 2, dim), full),
        gate_rows=((count, lane), full),
        q_t=((width, count), low),
        v_t=((width, count), low),
        mix=((count, width), low),
    )
    results = FrontOut(*weights, *kept)
    values = pl.pallas_call(
        functools.partial(front_kernel, line_size, heads, scale, pieces, plan),
        out_shape=shapes_of(results),
        in_specs=specs_of(len(inputs), 0),
        out_specs=specs_of(len(results), 0),
        scratch_shapes=scratch_of(kept)
        + scratch_of(scratch)
        + sems((len(pieces), 5), (len(pieces), n_docs), len(pieces), 39, 26, 26),
        compiler_params=pltpu.CompilerParams(
            collective_id=0, has_side_effects=True, vmem_limit_bytes=vmem_limit
        ),
        name="gather_and_front",
    )(*inputs)
    return FrontOut(*values)


def scatter_buffers(pieces, arrays, splits, n_docs):
    line_size = n_docs // 4
    group = []
    for piece in pieces:
        ends = line_size // 2 if splits[piece.array] else line_size
        block = (piece.rows, arrays[piece.array][0][2])
        if piece.route == lines_first:
            group += [((ends, *block), low)] * 5
        elif piece.route == line_only:
            group += [((1, row_tile, lane), low)] * 3 + [((ends, 1, *block), low)] * 2
        else:
            group += [((1, *block), low)] * 3 + [((ends, 4, *block), low)] * 2
    return scratch_of(group)


def grouped(refs, size):
    return [refs[first : first + size] for first in range(0, len(refs), size)]


def norm_back(grad, normed, inverse, gain):
    scaled = grad * gain
    return inverse * (
        scaled
        - jnp.mean(scaled, -1, keepdims=True)
        - normed * jnp.mean(scaled * normed, -1, keepdims=True)
    )


class FfnIn(NamedTuple):
    full_down: object
    dy: object
    slope: object
    full_up: object
    part_down: object
    hm: object
    middle: object
    gains: object
    act: object
    full_out: object
    mix_t: object
    text_t: object
    visual_t: object
    gates_t: object
    full_down_v: object
    dy_v: object
    slope_v: object
    full_up_v: object
    part_down_v: object
    hm_v: object
    act_v: object


class FfnLoaded(NamedTuple):
    s_full_down: object
    s_dy: object
    s_slope: object
    s_full_up: object
    s_part_down: object
    s_hm: object
    s_middle: object
    s_gains: object
    s_act: object
    s_full_out: object
    s_mix_t: object
    s_text_t: object
    s_visual_t: object
    s_gates_t: object
    s_full_down_v: object
    s_dy_v: object
    s_slope_v: object
    s_full_up_v: object
    s_part_down_v: object
    s_hm_v: object
    s_act_v: object


class FfnOut(NamedTuple):
    text_out: object
    visual_out: object
    stage_down: object
    part_up: object
    part_up_v: object
    part_out: object
    grad_middle: object
    gain_part: object
    gate_grad_t: object
    text_grad_t: object
    visual_grad_t: object


class FfnScratch(NamedTuple):
    s_part_up: object
    s_part_up_v: object
    s_part_out: object
    s_grad_middle: object
    s_gain_part: object
    s_gate_grad_t: object
    s_text_grad_t: object
    s_visual_grad_t: object
    stage: object
    wide: object
    wide_out: object
    received: object
    received_out: object
    branch: object
    result: object
    mix_grad: object
    mix_grad_t: object
    wide_v: object
    received_v: object
    outgoing_v: object
    landing_v: object
    wide_out_v: object
    received_out_v: object
    outgoing_out_v: object
    landing_out_v: object


def ffn_kernel(line_size, heads, pieces, plan, *refs):
    groups = []
    for group in (FfnIn, FfnOut, FfnLoaded, FfnScratch):
        count = len(group._fields)
        groups.append(group(*refs[:count]))
        refs = refs[count:]
    v = merged(*groups)
    buffers = grouped(refs[: 5 * len(pieces)], 5)
    send_sems, recv_sems, *move_sems = refs[5 * len(pieces) :]
    place = Place(line_size)
    moves = Moves(place, *move_sems)
    rows = Rows(v.text_out.shape[1], v.visual_out.shape[1])
    width = v.mix_t.shape[0]
    head_width = width // heads
    dim = v.hm.shape[1]
    arrivals = {}

    plane = Plane(place, moves, rows.visual)

    def finish_rows(piece, total):
        add_rows(v.stage.at[piece.array], total, piece.first)

    scatter = Scatter(
        place,
        pieces,
        (False, False),
        (v.part_down, v.part_down_v),
        (v.s_part_down, v.s_part_down_v),
        buffers,
        send_sems,
        recv_sems,
        finish_rows,
    )
    place.greet()
    loads = FfnIn(*(moves.local(source, target) for source, target in zip(groups[0], groups[2])))
    place.meet()

    def hidden(dy, w_down, slope):
        count = slope.shape[1]

        def columns(piece):
            grad = dot_back(dy[...], w_down[0, piece, :])
            slope[:, piece] = (grad * slope[:, piece].astype(full)).astype(low)

        over_columns(0, count, 256 if count % 256 == 0 else lane, columns)

    def hidden_visual():
        loads.full_down_v.wait()
        loads.dy_v.wait()
        loads.slope_v.wait()
        hidden(v.s_dy_v, v.s_full_down_v, v.s_slope_v)

    def hidden_text():
        loads.full_down.wait()
        loads.dy.wait()
        loads.slope.wait()
        hidden(v.s_dy, v.s_full_down, v.s_slope)
        loads.part_down.wait()
        loads.part_down_v.wait()

    def back_visual():
        loads.full_up_v.wait()
        v.wide_v[...] = dot_back(v.s_slope_v[...], v.s_full_up_v[0, :, :])
        arrivals[0] = plane.halve(v.wide_v, v.received_v)

    def share_visual():
        arrivals[0].wait_recv()
        arrivals[1] = plane.share(v.wide_v, v.received_v, v.outgoing_v, v.landing_v)

    def back_text():
        loads.full_up.wait()

        def columns(piece):
            v.wide[:, piece] = dot_back(v.s_slope[...], v.s_full_up[0, piece, :])

        over_columns(0, dim, 256, columns)
        arrivals[2] = rows.swap_parts(moves, v.wide, v.received, (0,))[0]

    def up_part(hm, slope, part):
        def columns(piece):
            part[0, piece, :] = dot_rows(hm[:, piece], slope[...]).astype(low)

        over_columns(0, dim, 256, columns)

    def up_text():
        loads.hm.wait()
        up_part(v.s_hm, v.s_slope, v.s_part_up)
        moves.save(v.s_part_up, v.part_up)

    def up_visual():
        loads.hm_v.wait()
        up_part(v.s_hm_v, v.s_slope_v, v.s_part_up_v)
        moves.save(v.s_part_up_v, v.part_up_v)

    def middle_rows(s, piece, packed, grad, dy):
        normed, inverse = normalize(v.s_middle[packed, :])
        v.s_gain_part[s, 0:1, :] += jnp.sum(grad * normed, 0, keepdims=True)
        grad = dy.astype(full) + norm_back(grad, normed, inverse, v.s_gains[s, 1:2, :])
        v.s_grad_middle[packed, :] = grad
        v.branch[piece, :] = grad.astype(low)

    def middle_visual():
        loads.middle.wait()
        loads.gains.wait()
        v.s_gain_part[...] = jnp.zeros_like(v.s_gain_part)
        for arrival in arrivals[1]:
            arrival.wait_recv()
        grad = plane.total(v.wide_v, v.received_v, v.landing_v)
        middle_rows(1, slice(*rows.own[1]), slice(*rows.packed[1]), grad, v.s_dy_v[: rows.visual, :])
        arrivals[3] = rows.swap_own(moves, v.branch, 1)

    def middle_text():
        arrivals[2].wait_recv()

        def body(piece, packed):
            grad = v.wide[piece, :] + v.received[packed, :]
            middle_rows(0, piece, packed, grad, v.s_dy[piece, :])

        rows.over_own(0, body)
        arrivals[4] = rows.swap_own(moves, v.branch, 0)
        moves.save(v.s_gain_part, v.gain_part)
        moves.save(v.s_grad_middle, v.grad_middle)

    def result_text():
        loads.act.wait()

        def columns(piece):
            v.wide_out[:, piece] = dot(v.s_act[...], v.s_full_down[0, :, piece])

        over_columns(0, dim, 256, columns)
        arrivals[5] = rows.swap_parts(moves, v.wide_out, v.received_out, (0,))[0]

    def result_visual():
        loads.act_v.wait()
        v.wide_out_v[...] = dot(v.s_act_v[...], v.s_full_down_v[0, :, :])
        arrivals[6] = plane.halve(v.wide_out_v, v.received_out_v)

    def share_result():
        arrivals[6].wait_recv()
        arrivals[7] = plane.share(v.wide_out_v, v.received_out_v, v.outgoing_out_v, v.landing_out_v)

    def out_part():
        loads.full_out.wait()
        loads.mix_t.wait()
        for s, (first, last) in enumerate(rows.spans):
            arrivals[4 - s].wait_recv()
            v.s_part_out[s, :, :] = dot(v.s_mix_t[:, first:last], v.branch[first:last, :]).astype(low)
            v.mix_grad[first:last, :] = dot_back(v.branch[first:last, :], v.s_full_out[s, :, :])
        moves.save(v.s_part_out, v.part_out)

    def gates():
        loads.text_t.wait()
        loads.visual_t.wait()
        loads.gates_t.wait()
        v.mix_grad_t[...] = v.mix_grad[...].T
        is_text = lax.broadcasted_iota(jnp.int32, (1, rows.count), 1) < rows.split
        for head in range(heads):
            span = slice(head * head_width, (head + 1) * head_width)
            gate = v.s_gates_t[head : head + 1, :]
            to_text = jnp.where(is_text, gate, 1.0 - gate)
            grad = v.mix_grad_t[span, :]
            toward = jnp.sum(grad * (v.s_text_t[span, :] - v.s_visual_t[span, :]), 0, keepdims=True)
            v.s_gate_grad_t[head : head + 1, :] = (
                jnp.where(is_text, toward, -toward) * gate * (1.0 - gate)
            )
            v.s_text_grad_t[span, :] = (to_text * grad).astype(low)
            v.s_visual_grad_t[span, :] = ((1.0 - to_text) * grad).astype(low)
        v.s_gate_grad_t[heads:, :] = jnp.zeros((8 - heads, rows.count), full)
        moves.save(v.s_gate_grad_t, v.gate_grad_t)
        moves.save(v.s_text_grad_t, v.text_grad_t)
        moves.save(v.s_visual_grad_t, v.visual_grad_t)

    def finish_text():
        arrivals[5].wait_recv()

        def body(piece, packed):
            v.result[packed, :] = (
                v.s_middle[packed, :] + v.wide_out[piece, :] + v.received_out[packed, :]
            ).astype(low)

        rows.over_own(0, body)
        moves.save(v.result.at[slice(*rows.packed[0])], v.text_out.at[0])

    def finish_visual():
        for arrival in arrivals[7]:
            arrival.wait_recv()
        packed = slice(*rows.packed[1])
        total = plane.total(v.wide_out_v, v.received_out_v, v.landing_out_v)
        v.result[packed, :] = (v.s_middle[packed, :] + total).astype(low)
        moves.save(v.result.at[packed], v.visual_out.at[0])

    stages = [hidden_visual, back_visual, hidden_text, share_visual, back_text, up_text, up_visual]
    stages += [middle_visual, middle_text, result_text, result_visual, out_part, gates, share_result]
    scatter.run(plan, stages + [finish_text, finish_visual])
    moves.save(v.stage, v.stage_down)
    moves.finish()
    scatter.finish()


def ffn_back(n_docs, heads, pieces, plan, text, visual, inputs):
    line_size = n_docs // 4
    hidden = inputs.act.shape[1]
    width, count = inputs.mix_t.shape
    dim = inputs.hm.shape[1]
    rows = inputs.part_down.shape[1] // n_docs
    plane = 8 * visual.shape[1]
    scratch = FfnScratch(
        s_part_up=((1, dim, hidden), low),
        s_part_up_v=((1, dim, hidden // 4), low),
        s_part_out=((2, width, dim), low),
        s_grad_middle=((count // 2, dim), full),
        s_gain_part=((2, 8, dim), full),
        s_gate_grad_t=((8, count), full),
        s_text_grad_t=((width, count), low),
        s_visual_grad_t=((width, count), low),
        stage=((2, rows, dim), full),
        wide=((2 * text.shape[1], dim), full),
        wide_out=((2 * text.shape[1], dim), full),
        received=((text.shape[1], dim), full),
        received_out=((text.shape[1], dim), full),
        branch=((count, dim), low),
        result=((count // 2, dim), low),
        mix_grad=((count, width), full),
        mix_grad_t=((width, count), full),
        wide_v=((plane, dim), full),
        received_v=((plane // 2, dim), full),
        outgoing_v=((3 * plane // 8, dim), low),
        landing_v=((3 * plane // 8, dim), low),
        wide_out_v=((plane, dim), full),
        received_out_v=((plane // 2, dim), full),
        outgoing_out_v=((3 * plane // 8, dim), low),
        landing_out_v=((3 * plane // 8, dim), low),
    )
    results = FfnOut(
        (text.shape, low), (visual.shape, low), scratch.stage, *scratch[:8]
    )
    loaded = same_as(inputs)
    values = pl.pallas_call(
        functools.partial(ffn_kernel, line_size, heads, pieces, plan),
        out_shape=shapes_of(results),
        in_specs=specs_of(len(inputs), 0),
        out_specs=specs_of(len(results), 0),
        scratch_shapes=scratch_of(loaded)
        + scratch_of(scratch)
        + scatter_buffers(pieces, same_as([inputs.part_down, inputs.part_down_v]), (False, False), n_docs)
        + sems(len(pieces), arrival_offsets(pieces, line_size)[-1], 32, 12, 12),
        compiler_params=pltpu.CompilerParams(
            collective_id=1, has_side_effects=True, vmem_limit_bytes=vmem_limit
        ),
        name="ffn_back_and_scatter",
    )(*inputs)
    return FfnOut(*values)


class AttentionIn(NamedTuple):
    qkv: object
    logs: object
    text_t: object
    visual_t: object
    text_grad_t: object
    visual_grad_t: object
    bias: object
    part_up: object
    part_up_v: object
    part_out: object
    gate_grad_t: object
    full_qkv: object
    full_qkv_v: object
    full_small_v: object
    h: object
    h_v: object
    grad_middle: object
    gains: object
    gain_part: object
    stage_down: object
    text: object
    visual: object


class AttentionLoaded(NamedTuple):
    s_qkv: object
    s_logs: object
    s_text_t: object
    s_visual_t: object
    s_text_grad_t: object
    s_visual_grad_t: object
    s_bias: object
    s_part_up: object
    s_part_up_v: object
    s_part_out: object
    s_gate_grad_t: object
    s_full_qkv: object
    s_full_qkv_v: object
    s_full_small_v: object
    s_h: object
    s_h_v: object
    s_grad_middle: object
    s_gains: object
    s_gain_part: object
    s_stage_down: object


class AttentionOut(NamedTuple):
    text_grad: object
    visual_grad: object
    grad_down: object
    grad_qkv: object
    grad_gate: object
    grad_up: object
    grad_out: object
    grad_gain_attn: object
    grad_gain_ffn: object


class AttentionScratch(NamedTuple):
    part_qkv: object
    part_qkv_v: object
    part_small: object
    x: object
    q_t: object
    k_t: object
    query_grad_t: object
    text_grad_n: object
    visual_grad_n: object
    key_sum: object
    value_sum: object
    grad_wide: object
    wide: object
    received: object
    grad_v: object
    wide_v: object
    received_v: object
    outgoing_v: object
    landing_v: object
    gain_sum: object
    gains_row: object
    stage_up: object
    stage_out: object
    stage_qkv: object
    stage_up_v: object
    stage_qkv_v: object
    stage_small: object
    own_qkv: object
    peer_up: object
    peer_up_v: object
    peer_small: object
    s_grad_up: object
    s_grad_gate: object
    s_grad_gain_attn: object
    s_grad_gain_ffn: object


def attend_head_back(rows, head_width, scale, v, number):
    pair = 2 * head_width
    at, odd = number // 2, number % 2
    columns = [slice((3 * at + third) * pair, (3 * at + third + 1) * pair) for third in range(3)]
    wide = slice(at * pair, (at + 1) * pair)
    keys, values = v.s_qkv[:, columns[1]], v.s_qkv[:, columns[2]]
    if not odd:
        v.key_sum[...] = jnp.zeros_like(v.key_sum)
        v.value_sum[...] = jnp.zeros_like(v.value_sum)
    mine = lax.broadcasted_iota(jnp.int32, (1, pair), 1) // head_width == odd
    bias = v.s_bias[:, 0:1]
    sets = (
        (v.s_text_t, v.s_text_grad_t, v.text_grad_n),
        (v.s_visual_t, v.s_visual_grad_t, v.visual_grad_n),
    )
    head = slice(number * head_width, (number + 1) * head_width)
    for first, last in query_spans(rows.count):
        scores = dot(keys, head_wide(v.q_t[head, first:last], odd)) + bias
        queries = jnp.where(mine, v.s_qkv[first:last, columns[0]] * jnp.asarray(scale, low), 0)
        pieces = []
        for t, (output_t, grad_t, grad) in enumerate(sets):
            start, stop = rows.spans[t]
            out_grad = grad_t[head, first:last]
            delta = jnp.sum(out_grad.astype(full) * output_t[head, first:last], 0, keepdims=True)
            row = 8 * t + number
            probs = jnp.exp(scores[start:stop] - v.s_logs[row : row + 1, first:last])
            grad_probs = dot(values[start:stop], head_wide(out_grad, odd))
            grad_scores = (probs * (grad_probs - delta)).astype(low)
            natural = jnp.where(mine, grad[first:last, wide], 0)
            v.value_sum[start:stop, :] += dot(probs.astype(low), natural)
            v.key_sum[start:stop, :] += dot(grad_scores, queries)
            pieces.append(grad_scores)
        v.query_grad_t[head, first:last] = (
            dot(v.k_t[head, :], jnp.concatenate(pieces, 0)) * scale
        ).astype(low)
    if odd:
        v.grad_wide[:, columns[0]] = v.query_grad_t[wide, :].T
        v.grad_wide[:, columns[1]] = v.key_sum[...].astype(low)
        v.grad_wide[:, columns[2]] = v.value_sum[...].astype(low)


def attention_kernel(line_size, heads, scale, block, pieces, plan, *refs):
    groups = []
    for group in (AttentionIn, AttentionOut, AttentionLoaded, AttentionScratch):
        count = len(group._fields)
        groups.append(group(*refs[:count]))
        refs = refs[count:]
    v = merged(*groups)
    buffers = grouped(refs[: 5 * len(pieces)], 5)
    send_sems, recv_sems, *move_sems = refs[5 * len(pieces) :]
    place = Place(line_size)
    core = place.core
    moves = Moves(place, *move_sems)
    rows = Rows(v.text.shape[1], v.visual.shape[1])
    width = v.qkv.shape[1] // 3
    head_width = width // heads
    dim = v.h.shape[1]
    stages_of = (v.stage_up, v.stage_out, v.stage_qkv, v.stage_up_v, v.stage_qkv_v, v.stage_small)
    arrivals = {}
    plane = Plane(place, moves, rows.visual)

    def finish_rows(piece, total, quad=quads[0]):
        part = place.index(0, *quad) if piece.route == plane_shared else piece.part
        add_rows(stages_of[piece.array].at[part], total, piece.first)

    scatter = Scatter(
        place,
        pieces,
        (False, True, False, False, False, False),
        (v.part_up, v.part_out, v.part_qkv, v.part_up_v, v.part_qkv_v, v.part_small),
        (v.s_part_up, v.s_part_out, v.part_qkv, v.s_part_up_v, v.part_qkv_v, v.part_small),
        buffers,
        send_sems,
        recv_sems,
        finish_rows,
    )
    place.greet()
    loads = AttentionIn(
        *(moves.local(source, target) for source, target in zip(groups[0], groups[2])),
        *(moves.local(ref.at[0], v.x.at[slice(*rows.packed[s])]) for s, ref in enumerate((v.text, v.visual))),
    )
    place.meet()

    def prepare():
        for load in loads[:7]:
            load.wait()
        for at in range(heads // 2):
            span, first = slice(at * lane, (at + 1) * lane), 3 * at * lane
            v.q_t[span, :] = (v.s_qkv[:, first : first + lane] * jnp.asarray(scale, low)).T
            v.k_t[span, :] = v.s_qkv[:, first + lane : first + 2 * lane].T
        v.text_grad_n[...] = v.s_text_grad_t[...].T
        v.visual_grad_n[...] = v.s_visual_grad_t[...].T
        loads.part_up.wait()
        loads.part_up_v.wait()
        loads.part_out.wait()

    def send_visual():
        loads.gate_grad_t.wait()
        empty = jnp.zeros((lane - 8, rows.count), full)
        v.grad_wide[:, 3 * width : 3 * width + lane] = (
            jnp.concatenate([v.s_gate_grad_t[...], empty], 0).T.astype(low)
        )
        v.grad_wide[:, 3 * width + lane :] = jnp.zeros((rows.count, 2 * lane), low)
        arrivals[4] = []
        pair = 3 * lane
        for half, piece in enumerate(plane.document(0)):
            first = rows.split + half * rows.visual
            span = slice(first, first + rows.visual)
            of = lambda step: v.grad_wide.at[span, pl.ds(pl.multiple_of(plane.chip(step) * pair, lane), pair)]
            arrivals[4].append(moves.local(of(None), v.grad_v.at[piece]).wait)
            for at, step in enumerate(plane.steps):
                target = v.grad_v.at[plane.document(1 + at)[half]]
                arrivals[4].append(moves.peer(of(step), target, step).wait_recv)

    def back_text():
        loads.full_qkv.wait()

        def columns(piece):
            grad = v.grad_wide[: rows.split, : 3 * width + lane]
            v.wide[:, piece] = dot_back(grad, v.s_full_qkv[0, piece, :])

        over_columns(0, dim, 256, columns)
        arrivals[0] = rows.swap_parts(moves, v.wide, v.received, (0,))[0]

    def text_part():
        loads.h.wait()

        def columns(piece):
            grad = dot_rows(v.s_h[:, piece], v.grad_wide[: rows.split, : 3 * width + lane])
            v.part_qkv[0, piece, :] = grad[:, : 3 * width].astype(low)
            v.gain_sum[0, piece, :] = grad[:, 3 * width :]

        over_columns(0, dim, 256, columns)

    def back_visual():
        loads.full_qkv_v.wait()
        loads.full_small_v.wait()
        for wait in arrivals[4]:
            wait()
        v.wide_v[...] = dot_back(v.grad_v[...], v.s_full_qkv_v[0, :, :])
        for half, piece in enumerate(plane.document(0)):
            first = rows.split + half * rows.visual
            small = v.grad_wide[first : first + rows.visual, 3 * width : 3 * width + lane]
            v.wide_v[piece, :] += dot_back(small, v.s_full_small_v[0, :, :])
        arrivals[5] = plane.halve(v.wide_v, v.received_v)

    def visual_part():
        loads.h_v.wait()

        def columns(piece):
            v.part_qkv_v[0, piece, :] = dot_rows(v.s_h_v[:, piece], v.grad_v[...]).astype(low)

        over_columns(0, dim, 256, columns)
        total = 0.0
        for half, piece in enumerate(plane.document(0)):
            first = rows.split + half * rows.visual
            small = v.grad_wide[first : first + rows.visual, 3 * width : 3 * width + lane]
            total = total + dot_rows(v.s_h_v[piece, :], small)
        v.gain_sum[1, :, :] = total

    def share_visual():
        arrivals[5].wait_recv()
        arrivals[6] = plane.share(v.wide_v, v.received_v, v.outgoing_v, v.landing_v)

    def token_rows(s, packed, grad):
        normed, inverse = normalize(v.x[packed, :].astype(full))
        v.gains_row[s, heads : heads + 1, :] += jnp.sum(grad * normed, 0, keepdims=True)
        v.s_grad_middle[packed, :] += norm_back(grad, normed, inverse, v.s_gains[s, 0:1, :])

    def small_part(s):
        small = v.gain_sum[s, :, :] + v.gains_row[s, :, :].T
        v.part_small[s, :, :] = small.astype(low)
        ref = (v.text_grad, v.visual_grad)[s]
        moves.save(v.s_grad_middle.at[slice(*rows.packed[s])], ref.at[0])

    def tokens_text():
        loads.grad_middle.wait()
        loads.gains.wait()
        loads.gain_part.wait()
        v.gains_row[...] = jnp.zeros_like(v.gains_row)
        for s in range(2):
            loads[-2 + s].wait()
            v.gains_row[s, heads + 1 : heads + 2, :] = v.s_gain_part[s, 0:1, :]
        arrivals[0].wait_recv()

        def body(piece, packed):
            token_rows(0, packed, v.wide[piece, :] + v.received[packed, :])

        rows.over_own(0, body)
        small_part(0)

    def tokens_visual():
        for arrival in arrivals[6]:
            arrival.wait_recv()
        grad = plane.total(v.wide_v, v.received_v, v.landing_v)
        token_rows(1, slice(*rows.packed[1]), grad)
        small_part(1)

    def share_down():
        loads.stage_down.wait()
        block = v.s_stage_down.shape[1]
        mine = lambda of: v.grad_down.at[:, pl.ds(pl.multiple_of(of * block, row_tile), block), :]
        moves.save(v.s_stage_down, mine(core))
        arrivals[3] = moves.across(v.s_stage_down, mine(core), mine(1 - core))

    def share_up():
        arrivals[1] = moves.across(v.stage_up, v.peer_up)
        arrivals[2] = moves.across(v.stage_up_v, v.peer_up_v)

    def share_out():
        owner = place.z // (line_size // 2) == core
        moves_out = (
            pltpu.make_async_copy(v.stage_out, v.grad_out, moves.local_sems.at[moves.locals]),
            pltpu.make_async_remote_copy(
                src_ref=v.stage_out,
                dst_ref=v.grad_out,
                send_sem=moves.send_sems.at[moves.remotes],
                recv_sem=moves.recv_sems.at[moves.remotes],
                device_id=moves.other,
                device_id_type=MESH,
            ),
        )
        moves.locals += 1
        moves.remotes += 1

        def start():
            for move in moves_out:
                move.start()

        def wait():
            moves_out[0].wait()
            moves_out[1].wait_send()

        pl.when(owner)(start)
        moves.to_end.append(lambda: pl.when(owner)(wait))
        moves.to_end.append(lambda: pl.when(jnp.logical_not(owner))(lambda: moves_out[1].wait_recv()))

    def finish_up():
        arrivals[1].wait_recv()
        arrivals[2].wait_recv()
        first = core == 0
        count = v.stage_up.shape[2] // block
        for s in range(2):
            pieces = []
            for at in range(count):
                if s == 0:
                    span = slice(at * block, (at + 1) * block)
                    own, peer = (ref[0, :, span] for ref in (v.stage_up, v.peer_up))
                else:
                    span = slice(at // 4 * block, (at // 4 + 1) * block)
                    own, peer = (ref[at % 4, :, span] for ref in (v.stage_up_v, v.peer_up_v))
                pieces += [jnp.where(first, own, peer), jnp.where(first, peer, own)]
            v.s_grad_up[s, :, :] = jnp.concatenate(pieces, 1)
        moves.save(v.s_grad_up, v.grad_up)

    stages = [prepare]
    stages += [functools.partial(attend_head_back, rows, head_width, scale, v, head) for head in range(heads)]
    stages += [send_visual, back_text, text_part, back_visual, visual_part, share_visual]
    stages += [tokens_text, tokens_visual, share_up, share_out, finish_up, share_down]
    scatter.run(plan, stages)

    def mine(third, of):
        first = third * 2 * width + of * width
        return v.grad_qkv.at[:, :, pl.ds(pl.multiple_of(first, lane), width)]

    last = [moves.across(v.stage_small, v.peer_small)]
    for third in range(3):
        for at in range(heads // 2):
            to = slice(at * lane, (at + 1) * lane)
            v.own_qkv[third, 0, :, to] = v.stage_qkv[0, :, (3 * at + third) * lane : (3 * at + third + 1) * lane]
            v.own_qkv[third, 1, :, to] = v.stage_qkv_v[at, :, third * lane : (third + 1) * lane]
        source = v.own_qkv.at[third]
        moves.save(source, mine(third, core))
        last.append(moves.across(source, mine(third, core), mine(third, 1 - core)))
    last[0].wait_recv()
    for s in range(2):
        own, peer = v.stage_small[s, :, :], v.peer_small[s, :, :]
        columns = own.shape[0]
        empty = jnp.zeros((lane - columns, lane), full)
        own, peer = (jnp.concatenate([value, empty], 0).T[:, :columns] for value in (own, peer))
        v.s_grad_gate[:heads, s, :] = jnp.where(core == 0, own, peer)[:heads]
        v.s_grad_gate[heads:, s, :] = jnp.where(core == 0, peer, own)[:heads]
        both = own + peer
        v.s_grad_gain_attn[s : s + 1, :] = both[heads : heads + 1]
        v.s_grad_gain_ffn[s : s + 1, :] = both[heads + 1 : heads + 2]
    moves.save(v.s_grad_gate, v.grad_gate)
    moves.save(v.s_grad_gain_attn, v.grad_gain_attn)
    moves.save(v.s_grad_gain_ffn, v.grad_gain_ffn)
    for arrival in last[1:] + [arrivals[3]]:
        arrival.wait_recv()
    moves.finish()
    scatter.finish()


def attention_back(n_docs, heads, scale, pieces, plan, inputs):
    line_size = n_docs // 4
    count, dim = inputs.qkv.shape[0], inputs.h.shape[1]
    width = inputs.qkv.shape[1] // 3
    text, visual = inputs.text.shape[1], inputs.visual.shape[1]
    hidden = inputs.part_up.shape[2]
    rows = dim // n_docs
    block = hidden // n_docs
    splits = (False, True, False, False, False, False)
    parts = (((1, dim, 3 * width), low), ((1, dim, 3 * lane), low), ((2, dim, lane), low))
    arrays = same_as([inputs.part_up, inputs.part_out]) + [parts[0]] + same_as([inputs.part_up_v])
    arrays += parts[1:]
    results = AttentionOut(
        text_grad=(inputs.text.shape, full),
        visual_grad=(inputs.visual.shape, full),
        grad_down=((2, 2 * inputs.stage_down.shape[1], dim), full),
        grad_qkv=((2, rows, 6 * width), full),
        grad_gate=((2 * heads, 2, rows), full),
        grad_up=((2, rows, 2 * hidden), full),
        grad_out=((2, rows, dim), full),
        grad_gain_attn=((2, rows), full),
        grad_gain_ffn=((2, rows), full),
    )
    scratch = AttentionScratch(
        part_qkv=parts[0],
        part_qkv_v=parts[1],
        part_small=parts[2],
        x=((count // 2, dim), low),
        q_t=((width, count), low),
        k_t=((width, count), low),
        query_grad_t=((width, count), low),
        text_grad_n=((count, width), low),
        visual_grad_n=((count, width), low),
        key_sum=((count, lane), full),
        value_sum=((count, lane), full),
        grad_wide=((count, 3 * width + 3 * lane), low),
        wide=((2 * text, dim), full),
        received=((text, dim), full),
        grad_v=((8 * visual, 3 * lane), low),
        wide_v=((8 * visual, dim), full),
        received_v=((4 * visual, dim), full),
        outgoing_v=((3 * visual, dim), low),
        landing_v=((3 * visual, dim), low),
        gain_sum=((2, dim, lane), full),
        gains_row=((2, lane, dim), full),
        stage_up=((1, rows, hidden), full),
        stage_out=((2, rows, dim), full),
        stage_qkv=((1, rows, 3 * width), full),
        stage_up_v=((4, rows, hidden // 4), full),
        stage_qkv_v=((4, rows, 3 * lane), full),
        stage_small=((2, rows, lane), full),
        own_qkv=((3, 2, rows, width), full),
        peer_up=((1, rows, hidden), full),
        peer_up_v=((4, rows, hidden // 4), full),
        peer_small=((2, rows, lane), full),
        s_grad_up=results.grad_up,
        s_grad_gate=results.grad_gate,
        s_grad_gain_attn=results.grad_gain_attn,
        s_grad_gain_ffn=results.grad_gain_ffn,
    )
    loaded = same_as(inputs[:-2])
    values = pl.pallas_call(
        functools.partial(attention_kernel, line_size, heads, scale, block, pieces, plan),
        out_shape=scratch_of(results),
        in_specs=specs_of(len(inputs), 0),
        out_specs=specs_of(len(results), len(results)),
        scratch_shapes=scratch_of(loaded)
        + scratch_of(scratch)
        + scatter_buffers(pieces, arrays, splits, n_docs)
        + sems(len(pieces), arrival_offsets(pieces, line_size)[-1], 35, 19, 19),
        compiler_params=pltpu.CompilerParams(
            collective_id=2, has_side_effects=True, vmem_limit_bytes=50 * 1024 * 1024
        ),
        name="attention_back_and_scatter",
    )(*inputs)
    return AttentionOut(*values)


def publish_kernel(held, count, *refs):
    sources, results, passing = refs[:count], refs[count : 2 * count], refs[2 * count : 3 * count - held]
    arriving, leaving = refs[3 * count - held :]
    copies_in = [
        pltpu.make_async_copy(source, target, arriving.at[at])
        for at, (source, target) in enumerate(zip(sources[held:], passing))
    ]
    ready = [*sources[:held], *passing]
    copies_out = [pltpu.make_async_copy(ready[at], results[at], leaving.at[at]) for at in range(count)]
    for copy in copies_in:
        copy.start()
    for copy in copies_out[:held]:
        copy.start()
    for copy_in, copy_out in zip(copies_in, copies_out[held:]):
        copy_in.wait()
        copy_out.start()
    for copy in copies_out:
        copy.wait()


def publish(held, others):
    arrays = (*held, *others)
    count = len(arrays)
    return pl.pallas_call(
        functools.partial(publish_kernel, len(held), count),
        out_shape=shapes_of(same_as(arrays)),
        in_specs=specs_of(count, len(held)),
        out_specs=specs_of(count, 0),
        scratch_shapes=scratch_of(same_as(others)) + sems(len(others), count),
        compiler_params=pltpu.CompilerParams(vmem_limit_bytes=8 * 1024 * 1024),
        name="publish",
    )(*arrays)


def kernel_path(n_docs, heads, scale, inputs):
    made = [tuple(Piece(*each) for each in pieces) for pieces in (front_pieces, ffn_pieces, attention_pieces)]
    first = front(n_docs, heads, scale, made[0], front_plan, inputs)
    ffn_inputs = FfnIn(*(getattr(first, name) for name in FfnIn._fields))
    second = ffn_back(n_docs, heads, made[1], ffn_plan, inputs.text, inputs.visual, ffn_inputs)
    known = merged(inputs, first, second)
    attention_inputs = AttentionIn(*(getattr(known, name) for name in AttentionIn._fields))
    third = attention_back(n_docs, heads, scale, made[2], attention_plan, attention_inputs)
    held = publish(third, (second.text_out, second.visual_out))
    done = AttentionOut(*held[: len(third)])
    return (
        *held[len(third) :],
        done.text_grad,
        done.visual_grad,
        done.grad_qkv,
        done.grad_out,
        jnp.transpose(done.grad_gate, (1, 2, 0)),
        done.grad_up,
        done.grad_down,
        done.grad_gain_attn,
        done.grad_gain_ffn,
    )


def swap(value):
    return lax.ppermute(value, core_axis, [(0, 1), (1, 0)])


def both(own):
    return jnp.concatenate([own, swap(own)], 0)


def own_sum(partial):
    rows = partial.shape[0] // 2
    return partial[:rows] + swap(partial[rows:])


def normalize_back(gradient, normed, inverse, gain):
    scaled = gradient * gain
    grad_gain = jnp.sum(gradient * normed, 0)
    grad_input = inverse * (
        scaled
        - jnp.mean(scaled, -1, keepdims=True)
        - normed * jnp.mean(scaled * normed, -1, keepdims=True)
    )
    return grad_input, grad_gain


def heads_of(values, heads):
    return values.reshape(values.shape[0], heads, -1)


def attend(queries, keys, values, valid, scale):
    scores = jnp.einsum("qhe,khe->hqk", queries, keys, preferred_element_type=full) * scale
    scores = jnp.where(valid, scores, big_negative)
    top = jnp.max(scores, -1)
    probs = jnp.where(valid, jnp.exp(scores - top[..., None]), 0.0)
    total = jnp.sum(probs, -1)
    weighted = jnp.einsum(
        "hqk,khe->qhe", probs.astype(low), values, preferred_element_type=full
    )
    return weighted / total.T[..., None], top + jnp.log(total)


def attend_back(queries, keys, values, valid, scale, log_total, grad_output, output):
    delta = jnp.sum(grad_output.astype(full) * output, -1).T
    scores = jnp.einsum("qhe,khe->hqk", queries, keys, preferred_element_type=full) * scale
    probs = jnp.where(valid, jnp.exp(scores - log_total[..., None]), 0.0)
    grad_values = jnp.einsum(
        "hqk,qhe->khe", probs.astype(low), grad_output, preferred_element_type=full
    )
    grad_probs = jnp.einsum("qhe,khe->hqk", grad_output, values, preferred_element_type=full)
    grad_scores = (probs * (grad_probs - delta[..., None])).astype(low)
    grad_queries = (
        jnp.einsum("hqk,khe->qhe", grad_scores, keys, preferred_element_type=full) * scale
    )
    grad_keys = (
        jnp.einsum("hqk,qhe->khe", grad_scores, queries, preferred_element_type=full) * scale
    )
    return grad_queries, grad_keys, grad_values


def on_device(
    n_docs,
    text_tokens,
    visual_tokens,
    text_mask,
    visual_mask,
    w_qkv,
    w_out,
    w_gate,
    w_up,
    w_down,
    gain_attn,
    gain_ffn,
    text_cotangent,
    visual_cotangent,
):
    core = lax.axis_index(core_axis)
    width = w_out.shape[2]
    all_heads = w_gate.shape[2]
    heads = all_heads // 2
    half = width // 2
    scale = (width // all_heads) ** (-0.5)
    if n_docs == 16 and w_qkv.shape[1] % row_tile == 0:
        inputs = FrontIn(
            w_qkv=w_qkv,
            w_gate=jnp.transpose(w_gate, (2, 0, 1)),
            w_up=w_up,
            gain_attn=gain_attn,
            gain_ffn=gain_ffn,
            text_mask=text_mask,
            visual_mask=visual_mask,
            text=text_tokens,
            visual=visual_tokens,
            text_dy=text_cotangent,
            visual_dy=visual_cotangent,
            w_out=w_out,
            w_down=w_down,
        )
        return kernel_path(n_docs, heads, scale, inputs)

    def own_columns(array, size, start=0):
        return lax.dynamic_slice_in_dim(array, start + core * size, size, 2)

    own_tokens = (text_tokens[0], visual_tokens[0])
    own_grads = (text_cotangent[0], visual_cotangent[0])

    def reorder(mask):
        rows = mask.shape[1] // 2
        return (
            jnp.concatenate(
                [
                    lax.dynamic_slice_in_dim(mask[0], core * rows, rows),
                    lax.dynamic_slice_in_dim(mask[0], (1 - core) * rows, rows),
                ]
            )
            > 0
        )

    valids = (reorder(text_mask), reorder(visual_mask))

    pad = lane - heads - 2
    shard = jnp.concatenate(
        [own_columns(w_qkv, half, column * width) for column in range(3)]
        + [
            own_columns(w_gate, heads),
            gain_attn[..., None],
            gain_ffn[..., None],
            jnp.zeros(w_gate.shape[:2] + (pad,), low),
        ],
        2,
    )
    tokens = tuple(both(value) for value in own_tokens)
    grads_out = tuple(both(value) for value in own_grads)
    gather = lambda array: lax.all_gather(array, docs_axis, axis=1, tiled=True)
    rows_half = lambda array: lax.dynamic_slice_in_dim(
        array, core * (array.shape[1] // 2), array.shape[1] // 2, 1
    )
    full_qkv = gather(shard)
    full_up = gather(own_columns(w_up, w_up.shape[2] // 2))
    full_out, full_down = rows_half(gather(w_out)), rows_half(gather(w_down))
    gains_attn = full_qkv[:, :, 3 * half + heads].astype(full)
    gains_ffn = full_qkv[:, :, 3 * half + heads + 1].astype(full)

    fronts = []
    for s in range(2):
        normed, inverse = normalize(tokens[s].astype(full))
        lowered = (normed * gains_attn[s]).astype(low)
        wide = dot(lowered, full_qkv[s])
        narrow = wide[:, : 3 * half].astype(low)
        gates = jax.nn.sigmoid(wide[:, 3 * half : 3 * half + heads])
        queries, keys, values = (
            heads_of(narrow[:, column * half : (column + 1) * half], heads) for column in range(3)
        )
        fronts.append((normed, inverse, lowered, gates, queries, keys, values))

    outputs, totals = {}, {}
    for s in range(2):
        for t in range(2):
            outputs[s, t], totals[s, t] = attend(
                fronts[s][4], fronts[t][5], fronts[t][6], valids[t], scale
            )

    results, tails = [], []
    for s in range(2):
        gates = fronts[s][3][..., None]
        own, cross = outputs[s, s], outputs[s, 1 - s]
        mixed = gates * own + (1.0 - gates) * cross
        mix = mixed.reshape(mixed.shape[0], -1).astype(low)
        middle = own_tokens[s].astype(full) + own_sum(dot(mix, full_out[s]))
        normed, inverse = normalize(middle)
        lowered = both((normed * gains_ffn[s]).astype(low))
        upward = dot(lowered, full_up[s])
        activated, gelu_back = jax.vjp(jax.nn.gelu, upward)
        act = activated.astype(low)
        results.append((middle + own_sum(dot(act, full_down[s]))).astype(low))
        part_down = dot_rows(act, grads_out[s]).astype(low)
        grad_up = gelu_back(dot_back(grads_out[s], full_down[s]))[0].astype(low)
        part_up = dot_rows(lowered, grad_up).astype(low)
        grad_in, part_gain = normalize_back(
            own_sum(dot_back(grad_up, full_up[s])), normed, inverse, gains_ffn[s]
        )
        grad_middle = own_grads[s].astype(full) + grad_in
        grad_branch = both(grad_middle.astype(low))
        part_out = dot_rows(mix, grad_branch).astype(low)
        grad_mix = heads_of(dot_back(grad_branch, full_out[s]), heads)
        grad_gate = (
            jnp.sum(grad_mix * (own - cross), -1) * fronts[s][3] * (1.0 - fronts[s][3])
        ).astype(low)
        grad_own = (gates * grad_mix).astype(low)
        grad_cross = ((1.0 - gates) * grad_mix).astype(low)
        tails.append(
            (grad_middle, grad_gate, grad_own, grad_cross, part_out, part_up, part_down, part_gain)
        )

    backs = {}
    for s in range(2):
        for t in range(2):
            backs[s, t] = attend_back(
                fronts[s][4],
                fronts[t][5],
                fronts[t][6],
                valids[t],
                scale,
                totals[s, t],
                tails[s][2 if s == t else 3],
                outputs[s, t],
            )

    token_grads, parts_qkv = [], []
    for s in range(2):
        normed, inverse, lowered = fronts[s][:3]
        rows = lowered.shape[0]
        grad_q = backs[s, s][0] + backs[s, 1 - s][0]
        grad_k = backs[s, s][1] + backs[1 - s, s][1]
        grad_v = backs[s, s][2] + backs[1 - s, s][2]
        grad_wide = jnp.concatenate(
            [grad.reshape(rows, -1).astype(low) for grad in (grad_q, grad_k, grad_v)]
            + [tails[s][1], jnp.zeros((rows, lane - heads), low)],
            1,
        )
        part = dot_rows(lowered, grad_wide)
        own_rows = rows // 2
        grad_in, part_gain = normalize_back(
            own_sum(dot_back(grad_wide, full_qkv[s])),
            normed[:own_rows],
            inverse[:own_rows],
            gains_attn[s],
        )
        token_grads.append((tails[s][0] + grad_in)[None])
        parts_qkv.append(
            jnp.concatenate(
                [
                    part[:, : 3 * half + heads],
                    part_gain[:, None],
                    tails[s][7][:, None],
                    part[:, 3 * half + heads + 2 :],
                ],
                1,
            ).astype(low)
        )
    part_qkv = jnp.stack(parts_qkv)
    part_out, part_up, part_down = (
        jnp.stack([tails[0][at], tails[1][at]]) for at in (4, 5, 6)
    )
    scatter = lambda array: lax.psum_scatter(
        array.astype(full), docs_axis, scatter_dimension=1, tiled=True
    )

    def columns(own):
        other = swap(own)
        first = jnp.where(core == 0, own, other)
        second = jnp.where(core == 0, other, own)
        return first, second

    def rows_both(part):
        empty = jnp.zeros_like(part)
        first = jnp.where(core == 0, part, empty)
        second = jnp.where(core == 0, empty, part)
        return lax.psum(scatter(jnp.concatenate([first, second], 1)), core_axis)

    qkv_first, qkv_second = columns(scatter(part_qkv))
    grad_qkv = jnp.concatenate(
        [
            piece[:, :, column * half : (column + 1) * half]
            for column in range(3)
            for piece in (qkv_first, qkv_second)
        ],
        2,
    )
    small = jnp.stack([qkv_first[:, :, 3 * half :], qkv_second[:, :, 3 * half :]])
    grad_up = jnp.concatenate(columns(scatter(part_up)), 2)
    grad_out, grad_down = rows_both(part_out), rows_both(part_down)
    grad_gate = jnp.concatenate([small[0, :, :, :heads], small[1, :, :, :heads]], 2)
    gains = small[0] + small[1]
    return (
        results[0][None],
        results[1][None],
        token_grads[0],
        token_grads[1],
        grad_qkv,
        grad_out,
        grad_gate,
        grad_up,
        grad_down,
        gains[:, :, heads],
        gains[:, :, heads + 1],
    )


def solution(mesh):
    rows = P(docs_axis, core_axis, None)
    weights = P(None, docs_axis, None)
    gains = P(None, docs_axis)
    in_specs = (
        (rows, rows, P(docs_axis, None), P(docs_axis, None)) + (weights,) * 5 + (gains,) * 2 + (rows,) * 2
    )
    out_specs = (rows,) * 4 + (weights,) * 5 + (gains,) * 2
    return jax.shard_map(
        functools.partial(on_device, mesh.shape[docs_axis]),
        mesh=mesh,
        in_specs=in_specs,
        out_specs=out_specs,
        check_vma=False,
    )
```

```python
import functools
import types
from typing import NamedTuple

import jax
import jax.numpy as jnp
from jax import lax
from jax.experimental import pallas as pl
from jax.experimental.pallas import tpu as pltpu
from jax.sharding import PartitionSpec as P

epsilon = 1e-05
big_negative = -1e30
MESH = pl.DeviceIdType.MESH
docs_axis, core_axis = "docs", "blk"
lane = 128
row_tile = 16
vmem_limit = 61 * 1024 * 1024
low, full = jnp.bfloat16, jnp.float32
by_x, by_y, upward, downward, crosswise = range(5)
lines_first, planes_first, line_only, plane_shared = range(4)
quads = ((False, False), (False, True), (True, False), (True, True))


def dot(left, right):
    return jnp.dot(left, right, preferred_element_type=full)


def dot_back(left, right):
    return lax.dot_general(left, right, (((1,), (1,)), ((), ())), preferred_element_type=full)


def dot_rows(left, right):
    return lax.dot_general(left, right, (((0,), (0,)), ((), ())), preferred_element_type=full)


def normalize(values):
    centred = values - jnp.mean(values, -1, keepdims=True)
    inverse = lax.rsqrt(jnp.mean(centred * centred, -1, keepdims=True) + epsilon)
    return centred * inverse, inverse


def over_rows(first, last, size, body):
    def step(at, carry):
        body(pl.ds(pl.multiple_of(first + at * size, row_tile), size))
        return carry

    lax.fori_loop(0, (last - first) // size, step, 0)


def over_columns(first, last, size, body):
    def step(at, carry):
        body(pl.ds(pl.multiple_of(first + at * size, lane), size))
        return carry

    lax.fori_loop(0, (last - first) // size, step, 0)


def gelu_both(value):
    root = 0.7978845608028654
    square = value * value
    bent = jnp.tanh(root * (value + 0.044715 * value * square))
    cdf = 0.5 * (1.0 + bent)
    slope = cdf + 0.5 * value * (1.0 - bent * bent) * (root * (1.0 + 0.134145 * square))
    return value * cdf, slope


def add_rows(target, others, first=0):
    size = max(size for size in (16, 32, 48) if others[0].shape[0] % size == 0)

    def body(step, carry):
        at = pl.multiple_of(step * size, row_tile)
        total = others[0][pl.ds(at, size), :].astype(full)
        for other in others[1:]:
            total = total + other[pl.ds(at, size), :].astype(full)
        target[pl.ds(first + at, size), :] = total.astype(target.dtype)
        return carry

    lax.fori_loop(0, others[0].shape[0] // size, body, 0)


def when(conditions, body):
    conditions = [condition for condition in conditions if condition is not None]
    if not conditions:
        body()
        return
    pl.when(functools.reduce(jnp.logical_and, conditions))(body)


def merged(*groups):
    space = types.SimpleNamespace()
    for group in groups:
        vars(space).update(group._asdict())
    return space


class Place:
    def __init__(self, line_size):
        docs = lax.axis_index(docs_axis)
        self.core = lax.axis_index(core_axis)
        self.line_size = line_size
        self.z, self.y, self.x = docs // 4, (docs // 2) % 2, docs % 2
        self.up_valid = self.z < line_size - 1
        self.down_valid = self.z > 0

    def index(self, z, flip_y=False, flip_x=False):
        y = 1 - self.y if flip_y else self.y
        x = 1 - self.x if flip_x else self.x
        return z * 4 + y * 2 + x

    def device(self, step):
        z, y, x = self.z, self.y, self.x
        docs = (
            z * 4 + y * 2 + 1 - x,
            z * 4 + (1 - y) * 2 + x,
            (z + 1) * 4 + y * 2 + x,
            (z - 1) * 4 + y * 2 + x,
            z * 4 + (1 - y) * 2 + 1 - x,
        )[step]
        return (docs, self.core)

    def greet(self):
        barrier = pltpu.get_barrier_semaphore()

        def signal(device):
            pl.semaphore_signal(barrier, inc=1, device_id=device, device_id_type=MESH)

        for step in (by_x, by_y, crosswise):
            signal(self.device(step))
        pl.when(self.up_valid)(lambda: signal(self.device(upward)))
        pl.when(self.down_valid)(lambda: signal(self.device(downward)))
        signal((self.index(self.z), 1 - self.core))

    def meet(self):
        peers = 4
        for valid in (self.up_valid, self.down_valid):
            peers = peers + jnp.where(valid, 1, 0)
        pl.semaphore_wait(pltpu.get_barrier_semaphore(), peers)


class Piece(NamedTuple):
    array: int
    part: int
    first: int
    rows: int
    flip: int
    route: int


class Gather:
    def __init__(self, place, pieces, sizes, splits, owns, outs, send_sems, recv_sems, local_sems):
        self.place, self.pieces, self.sizes, self.splits = place, pieces, sizes, splits
        self.owns, self.outs = owns, outs
        self.send_sems, self.recv_sems, self.local_sems = send_sems, recv_sems, local_sems

    def has(self, at, source_z):
        half = self.place.line_size // 2
        return source_z // half == self.place.core if self.splits[self.pieces[at].array] else None

    def block(self, at, source):
        piece = self.pieces[at]
        if self.splits[piece.array]:
            source = source - self.place.core * (self.place.line_size // 2) * 4
        if piece.route == line_only:
            source = source // 4
        first = source * self.sizes[piece.array] + piece.first
        rows = pl.ds(pl.multiple_of(first, row_tile), piece.rows)
        return self.outs[piece.array].at[piece.part, rows, :]

    def mine(self, at, step=None):
        piece = self.pieces[at]
        ref, offset = self.owns[piece.array]
        if piece.route == plane_shared:
            to = self.place.index(0, step in (by_y, crosswise), step in (by_x, crosswise))
            return ref.at[to, pl.ds(piece.first, piece.rows), :]
        first = pl.multiple_of(offset + piece.first, row_tile)
        return ref.at[piece.part, pl.ds(first, piece.rows), :]

    def copy(self, at, source, step, own=False):
        return pltpu.make_async_remote_copy(
            src_ref=self.mine(at, step) if own else self.block(at, source),
            dst_ref=self.block(at, source),
            send_sem=self.send_sems.at[at, step],
            recv_sem=self.recv_sems.at[at, source],
            device_id=self.place.device(step),
            device_id_type=MESH,
        )

    def local(self, at):
        here = self.place.index(self.place.z)
        return pltpu.make_async_copy(self.mine(at), self.block(at, here), self.local_sems.at[at])

    def send(self, conditions, *which):
        when(conditions, lambda: self.copy(*which).start())

    def wait(self, conditions, at, source):
        when(conditions, lambda: self.copy(at, source, by_x).wait_recv())

    def units(self, distance):
        place = self.place
        if distance == 0:
            return [(place.z, None, None)]
        return [
            (place.z - distance, place.z >= distance, (upward, place.up_valid)),
            (place.z + distance, place.z < place.line_size - distance, (downward, place.down_valid)),
        ]

    def both_ways(self, conditions, at, source, own=False):
        self.send(conditions + [self.place.up_valid], at, source, upward, own)
        self.send(conditions + [self.place.down_valid], at, source, downward, own)

    def own(self, at):
        place = self.place
        here = place.index(place.z)
        held = [self.has(at, place.z)]
        when(held, lambda: self.local(at).start())
        self.both_ways(held, at, here, True)
        route = self.pieces[at].route
        if route != line_only:
            self.send(held, at, here, by_x, True)
            self.send(held, at, here, by_y, True)
        if route == plane_shared:
            self.send(held, at, here, crosswise, True)

    def beside(self, at, distance):
        piece = self.pieces[at]
        for source_z, valid, _ in self.units(distance):
            conditions = [valid, self.has(at, source_z)]
            for other in (0, 1):
                source = self.place.index(source_z, other == 1, other == 0)
                if other == piece.flip or piece.route != lines_first:
                    self.wait(conditions, at, source)
                if other == piece.flip and piece.route != plane_shared:
                    self.send(conditions, at, source, by_x if other else by_y)
                if piece.route != lines_first:
                    self.both_ways(conditions, at, source)

    def along(self, at, distance, quad=quads[0]):
        for source_z, valid, (step, onward) in self.units(distance):
            source = self.place.index(source_z, *quad)
            conditions = [valid, self.has(at, source_z)]
            self.wait(conditions, at, source)
            self.send(conditions + [onward], at, source, step)
            if self.pieces[at].route == lines_first:
                self.send(conditions, at, source, by_x)
                self.send(conditions, at, source, by_y)

    def late_round(self, at, number):
        place = self.place
        last = place.line_size - 1
        if number == 1:
            self.beside(at, 0)
        if number == 2:
            held = [self.has(at, place.z)]
            fourth = place.index(place.z, *quads[3])
            self.wait(held, at, fourth)
            self.both_ways(held, at, fourth)
        for quad, behind in zip(quads, (0, 1, 1, 2)):
            if 1 <= number - behind <= last:
                self.along(at, number - behind, quad)

    def rest(self, array):
        for at, piece in enumerate(self.pieces):
            if piece.array != array:
                continue
            if piece.route in (planes_first, plane_shared):
                self.along(at, self.place.line_size - 1, quads[3])
            elif piece.route == lines_first:
                for distance in range(self.place.line_size):
                    for source_z, valid, _ in self.units(distance):
                        conditions = [valid, self.has(at, source_z)]
                        beside = (piece.flip == 0, piece.flip == 1)
                        self.wait(conditions, at, self.place.index(source_z, *beside))
                        self.wait(conditions, at, self.place.index(source_z, *quads[3]))
            when([self.has(at, self.place.z)], lambda: self.local(at).wait())

    def run(self, plan, stages):
        for kind, at, number in plan:
            if kind == 0:
                self.own(at)
            elif kind == 1:
                self.beside(at, number)
            elif kind == 2:
                self.along(at, number)
            elif kind == 3:
                self.late_round(at, number)
            elif kind == 4:
                self.rest(at)
            else:
                stages[at]()

    def sent(self, at, step, blocks):
        piece = self.pieces[at]
        total = self.outs[piece.array].at[piece.part, pl.ds(0, blocks * piece.rows), :]
        pltpu.make_async_remote_copy(
            src_ref=total,
            dst_ref=total,
            send_sem=self.send_sems.at[at, step],
            recv_sem=self.recv_sems.at[at, 0],
            device_id=self.place.device(step),
            device_id_type=MESH,
        ).wait_send()

    def finish(self):
        size, place = self.place.line_size, self.place
        for at, piece in enumerate(self.pieces):
            split = self.splits[piece.array]
            planes = size // 2 if split else size
            if piece.route == lines_first:
                self.sent(at, by_x, planes * (1 + piece.flip))
                self.sent(at, by_y, planes * (2 - piece.flip))
            elif piece.route == planes_first:
                self.sent(at, by_x, 1 + piece.flip)
                self.sent(at, by_y, 2 - piece.flip)
            elif piece.route == plane_shared:
                for step in (by_x, by_y, crosswise):
                    self.sent(at, step, 1)
            chips = 4 if piece.route in (planes_first, plane_shared) else 1
            for z in range(size):
                for core in range(2 if split else 1):
                    held = [source for source in range(size) if not split or source // (size // 2) == core]
                    here = [place.z == z] + ([place.core == core] if split else [])
                    up = chips * sum(source <= z for source in held) if z < size - 1 else 0
                    down = chips * sum(source >= z for source in held) if z > 0 else 0
                    if up:
                        when(here, lambda: self.sent(at, upward, up))
                    if down:
                        when(here, lambda: self.sent(at, downward, down))


class Scatter:
    def __init__(self, place, pieces, splits, raws, parts, buffers, send_sems, recv_sems, finish):
        self.place, self.pieces, self.splits = place, pieces, splits
        self.raws, self.parts, self.buffers = raws, parts, buffers
        self.send_sems, self.recv_sems, self.finish_rows = send_sems, recv_sems, finish
        self.first = arrival_offsets(pieces, place.line_size)

    shares = ((quads[1], 1, by_x), (quads[2], 2, by_y), (quads[3], 0, crosswise))

    def has(self, at, z_to):
        half = self.place.line_size // 2
        return z_to // half == self.place.core if self.splits[self.pieces[at].array] else None

    def slot(self, at, z_to):
        half = self.place.line_size // 2
        return z_to - self.place.core * half if self.splits[self.pieces[at].array] else z_to

    def block(self, refs, at, z_to, quad):
        piece = self.pieces[at]
        ref = refs[piece.array]
        if piece.route == line_only:
            first = z_to * (ref.shape[1] // self.place.line_size) + piece.first
        else:
            split = 2 if self.splits[piece.array] else 1
            rows = ref.shape[1] // (4 * self.place.line_size // split)
            first = self.place.index(self.slot(at, z_to), *quad) * rows + piece.first
        return ref.at[piece.part, pl.ds(pl.multiple_of(first, row_tile), piece.rows), :]

    def quads(self, at):
        return quads[:1] if self.pieces[at].route == line_only else quads

    def raw_of(self, at, z_to, quad):
        return self.block(self.raws, at, z_to, quad)

    def part_of(self, at, z_to, quad):
        return self.block(self.parts, at, z_to, quad)

    def landed(self, at, kind, z_to, quad=0):
        ref = self.buffers[at][kind]
        if self.pieces[at].route == lines_first:
            return ref.at[self.slot(at, z_to)]
        return ref.at[self.slot(at, z_to), quad] if kind >= 3 else ref.at[0]

    def arrival(self, at, kind, z_to, quad):
        route = self.pieces[at].route
        if route == lines_first:
            return self.first[at] + z_to * 5 + kind
        if kind < 3:
            return self.first[at] + kind
        chips = len(self.quads(at))
        return self.first[at] + 3 + (z_to * 2 + kind - 3) * chips + quad

    def copy(self, source, at, kind, z_to, step, quad=0):
        return pltpu.make_async_remote_copy(
            src_ref=source,
            dst_ref=self.landed(at, kind, z_to, quad),
            send_sem=self.send_sems.at[at],
            recv_sem=self.recv_sems.at[self.arrival(at, kind, z_to, quad)],
            device_id=self.place.device(step),
            device_id_type=MESH,
        )

    def arrived(self, at, kind, z_to, quad=0):
        held = self.landed(at, kind, z_to, quad)
        self.copy(held, at, kind, z_to, by_x, quad).wait_recv()

    def send(self, conditions, *which):
        when(conditions, lambda: self.copy(*which).start())

    def destination(self, step):
        size = self.place.line_size
        chosen = 0
        for at in range(size):
            order = sorted(range(size), key=lambda other: (-abs(other - at), other))
            chosen = chosen + jnp.where(self.place.z == at, order[step], 0)
        return chosen

    def raw(self, at, step):
        place = self.place
        z_to = self.destination(step)
        conditions = [self.has(at, z_to)]
        if self.pieces[at].route == lines_first:
            self.plane_raw(conditions, self.raw_of, at, z_to)
            return
        first, last = place.z == 0, place.z == place.line_size - 1
        for number, quad in enumerate(self.quads(at)):
            source = self.raw_of(at, z_to, quad)
            up = conditions + [first, z_to > place.z]
            self.send(up, source, at, 3, z_to, upward, number)
            down = conditions + [last, z_to < place.z]
            self.send(down, source, at, 4, z_to, downward, number)

    def plane_raw(self, conditions, source, at, z_to):
        if self.pieces[at].flip == 0:
            self.send(conditions, source(at, z_to, (True, True)), at, 0, z_to, by_y)
            self.send(conditions, source(at, z_to, (True, False)), at, 2, z_to, by_y)
        else:
            self.send(conditions, source(at, z_to, (True, True)), at, 0, z_to, by_x)
            self.send(conditions, source(at, z_to, (False, True)), at, 1, z_to, by_x)

    def plane_pair(self, conditions, at, z_to):
        flip = self.pieces[at].flip
        held = self.landed(at, 0, z_to)

        def body():
            self.arrived(at, 0, z_to)
            add_rows(held, [held, self.part_of(at, z_to, (flip == 1, flip == 0))])

        when(conditions, body)
        if flip == 0:
            self.send(conditions, held, at, 1, z_to, by_x)
        else:
            self.send(conditions, held, at, 2, z_to, by_y)

    def pair(self, at, step):
        z_to = self.destination(step)
        self.plane_pair([self.has(at, z_to)], at, z_to)

    def line(self, at, step):
        place, piece = self.place, self.pieces[at]
        z = place.z
        z_to = self.destination(step)
        conditions = [self.has(at, z_to)]
        first, last = z == 0, z == place.line_size - 1
        inner = jnp.logical_and(z > 0, z < place.line_size - 1)
        ways = (
            (3, [z_to > z], [first], [z > 0], upward),
            (4, [z_to < z], [last], [z < place.line_size - 1], downward),
        )
        ends = (([first], (4,)), ([last], (3,)), ([inner], (3, 4)))
        if piece.route == lines_first:
            held = self.landed(at, 1, z_to)
            base = [held, self.landed(at, 2, z_to), self.part_of(at, z_to, quads[0])]

            def wait():
                self.arrived(at, 1, z_to)
                self.arrived(at, 2, z_to)

            when(conditions, wait)
            for kind, onward, starts, passes, step_to in ways:
                when(conditions + onward + starts, lambda: add_rows(held, base))

                def passing():
                    self.arrived(at, kind, z_to)
                    add_rows(held, base + [self.landed(at, kind, z_to)])

                when(conditions + onward + passes, passing)
                self.send(conditions + onward, held, at, kind, z_to, step_to)
            for which, kinds in ends:

                def end():
                    for kind in kinds:
                        self.arrived(at, kind, z_to)
                    self.finish_rows(piece, base + [self.landed(at, kind, z_to) for kind in kinds])

                when(conditions + [z_to == z] + which, end)
            return
        for kind, onward, _, passes, step_to in ways:
            for at_quad, quad in enumerate(self.quads(at)):
                held = self.landed(at, kind, z_to, at_quad)

                def passing():
                    self.arrived(at, kind, z_to, at_quad)
                    add_rows(held, [held, self.part_of(at, z_to, quad)])

                which = conditions + onward + passes
                when(which, passing)
                self.send(which, held, at, kind, z_to, step_to, at_quad)
        here = conditions + [z_to == z]
        for which, kinds in ends:

            def end():
                for at_quad, quad in reversed(list(enumerate(self.quads(at)))):
                    own = self.part_of(at, z_to, quad)
                    for kind in kinds:
                        self.arrived(at, kind, z_to, at_quad)
                    total = [own] + [self.landed(at, kind, z_to, at_quad) for kind in kinds]
                    if piece.route == planes_first or at_quad:
                        add_rows(own, total)
                    else:
                        self.finish_rows(piece, total)

            when(here + which, end)
        if step == place.line_size - 1 and piece.route == planes_first:
            self.plane_raw(here, self.part_of, at, z_to)
        if step == place.line_size - 1 and piece.route == plane_shared:
            for quad, kind, step_to in self.shares:
                self.send(here, self.part_of(at, z_to, quad), at, kind, z_to, step_to)

    def tail(self, at):
        z, piece = self.place.z, self.pieces[at]
        if piece.route == plane_shared:
            for quad, kind, _ in self.shares:
                self.arrived(at, kind, z)
                self.finish_rows(piece, [self.landed(at, kind, z)], quad)
            return
        conditions = [self.has(at, z)]
        self.plane_pair(conditions, at, z)

        def end():
            self.arrived(at, 1, z)
            self.arrived(at, 2, z)
            total = [self.landed(at, kind, z) for kind in (1, 2)] + [self.part_of(at, z, quads[0])]
            self.finish_rows(piece, total)

        when(conditions, end)

    def run(self, plan, stages):
        for kind, at, number in plan:
            if kind == 0:
                self.raw(at, number)
            elif kind == 1:
                self.pair(at, number)
            elif kind == 2:
                self.line(at, number)
            elif kind == 3:
                self.tail(at)
            else:
                stages[at]()

    def sent(self, at, blocks):
        piece = self.pieces[at]
        total = self.raws[piece.array].at[piece.part, pl.ds(0, blocks * piece.rows), :]
        pltpu.make_async_remote_copy(
            src_ref=total,
            dst_ref=total,
            send_sem=self.send_sems.at[at],
            recv_sem=self.recv_sems.at[0],
            device_id=self.place.device(by_x),
            device_id_type=MESH,
        ).wait_send()

    def finish(self):
        size, place = self.place.line_size, self.place
        for at, piece in enumerate(self.pieces):
            if self.splits[piece.array]:
                half = place.z // (size // 2) == place.core
                when([half], lambda: self.sent(at, 3 * (size // 2) + size // 2 - 1))
                when([jnp.logical_not(half)], lambda: self.sent(at, 4 * (size // 2)))
            elif piece.route == lines_first:
                self.sent(at, 4 * size - 1)
            elif piece.route == line_only:
                self.sent(at, size - 1)
            else:
                self.sent(at, 4 * (size - 1) + 3)


def arrival_offsets(pieces, line_size):
    offsets = [0]
    for piece in pieces:
        chips = 1 if piece.route == line_only else 4
        count = 5 * line_size if piece.route == lines_first else 3 + 2 * line_size * chips
        offsets.append(offsets[-1] + count)
    return offsets


class Moves:
    def __init__(self, place, local_sems, send_sems, recv_sems):
        self.place = place
        self.other = (place.index(place.z), 1 - place.core)
        self.local_sems, self.send_sems, self.recv_sems = local_sems, send_sems, recv_sems
        self.locals, self.remotes = 0, 0
        self.to_end = []

    def local(self, source, target):
        made = pltpu.make_async_copy(source, target, self.local_sems.at[self.locals])
        self.locals += 1
        made.start()
        return made

    def save(self, source, target):
        self.to_end.append(self.local(source, target).wait)

    def across(self, source, target, arrives=None):
        sems = dict(
            send_sem=self.send_sems.at[self.remotes],
            recv_sem=self.recv_sems.at[self.remotes],
            device_id=self.other,
            device_id_type=MESH,
        )
        self.remotes += 1
        made = pltpu.make_async_remote_copy(src_ref=source, dst_ref=target, **sems)
        made.start()
        self.to_end.append(made.wait_send)
        arrives = target if arrives is None else arrives
        return pltpu.make_async_remote_copy(src_ref=arrives, dst_ref=arrives, **sems)

    def peer(self, source, target, step, arrives=None):
        sems = dict(
            send_sem=self.send_sems.at[self.remotes],
            recv_sem=self.recv_sems.at[self.remotes],
            device_id=self.place.device(step),
            device_id_type=MESH,
        )
        self.remotes += 1
        made = pltpu.make_async_remote_copy(src_ref=source, dst_ref=target, **sems)
        made.start()
        self.to_end.append(made.wait_send)
        arrives = target if arrives is None else arrives
        return pltpu.make_async_remote_copy(src_ref=arrives, dst_ref=arrives, **sems)

    def finish(self):
        assert self.locals == self.local_sems.shape[0] and self.remotes == self.send_sems.shape[0]
        for wait in self.to_end:
            wait()


class Rows:
    def __init__(self, text, visual):
        self.text, self.visual = text, visual
        self.split = 2 * text
        self.count = 2 * (text + visual)
        self.spans = ((0, self.split), (self.split, self.count))
        self.own = ((0, text), (self.split, self.split + visual))
        self.other = ((text, self.split), (self.split + visual, self.count))
        self.packed = ((0, text), (text, text + visual))
        self.sizes = (chunk_of(text), chunk_of(visual))

    def over_own(self, s, body):
        shift = self.own[s][0] - self.packed[s][0]

        def shifted(piece):
            body(pl.ds(pl.multiple_of(piece.start + shift, row_tile), piece.size), piece)

        over_rows(*self.packed[s], self.sizes[s], shifted)

    def swap_parts(self, moves, wide, received, which=(0, 1)):
        return [
            moves.across(wide.at[slice(*self.other[s])], received.at[slice(*self.packed[s])])
            for s in which
        ]

    def swap_own(self, moves, ref, s):
        return moves.across(ref.at[slice(*self.own[s])], ref.at[slice(*self.other[s])])


class Plane:
    steps = (by_x, by_y, crosswise)

    def __init__(self, place, moves, size):
        self.place, self.moves, self.size = place, moves, size
        self.half = 4 * size

    def chip(self, step=None):
        return self.place.index(0, step in (by_y, crosswise), step in (by_x, crosswise))

    def document(self, at):
        return [slice(first, first + self.size) for first in (at * self.size, self.half + at * self.size)]

    def part(self, ref, at, count=1):
        return ref.at[at * self.size : (at + count) * self.size]

    def spread(self, own, target):
        other = self.moves.across(own, self.part(target, 4))
        return other, [
            self.moves.peer(own, self.part(target, 1 + at), step) for at, step in enumerate(self.steps[:2])
        ]

    def relay(self, target, arrivals):
        moves, core = self.moves, self.place.core
        made = [
            pltpu.make_async_remote_copy(
                src_ref=self.part(target, 1 + at),
                dst_ref=self.part(target, 3),
                send_sem=moves.send_sems.at[moves.remotes],
                recv_sem=moves.recv_sems.at[moves.remotes],
                device_id=self.place.device(step),
                device_id_type=MESH,
            )
            for at, step in enumerate((by_y, by_x))
        ]
        moves.remotes += 1
        for at in range(2):

            def pass_along():
                arrivals[at].wait_recv()
                made[at].start()

            pl.when(core == at)(pass_along)
            moves.to_end.append(functools.partial(pl.when(core == at), made[at].wait_send))
        return made[0]

    def pass_on(self, target, arrivals, fourth):
        for at in range(2):
            pl.when(self.place.core != at)(arrivals[at].wait_recv)
        fourth.wait_recv()
        return self.moves.across(self.part(target, 1, 3), self.part(target, 5, 3))

    def halve(self, wide, received):
        return self.moves.across(self.part(wide, 4, 4), received)

    def share(self, wide, received, outgoing, landing):
        outgoing[...] = (
            wide[self.size : self.half, :] + received[self.size : self.half, :]
        ).astype(outgoing.dtype)
        return [
            self.moves.peer(self.part(outgoing, at), self.part(landing, at), step)
            for at, step in enumerate(self.steps)
        ]

    def total(self, wide, received, landing):
        value = wide[: self.size, :] + received[: self.size, :]
        for at in range(3):
            value = value + landing[at * self.size : (at + 1) * self.size, :].astype(full)
        return value


def chunk_of(count):
    return max(size for size in range(row_tile, 385, row_tile) if count % size == 0)


def query_spans(count):
    edges = list(range(0, count - 256, 512)) + [count]
    return list(zip(edges[:-1], edges[1:]))


def head_wide(values, odd):
    empty = jnp.zeros_like(values)
    return jnp.concatenate([empty, values] if odd else [values, empty], 0)


def column_of(row, count):
    return jnp.broadcast_to(row, (lane, count)).T


def scratch_of(group):
    return [pltpu.VMEM(shape, dtype) for shape, dtype in group]


def shapes_of(group):
    return [jax.ShapeDtypeStruct(shape, dtype) for shape, dtype in group]


def same_as(arrays):
    return [(array.shape, array.dtype) for array in arrays]


def sems(*counts):
    return [pltpu.SemaphoreType.DMA(count if isinstance(count, tuple) else (count,)) for count in counts]


def specs_of(count, in_vmem):
    spaces = [pltpu.VMEM] * in_vmem + [pl.ANY] * (count - in_vmem)
    return [pl.BlockSpec(memory_space=space) for space in spaces]


front_pieces = (
    (0, 0, 0, 32, 0, 0), (0, 0, 32, 16, 1, 0), (1, 0, 0, 16, 0, 0), (1, 0, 16, 32, 1, 0),
    (3, 0, 0, 32, 0, 0), (3, 0, 32, 16, 1, 0), (3, 0, 48, 48, 0, 1), (2, 0, 0, 48, 0, 0),
    (2, 1, 0, 48, 1, 0), (4, 0, 0, 48, 0, 3), (5, 0, 0, 96, 0, 2), (6, 0, 0, 48, 0, 3),
    (7, 0, 0, 48, 1, 0),
)
front_plan = (
    (0, 8, 0), (5, 27, 0), (0, 0, 0), (0, 11, 0), (5, 0, 0), (0, 12, 0), (0, 7, 0), (2, 8, 1), (0, 5, 0),
    (0, 1, 0), (0, 6, 0), (2, 12, 1), (2, 7, 1), (2, 0, 1), (2, 1, 1), (2, 5, 1), (3, 11, 1), (5, 25, 0),
    (2, 12, 2), (2, 7, 2), (2, 1, 2), (0, 9, 0), (2, 0, 2), (5, 1, 0), (3, 11, 2), (2, 8, 2), (5, 28, 0),
    (2, 0, 3), (2, 5, 2), (1, 12, 0), (2, 1, 3), (3, 11, 3), (3, 9, 1), (2, 12, 3), (1, 12, 2), (1, 12, 1),
    (1, 0, 0), (1, 0, 2), (0, 2, 0), (1, 0, 1), (1, 1, 1), (1, 5, 0), (0, 3, 0), (1, 12, 3), (1, 0, 3),
    (1, 1, 0), (2, 8, 3), (2, 5, 3), (2, 7, 3), (1, 1, 3), (3, 11, 4), (5, 26, 0), (3, 9, 2), (1, 1, 2),
    (1, 8, 1), (4, 7, 0), (4, 6, 0), (5, 4, 0), (5, 5, 0), (1, 7, 0), (2, 3, 1), (2, 2, 1), (0, 4, 0),
    (3, 6, 1), (4, 0, 0), (1, 7, 2), (5, 2, 0), (1, 8, 0), (1, 7, 1), (1, 8, 2), (5, 3, 0), (1, 5, 3),
    (2, 4, 1), (2, 3, 2), (1, 7, 3), (5, 6, 0), (5, 7, 0), (2, 2, 2), (0, 10, 0), (1, 8, 3), (5, 8, 0),
    (5, 9, 0), (2, 4, 2), (2, 2, 3), (2, 3, 3), (1, 2, 0), (3, 9, 3), (1, 3, 0), (5, 10, 0), (5, 23, 0),
    (5, 11, 0), (1, 3, 1), (3, 6, 2), (4, 2, 0), (5, 12, 0), (5, 13, 0), (5, 14, 0), (1, 2, 3), (1, 3, 2),
    (1, 3, 3), (2, 10, 1), (1, 2, 2), (1, 2, 1), (1, 4, 2), (5, 15, 0), (5, 16, 0), (1, 5, 2), (1, 4, 0),
    (3, 9, 4), (2, 4, 3), (5, 29, 0), (3, 6, 3), (2, 10, 2), (4, 1, 0), (5, 18, 0), (5, 30, 0), (4, 4, 0),
    (5, 19, 0), (1, 4, 1), (1, 4, 3), (1, 5, 1), (3, 6, 4), (5, 24, 0), (5, 17, 0), (5, 21, 0), (5, 20, 0),
    (2, 10, 3), (4, 5, 0), (5, 22, 0), (4, 3, 0),
)
ffn_pieces = (
    (0, 0, 0, 48, 0, 0), (0, 0, 48, 48, 1, 0), (1, 0, 0, 96, 0, 2),
)
ffn_plan = (
    (0, 1, 0), (0, 2, 0), (0, 0, 0), (0, 2, 1), (0, 1, 1), (0, 1, 2), (0, 0, 1), (4, 2, 0), (2, 2, 0),
    (0, 2, 2), (1, 1, 0), (4, 0, 0), (1, 0, 0), (4, 1, 0), (2, 2, 1), (1, 1, 1), (0, 0, 2), (4, 4, 0),
    (4, 3, 0), (4, 6, 0), (1, 0, 1), (4, 10, 0), (2, 2, 2), (1, 1, 2), (0, 1, 3), (2, 1, 0), (4, 9, 0),
    (0, 0, 3), (2, 0, 0), (1, 0, 2), (4, 13, 0), (2, 1, 1), (0, 2, 3), (4, 7, 0), (4, 8, 0), (1, 1, 3),
    (2, 0, 1), (2, 1, 2), (4, 5, 0), (2, 0, 2), (2, 2, 3), (1, 0, 3), (4, 11, 0), (4, 12, 0), (4, 15, 0),
    (2, 1, 3), (4, 14, 0), (2, 0, 3),
)
attention_pieces = (
    (0, 0, 0, 32, 0, 0), (0, 0, 32, 16, 1, 0), (1, 0, 0, 48, 0, 0), (1, 1, 0, 48, 1, 0),
    (2, 0, 0, 32, 1, 0), (2, 0, 32, 16, 0, 0), (3, 0, 0, 48, 0, 3), (4, 0, 0, 48, 0, 3),
    (5, 0, 0, 48, 0, 0), (5, 1, 0, 48, 1, 0),
)
attention_plan = (
    (0, 3, 0), (0, 1, 0), (0, 0, 0), (0, 0, 1), (0, 3, 1), (4, 0, 0), (4, 1, 0), (0, 6, 0), (0, 2, 0),
    (1, 0, 0), (0, 3, 2), (0, 3, 3), (0, 1, 1), (0, 1, 2), (4, 2, 0), (0, 2, 1), (1, 3, 0), (0, 6, 1),
    (1, 0, 1), (4, 3, 0), (1, 1, 0), (2, 6, 0), (4, 4, 0), (2, 6, 1), (1, 2, 0), (1, 2, 1), (0, 0, 2),
    (1, 3, 1), (0, 6, 2), (4, 5, 0), (1, 3, 2), (0, 2, 2), (4, 6, 0), (4, 7, 0), (2, 0, 0), (4, 9, 0),
    (0, 4, 0), (1, 1, 1), (2, 3, 0), (0, 4, 1), (0, 0, 3), (1, 1, 2), (2, 0, 1), (1, 2, 2), (4, 10, 0),
    (4, 11, 0), (0, 7, 0), (4, 8, 0), (4, 12, 0), (2, 1, 0), (2, 7, 0), (2, 6, 2), (1, 0, 2), (2, 3, 1),
    (1, 4, 0), (0, 4, 2), (1, 4, 1), (2, 1, 1), (0, 1, 3), (4, 13, 0), (0, 7, 1), (0, 5, 0), (0, 7, 2),
    (4, 14, 0), (0, 8, 0), (0, 9, 0), (0, 9, 1), (4, 18, 0), (2, 1, 2), (0, 8, 1), (0, 8, 2), (2, 7, 1),
    (0, 5, 1), (0, 6, 3), (2, 7, 2), (1, 5, 0), (0, 5, 2), (0, 8, 3), (2, 2, 0), (1, 8, 0), (1, 8, 1),
    (2, 6, 3), (2, 4, 0), (0, 9, 2), (1, 5, 1), (1, 9, 0), (2, 2, 1), (0, 2, 3), (0, 7, 3), (2, 0, 2),
    (1, 0, 3), (0, 9, 3), (1, 8, 2), (0, 4, 3), (1, 1, 3), (1, 9, 1), (2, 8, 0), (1, 5, 2), (3, 6, 0),
    (1, 4, 2), (2, 5, 0), (0, 5, 3), (2, 9, 0), (2, 4, 1), (1, 9, 2), (1, 2, 3), (2, 8, 1), (1, 8, 3),
    (2, 2, 2), (2, 5, 1), (2, 1, 3), (2, 9, 1), (1, 3, 3), (2, 3, 2), (2, 0, 3), (1, 9, 3), (4, 15, 0),
    (2, 8, 2), (2, 4, 2), (1, 4, 3), (1, 5, 3), (2, 9, 2), (2, 7, 3), (2, 5, 2), (2, 2, 3), (4, 17, 0),
    (2, 8, 3), (2, 4, 3), (2, 3, 3), (2, 9, 3), (4, 16, 0), (3, 7, 0), (2, 5, 3),
)


class FrontIn(NamedTuple):
    w_qkv: object
    w_gate: object
    w_up: object
    gain_attn: object
    gain_ffn: object
    text_mask: object
    visual_mask: object
    text: object
    visual: object
    text_dy: object
    visual_dy: object
    w_out: object
    w_down: object


class FrontOut(NamedTuple):
    full_qkv: object
    full_up: object
    full_out: object
    full_down: object
    full_up_v: object
    full_down_v: object
    full_qkv_v: object
    full_small_v: object
    h: object
    h_v: object
    qkv: object
    gates_t: object
    text_t: object
    visual_t: object
    logs: object
    mix_t: object
    middle: object
    hm: object
    hm_v: object
    act: object
    act_v: object
    slope: object
    slope_v: object
    part_down: object
    part_down_v: object
    dy: object
    dy_v: object
    gains: object
    bias: object


class FrontKept(NamedTuple):
    s_h: object
    s_h_v: object
    s_qkv: object
    s_gates_t: object
    s_text_t: object
    s_visual_t: object
    s_logs: object
    s_mix_t: object
    s_middle: object
    s_hm: object
    s_hm_v: object
    s_act: object
    s_act_v: object
    s_slope: object
    s_slope_v: object
    s_part_down: object
    s_part_down_v: object
    s_dy: object
    s_dy_v: object
    s_gains: object
    s_bias: object


class FrontScratch(NamedTuple):
    shard_qkv: object
    shard_gate: object
    shard_up: object
    shard_attn: object
    shard_ffn: object
    shard_text_mask: object
    shard_visual_mask: object
    own_qkv: object
    own_qkv_v: object
    own_small_v: object
    own_up: object
    own_up_v: object
    s_w_qkv: object
    s_w_qkv_v: object
    s_w_small_v: object
    s_w_up: object
    s_w_up_v: object
    s_w_out: object
    x: object
    x_v: object
    wide: object
    qkv_v: object
    landing_qkv: object
    received: object
    gate_rows: object
    q_t: object
    v_t: object
    mix: object


def prepare_shards(v, core, heads):
    first = core == 0
    rows = v.shard_qkv.shape[1]
    third = v.shard_qkv.shape[2] // 3
    half = third // 2
    for s in range(2):
        for pair in range(half // lane):
            for at in range(3):
                start = at * third + pair * lane
                columns = [v.shard_qkv[s, :, start + way * half : start + way * half + lane] for way in (0, 1)]
                chosen = jnp.where(first, *columns)
                if s == 0:
                    to = (3 * pair + at) * lane
                    v.own_qkv[0, :, to : to + lane] = chosen
                else:
                    v.own_qkv_v[pair, :, at * lane : (at + 1) * lane] = chosen
        gate = v.shard_gate[:, s, :].astype(full)
        gate = jnp.where(first, gate[:heads], gate[heads:])
        gains = [ref[s : s + 1, :].astype(full) for ref in (v.shard_attn, v.shard_ffn)]
        small = jnp.concatenate([gate, *gains, jnp.zeros((lane - heads - 2, rows), full)], 0)
        small = jnp.concatenate([small, jnp.zeros((lane, lane - rows), full)], 1).T[:rows]
        if s == 0:
            v.own_qkv[0, :, 3 * half :] = small.astype(low)
        else:
            v.own_small_v[0, :, :] = small.astype(low)
    for pair in range(half // lane, 4):
        v.own_qkv_v[pair, :, :] = jnp.zeros(v.own_qkv_v.shape[1:], low)


def prepare_hidden(v, core, block):
    first = core == 0
    pieces = []
    for s in range(2):
        for start in range(0, v.shard_up.shape[2], 2 * block):
            ways = [v.shard_up[s, :, start + way * block : start + (way + 1) * block].astype(full) for way in (0, 1)]
            pieces.append(jnp.where(first, *ways))
    count = len(pieces) // 2
    v.own_up[0, :, :] = jnp.concatenate(pieces[:count], 1).astype(low)
    for quad in range(4):
        v.own_up_v[quad, :, :] = jnp.concatenate(pieces[count + quad :: 4], 1).astype(low)


def prepare_bias(v, core):
    pieces = []
    for ref in (v.shard_text_mask, v.shard_visual_mask):
        mask = ref[...].astype(full)
        half = mask.shape[1] // 2
        swapped = jnp.concatenate([mask[:, half:], mask[:, :half]], 1)
        pieces.append(jnp.where(core == 0, mask, swapped))
    row = jnp.concatenate(pieces, 1)
    v.s_bias[...] = column_of(jnp.where(row > 0.0, 0.0, big_negative), row.shape[1])


def attend_head(rows, head_width, v, number):
    pair = 2 * head_width
    at, odd = number // 2, number % 2
    keys = v.s_qkv[:, (3 * at + 1) * pair : (3 * at + 2) * pair]
    bias = v.s_bias[:, 0:1]
    head = slice(number * head_width, (number + 1) * head_width)
    for first, last in query_spans(rows.count):
        scores = dot(keys, head_wide(v.q_t[head, first:last], odd)) + bias
        for t, target in enumerate((v.s_text_t, v.s_visual_t)):
            start, stop = rows.spans[t]
            part = scores[start:stop]
            top = jnp.max(part, 0, keepdims=True)
            raised = jnp.exp(part - top)
            total = jnp.sum(raised, 0, keepdims=True)
            probs = (raised * (1.0 / total)).astype(low)
            target[head, first:last] = dot(v.v_t[head, start:stop], probs)
            row = 8 * t + number
            v.s_logs[row : row + 1, first:last] = top + jnp.log(total)


def front_kernel(line_size, heads, scale, pieces, plan, *refs):
    groups = []
    for group in (FrontIn, FrontOut, FrontKept, FrontScratch):
        count = len(group._fields)
        groups.append(group(*refs[:count]))
        refs = refs[count:]
    v = merged(*groups)
    place = Place(line_size)
    core = place.core
    rows = Rows(v.text.shape[1], v.visual.shape[1])
    shard, block = v.shard_qkv.shape[1], v.w_down.shape[1] // 2
    owns = (
        (v.own_qkv, 0),
        (v.own_up, 0),
        (v.w_out, 0),
        (v.w_down, core * block),
        (v.own_up_v, 0),
        (v.w_down.at[pl.ds(1, 1)], core * block),
        (v.own_qkv_v, 0),
        (v.own_small_v, 0),
    )
    gather = Gather(
        place,
        pieces,
        (shard, shard, shard, block, shard, block, shard, shard),
        (False, False, True, False, False, False, False, False),
        owns,
        (
            v.s_w_qkv, v.s_w_up, v.s_w_out, v.full_down, v.s_w_up_v, v.full_down_v, v.s_w_qkv_v,
            v.s_w_small_v,
        ),
        *refs[:3],
    )
    moves = Moves(place, *refs[3:])
    width = v.s_qkv.shape[1] // 3
    head_width = width // heads
    hidden = v.s_act.shape[1]
    arrivals = {}

    place.greet()
    shards = [moves.local(source, target) for source, target in zip(groups[0][:7], groups[3][:7])]
    place.meet()
    plane = Plane(place, moves, rows.visual)
    loads = [
        moves.local(v.text.at[0], v.x.at[slice(*rows.own[0])]),
        moves.local(v.visual.at[0], plane.part(v.x_v, 0)),
        moves.local(v.text_dy.at[0], v.s_dy.at[slice(*rows.own[0])]),
        moves.local(v.visual_dy.at[0], plane.part(v.s_dy_v, 0)),
    ]
    swaps = [
        moves.across(v.text.at[0], v.x.at[slice(*rows.other[0])]),
        moves.across(v.text_dy.at[0], v.s_dy.at[slice(*rows.other[0])]),
    ]

    def prepare_qkv():
        for at in (0, 1, 3, 4):
            shards[at].wait()
        prepare_shards(v, core, heads)

    def prepare():
        shards[2].wait()
        prepare_hidden(v, core, block)

    def norm():
        shards[5].wait()
        shards[6].wait()
        prepare_bias(v, core)
        moves.save(v.s_bias, v.bias)
        loads[0].wait()
        swaps[0].wait_recv()

        def body(piece):
            v.wide[piece, :] = normalize(v.x[piece, :].astype(full))[0]

        over_rows(0, rows.split, rows.sizes[0], body)

    def gains_of(s, small):
        v.s_gains[s, :, :] = small.astype(full).T[heads : heads + 2]

    def lower_text():
        moves.save(v.s_w_qkv, v.full_qkv)
        gains_of(0, v.s_w_qkv[0, :, 3 * width :])

        def body(piece):
            v.s_h[piece, :] = (v.wide[piece, :] * v.s_gains[0, 0:1, :]).astype(low)

        over_rows(0, rows.split, rows.sizes[0], body)
        moves.save(v.s_h, v.h)

    def project_text():
        even = 3 * width // 256 * 256

        def columns(piece):
            v.s_qkv[: rows.split, piece] = dot(v.s_h[...], v.s_w_qkv[0, :, piece]).astype(low)

        over_columns(0, even, 256, columns)
        rest = dot(v.s_h[...], v.s_w_qkv[0, :, even:])
        v.s_qkv[: rows.split, even:] = rest[:, : 3 * width - even].astype(low)
        v.gate_rows[: rows.split, :] = rest[:, 3 * width - even :]

    def spread_x():
        arrivals[6] = plane.spread(v.visual.at[0], v.x_v)

    def relay_x():
        arrivals[9] = plane.relay(v.x_v, arrivals[6][1])

    def pass_x():
        arrivals[7] = plane.pass_on(v.x_v, arrivals[6][1], arrivals[9])

    def lower_visual():
        moves.save(v.s_w_small_v, v.full_small_v)
        loads[1].wait()
        arrivals[6][0].wait_recv()
        arrivals[7].wait_recv()
        gains_of(1, v.s_w_small_v[0, :, :])
        v.s_h_v[...] = (normalize(v.x_v[...].astype(full))[0] * v.s_gains[1, 0:1, :]).astype(low)
        moves.save(v.s_h_v, v.h_v)
        for at, piece in enumerate(plane.document(0)):
            first = rows.split + at * rows.visual
            v.gate_rows[first : first + rows.visual, :] = dot(v.s_h_v[piece, :], v.s_w_small_v[0, :, :])

    def project_visual():
        moves.save(v.s_w_qkv_v, v.full_qkv_v)
        v.qkv_v[...] = dot(v.s_h_v[...], v.s_w_qkv_v[0, :, :]).astype(low)
        landing = lambda chip, half: v.landing_qkv.at[chip, half * rows.visual : (half + 1) * rows.visual]
        arrivals[8] = []
        for half, piece in enumerate(plane.document(0)):
            v.landing_qkv[plane.chip(), half * rows.visual : (half + 1) * rows.visual, :] = v.qkv_v[piece, :]
        for at, step in enumerate(plane.steps):
            for half, piece in enumerate(plane.document(1 + at)):
                source = v.qkv_v.at[piece]
                arrivals[8].append(
                    moves.peer(source, landing(plane.chip(), half), step, landing(plane.chip(step), half))
                )

    def receive_visual():
        for arrival in arrivals[8]:
            arrival.wait_recv()
        pair = 3 * lane
        for at in range(heads // 2):
            v.s_qkv[rows.split :, at * pair : (at + 1) * pair] = v.landing_qkv[at, :, :]
            span = slice(at * lane, (at + 1) * lane)
            queries = v.s_qkv[:, at * pair : at * pair + lane] * jnp.asarray(scale, low)
            v.q_t[span, :] = queries.T
            v.v_t[span, :] = v.s_qkv[:, at * pair + 2 * lane : (at + 1) * pair].T
        v.s_gates_t[...] = jax.nn.sigmoid(v.gate_rows[...].T[:8, :])
        moves.save(v.s_gains, v.gains)
        moves.save(v.s_qkv, v.qkv)
        moves.save(v.s_gates_t, v.gates_t)

    def mix():
        moves.save(v.s_text_t, v.text_t)
        moves.save(v.s_visual_t, v.visual_t)
        moves.save(v.s_logs, v.logs)
        is_text = lax.broadcasted_iota(jnp.int32, (1, rows.count), 1) < rows.split
        for head in range(heads):
            span = slice(head * head_width, (head + 1) * head_width)
            gate = v.s_gates_t[head : head + 1, :]
            to_text = jnp.where(is_text, gate, 1.0 - gate)
            v.s_mix_t[span, :] = (
                to_text * v.s_text_t[span, :] + (1.0 - to_text) * v.s_visual_t[span, :]
            ).astype(low)
        v.mix[...] = v.s_mix_t[...].T
        moves.save(v.s_mix_t, v.mix_t)

    def branch():
        moves.save(v.s_w_out, v.full_out)
        for s, (first, last) in enumerate(rows.spans):

            def columns(piece):
                v.wide[first:last, piece] = dot(v.mix[first:last, :], v.s_w_out[s, :, piece])

            over_columns(0, v.wide.shape[1], 256, columns)
        arrivals[0] = rows.swap_parts(moves, v.wide, v.received)

    def spread_dy():
        arrivals[2] = plane.spread(v.visual_dy.at[0], v.s_dy_v)

    def relay_dy():
        arrivals[10] = plane.relay(v.s_dy_v, arrivals[2][1])

    def pass_dy():
        arrivals[3] = plane.pass_on(v.s_dy_v, arrivals[2][1], arrivals[10])

    def middle_rows(s, x, ref, start):
        arrivals[0][s].wait_recv()

        def body(piece, packed):
            to = pl.ds(pl.multiple_of(packed.start - start, row_tile), packed.size)
            value = x[to, :].astype(full) + v.wide[piece, :] + v.received[packed, :]
            v.s_middle[packed, :] = value
            ref[to, :] = (normalize(value)[0] * v.s_gains[s, 1:2, :]).astype(low)

        rows.over_own(s, body)
        packed = slice(*rows.packed[s])
        moves.save(v.s_middle.at[packed], v.middle.at[packed])

    def middle_visual():
        middle_rows(1, v.x_v, v.s_hm_v, rows.packed[1][0])
        arrivals[4] = plane.spread(plane.part(v.s_hm_v, 0), v.s_hm_v)

    def middle_text():
        middle_rows(0, v.x, v.s_hm, 0)
        arrivals[1] = rows.swap_own(moves, v.s_hm, 0)

    def relay_hm():
        arrivals[11] = plane.relay(v.s_hm_v, arrivals[4][1])

    def pass_hm():
        arrivals[5] = plane.pass_on(v.s_hm_v, arrivals[4][1], arrivals[11])

    def up_part(hm, w_up, act_ref, slope_ref, start, stop):
        size = 256 if (stop - start) % 256 == 0 else lane

        def columns(piece):
            act, slope = gelu_both(dot(hm[...], w_up[0, :, piece]))
            act_ref[:, piece] = act.astype(low)
            slope_ref[:, piece] = slope.astype(low)

        over_columns(start, stop, size, columns)

    def up_first():
        moves.save(v.s_w_up, v.full_up)
        arrivals[1].wait_recv()
        loads[2].wait()
        swaps[1].wait_recv()
        moves.save(v.s_hm, v.hm)
        moves.save(v.s_dy, v.dy)
        up_part(v.s_hm, v.s_w_up, v.s_act, v.s_slope, 0, hidden // 2)

    def up_second():
        up_part(v.s_hm, v.s_w_up, v.s_act, v.s_slope, hidden // 2, hidden)
        moves.save(v.s_act, v.act)
        moves.save(v.s_slope, v.slope)

    def up_visual():
        moves.save(v.s_w_up_v, v.full_up_v)
        arrivals[4][0].wait_recv()
        arrivals[5].wait_recv()
        moves.save(v.s_hm_v, v.hm_v)
        up_part(v.s_hm_v, v.s_w_up_v, v.s_act_v, v.s_slope_v, 0, v.s_act_v.shape[1])
        moves.save(v.s_act_v, v.act_v)
        moves.save(v.s_slope_v, v.slope_v)

    def down_part(act, dy, part):
        count = act.shape[1]

        def columns(piece):
            part[0, piece, :] = dot_rows(act[:, piece], dy[...]).astype(low)

        over_columns(0, count, 256 if count % 256 == 0 else lane, columns)

    def down_text():
        down_part(v.s_act, v.s_dy, v.s_part_down)
        moves.save(v.s_part_down, v.part_down)

    def down_visual():
        loads[3].wait()
        arrivals[2][0].wait_recv()
        arrivals[3].wait_recv()
        moves.save(v.s_dy_v, v.dy_v)
        down_part(v.s_act_v, v.s_dy_v, v.s_part_down_v)
        moves.save(v.s_part_down_v, v.part_down_v)

    stages = [prepare, norm, lower_text, project_text, lower_visual, project_visual, receive_visual]
    stages += [functools.partial(attend_head, rows, head_width, v, head) for head in range(heads)]
    stages += [mix, branch, middle_visual, middle_text, pass_hm, up_first, up_second, up_visual]
    stages += [down_text, down_visual, spread_dy, pass_dy, spread_x, pass_x]
    stages += [prepare_qkv, relay_x, relay_dy, relay_hm]
    gather.run(plan, stages)
    moves.finish()
    gather.finish()


def front(n_docs, heads, scale, pieces, plan, inputs):
    line_size = n_docs // 4
    count = 2 * (inputs.text.shape[1] + inputs.visual.shape[1])
    dim = inputs.w_out.shape[2]
    width, hidden = inputs.w_qkv.shape[2] // 6, inputs.w_up.shape[2] // 2
    text, plane = 2 * inputs.text.shape[1], 8 * inputs.visual.shape[1]
    wide = 3 * width + lane
    shard = inputs.w_qkv.shape[1]
    kept = FrontKept(
        s_h=((text, dim), low),
        s_h_v=((plane, dim), low),
        s_qkv=((count, 3 * width), low),
        s_gates_t=((8, count), full),
        s_text_t=((width, count), full),
        s_visual_t=((width, count), full),
        s_logs=((16, count), full),
        s_mix_t=((width, count), low),
        s_middle=((count // 2, dim), full),
        s_hm=((text, dim), low),
        s_hm_v=((plane, dim), low),
        s_act=((text, hidden), low),
        s_act_v=((plane, hidden // 4), low),
        s_slope=((text, hidden), low),
        s_slope_v=((plane, hidden // 4), low),
        s_part_down=((1, hidden, dim), low),
        s_part_down_v=((1, hidden // 4, dim), low),
        s_dy=((text, dim), low),
        s_dy_v=((plane, dim), low),
        s_gains=((2, 2, dim), full),
        s_bias=((count, lane), full),
    )
    weights = (
        ((1, dim, wide), low),
        ((1, dim, hidden), low),
        ((2, width, dim), low),
        ((1, hidden, dim), low),
        ((1, dim, hidden // 4), low),
        ((1, hidden // 4, dim), low),
        ((1, dim, 3 * lane), low),
        ((1, dim, lane), low),
    )
    shards = same_as(inputs[:7])
    scratch = FrontScratch(
        shard_qkv=shards[0],
        shard_gate=shards[1],
        shard_up=shards[2],
        shard_attn=shards[3],
        shard_ffn=shards[4],
        shard_text_mask=shards[5],
        shard_visual_mask=shards[6],
        own_qkv=((1, shard, wide), low),
        own_qkv_v=((4, shard, 3 * lane), low),
        own_small_v=((1, shard, lane), low),
        own_up=((1, shard, hidden), low),
        own_up_v=((4, shard, hidden // 4), low),
        s_w_qkv=weights[0],
        s_w_qkv_v=weights[6],
        s_w_small_v=weights[7],
        s_w_up=weights[1],
        s_w_up_v=weights[4],
        s_w_out=weights[2],
        x=((text, dim), low),
        x_v=((plane, dim), low),
        wide=((count, dim), full),
        qkv_v=((plane, 3 * lane), low),
        landing_qkv=((4, 2 * inputs.visual.shape[1], 3 * lane), low),
        received=((count // 2, dim), full),
        gate_rows=((count, lane), full),
        q_t=((width, count), low),
        v_t=((width, count), low),
        mix=((count, width), low),
    )
    results = FrontOut(*weights, *kept)
    values = pl.pallas_call(
        functools.partial(front_kernel, line_size, heads, scale, pieces, plan),
        out_shape=shapes_of(results),
        in_specs=specs_of(len(inputs), 0),
        out_specs=specs_of(len(results), 0),
        scratch_shapes=scratch_of(kept)
        + scratch_of(scratch)
        + sems((len(pieces), 5), (len(pieces), n_docs), len(pieces), 39, 26, 26),
        compiler_params=pltpu.CompilerParams(
            collective_id=0, has_side_effects=True, vmem_limit_bytes=vmem_limit
        ),
        name="gather_and_front",
    )(*inputs)
    return FrontOut(*values)


def scatter_buffers(pieces, arrays, splits, n_docs):
    line_size = n_docs // 4
    group = []
    for piece in pieces:
        ends = line_size // 2 if splits[piece.array] else line_size
        block = (piece.rows, arrays[piece.array][0][2])
        if piece.route == lines_first:
            group += [((ends, *block), low)] * 5
        elif piece.route == line_only:
            group += [((1, row_tile, lane), low)] * 3 + [((ends, 1, *block), low)] * 2
        else:
            group += [((1, *block), low)] * 3 + [((ends, 4, *block), low)] * 2
    return scratch_of(group)


def grouped(refs, size):
    return [refs[first : first + size] for first in range(0, len(refs), size)]


def norm_back(grad, normed, inverse, gain):
    scaled = grad * gain
    return inverse * (
        scaled
        - jnp.mean(scaled, -1, keepdims=True)
        - normed * jnp.mean(scaled * normed, -1, keepdims=True)
    )


class FfnIn(NamedTuple):
    full_down: object
    dy: object
    slope: object
    full_up: object
    part_down: object
    hm: object
    middle: object
    gains: object
    act: object
    full_out: object
    mix_t: object
    text_t: object
    visual_t: object
    gates_t: object
    full_down_v: object
    dy_v: object
    slope_v: object
    full_up_v: object
    part_down_v: object
    hm_v: object
    act_v: object


class FfnLoaded(NamedTuple):
    s_full_down: object
    s_dy: object
    s_slope: object
    s_full_up: object
    s_part_down: object
    s_hm: object
    s_middle: object
    s_gains: object
    s_act: object
    s_full_out: object
    s_mix_t: object
    s_text_t: object
    s_visual_t: object
    s_gates_t: object
    s_full_down_v: object
    s_dy_v: object
    s_slope_v: object
    s_full_up_v: object
    s_part_down_v: object
    s_hm_v: object
    s_act_v: object


class FfnOut(NamedTuple):
    text_out: object
    visual_out: object
    stage_down: object
    part_up: object
    part_up_v: object
    part_out: object
    grad_middle: object
    gain_part: object
    gate_grad_t: object
    text_grad_t: object
    visual_grad_t: object


class FfnScratch(NamedTuple):
    s_part_up: object
    s_part_up_v: object
    s_part_out: object
    s_grad_middle: object
    s_gain_part: object
    s_gate_grad_t: object
    s_text_grad_t: object
    s_visual_grad_t: object
    stage: object
    wide: object
    wide_out: object
    received: object
    received_out: object
    branch: object
    result: object
    mix_grad: object
    mix_grad_t: object
    wide_v: object
    received_v: object
    outgoing_v: object
    landing_v: object
    wide_out_v: object
    received_out_v: object
    outgoing_out_v: object
    landing_out_v: object


def ffn_kernel(line_size, heads, pieces, plan, *refs):
    groups = []
    for group in (FfnIn, FfnOut, FfnLoaded, FfnScratch):
        count = len(group._fields)
        groups.append(group(*refs[:count]))
        refs = refs[count:]
    v = merged(*groups)
    buffers = grouped(refs[: 5 * len(pieces)], 5)
    send_sems, recv_sems, *move_sems = refs[5 * len(pieces) :]
    place = Place(line_size)
    moves = Moves(place, *move_sems)
    rows = Rows(v.text_out.shape[1], v.visual_out.shape[1])
    width = v.mix_t.shape[0]
    head_width = width // heads
    dim = v.hm.shape[1]
    arrivals = {}

    plane = Plane(place, moves, rows.visual)

    def finish_rows(piece, total):
        add_rows(v.stage.at[piece.array], total, piece.first)

    scatter = Scatter(
        place,
        pieces,
        (False, False),
        (v.part_down, v.part_down_v),
        (v.s_part_down, v.s_part_down_v),
        buffers,
        send_sems,
        recv_sems,
        finish_rows,
    )
    place.greet()
    loads = FfnIn(*(moves.local(source, target) for source, target in zip(groups[0], groups[2])))
    place.meet()

    def hidden(dy, w_down, slope):
        count = slope.shape[1]

        def columns(piece):
            grad = dot_back(dy[...], w_down[0, piece, :])
            slope[:, piece] = (grad * slope[:, piece].astype(full)).astype(low)

        over_columns(0, count, 256 if count % 256 == 0 else lane, columns)

    def hidden_visual():
        loads.full_down_v.wait()
        loads.dy_v.wait()
        loads.slope_v.wait()
        hidden(v.s_dy_v, v.s_full_down_v, v.s_slope_v)

    def hidden_text():
        loads.full_down.wait()
        loads.dy.wait()
        loads.slope.wait()
        hidden(v.s_dy, v.s_full_down, v.s_slope)
        loads.part_down.wait()
        loads.part_down_v.wait()

    def back_visual():
        loads.full_up_v.wait()
        v.wide_v[...] = dot_back(v.s_slope_v[...], v.s_full_up_v[0, :, :])
        arrivals[0] = plane.halve(v.wide_v, v.received_v)

    def share_visual():
        arrivals[0].wait_recv()
        arrivals[1] = plane.share(v.wide_v, v.received_v, v.outgoing_v, v.landing_v)

    def back_text():
        loads.full_up.wait()

        def columns(piece):
            v.wide[:, piece] = dot_back(v.s_slope[...], v.s_full_up[0, piece, :])

        over_columns(0, dim, 256, columns)
        arrivals[2] = rows.swap_parts(moves, v.wide, v.received, (0,))[0]

    def up_part(hm, slope, part):
        def columns(piece):
            part[0, piece, :] = dot_rows(hm[:, piece], slope[...]).astype(low)

        over_columns(0, dim, 256, columns)

    def up_text():
        loads.hm.wait()
        up_part(v.s_hm, v.s_slope, v.s_part_up)
        moves.save(v.s_part_up, v.part_up)

    def up_visual():
        loads.hm_v.wait()
        up_part(v.s_hm_v, v.s_slope_v, v.s_part_up_v)
        moves.save(v.s_part_up_v, v.part_up_v)

    def middle_rows(s, piece, packed, grad, dy):
        normed, inverse = normalize(v.s_middle[packed, :])
        v.s_gain_part[s, 0:1, :] += jnp.sum(grad * normed, 0, keepdims=True)
        grad = dy.astype(full) + norm_back(grad, normed, inverse, v.s_gains[s, 1:2, :])
        v.s_grad_middle[packed, :] = grad
        v.branch[piece, :] = grad.astype(low)

    def middle_visual():
        loads.middle.wait()
        loads.gains.wait()
        v.s_gain_part[...] = jnp.zeros_like(v.s_gain_part)
        for arrival in arrivals[1]:
            arrival.wait_recv()
        grad = plane.total(v.wide_v, v.received_v, v.landing_v)
        middle_rows(1, slice(*rows.own[1]), slice(*rows.packed[1]), grad, v.s_dy_v[: rows.visual, :])
        arrivals[3] = rows.swap_own(moves, v.branch, 1)

    def middle_text():
        arrivals[2].wait_recv()

        def body(piece, packed):
            grad = v.wide[piece, :] + v.received[packed, :]
            middle_rows(0, piece, packed, grad, v.s_dy[piece, :])

        rows.over_own(0, body)
        arrivals[4] = rows.swap_own(moves, v.branch, 0)
        moves.save(v.s_gain_part, v.gain_part)
        moves.save(v.s_grad_middle, v.grad_middle)

    def result_text():
        loads.act.wait()

        def columns(piece):
            v.wide_out[:, piece] = dot(v.s_act[...], v.s_full_down[0, :, piece])

        over_columns(0, dim, 256, columns)
        arrivals[5] = rows.swap_parts(moves, v.wide_out, v.received_out, (0,))[0]

    def result_visual():
        loads.act_v.wait()
        v.wide_out_v[...] = dot(v.s_act_v[...], v.s_full_down_v[0, :, :])
        arrivals[6] = plane.halve(v.wide_out_v, v.received_out_v)

    def share_result():
        arrivals[6].wait_recv()
        arrivals[7] = plane.share(v.wide_out_v, v.received_out_v, v.outgoing_out_v, v.landing_out_v)

    def out_part():
        loads.full_out.wait()
        loads.mix_t.wait()
        for s, (first, last) in enumerate(rows.spans):
            arrivals[4 - s].wait_recv()
            v.s_part_out[s, :, :] = dot(v.s_mix_t[:, first:last], v.branch[first:last, :]).astype(low)
            v.mix_grad[first:last, :] = dot_back(v.branch[first:last, :], v.s_full_out[s, :, :])
        moves.save(v.s_part_out, v.part_out)

    def gates():
        loads.text_t.wait()
        loads.visual_t.wait()
        loads.gates_t.wait()
        v.mix_grad_t[...] = v.mix_grad[...].T
        is_text = lax.broadcasted_iota(jnp.int32, (1, rows.count), 1) < rows.split
        for head in range(heads):
            span = slice(head * head_width, (head + 1) * head_width)
            gate = v.s_gates_t[head : head + 1, :]
            to_text = jnp.where(is_text, gate, 1.0 - gate)
            grad = v.mix_grad_t[span, :]
            toward = jnp.sum(grad * (v.s_text_t[span, :] - v.s_visual_t[span, :]), 0, keepdims=True)
            v.s_gate_grad_t[head : head + 1, :] = (
                jnp.where(is_text, toward, -toward) * gate * (1.0 - gate)
            )
            v.s_text_grad_t[span, :] = (to_text * grad).astype(low)
            v.s_visual_grad_t[span, :] = ((1.0 - to_text) * grad).astype(low)
        v.s_gate_grad_t[heads:, :] = jnp.zeros((8 - heads, rows.count), full)
        moves.save(v.s_gate_grad_t, v.gate_grad_t)
        moves.save(v.s_text_grad_t, v.text_grad_t)
        moves.save(v.s_visual_grad_t, v.visual_grad_t)

    def finish_text():
        arrivals[5].wait_recv()

        def body(piece, packed):
            v.result[packed, :] = (
                v.s_middle[packed, :] + v.wide_out[piece, :] + v.received_out[packed, :]
            ).astype(low)

        rows.over_own(0, body)
        moves.save(v.result.at[slice(*rows.packed[0])], v.text_out.at[0])

    def finish_visual():
        for arrival in arrivals[7]:
            arrival.wait_recv()
        packed = slice(*rows.packed[1])
        total = plane.total(v.wide_out_v, v.received_out_v, v.landing_out_v)
        v.result[packed, :] = (v.s_middle[packed, :] + total).astype(low)
        moves.save(v.result.at[packed], v.visual_out.at[0])

    stages = [hidden_visual, back_visual, hidden_text, share_visual, back_text, up_text, up_visual]
    stages += [middle_visual, middle_text, result_text, result_visual, out_part, gates, share_result]
    scatter.run(plan, stages + [finish_text, finish_visual])
    moves.save(v.stage, v.stage_down)
    moves.finish()
    scatter.finish()


def ffn_back(n_docs, heads, pieces, plan, text, visual, inputs):
    line_size = n_docs // 4
    hidden = inputs.act.shape[1]
    width, count = inputs.mix_t.shape
    dim = inputs.hm.shape[1]
    rows = inputs.part_down.shape[1] // n_docs
    plane = 8 * visual.shape[1]
    scratch = FfnScratch(
        s_part_up=((1, dim, hidden), low),
        s_part_up_v=((1, dim, hidden // 4), low),
        s_part_out=((2, width, dim), low),
        s_grad_middle=((count // 2, dim), full),
        s_gain_part=((2, 8, dim), full),
        s_gate_grad_t=((8, count), full),
        s_text_grad_t=((width, count), low),
        s_visual_grad_t=((width, count), low),
        stage=((2, rows, dim), full),
        wide=((2 * text.shape[1], dim), full),
        wide_out=((2 * text.shape[1], dim), full),
        received=((text.shape[1], dim), full),
        received_out=((text.shape[1], dim), full),
        branch=((count, dim), low),
        result=((count // 2, dim), low),
        mix_grad=((count, width), full),
        mix_grad_t=((width, count), full),
        wide_v=((plane, dim), full),
        received_v=((plane // 2, dim), full),
        outgoing_v=((3 * plane // 8, dim), low),
        landing_v=((3 * plane // 8, dim), low),
        wide_out_v=((plane, dim), full),
        received_out_v=((plane // 2, dim), full),
        outgoing_out_v=((3 * plane // 8, dim), low),
        landing_out_v=((3 * plane // 8, dim), low),
    )
    results = FfnOut(
        (text.shape, low), (visual.shape, low), scratch.stage, *scratch[:8]
    )
    loaded = same_as(inputs)
    values = pl.pallas_call(
        functools.partial(ffn_kernel, line_size, heads, pieces, plan),
        out_shape=shapes_of(results),
        in_specs=specs_of(len(inputs), 0),
        out_specs=specs_of(len(results), 0),
        scratch_shapes=scratch_of(loaded)
        + scratch_of(scratch)
        + scatter_buffers(pieces, same_as([inputs.part_down, inputs.part_down_v]), (False, False), n_docs)
        + sems(len(pieces), arrival_offsets(pieces, line_size)[-1], 32, 12, 12),
        compiler_params=pltpu.CompilerParams(
            collective_id=1, has_side_effects=True, vmem_limit_bytes=vmem_limit
        ),
        name="ffn_back_and_scatter",
    )(*inputs)
    return FfnOut(*values)


class AttentionIn(NamedTuple):
    qkv: object
    logs: object
    text_t: object
    visual_t: object
    text_grad_t: object
    visual_grad_t: object
    bias: object
    part_up: object
    part_up_v: object
    part_out: object
    gate_grad_t: object
    full_qkv: object
    full_qkv_v: object
    full_small_v: object
    h: object
    h_v: object
    grad_middle: object
    gains: object
    gain_part: object
    stage_down: object
    text: object
    visual: object


class AttentionLoaded(NamedTuple):
    s_qkv: object
    s_logs: object
    s_text_t: object
    s_visual_t: object
    s_text_grad_t: object
    s_visual_grad_t: object
    s_bias: object
    s_part_up: object
    s_part_up_v: object
    s_part_out: object
    s_gate_grad_t: object
    s_full_qkv: object
    s_full_qkv_v: object
    s_full_small_v: object
    s_h: object
    s_h_v: object
    s_grad_middle: object
    s_gains: object
    s_gain_part: object
    s_stage_down: object


class AttentionOut(NamedTuple):
    text_grad: object
    visual_grad: object
    grad_down: object
    grad_qkv: object
    grad_gate: object
    grad_up: object
    grad_out: object
    grad_gain_attn: object
    grad_gain_ffn: object


class AttentionScratch(NamedTuple):
    part_qkv: object
    part_qkv_v: object
    part_small: object
    x: object
    q_t: object
    k_t: object
    query_grad_t: object
    text_grad_n: object
    visual_grad_n: object
    key_sum: object
    value_sum: object
    grad_wide: object
    wide: object
    received: object
    grad_v: object
    wide_v: object
    received_v: object
    outgoing_v: object
    landing_v: object
    gain_sum: object
    gains_row: object
    stage_up: object
    stage_out: object
    stage_qkv: object
    stage_up_v: object
    stage_qkv_v: object
    stage_small: object
    own_qkv: object
    peer_up: object
    peer_up_v: object
    peer_small: object
    s_grad_up: object
    s_grad_gate: object
    s_grad_gain_attn: object
    s_grad_gain_ffn: object


def attend_head_back(rows, head_width, scale, v, number):
    pair = 2 * head_width
    at, odd = number // 2, number % 2
    columns = [slice((3 * at + third) * pair, (3 * at + third + 1) * pair) for third in range(3)]
    wide = slice(at * pair, (at + 1) * pair)
    keys, values = v.s_qkv[:, columns[1]], v.s_qkv[:, columns[2]]
    if not odd:
        v.key_sum[...] = jnp.zeros_like(v.key_sum)
        v.value_sum[...] = jnp.zeros_like(v.value_sum)
    mine = lax.broadcasted_iota(jnp.int32, (1, pair), 1) // head_width == odd
    bias = v.s_bias[:, 0:1]
    sets = (
        (v.s_text_t, v.s_text_grad_t, v.text_grad_n),
        (v.s_visual_t, v.s_visual_grad_t, v.visual_grad_n),
    )
    head = slice(number * head_width, (number + 1) * head_width)
    for first, last in query_spans(rows.count):
        scores = dot(keys, head_wide(v.q_t[head, first:last], odd)) + bias
        queries = jnp.where(mine, v.s_qkv[first:last, columns[0]] * jnp.asarray(scale, low), 0)
        pieces = []
        for t, (output_t, grad_t, grad) in enumerate(sets):
            start, stop = rows.spans[t]
            out_grad = grad_t[head, first:last]
            delta = jnp.sum(out_grad.astype(full) * output_t[head, first:last], 0, keepdims=True)
            row = 8 * t + number
            probs = jnp.exp(scores[start:stop] - v.s_logs[row : row + 1, first:last])
            grad_probs = dot(values[start:stop], head_wide(out_grad, odd))
            grad_scores = (probs * (grad_probs - delta)).astype(low)
            natural = jnp.where(mine, grad[first:last, wide], 0)
            v.value_sum[start:stop, :] += dot(probs.astype(low), natural)
            v.key_sum[start:stop, :] += dot(grad_scores, queries)
            pieces.append(grad_scores)
        v.query_grad_t[head, first:last] = (
            dot(v.k_t[head, :], jnp.concatenate(pieces, 0)) * scale
        ).astype(low)
    if odd:
        v.grad_wide[:, columns[0]] = v.query_grad_t[wide, :].T
        v.grad_wide[:, columns[1]] = v.key_sum[...].astype(low)
        v.grad_wide[:, columns[2]] = v.value_sum[...].astype(low)


def attention_kernel(line_size, heads, scale, block, pieces, plan, *refs):
    groups = []
    for group in (AttentionIn, AttentionOut, AttentionLoaded, AttentionScratch):
        count = len(group._fields)
        groups.append(group(*refs[:count]))
        refs = refs[count:]
    v = merged(*groups)
    buffers = grouped(refs[: 5 * len(pieces)], 5)
    send_sems, recv_sems, *move_sems = refs[5 * len(pieces) :]
    place = Place(line_size)
    core = place.core
    moves = Moves(place, *move_sems)
    rows = Rows(v.text.shape[1], v.visual.shape[1])
    width = v.qkv.shape[1] // 3
    head_width = width // heads
    dim = v.h.shape[1]
    stages_of = (v.stage_up, v.stage_out, v.stage_qkv, v.stage_up_v, v.stage_qkv_v, v.stage_small)
    arrivals = {}
    plane = Plane(place, moves, rows.visual)

    def finish_rows(piece, total, quad=quads[0]):
        part = place.index(0, *quad) if piece.route == plane_shared else piece.part
        add_rows(stages_of[piece.array].at[part], total, piece.first)

    scatter = Scatter(
        place,
        pieces,
        (False, True, False, False, False, False),
        (v.part_up, v.part_out, v.part_qkv, v.part_up_v, v.part_qkv_v, v.part_small),
        (v.s_part_up, v.s_part_out, v.part_qkv, v.s_part_up_v, v.part_qkv_v, v.part_small),
        buffers,
        send_sems,
        recv_sems,
        finish_rows,
    )
    place.greet()
    loads = AttentionIn(
        *(moves.local(source, target) for source, target in zip(groups[0], groups[2])),
        *(moves.local(ref.at[0], v.x.at[slice(*rows.packed[s])]) for s, ref in enumerate((v.text, v.visual))),
    )
    place.meet()

    def prepare():
        for load in loads[:7]:
            load.wait()
        for at in range(heads // 2):
            span, first = slice(at * lane, (at + 1) * lane), 3 * at * lane
            v.q_t[span, :] = (v.s_qkv[:, first : first + lane] * jnp.asarray(scale, low)).T
            v.k_t[span, :] = v.s_qkv[:, first + lane : first + 2 * lane].T
        v.text_grad_n[...] = v.s_text_grad_t[...].T
        v.visual_grad_n[...] = v.s_visual_grad_t[...].T
        loads.part_up.wait()
        loads.part_up_v.wait()
        loads.part_out.wait()

    def send_visual():
        loads.gate_grad_t.wait()
        empty = jnp.zeros((lane - 8, rows.count), full)
        v.grad_wide[:, 3 * width : 3 * width + lane] = (
            jnp.concatenate([v.s_gate_grad_t[...], empty], 0).T.astype(low)
        )
        v.grad_wide[:, 3 * width + lane :] = jnp.zeros((rows.count, 2 * lane), low)
        arrivals[4] = []
        pair = 3 * lane
        for half, piece in enumerate(plane.document(0)):
            first = rows.split + half * rows.visual
            span = slice(first, first + rows.visual)
            of = lambda step: v.grad_wide.at[span, pl.ds(pl.multiple_of(plane.chip(step) * pair, lane), pair)]
            arrivals[4].append(moves.local(of(None), v.grad_v.at[piece]).wait)
            for at, step in enumerate(plane.steps):
                target = v.grad_v.at[plane.document(1 + at)[half]]
                arrivals[4].append(moves.peer(of(step), target, step).wait_recv)

    def back_text():
        loads.full_qkv.wait()

        def columns(piece):
            grad = v.grad_wide[: rows.split, : 3 * width + lane]
            v.wide[:, piece] = dot_back(grad, v.s_full_qkv[0, piece, :])

        over_columns(0, dim, 256, columns)
        arrivals[0] = rows.swap_parts(moves, v.wide, v.received, (0,))[0]

    def text_part():
        loads.h.wait()

        def columns(piece):
            grad = dot_rows(v.s_h[:, piece], v.grad_wide[: rows.split, : 3 * width + lane])
            v.part_qkv[0, piece, :] = grad[:, : 3 * width].astype(low)
            v.gain_sum[0, piece, :] = grad[:, 3 * width :]

        over_columns(0, dim, 256, columns)

    def back_visual():
        loads.full_qkv_v.wait()
        loads.full_small_v.wait()
        for wait in arrivals[4]:
            wait()
        v.wide_v[...] = dot_back(v.grad_v[...], v.s_full_qkv_v[0, :, :])
        for half, piece in enumerate(plane.document(0)):
            first = rows.split + half * rows.visual
            small = v.grad_wide[first : first + rows.visual, 3 * width : 3 * width + lane]
            v.wide_v[piece, :] += dot_back(small, v.s_full_small_v[0, :, :])
        arrivals[5] = plane.halve(v.wide_v, v.received_v)

    def visual_part():
        loads.h_v.wait()

        def columns(piece):
            v.part_qkv_v[0, piece, :] = dot_rows(v.s_h_v[:, piece], v.grad_v[...]).astype(low)

        over_columns(0, dim, 256, columns)
        total = 0.0
        for half, piece in enumerate(plane.document(0)):
            first = rows.split + half * rows.visual
            small = v.grad_wide[first : first + rows.visual, 3 * width : 3 * width + lane]
            total = total + dot_rows(v.s_h_v[piece, :], small)
        v.gain_sum[1, :, :] = total

    def share_visual():
        arrivals[5].wait_recv()
        arrivals[6] = plane.share(v.wide_v, v.received_v, v.outgoing_v, v.landing_v)

    def token_rows(s, packed, grad):
        normed, inverse = normalize(v.x[packed, :].astype(full))
        v.gains_row[s, heads : heads + 1, :] += jnp.sum(grad * normed, 0, keepdims=True)
        v.s_grad_middle[packed, :] += norm_back(grad, normed, inverse, v.s_gains[s, 0:1, :])

    def small_part(s):
        small = v.gain_sum[s, :, :] + v.gains_row[s, :, :].T
        v.part_small[s, :, :] = small.astype(low)
        ref = (v.text_grad, v.visual_grad)[s]
        moves.save(v.s_grad_middle.at[slice(*rows.packed[s])], ref.at[0])

    def tokens_text():
        loads.grad_middle.wait()
        loads.gains.wait()
        loads.gain_part.wait()
        v.gains_row[...] = jnp.zeros_like(v.gains_row)
        for s in range(2):
            loads[-2 + s].wait()
            v.gains_row[s, heads + 1 : heads + 2, :] = v.s_gain_part[s, 0:1, :]
        arrivals[0].wait_recv()

        def body(piece, packed):
            token_rows(0, packed, v.wide[piece, :] + v.received[packed, :])

        rows.over_own(0, body)
        small_part(0)

    def tokens_visual():
        for arrival in arrivals[6]:
            arrival.wait_recv()
        grad = plane.total(v.wide_v, v.received_v, v.landing_v)
        token_rows(1, slice(*rows.packed[1]), grad)
        small_part(1)

    def share_down():
        loads.stage_down.wait()
        block = v.s_stage_down.shape[1]
        mine = lambda of: v.grad_down.at[:, pl.ds(pl.multiple_of(of * block, row_tile), block), :]
        moves.save(v.s_stage_down, mine(core))
        arrivals[3] = moves.across(v.s_stage_down, mine(core), mine(1 - core))

    def share_up():
        arrivals[1] = moves.across(v.stage_up, v.peer_up)
        arrivals[2] = moves.across(v.stage_up_v, v.peer_up_v)

    def share_out():
        owner = place.z // (line_size // 2) == core
        moves_out = (
            pltpu.make_async_copy(v.stage_out, v.grad_out, moves.local_sems.at[moves.locals]),
            pltpu.make_async_remote_copy(
                src_ref=v.stage_out,
                dst_ref=v.grad_out,
                send_sem=moves.send_sems.at[moves.remotes],
                recv_sem=moves.recv_sems.at[moves.remotes],
                device_id=moves.other,
                device_id_type=MESH,
            ),
        )
        moves.locals += 1
        moves.remotes += 1

        def start():
            for move in moves_out:
                move.start()

        def wait():
            moves_out[0].wait()
            moves_out[1].wait_send()

        pl.when(owner)(start)
        moves.to_end.append(lambda: pl.when(owner)(wait))
        moves.to_end.append(lambda: pl.when(jnp.logical_not(owner))(lambda: moves_out[1].wait_recv()))

    def finish_up():
        arrivals[1].wait_recv()
        arrivals[2].wait_recv()
        first = core == 0
        count = v.stage_up.shape[2] // block
        for s in range(2):
            pieces = []
            for at in range(count):
                if s == 0:
                    span = slice(at * block, (at + 1) * block)
                    own, peer = (ref[0, :, span] for ref in (v.stage_up, v.peer_up))
                else:
                    span = slice(at // 4 * block, (at // 4 + 1) * block)
                    own, peer = (ref[at % 4, :, span] for ref in (v.stage_up_v, v.peer_up_v))
                pieces += [jnp.where(first, own, peer), jnp.where(first, peer, own)]
            v.s_grad_up[s, :, :] = jnp.concatenate(pieces, 1)
        moves.save(v.s_grad_up, v.grad_up)

    stages = [prepare]
    stages += [functools.partial(attend_head_back, rows, head_width, scale, v, head) for head in range(heads)]
    stages += [send_visual, back_text, text_part, back_visual, visual_part, share_visual]
    stages += [tokens_text, tokens_visual, share_up, share_out, finish_up, share_down]
    scatter.run(plan, stages)

    def mine(third, of):
        first = third * 2 * width + of * width
        return v.grad_qkv.at[:, :, pl.ds(pl.multiple_of(first, lane), width)]

    last = [moves.across(v.stage_small, v.peer_small)]
    for third in range(3):
        for at in range(heads // 2):
            to = slice(at * lane, (at + 1) * lane)
            v.own_qkv[third, 0, :, to] = v.stage_qkv[0, :, (3 * at + third) * lane : (3 * at + third + 1) * lane]
            v.own_qkv[third, 1, :, to] = v.stage_qkv_v[at, :, third * lane : (third + 1) * lane]
        source = v.own_qkv.at[third]
        moves.save(source, mine(third, core))
        last.append(moves.across(source, mine(third, core), mine(third, 1 - core)))
    last[0].wait_recv()
    for s in range(2):
        own, peer = v.stage_small[s, :, :], v.peer_small[s, :, :]
        columns = own.shape[0]
        empty = jnp.zeros((lane - columns, lane), full)
        own, peer = (jnp.concatenate([value, empty], 0).T[:, :columns] for value in (own, peer))
        v.s_grad_gate[:heads, s, :] = jnp.where(core == 0, own, peer)[:heads]
        v.s_grad_gate[heads:, s, :] = jnp.where(core == 0, peer, own)[:heads]
        both = own + peer
        v.s_grad_gain_attn[s : s + 1, :] = both[heads : heads + 1]
        v.s_grad_gain_ffn[s : s + 1, :] = both[heads + 1 : heads + 2]
    moves.save(v.s_grad_gate, v.grad_gate)
    moves.save(v.s_grad_gain_attn, v.grad_gain_attn)
    moves.save(v.s_grad_gain_ffn, v.grad_gain_ffn)
    for arrival in last[1:] + [arrivals[3]]:
        arrival.wait_recv()
    moves.finish()
    scatter.finish()


def attention_back(n_docs, heads, scale, pieces, plan, inputs):
    line_size = n_docs // 4
    count, dim = inputs.qkv.shape[0], inputs.h.shape[1]
    width = inputs.qkv.shape[1] // 3
    text, visual = inputs.text.shape[1], inputs.visual.shape[1]
    hidden = inputs.part_up.shape[2]
    rows = dim // n_docs
    block = hidden // n_docs
    splits = (False, True, False, False, False, False)
    parts = (((1, dim, 3 * width), low), ((1, dim, 3 * lane), low), ((2, dim, lane), low))
    arrays = same_as([inputs.part_up, inputs.part_out]) + [parts[0]] + same_as([inputs.part_up_v])
    arrays += parts[1:]
    results = AttentionOut(
        text_grad=(inputs.text.shape, full),
        visual_grad=(inputs.visual.shape, full),
        grad_down=((2, 2 * inputs.stage_down.shape[1], dim), full),
        grad_qkv=((2, rows, 6 * width), full),
        grad_gate=((2 * heads, 2, rows), full),
        grad_up=((2, rows, 2 * hidden), full),
        grad_out=((2, rows, dim), full),
        grad_gain_attn=((2, rows), full),
        grad_gain_ffn=((2, rows), full),
    )
    scratch = AttentionScratch(
        part_qkv=parts[0],
        part_qkv_v=parts[1],
        part_small=parts[2],
        x=((count // 2, dim), low),
        q_t=((width, count), low),
        k_t=((width, count), low),
        query_grad_t=((width, count), low),
        text_grad_n=((count, width), low),
        visual_grad_n=((count, width), low),
        key_sum=((count, lane), full),
        value_sum=((count, lane), full),
        grad_wide=((count, 3 * width + 3 * lane), low),
        wide=((2 * text, dim), full),
        received=((text, dim), full),
        grad_v=((8 * visual, 3 * lane), low),
        wide_v=((8 * visual, dim), full),
        received_v=((4 * visual, dim), full),
        outgoing_v=((3 * visual, dim), low),
        landing_v=((3 * visual, dim), low),
        gain_sum=((2, dim, lane), full),
        gains_row=((2, lane, dim), full),
        stage_up=((1, rows, hidden), full),
        stage_out=((2, rows, dim), full),
        stage_qkv=((1, rows, 3 * width), full),
        stage_up_v=((4, rows, hidden // 4), full),
        stage_qkv_v=((4, rows, 3 * lane), full),
        stage_small=((2, rows, lane), full),
        own_qkv=((3, 2, rows, width), full),
        peer_up=((1, rows, hidden), full),
        peer_up_v=((4, rows, hidden // 4), full),
        peer_small=((2, rows, lane), full),
        s_grad_up=results.grad_up,
        s_grad_gate=results.grad_gate,
        s_grad_gain_attn=results.grad_gain_attn,
        s_grad_gain_ffn=results.grad_gain_ffn,
    )
    loaded = same_as(inputs[:-2])
    values = pl.pallas_call(
        functools.partial(attention_kernel, line_size, heads, scale, block, pieces, plan),
        out_shape=scratch_of(results),
        in_specs=specs_of(len(inputs), 0),
        out_specs=specs_of(len(results), len(results)),
        scratch_shapes=scratch_of(loaded)
        + scratch_of(scratch)
        + scatter_buffers(pieces, arrays, splits, n_docs)
        + sems(len(pieces), arrival_offsets(pieces, line_size)[-1], 35, 19, 19),
        compiler_params=pltpu.CompilerParams(
            collective_id=2, has_side_effects=True, vmem_limit_bytes=50 * 1024 * 1024
        ),
        name="attention_back_and_scatter",
    )(*inputs)
    return AttentionOut(*values)


def publish_kernel(held, count, *refs):
    sources, results, passing = refs[:count], refs[count : 2 * count], refs[2 * count : 3 * count - held]
    arriving, leaving = refs[3 * count - held :]
    copies_in = [
        pltpu.make_async_copy(source, target, arriving.at[at])
        for at, (source, target) in enumerate(zip(sources[held:], passing))
    ]
    ready = [*sources[:held], *passing]
    copies_out = [pltpu.make_async_copy(ready[at], results[at], leaving.at[at]) for at in range(count)]
    for copy in copies_in:
        copy.start()
    for copy in copies_out[:held]:
        copy.start()
    for copy_in, copy_out in zip(copies_in, copies_out[held:]):
        copy_in.wait()
        copy_out.start()
    for copy in copies_out:
        copy.wait()


def publish(held, others):
    arrays = (*held, *others)
    count = len(arrays)
    return pl.pallas_call(
        functools.partial(publish_kernel, len(held), count),
        out_shape=shapes_of(same_as(arrays)),
        in_specs=specs_of(count, len(held)),
        out_specs=specs_of(count, 0),
        scratch_shapes=scratch_of(same_as(others)) + sems(len(others), count),
        compiler_params=pltpu.CompilerParams(vmem_limit_bytes=8 * 1024 * 1024),
        name="publish",
    )(*arrays)


def kernel_path(n_docs, heads, scale, inputs):
    made = [tuple(Piece(*each) for each in pieces) for pieces in (front_pieces, ffn_pieces, attention_pieces)]
    first = front(n_docs, heads, scale, made[0], front_plan, inputs)
    ffn_inputs = FfnIn(*(getattr(first, name) for name in FfnIn._fields))
    second = ffn_back(n_docs, heads, made[1], ffn_plan, inputs.text, inputs.visual, ffn_inputs)
    known = merged(inputs, first, second)
    attention_inputs = AttentionIn(*(getattr(known, name) for name in AttentionIn._fields))
    third = attention_back(n_docs, heads, scale, made[2], attention_plan, attention_inputs)
    held = publish(third, (second.text_out, second.visual_out))
    done = AttentionOut(*held[: len(third)])
    return (
        *held[len(third) :],
        done.text_grad,
        done.visual_grad,
        done.grad_qkv,
        done.grad_out,
        jnp.transpose(done.grad_gate, (1, 2, 0)),
        done.grad_up,
        done.grad_down,
        done.grad_gain_attn,
        done.grad_gain_ffn,
    )


def swap(value):
    return lax.ppermute(value, core_axis, [(0, 1), (1, 0)])


def both(own):
    return jnp.concatenate([own, swap(own)], 0)


def own_sum(partial):
    rows = partial.shape[0] // 2
    return partial[:rows] + swap(partial[rows:])


def normalize_back(gradient, normed, inverse, gain):
    scaled = gradient * gain
    grad_gain = jnp.sum(gradient * normed, 0)
    grad_input = inverse * (
        scaled
        - jnp.mean(scaled, -1, keepdims=True)
        - normed * jnp.mean(scaled * normed, -1, keepdims=True)
    )
    return grad_input, grad_gain


def heads_of(values, heads):
    return values.reshape(values.shape[0], heads, -1)


def attend(queries, keys, values, valid, scale):
    scores = jnp.einsum("qhe,khe->hqk", queries, keys, preferred_element_type=full) * scale
    scores = jnp.where(valid, scores, big_negative)
    top = jnp.max(scores, -1)
    probs = jnp.where(valid, jnp.exp(scores - top[..., None]), 0.0)
    total = jnp.sum(probs, -1)
    weighted = jnp.einsum(
        "hqk,khe->qhe", probs.astype(low), values, preferred_element_type=full
    )
    return weighted / total.T[..., None], top + jnp.log(total)


def attend_back(queries, keys, values, valid, scale, log_total, grad_output, output):
    delta = jnp.sum(grad_output.astype(full) * output, -1).T
    scores = jnp.einsum("qhe,khe->hqk", queries, keys, preferred_element_type=full) * scale
    probs = jnp.where(valid, jnp.exp(scores - log_total[..., None]), 0.0)
    grad_values = jnp.einsum(
        "hqk,qhe->khe", probs.astype(low), grad_output, preferred_element_type=full
    )
    grad_probs = jnp.einsum("qhe,khe->hqk", grad_output, values, preferred_element_type=full)
    grad_scores = (probs * (grad_probs - delta[..., None])).astype(low)
    grad_queries = (
        jnp.einsum("hqk,khe->qhe", grad_scores, keys, preferred_element_type=full) * scale
    )
    grad_keys = (
        jnp.einsum("hqk,qhe->khe", grad_scores, queries, preferred_element_type=full) * scale
    )
    return grad_queries, grad_keys, grad_values


def on_device(
    n_docs,
    text_tokens,
    visual_tokens,
    text_mask,
    visual_mask,
    w_qkv,
    w_out,
    w_gate,
    w_up,
    w_down,
    gain_attn,
    gain_ffn,
    text_cotangent,
    visual_cotangent,
):
    core = lax.axis_index(core_axis)
    width = w_out.shape[2]
    all_heads = w_gate.shape[2]
    heads = all_heads // 2
    half = width // 2
    scale = (width // all_heads) ** (-0.5)
    if n_docs == 16 and w_qkv.shape[1] % row_tile == 0:
        inputs = FrontIn(
            w_qkv=w_qkv,
            w_gate=jnp.transpose(w_gate, (2, 0, 1)),
            w_up=w_up,
            gain_attn=gain_attn,
            gain_ffn=gain_ffn,
            text_mask=text_mask,
            visual_mask=visual_mask,
            text=text_tokens,
            visual=visual_tokens,
            text_dy=text_cotangent,
            visual_dy=visual_cotangent,
            w_out=w_out,
            w_down=w_down,
        )
        return kernel_path(n_docs, heads, scale, inputs)

    def own_columns(array, size, start=0):
        return lax.dynamic_slice_in_dim(array, start + core * size, size, 2)

    own_tokens = (text_tokens[0], visual_tokens[0])
    own_grads = (text_cotangent[0], visual_cotangent[0])

    def reorder(mask):
        rows = mask.shape[1] // 2
        return (
            jnp.concatenate(
                [
                    lax.dynamic_slice_in_dim(mask[0], core * rows, rows),
                    lax.dynamic_slice_in_dim(mask[0], (1 - core) * rows, rows),
                ]
            )
            > 0
        )

    valids = (reorder(text_mask), reorder(visual_mask))

    pad = lane - heads - 2
    shard = jnp.concatenate(
        [own_columns(w_qkv, half, column * width) for column in range(3)]
        + [
            own_columns(w_gate, heads),
            gain_attn[..., None],
            gain_ffn[..., None],
            jnp.zeros(w_gate.shape[:2] + (pad,), low),
        ],
        2,
    )
    tokens = tuple(both(value) for value in own_tokens)
    grads_out = tuple(both(value) for value in own_grads)
    gather = lambda array: lax.all_gather(array, docs_axis, axis=1, tiled=True)
    rows_half = lambda array: lax.dynamic_slice_in_dim(
        array, core * (array.shape[1] // 2), array.shape[1] // 2, 1
    )
    full_qkv = gather(shard)
    full_up = gather(own_columns(w_up, w_up.shape[2] // 2))
    full_out, full_down = rows_half(gather(w_out)), rows_half(gather(w_down))
    gains_attn = full_qkv[:, :, 3 * half + heads].astype(full)
    gains_ffn = full_qkv[:, :, 3 * half + heads + 1].astype(full)

    fronts = []
    for s in range(2):
        normed, inverse = normalize(tokens[s].astype(full))
        lowered = (normed * gains_attn[s]).astype(low)
        wide = dot(lowered, full_qkv[s])
        narrow = wide[:, : 3 * half].astype(low)
        gates = jax.nn.sigmoid(wide[:, 3 * half : 3 * half + heads])
        queries, keys, values = (
            heads_of(narrow[:, column * half : (column + 1) * half], heads) for column in range(3)
        )
        fronts.append((normed, inverse, lowered, gates, queries, keys, values))

    outputs, totals = {}, {}
    for s in range(2):
        for t in range(2):
            outputs[s, t], totals[s, t] = attend(
                fronts[s][4], fronts[t][5], fronts[t][6], valids[t], scale
            )

    results, tails = [], []
    for s in range(2):
        gates = fronts[s][3][..., None]
        own, cross = outputs[s, s], outputs[s, 1 - s]
        mixed = gates * own + (1.0 - gates) * cross
        mix = mixed.reshape(mixed.shape[0], -1).astype(low)
        middle = own_tokens[s].astype(full) + own_sum(dot(mix, full_out[s]))
        normed, inverse = normalize(middle)
        lowered = both((normed * gains_ffn[s]).astype(low))
        upward = dot(lowered, full_up[s])
        activated, gelu_back = jax.vjp(jax.nn.gelu, upward)
        act = activated.astype(low)
        results.append((middle + own_sum(dot(act, full_down[s]))).astype(low))
        part_down = dot_rows(act, grads_out[s]).astype(low)
        grad_up = gelu_back(dot_back(grads_out[s], full_down[s]))[0].astype(low)
        part_up = dot_rows(lowered, grad_up).astype(low)
        grad_in, part_gain = normalize_back(
            own_sum(dot_back(grad_up, full_up[s])), normed, inverse, gains_ffn[s]
        )
        grad_middle = own_grads[s].astype(full) + grad_in
        grad_branch = both(grad_middle.astype(low))
        part_out = dot_rows(mix, grad_branch).astype(low)
        grad_mix = heads_of(dot_back(grad_branch, full_out[s]), heads)
        grad_gate = (
            jnp.sum(grad_mix * (own - cross), -1) * fronts[s][3] * (1.0 - fronts[s][3])
        ).astype(low)
        grad_own = (gates * grad_mix).astype(low)
        grad_cross = ((1.0 - gates) * grad_mix).astype(low)
        tails.append(
            (grad_middle, grad_gate, grad_own, grad_cross, part_out, part_up, part_down, part_gain)
        )

    backs = {}
    for s in range(2):
        for t in range(2):
            backs[s, t] = attend_back(
                fronts[s][4],
                fronts[t][5],
                fronts[t][6],
                valids[t],
                scale,
                totals[s, t],
                tails[s][2 if s == t else 3],
                outputs[s, t],
            )

    token_grads, parts_qkv = [], []
    for s in range(2):
        normed, inverse, lowered = fronts[s][:3]
        rows = lowered.shape[0]
        grad_q = backs[s, s][0] + backs[s, 1 - s][0]
        grad_k = backs[s, s][1] + backs[1 - s, s][1]
        grad_v = backs[s, s][2] + backs[1 - s, s][2]
        grad_wide = jnp.concatenate(
            [grad.reshape(rows, -1).astype(low) for grad in (grad_q, grad_k, grad_v)]
            + [tails[s][1], jnp.zeros((rows, lane - heads), low)],
            1,
        )
        part = dot_rows(lowered, grad_wide)
        own_rows = rows // 2
        grad_in, part_gain = normalize_back(
            own_sum(dot_back(grad_wide, full_qkv[s])),
            normed[:own_rows],
            inverse[:own_rows],
            gains_attn[s],
        )
        token_grads.append((tails[s][0] + grad_in)[None])
        parts_qkv.append(
            jnp.concatenate(
                [
                    part[:, : 3 * half + heads],
                    part_gain[:, None],
                    tails[s][7][:, None],
                    part[:, 3 * half + heads + 2 :],
                ],
                1,
            ).astype(low)
        )
    part_qkv = jnp.stack(parts_qkv)
    part_out, part_up, part_down = (
        jnp.stack([tails[0][at], tails[1][at]]) for at in (4, 5, 6)
    )
    scatter = lambda array: lax.psum_scatter(
        array.astype(full), docs_axis, scatter_dimension=1, tiled=True
    )

    def columns(own):
        other = swap(own)
        first = jnp.where(core == 0, own, other)
        second = jnp.where(core == 0, other, own)
        return first, second

    def rows_both(part):
        empty = jnp.zeros_like(part)
        first = jnp.where(core == 0, part, empty)
        second = jnp.where(core == 0, empty, part)
        return lax.psum(scatter(jnp.concatenate([first, second], 1)), core_axis)

    qkv_first, qkv_second = columns(scatter(part_qkv))
    grad_qkv = jnp.concatenate(
        [
            piece[:, :, column * half : (column + 1) * half]
            for column in range(3)
            for piece in (qkv_first, qkv_second)
        ],
        2,
    )
    small = jnp.stack([qkv_first[:, :, 3 * half :], qkv_second[:, :, 3 * half :]])
    grad_up = jnp.concatenate(columns(scatter(part_up)), 2)
    grad_out, grad_down = rows_both(part_out), rows_both(part_down)
    grad_gate = jnp.concatenate([small[0, :, :, :heads], small[1, :, :, :heads]], 2)
    gains = small[0] + small[1]
    return (
        results[0][None],
        results[1][None],
        token_grads[0],
        token_grads[1],
        grad_qkv,
        grad_out,
        grad_gate,
        grad_up,
        grad_down,
        gains[:, :, heads],
        gains[:, :, heads + 1],
    )


def solution(mesh):
    rows = P(docs_axis, core_axis, None)
    weights = P(None, docs_axis, None)
    gains = P(None, docs_axis)
    in_specs = (
        (rows, rows, P(docs_axis, None), P(docs_axis, None)) + (weights,) * 5 + (gains,) * 2 + (rows,) * 2
    )
    out_specs = (rows,) * 4 + (weights,) * 5 + (gains,) * 2
    return jax.shard_map(
        functools.partial(on_device, mesh.shape[docs_axis]),
        mesh=mesh,
        in_specs=in_specs,
        out_specs=out_specs,
        check_vma=False,
    )
```
